32 devices in a mesh: row: 4 (over y, core), seq: 8 (over z, x).
Axes of the slice: x: 2, y: 2, z: 4, core: 2. Of those that a mesh axis runs over, the one named last changes fastest.
Arguments:
- features: bfloat16 [8, 512, 768], P('row', 'seq'), may hold values from -6 to 6
- cotangent: bfloat16 [8, 512, 768], P('row', 'seq'), may hold values from -6 to 6
- segments: int32 [8, 512], P('row'), may hold values from 0 to 3, never falling along the last dimension, each value on 1 to 256 neighbouring positions
- stem_weight: bfloat16 [6144, 768], replicated, may hold values from -0.078125 to 0.078125
- projection_weight: bfloat16 [2, 768, 2304], replicated, may hold values from -0.21875 to 0.21875
- mixing_weight: bfloat16 [2, 768, 768], replicated, may hold values from -0.875 to 0.875
- feedforward_weight: bfloat16 [2, 768, 2, 3072], replicated, may hold values from -0.21875 to 0.21875
- norm_gains: float32 [5, 768], replicated, may hold values from 0.5 to 1.5
- biases: float32 [22, 768], replicated, may hold values from -3 to 3
- stem_moment: float32 [6144, 768], P('row', 'seq'), may hold values from -192 to 192
- projection_moment: float32 [2, 768, 2304], P(None, 'seq', 'row'), may hold values from -80 to 80
- mixing_moment: float32 [2, 768, 768], P(None, 'seq', 'row'), may hold values from -40 to 40
- feedforward_moment: float32 [2, 768, 2, 3072], P(None, 'seq', None, 'row'), may hold values from -192 to 192
- gain_moment: float32 [5, 768], P(None, 'seq'), may hold values from -256 to 256
- bias_moment: float32 [22, 768], P(None, 'seq'), may hold values from -384 to 384
- stem_average: float32 [6144, 768], P('row', 'seq'), may hold values from -0.078125 to 0.078125
- projection_average: float32 [2, 768, 2304], P(None, 'seq', 'row'), may hold values from -0.21875 to 0.21875
- mixing_average: float32 [2, 768, 768], P(None, 'seq', 'row'), may hold values from -0.875 to 0.875
- feedforward_average: float32 [2, 768, 2, 3072], P(None, 'seq', None, 'row'), may hold values from -0.21875 to 0.21875
- gain_average: float32 [5, 768], P(None, 'seq'), may hold values from 0.25 to 1.75
- bias_average: float32 [22, 768], P(None, 'seq'), may hold values from -3 to 3
Outputs:
- encoded: float32 [8, 512, 768], P('row', 'seq')
- features_gradient: float32 [8, 512, 768], P('row', 'seq')
- stem_momentum: float32 [6144, 768], P('row', 'seq')
- projection_momentum: float32 [2, 768, 2304], P(None, 'seq', 'row')
- mixing_momentum: float32 [2, 768, 768], P(None, 'seq', 'row')
- feedforward_momentum: float32 [2, 768, 2, 3072], P(None, 'seq', None, 'row')
- gain_momentum: float32 [5, 768], P(None, 'seq')
- bias_momentum: float32 [22, 768], P(None, 'seq')
- stem_averaged: float32 [6144, 768], P('row', 'seq')
- projection_averaged: float32 [2, 768, 2304], P(None, 'seq', 'row')
- mixing_averaged: float32 [2, 768, 768], P(None, 'seq', 'row')
- feedforward_averaged: float32 [2, 768, 2, 3072], P(None, 'seq', None, 'row')
- gain_averaged: float32 [5, 768], P(None, 'seq')
- bias_averaged: float32 [22, 768], P(None, 'seq')
- stem_updated: float32 [6144, 768], P('row', 'seq')
- projection_updated: float32 [2, 768, 2304], P(None, 'seq', 'row')
- mixing_updated: float32 [2, 768, 768], P(None, 'seq', 'row')
- feedforward_updated: float32 [2, 768, 2, 3072], P(None, 'seq', None, 'row')
- gain_updated: float32 [5, 768], P(None, 'seq')
- bias_updated: float32 [22, 768], P(None, 'seq')
The draws below stay inside these ranges and needn't reach their ends.
Inputs may be any that keep to these rules, and one draw needn't show every extreme that they name: `segments`: within a row the clip ids never fall; every clip spans 1 to 256 frames of one row.
All inputs are finite; a program needn't handle non-finite values.
Results may differ from the reference program's by a relative error of at most 0.02.
Values may be sent and summed in bfloat16 or wider, within the bound.
No kernel may reach another device: no remote copies, remote signals or barrier semaphores. Data moves between devices by JAX's collectives and lax.ppermute only.
A program may use at most 448 MiB of HBM per device.

```python
import math
import jax
import jax.numpy as jnp
import numpy as np
from jax import lax

D = 768
HEADS = 12
HEAD_DIM = 64
FF = 3072
KERNEL = 128
GROUPS = 16
LAYERS = 2
FRAMES = 512
ROWS = 8
SEGS = 4
SEG_MOST = 256


def strengthened(values, key, source, target, parts, factor):
    def block_of(position):
        return (jnp.arange(values.shape[position]) // (values.shape[position] // parts)).reshape((-1,) + (1,) * (values.ndim - 1 - position))

    near = jax.random.permutation(key, parts)[block_of(target)]
    other_side = (block_of(target) + parts // 2) % parts
    return jnp.where((block_of(source) == near) | (block_of(source) == other_side), factor * values, values)


def levels(key, dims, pieces, low, top_value):
    gain = 1.0
    for dim, blocks in pieces:
        draws = jax.random.uniform(jax.random.fold_in(jax.random.fold_in(key, 6), dim), (blocks,), jnp.float32, low / len(pieces), top_value / len(pieces))
        gain = gain * jnp.repeat(jnp.exp(draws), dims[dim] // blocks).reshape((-1,) + (1,) * (len(dims) - 1 - dim))
    return gain


def profile(count, total, limit, slope):
    weights = [(1 << 20) // math.isqrt(rank ** slope) + 1 for rank in range(2, count + 1)]
    rest, given = total - limit - (count - 1), [1] * (count - 1)
    while rest > 0:
        movable = [i for i in range(count - 1) if given[i] < limit]
        whole, left = sum([weights[i] for i in movable]), rest
        for i in movable:
            extra = min(limit - given[i], max(1, left * weights[i] // whole), rest)
            given[i] = given[i] + extra
            rest = rest - extra
    return np.array([limit] + given)


def ragged(own_key, count, total, most, lean):
    if count == 2:
        one = jax.random.randint(own_key, (), max(1, total - most), min(most, total - 1) + 1)
        return jnp.stack([one, total - one])
    tallies = jnp.asarray(profile(count, total, most, lean), jnp.int32)
    twos = (count - 1) // 2
    donor, taker = tallies[1:1 + 2 * twos:2], tallies[2:2 + 2 * twos:2]
    room = jnp.minimum(donor - 1, most - taker)
    passed = jax.random.randint(jax.random.fold_in(own_key, 1), (twos,), 0, 1 << 20) % (room + 1)
    tallies = tallies.at[1:1 + 2 * twos:2].set(donor - passed).at[2:2 + 2 * twos:2].set(taker + passed)
    return tallies[jax.random.permutation(jax.random.fold_in(own_key, 2), count)]


def bell_draw(own_key, extent, scale, reach, pieces=(), kind=jnp.bfloat16):
    values = scale * jax.random.normal(own_key, extent, jnp.float32)
    if pieces:
        values = values * levels(own_key, extent, pieces, -0.22, 0.18)
    return jnp.clip(values, -reach, reach).astype(kind)


def bell_draw_with(stream_key, dims, scale, limit, split, heavy, kind=jnp.bfloat16):
    array = scale * jax.random.normal(stream_key, dims, jnp.float32)
    if split:
        array = array * levels(stream_key, dims, split, -0.22, 0.18)
    return jnp.clip(strengthened(array, jax.random.fold_in(stream_key, 3), *heavy), -limit, limit).astype(kind)


def setup_inputs(seed: int = 0) -> dict:
    streams_of = jax.random.split(jax.random.key(seed), 22)
    return {
        "features": bell_draw(streams_of[0], (ROWS, FRAMES, D), 1.0, 6.0, ((0, 4), (1, 8))),
        "cotangent": bell_draw_with(streams_of[1], (ROWS, FRAMES, D), 1.0, 6.0, ((0, 4), (1, 8)), (1, 2, 8, 2.0)),
        "segments": jax.vmap(lambda own: jnp.searchsorted(jnp.cumsum(ragged(own, SEGS, FRAMES, SEG_MOST, 2)), jnp.arange(FRAMES), side="right"))(jax.random.split(streams_of[2], ROWS)).reshape((ROWS, FRAMES)).astype(jnp.int32),
        "stem_weight": bell_draw(streams_of[3], (KERNEL * D // GROUPS, D), (KERNEL * D // GROUPS) ** -0.5, 0.078125),
        "projection_weight": bell_draw(streams_of[4], (LAYERS, D, 3 * D), D ** -0.5, 0.21875),
        "mixing_weight": bell_draw(streams_of[5], (LAYERS, D, D), (D // 16) ** -0.5, 0.875),
        "feedforward_weight": bell_draw(streams_of[6], (LAYERS, D, 2, FF), D ** -0.5, 0.21875),
        "norm_gains": jnp.clip(1.0 + 0.1 * jax.random.normal(streams_of[7], (1 + 2 * LAYERS, D), jnp.float32), 0.5, 1.5),
        "biases": bell_draw(streams_of[8], (2 + LAYERS * (6 + FF // D), D), 0.2, 3.0, (), jnp.float32),
        "stem_moment": bell_draw(streams_of[9], (KERNEL * D // GROUPS, D), ((ROWS * FRAMES) ** 0.5 / 2), 192.0, ((0, 4), (1, 8)), jnp.float32),
        "projection_moment": bell_draw(streams_of[10], (LAYERS, D, 3 * D), ((ROWS * FRAMES) ** 0.5 / 5), 80.0, ((1, 8), (2, 4)), jnp.float32),
        "mixing_moment": bell_draw(streams_of[11], (LAYERS, D, D), ((ROWS * FRAMES) ** 0.5 / 10), 40.0, ((1, 8), (2, 4)), jnp.float32),
        "feedforward_moment": bell_draw(streams_of[12], (LAYERS, D, 2, FF), ((ROWS * FRAMES) ** 0.5 / 2), 192.0, ((1, 8), (3, 4)), jnp.float32),
        "gain_moment": bell_draw(streams_of[13], (1 + 2 * LAYERS, D), ((ROWS * FRAMES) ** 0.5 * 7 / 10), 256.0, ((1, 8),), jnp.float32),
        "bias_moment": bell_draw(streams_of[14], (2 + LAYERS * (6 + FF // D), D), ((ROWS * FRAMES) ** 0.5), 384.0, ((1, 8),), jnp.float32),
        "stem_average": bell_draw(streams_of[15], (KERNEL * D // GROUPS, D), (KERNEL * D // GROUPS) ** -0.5, 0.078125, ((0, 4), (1, 8)), jnp.float32),
        "projection_average": bell_draw(streams_of[16], (LAYERS, D, 3 * D), D ** -0.5, 0.21875, ((1, 8), (2, 4)), jnp.float32),
        "mixing_average": bell_draw(streams_of[17], (LAYERS, D, D), (D // 16) ** -0.5, 0.875, ((1, 8), (2, 4)), jnp.float32),
        "feedforward_average": bell_draw(streams_of[18], (LAYERS, D, 2, FF), D ** -0.5, 0.21875, ((1, 8), (3, 4)), jnp.float32),
        "gain_average": jnp.clip(0.25 + 1.5 * jax.random.uniform(streams_of[19], (1 + 2 * LAYERS, D), jnp.float32) ** levels(streams_of[19], (1 + 2 * LAYERS, D), ((1, 8),), -0.2, 0.2), 0.25, 1.75),
        "bias_average": bell_draw(streams_of[20], (2 + LAYERS * (6 + FF // D), D), 0.2, 3.0, ((1, 8),), jnp.float32),
    }


@jax.custom_vjp
def low(v):
    return lax.optimization_barrier(v.astype(jnp.bfloat16)).astype(jnp.float32)

@jax.custom_vjp
def low_back(v):
    return v

def low_keep(v):
    return (low(v), None)

def low_pass(kept, grad):
    return (grad,)

def back_keep(v):
    return (v, None)

def back_low(kept, grad):
    return (low(grad),)
low.defvjp(low_keep, low_pass)
low_back.defvjp(back_keep, back_low)
epsilon = 1e-05
masked_score = -1e+30
momentum_decay = 0.9
average_decay = 0.5
rate_factors = (0.012, 0.08, 0.6, 0.03, 0.06, 0.09)

def layer_norm(values, gain_row, shift_row):
    centre = lax.optimization_barrier(jnp.mean(values, axis=-1, keepdims=True))
    centred = values - centre
    spread = lax.optimization_barrier(jnp.mean(centred * centred, axis=-1, keepdims=True))
    return centred * lax.rsqrt(spread + epsilon) * gain_row + shift_row

def gelu_exact(values):
    return jax.nn.gelu(values, approximate=False)

def attention_rows(queries, keys, values, segments):
    row_count = queries.shape[0]
    query_block = math.gcd(FRAMES, 1024)
    query_heads = queries.reshape(row_count, FRAMES, HEADS, HEAD_DIM)
    key_heads = keys.reshape(row_count, FRAMES, HEADS, HEAD_DIM)
    value_heads = values.reshape(row_count, FRAMES, HEADS, HEAD_DIM)

    def one_row(row_items):
        query_row, key_row, value_row, segment_row = row_items

        def one_block(start):
            query_part = lax.dynamic_slice_in_dim(query_row, start, query_block, 0)
            segment_part = lax.dynamic_slice_in_dim(segment_row, start, query_block, 0)
            scores = low_back(jnp.einsum('qhe,khe->hqk', query_part, key_row, precision=lax.Precision.HIGHEST))
            allowed = segment_part[None, :, None] == segment_row[None, None, :]
            scores = jnp.where(allowed, scores, masked_score)
            log_sum = jax.nn.logsumexp(scores, axis=-1, keepdims=True)
            probability = low(jnp.exp(scores - log_sum))
            return jnp.einsum('hqk,khe->qhe', probability, value_row, precision=lax.Precision.HIGHEST)
        starts = jnp.arange(FRAMES // query_block, dtype=jnp.int32) * query_block
        blocks = lax.map(jax.checkpoint(one_block), starts)
        return blocks.reshape(FRAMES, HEADS * HEAD_DIM)
    return lax.map(one_row, (query_heads, key_heads, value_heads, segments))

def encode(inputs, stem, projection, mixing, feedforward, gains_all, biases_all, segments):
    group_width = D // GROUPS
    kernel_taps = stem.reshape(KERNEL, group_width, D)
    conv = lax.conv_general_dilated(inputs, kernel_taps, (1,), [(KERNEL // 2, KERNEL // 2 - 1)], dimension_numbers=('NWC', 'WIO', 'NWC'), feature_group_count=GROUPS, precision=lax.Precision.HIGHEST)
    pre_act = low_back(conv) + biases_all[0]
    hidden = layer_norm(inputs + gelu_exact(pre_act), gains_all[0], biases_all[1])
    score_scale = 1.0 / math.sqrt(HEAD_DIM)
    ff_rows = FF // D
    for layer_index in range(LAYERS):
        bias_base = 2 + layer_index * (6 + ff_rows)
        hidden_low = low(hidden)
        projected = jnp.einsum('rtd,de->rte', hidden_low, projection[layer_index], precision=lax.Precision.HIGHEST)
        queries = low(low_back((projected[..., :D] + biases_all[bias_base]) * score_scale))
        keys = low(low_back(projected[..., D:2 * D]))
        values = low(low_back(projected[..., 2 * D:] + biases_all[bias_base + 1]))
        attended = low(low_back(attention_rows(queries, keys, values, segments)))
        branch = low_back(jnp.einsum('rte,ed->rtd', attended, mixing[layer_index], precision=lax.Precision.HIGHEST)) + biases_all[bias_base + 2]
        first = layer_norm(hidden + branch, gains_all[1 + 2 * layer_index], biases_all[bias_base + 3])
        first_low = low(first)
        up_bias = biases_all[bias_base + 6:bias_base + 6 + ff_rows].reshape(FF)
        up_pre = low_back(jnp.einsum('rtd,dj->rtj', first_low, feedforward[layer_index, :, 0, :], precision=lax.Precision.HIGHEST)) + up_bias
        act_low = low(gelu_exact(up_pre))
        down = low_back(jnp.einsum('rtj,dj->rtd', act_low, feedforward[layer_index, :, 1, :], precision=lax.Precision.HIGHEST)) + biases_all[bias_base + 4]
        hidden = layer_norm(first + down, gains_all[2 + 2 * layer_index], biases_all[bias_base + 5])
    return hidden

def update_one(old_value, moment, average, gradient, factor):
    rate_base = 1.0 / math.sqrt(ROWS * FRAMES)
    moment_new = momentum_decay * moment + gradient
    weight_new = old_value - factor * rate_base * (gradient + momentum_decay * moment_new)
    average_new = average_decay * average + (1.0 - average_decay) * weight_new
    return (moment_new, average_new, weight_new)

def reference(features, cotangent, segments, stem_weight, projection_weight, mixing_weight, feedforward_weight, norm_gains, biases, stem_moment, projection_moment, mixing_moment, feedforward_moment, gain_moment, bias_moment, stem_average, projection_average, mixing_average, feedforward_average, gain_average, bias_average):
    stem_full = stem_weight.astype(jnp.float32)
    projection_full = projection_weight.astype(jnp.float32)
    mixing_full = mixing_weight.astype(jnp.float32)
    feedforward_full = feedforward_weight.astype(jnp.float32)

    def forward(inputs, stem, projection, mixing, feedforward, gains_all, biases_all):
        return encode(inputs, stem, projection, mixing, feedforward, gains_all, biases_all, segments)
    encoded, pullback = jax.vjp(forward, features.astype(jnp.float32), stem_full, projection_full, mixing_full, feedforward_full, norm_gains, biases)
    grads = pullback(cotangent.astype(jnp.float32))
    features_gradient = grads[0]
    stem_momentum, stem_averaged, stem_updated = update_one(stem_full, stem_moment, stem_average, grads[1], rate_factors[0])
    projection_momentum, projection_averaged, projection_updated = update_one(projection_full, projection_moment, projection_average, grads[2], rate_factors[1])
    mixing_momentum, mixing_averaged, mixing_updated = update_one(mixing_full, mixing_moment, mixing_average, grads[3], rate_factors[2])
    feedforward_momentum, feedforward_averaged, feedforward_updated = update_one(feedforward_full, feedforward_moment, feedforward_average, grads[4], rate_factors[3])
    gain_momentum, gain_averaged, gain_updated = update_one(norm_gains, gain_moment, gain_average, grads[5], rate_factors[4])
    bias_momentum, bias_averaged, bias_updated = update_one(biases, bias_moment, bias_average, grads[6], rate_factors[5])
    return (encoded, features_gradient, stem_momentum, projection_momentum, mixing_momentum, feedforward_momentum, gain_momentum, bias_momentum, stem_averaged, projection_averaged, mixing_averaged, feedforward_averaged, gain_averaged, bias_averaged, stem_updated, projection_updated, mixing_updated, feedforward_updated, gain_updated, bias_updated)
```

```python
import functools
import math

import jax
import jax.numpy as jnp
from jax import lax
from jax.experimental import pallas as pl
from jax.experimental.pallas import tpu as pltpu
from jax.sharding import Mesh
from jax.sharding import PartitionSpec as P

HEADS = 12
KERNEL = 128
GROUPS = 16


epsilon = 1e-05
masked_score = -1e30
momentum_decay = 0.9
average_decay = 0.5
rate_factors = (0.012, 0.08, 0.6, 0.03, 0.06, 0.09)
row_dims = (0, 2, 2, 3)


def extended_2(cells, sides, width):
    for axis, dim in sides:
        count = lax.axis_size(axis)
        ends = count - 1
        head = lax.slice_in_dim(cells, 0, width, axis=dim)
        tail = lax.slice_in_dim(cells, cells.shape[dim] - width, cells.shape[dim], axis=dim)
        cells = jnp.concatenate(
            [
                lax.ppermute(tail, axis, [(i, (i + 1) % count) for i in range(ends)]),
                cells,
                lax.ppermute(head, axis, [((i + 1) % count, i) for i in range(ends)]),
            ],
            axis=dim,
        )
    return cells


def layer_norm(values, gain_row, shift_row):
    centre = jnp.mean(values, axis=-1, keepdims=True)
    centred = values - centre
    spread = jnp.mean(centred * centred, axis=-1, keepdims=True)
    inverse = lax.rsqrt(spread + epsilon)
    normed = centred * inverse
    return (normed * gain_row + shift_row, normed, inverse)


def layer_norm_back(upstream, normed, inverse, gain_row):
    scaled = upstream * gain_row
    first_mean = jnp.mean(scaled, axis=-1, keepdims=True)
    second_mean = jnp.mean(scaled * normed, axis=-1, keepdims=True)
    downstream = inverse * (scaled - first_mean - normed * second_mean)
    return (downstream, jnp.sum(upstream * normed, axis=(0, 1)), jnp.sum(upstream, axis=(0, 1)))


def gelu_exact(values):
    return jax.nn.gelu(values, approximate=False)


def gelu_back(inputs, upstream):
    _, pullback = jax.vjp(gelu_exact, inputs)
    return pullback(upstream)[0]


def group_conv(extended, kernel_taps, group_count):
    return lax.conv_general_dilated(
        extended,
        kernel_taps,
        (1,),
        "VALID",
        dimension_numbers=("NWC", "WIO", "NWC"),
        feature_group_count=group_count,
        preferred_element_type=jnp.float32,
    )


def group_conv_kernel_grad(extended, upstream_low, group_count):
    return lax.conv_general_dilated(
        extended,
        upstream_low,
        (1,),
        "VALID",
        dimension_numbers=("CWN", "IWO", "WNC"),
        batch_group_count=group_count,
        preferred_element_type=jnp.float32,
    )


def flipped_taps(kernel_taps, group_count):
    tap_count, group_width, model_width = kernel_taps.shape
    split_taps = kernel_taps.reshape(tap_count, group_width, group_count, group_width)
    swapped = jnp.transpose(split_taps, (0, 3, 2, 1)).reshape(tap_count, group_width, model_width)
    return swapped[::-1]


def masked_scores(query_part, key_part, query_segments, key_segments):
    scores = jnp.einsum("rqhe,rkhe->rhqk", query_part, key_part, preferred_element_type=jnp.float32)
    allowed = query_segments[:, None, :, None] == key_segments[:, None, None, :]
    return jnp.where(allowed, scores, masked_score)


def key_slice(kv_whole, segments, start, key_block, head_count):
    row_count = kv_whole.shape[0]
    model_width = kv_whole.shape[2] // 2
    head_width = model_width // head_count
    part_rows = lax.dynamic_slice_in_dim(kv_whole, start, key_block, 1)
    part_segments = lax.dynamic_slice_in_dim(segments, start, key_block, 1)
    key_part = part_rows[:, :, :model_width].reshape(row_count, key_block, head_count, head_width)
    value_part = part_rows[:, :, model_width:].reshape(row_count, key_block, head_count, head_width)
    return (key_part, value_part, part_segments)


def attend(query_heads, kv_whole, query_segments, segments, head_count):
    row_count = query_heads.shape[0]
    tok_count = query_heads.shape[1]
    key_block = math.gcd(kv_whole.shape[1], 1024)
    block_count = kv_whole.shape[1] // key_block

    def stats_step(step_index, state):
        running_max, running_sum = state
        key_part, value_part, part_segments = key_slice(
            kv_whole, segments, step_index * key_block, key_block, head_count
        )
        scores = masked_scores(query_heads, key_part, query_segments, part_segments)
        new_max = jnp.maximum(running_max, jnp.max(scores, axis=-1))
        running_sum = running_sum * jnp.exp(running_max - new_max) + jnp.sum(
            jnp.exp(scores - new_max[..., None]), axis=-1
        )
        return (new_max, running_sum)

    start_state = (
        jnp.full((row_count, head_count, tok_count), masked_score, jnp.float32),
        jnp.zeros((row_count, head_count, tok_count), jnp.float32),
    )
    running_max, running_sum = lax.fori_loop(0, block_count, stats_step, start_state)
    log_sum = running_max + jnp.log(running_sum)

    def value_step(step_index, state):
        coarse, residue = state
        key_part, value_part, part_segments = key_slice(
            kv_whole, segments, step_index * key_block, key_block, head_count
        )
        probability = jnp.exp(
            masked_scores(query_heads, key_part, query_segments, part_segments) - log_sum[..., None]
        )
        probability_low = probability.astype(jnp.bfloat16)
        remainder_low = (probability - probability_low.astype(jnp.float32)).astype(jnp.bfloat16)
        coarse = coarse + jnp.einsum(
            "rhqk,rkhe->rqhe", probability_low, value_part, preferred_element_type=jnp.float32
        )
        residue = residue + jnp.einsum(
            "rhqk,rkhe->rqhe", remainder_low, value_part, preferred_element_type=jnp.float32
        )
        return (coarse, residue)

    zero_out = jnp.zeros(query_heads.shape, jnp.float32)
    coarse, residue = lax.fori_loop(0, block_count, value_step, (zero_out, zero_out))
    return (coarse, coarse + residue, log_sum)


def attend_back(
    query_heads, grad_heads, kv_whole, query_segments, segments, log_sum, delta, head_count
):
    row_count = query_heads.shape[0]
    frame_count = kv_whole.shape[1]
    model_width = kv_whole.shape[2] // 2
    key_block = math.gcd(frame_count, 1024)
    block_count = frame_count // key_block

    def back_step(step_index, state):
        grad_query, key_terms = state
        start = step_index * key_block
        key_part, value_part, part_segments = key_slice(
            kv_whole, segments, start, key_block, head_count
        )
        probability = jnp.exp(
            masked_scores(query_heads, key_part, query_segments, part_segments) - log_sum[..., None]
        )
        grad_prob = jnp.einsum(
            "rqhe,rkhe->rhqk", grad_heads, value_part, preferred_element_type=jnp.float32
        )
        grad_scores = (probability * (grad_prob - delta[..., None])).astype(jnp.bfloat16)
        grad_query = grad_query + jnp.einsum(
            "rhqk,rkhe->rqhe", grad_scores, key_part, preferred_element_type=jnp.float32
        )
        grad_keys = jnp.einsum(
            "rhqk,rqhe->rkhe", grad_scores, query_heads, preferred_element_type=jnp.float32
        )
        grad_values = jnp.einsum(
            "rhqk,rqhe->rkhe",
            probability.astype(jnp.bfloat16),
            grad_heads,
            preferred_element_type=jnp.float32,
        )
        both_terms = jnp.concatenate(
            [
                grad_keys.reshape(row_count, key_block, model_width),
                grad_values.reshape(row_count, key_block, model_width),
            ],
            axis=-1,
        )
        key_terms = lax.dynamic_update_slice_in_dim(key_terms, both_terms, start, 1)
        return (grad_query, key_terms)

    term_start = jnp.zeros((row_count, frame_count, 2 * model_width), jnp.float32)
    return lax.fori_loop(
        0, block_count, back_step, (jnp.zeros(query_heads.shape, jnp.float32), term_start)
    )


def local(
    features,
    cotangent,
    segments,
    stem_weight,
    projection_weight,
    mixing_weight,
    feedforward_weight,
    norm_gains,
    biases,
    stem_moment,
    projection_moment,
    mixing_moment,
    feedforward_moment,
    gain_moment,
    bias_moment,
    stem_average,
    projection_average,
    mixing_average,
    feedforward_average,
    gain_average,
    bias_average,
):
    row_count, tok_count, model_width = features.shape
    head_count = HEADS
    head_width = model_width // head_count
    group_count = GROUPS
    group_width = model_width // group_count
    tap_count = KERNEL
    half_taps = tap_count // 2
    layer_count = projection_weight.shape[0]
    ff_rows = feedforward_weight.shape[3] // model_width
    score_scale = 1.0 / math.sqrt(head_width)
    seq_index = lax.axis_index("seq")
    query_segments = lax.dynamic_slice_in_dim(segments, seq_index * tok_count, tok_count, 1)
    kernel_taps = stem_weight.reshape(tap_count, group_width, model_width)
    extended = extended_2(features, (("seq", 1),), half_taps)
    conv_input = extended[:, : tok_count + tap_count - 1]
    conv_pre = group_conv(conv_input, kernel_taps, group_count) + biases[0]
    summed = features.astype(jnp.float32) + gelu_exact(conv_pre)
    hidden, normed_stem, inverse_stem = layer_norm(summed, norm_gains[0], biases[1])
    saved_layers = []
    for layer_index in range(layer_count):
        bias_base = 2 + layer_index * (6 + ff_rows)
        hidden_low = hidden.astype(jnp.bfloat16)
        projected = jnp.einsum(
            "rtd,de->rte",
            hidden_low,
            projection_weight[layer_index],
            preferred_element_type=jnp.float32,
        )
        queries = ((projected[..., :model_width] + biases[bias_base]) * score_scale).astype(
            jnp.bfloat16
        )
        keys_low = projected[..., model_width : 2 * model_width].astype(jnp.bfloat16)
        values_low = (projected[..., 2 * model_width :] + biases[bias_base + 1]).astype(
            jnp.bfloat16
        )
        kv_local = jnp.concatenate([keys_low, values_low], axis=-1)
        kv_whole = lax.all_gather(kv_local, "seq", axis=1, tiled=True)
        query_heads = queries.reshape(row_count, tok_count, head_count, head_width)
        coarse, fine, log_sum = attend(query_heads, kv_whole, query_segments, segments, head_count)
        mixed_low = coarse.reshape(row_count, tok_count, model_width).astype(jnp.bfloat16)
        branch = (
            jnp.einsum(
                "rte,ed->rtd",
                mixed_low,
                mixing_weight[layer_index],
                preferred_element_type=jnp.float32,
            )
            + biases[bias_base + 2]
        )
        first_norm, normed_one, inverse_one = layer_norm(
            hidden + branch, norm_gains[1 + 2 * layer_index], biases[bias_base + 3]
        )
        first_low = first_norm.astype(jnp.bfloat16)
        up_bias = biases[bias_base + 6 : bias_base + 6 + ff_rows].reshape(-1)
        up_pre = (
            jnp.einsum(
                "rtd,dj->rtj",
                first_low,
                feedforward_weight[layer_index, :, 0, :],
                preferred_element_type=jnp.float32,
            )
            + up_bias
        )
        up_low = gelu_exact(up_pre).astype(jnp.bfloat16)
        down_out = (
            jnp.einsum(
                "rtj,dj->rtd",
                up_low,
                feedforward_weight[layer_index, :, 1, :],
                preferred_element_type=jnp.float32,
            )
            + biases[bias_base + 4]
        )
        hidden_next, normed_two, inverse_two = layer_norm(
            first_norm + down_out, norm_gains[2 + 2 * layer_index], biases[bias_base + 5]
        )
        saved_layers.append(
            (
                hidden_low,
                query_heads,
                kv_whole,
                log_sum,
                fine,
                mixed_low,
                normed_one,
                inverse_one,
                first_low,
                up_pre,
                up_low,
                normed_two,
                inverse_two,
            )
        )
        hidden = hidden_next
    upstream = cotangent.astype(jnp.float32)
    gain_grads = [None] * norm_gains.shape[0]
    bias_grads = [None] * biases.shape[0]
    projection_grads = [None] * layer_count
    mixing_grads = [None] * layer_count
    feedforward_grads = [None] * layer_count
    for layer_index in reversed(range(layer_count)):
        (
            hidden_low,
            query_heads,
            kv_whole,
            log_sum,
            fine,
            mixed_low,
            normed_one,
            inverse_one,
            first_low,
            up_pre,
            up_low,
            normed_two,
            inverse_two,
        ) = saved_layers[layer_index]
        bias_base = 2 + layer_index * (6 + ff_rows)
        in_matrix = projection_weight[layer_index]
        mix_matrix = mixing_weight[layer_index]
        up_matrix = feedforward_weight[layer_index, :, 0, :]
        down_matrix = feedforward_weight[layer_index, :, 1, :]
        grad_second, gain_grads[2 + 2 * layer_index], bias_grads[bias_base + 5] = layer_norm_back(
            upstream, normed_two, inverse_two, norm_gains[2 + 2 * layer_index]
        )
        bias_grads[bias_base + 4] = jnp.sum(grad_second, axis=(0, 1))
        down_low = grad_second.astype(jnp.bfloat16)
        grad_down = jnp.einsum("rtd,rtj->dj", down_low, up_low, preferred_element_type=jnp.float32)
        grad_act = jnp.einsum(
            "rtd,dj->rtj", down_low, down_matrix, preferred_element_type=jnp.float32
        )
        grad_up_pre = gelu_back(up_pre, grad_act)
        up_bias_grad = jnp.sum(grad_up_pre, axis=(0, 1)).reshape(ff_rows, model_width)
        for offset in range(ff_rows):
            bias_grads[bias_base + 6 + offset] = up_bias_grad[offset]
        up_grad_low = grad_up_pre.astype(jnp.bfloat16)
        grad_up = jnp.einsum(
            "rtd,rtj->dj", first_low, up_grad_low, preferred_element_type=jnp.float32
        )
        grad_first = grad_second + jnp.einsum(
            "rtj,dj->rtd", up_grad_low, up_matrix, preferred_element_type=jnp.float32
        )
        feedforward_grads[layer_index] = jnp.stack([grad_up, grad_down], axis=1)
        grad_resid, gain_grads[1 + 2 * layer_index], bias_grads[bias_base + 3] = layer_norm_back(
            grad_first, normed_one, inverse_one, norm_gains[1 + 2 * layer_index]
        )
        bias_grads[bias_base + 2] = jnp.sum(grad_resid, axis=(0, 1))
        branch_low = grad_resid.astype(jnp.bfloat16)
        mixing_grads[layer_index] = jnp.einsum(
            "rte,rtd->ed", mixed_low, branch_low, preferred_element_type=jnp.float32
        )
        grad_mixed = jnp.einsum(
            "rtd,ed->rte", branch_low, mix_matrix, preferred_element_type=jnp.float32
        )
        mixed_grad_low = grad_mixed.astype(jnp.bfloat16).reshape(
            row_count, tok_count, head_count, head_width
        )
        delta = jnp.transpose(
            jnp.sum(mixed_grad_low.astype(jnp.float32) * fine, axis=-1), (0, 2, 1)
        )
        grad_query, key_terms = attend_back(
            query_heads,
            mixed_grad_low,
            kv_whole,
            query_segments,
            segments,
            log_sum,
            delta,
            head_count,
        )
        grad_kv = lax.psum_scatter(key_terms, "seq", scatter_dimension=1, tiled=True)
        query_grad_low = grad_query.reshape(row_count, tok_count, model_width).astype(jnp.bfloat16)
        key_grad_low = grad_kv[..., :model_width].astype(jnp.bfloat16)
        value_grad_low = grad_kv[..., model_width:].astype(jnp.bfloat16)
        bias_grads[bias_base] = (
            jnp.sum(query_grad_low.astype(jnp.float32), axis=(0, 1)) * score_scale
        )
        bias_grads[bias_base + 1] = jnp.sum(value_grad_low.astype(jnp.float32), axis=(0, 1))
        grad_projected = jnp.concatenate(
            [query_grad_low * score_scale, key_grad_low, value_grad_low], axis=-1
        )
        projection_grads[layer_index] = jnp.einsum(
            "rtd,rte->de", hidden_low, grad_projected, preferred_element_type=jnp.float32
        )
        upstream = grad_resid + jnp.einsum(
            "rte,de->rtd", grad_projected, in_matrix, preferred_element_type=jnp.float32
        )
    grad_summed, gain_grads[0], bias_grads[1] = layer_norm_back(
        upstream, normed_stem, inverse_stem, norm_gains[0]
    )
    grad_conv = gelu_back(conv_pre, grad_summed)
    bias_grads[0] = jnp.sum(grad_conv, axis=(0, 1))
    conv_grad_low = grad_conv.astype(jnp.bfloat16)
    grad_extended = extended_2(conv_grad_low, (("seq", 1),), half_taps)
    features_gradient = grad_summed + group_conv(
        grad_extended[:, 1:], flipped_taps(kernel_taps, group_count), group_count
    )
    seq_count = lax.axis_size("seq")
    share_width = model_width // seq_count
    layer_partials = (
        jnp.stack(projection_grads),
        jnp.stack(mixing_grads),
        jnp.stack(feedforward_grads),
        jnp.stack(gain_grads),
        jnp.stack(bias_grads),
    )
    grad_stem = group_conv_kernel_grad(conv_input, conv_grad_low, group_count).reshape(
        tap_count * group_width, model_width
    )
    shares = (
        lax.psum_scatter(grad_stem, "seq", scatter_dimension=1, tiled=True),
        lax.psum_scatter(layer_partials[0], "seq", scatter_dimension=1, tiled=True),
        lax.psum_scatter(layer_partials[1], "seq", scatter_dimension=1, tiled=True),
        lax.psum_scatter(layer_partials[2], "seq", scatter_dimension=1, tiled=True),
        lax.psum_scatter(layer_partials[3], "seq", scatter_dimension=1, tiled=True),
        lax.psum_scatter(layer_partials[4], "seq", scatter_dimension=1, tiled=True),
    )
    matrix_totals = (
        lax.psum_scatter(
            shares[0].astype(jnp.bfloat16), "row", scatter_dimension=0, tiled=True
        ).astype(jnp.float32),
        lax.psum_scatter(
            shares[1].astype(jnp.bfloat16), "row", scatter_dimension=2, tiled=True
        ).astype(jnp.float32),
        lax.psum_scatter(
            shares[2].astype(jnp.bfloat16), "row", scatter_dimension=2, tiled=True
        ).astype(jnp.float32),
        lax.psum_scatter(
            shares[3].astype(jnp.bfloat16), "row", scatter_dimension=3, tiled=True
        ).astype(jnp.float32),
    )
    small_totals = lax.psum((shares[4], shares[5]), "row")
    totals = (
        matrix_totals[0],
        matrix_totals[1],
        matrix_totals[2],
        matrix_totals[3],
        small_totals[0],
        small_totals[1],
    )
    share_start = seq_index * share_width
    row_index = lax.axis_index("row")
    row_total = lax.axis_size("row")
    rate_base = 1.0 / math.sqrt(row_count * row_total * tok_count * seq_count)
    old_params = (
        stem_weight,
        projection_weight,
        mixing_weight,
        feedforward_weight,
        norm_gains,
        biases,
    )
    old_moments = (
        stem_moment,
        projection_moment,
        mixing_moment,
        feedforward_moment,
        gain_moment,
        bias_moment,
    )
    old_averages = (
        stem_average,
        projection_average,
        mixing_average,
        feedforward_average,
        gain_average,
        bias_average,
    )
    momenta = []
    averaged = []
    updated = []
    for param_index in range(6):
        old_share = lax.dynamic_slice_in_dim(old_params[param_index], share_start, share_width, 1)
        if param_index < 4:
            split_dim = row_dims[param_index]
            piece_size = old_share.shape[split_dim] // row_total
            old_share = lax.dynamic_slice_in_dim(
                old_share, row_index * piece_size, piece_size, split_dim
            )
        old_share = old_share.astype(jnp.float32)
        moment_new = momentum_decay * old_moments[param_index] + totals[param_index]
        weight_new = old_share - rate_factors[param_index] * rate_base * (
            totals[param_index] + momentum_decay * moment_new
        )
        momenta.append(moment_new)
        updated.append(weight_new)
        averaged.append(
            average_decay * old_averages[param_index] + (1.0 - average_decay) * weight_new
        )
    return (
        hidden,
        features_gradient,
        momenta[0],
        momenta[1],
        momenta[2],
        momenta[3],
        momenta[4],
        momenta[5],
        averaged[0],
        averaged[1],
        averaged[2],
        averaged[3],
        averaged[4],
        averaged[5],
        updated[0],
        updated[1],
        updated[2],
        updated[3],
        updated[4],
        updated[5],
    )


LANES = 128
PAIRS = 2
VMEM_BYTES = 48 * 1024 * 1024
bf16 = jnp.bfloat16
f32 = jnp.float32


def whole_call(kernel, outs, operands, scalars=0, scratch=(), flops=0, moved=0):
    in_specs = [
        pl.BlockSpec(memory_space=pltpu.SMEM if i < scalars else pltpu.VMEM)
        for i in range(len(operands))
    ]
    many = isinstance(outs, (list, tuple))
    out_specs = [pl.BlockSpec(memory_space=pltpu.VMEM) for _ in outs] if many else pl.BlockSpec(memory_space=pltpu.VMEM)
    shapes = list(outs) if many else [outs]
    size = sum(math.prod(o.shape) * o.dtype.itemsize for o in shapes) + sum(
        math.prod(o.shape) * o.dtype.itemsize for o in operands
    )
    return pl.pallas_call(
        kernel,
        out_shape=list(outs) if many else outs,
        in_specs=in_specs,
        out_specs=out_specs,
        scratch_shapes=list(scratch),
        compiler_params=pltpu.CompilerParams(vmem_limit_bytes=VMEM_BYTES),
        cost_estimate=pl.CostEstimate(flops=int(flops), bytes_accessed=int(size), transcendentals=0),
    )(*operands)


def sds(shape, dtype):
    return jax.ShapeDtypeStruct(shape, dtype)


def dot_nn(a, b):
    return lax.dot_general(a, b, (((1,), (0,)), ((), ())), preferred_element_type=f32)


def dot_nt(a, b):
    return lax.dot_general(a, b, (((1,), (1,)), ((), ())), preferred_element_type=f32)


def dot_tn(a, b):
    return lax.dot_general(a, b, (((0,), (0,)), ((), ())), preferred_element_type=f32)


def gelu_and_slope(v):
    cdf = 0.5 * (1.0 + lax.erf(v * math.sqrt(0.5)))
    return v * cdf, cdf + v * jnp.exp(-0.5 * v * v) * (1.0 / math.sqrt(2.0 * math.pi))


def lane_of(shape):
    return lax.broadcasted_iota(jnp.int32, shape, len(shape) - 1)


def piece_of(cols, j, width):
    off, v = (width * j) % LANES, (width * j) // LANES
    lane = lane_of(cols[0].shape)
    if off == 0:
        t = cols[v]
    else:
        t = pltpu.roll(cols[v], LANES - off, 1)
        if off + width > LANES:
            t = jnp.where(lane < LANES - off, t, pltpu.roll(cols[v + 1], LANES - off, 1))
    return jnp.where(lane < width, t, 0.0)


def tiles_of(pieces, width):
    count = len(pieces) * width // LANES
    cols = [None] * count

    def put(v, t):
        cols[v] = t if cols[v] is None else cols[v] + t

    for j, piece in enumerate(pieces):
        off, v = (width * j) % LANES, (width * j) // LANES
        if off == 0:
            put(v, piece)
            continue
        rolled = pltpu.roll(piece, off, 1)
        if off + width > LANES:
            lane = lane_of(piece.shape)
            put(v, jnp.where(lane >= off, rolled, 0.0))
            put(v + 1, jnp.where(lane < off, rolled, 0.0))
        else:
            put(v, rolled)
    return cols


def split_kernel(blocks, width, x_ref, o_ref):
    rows = x_ref.shape[0]
    for r in range(rows):
        x = x_ref[r].astype(f32)
        cols = [x[:, LANES * v : LANES * (v + 1)] for v in range(x.shape[1] // LANES)]
        for j in range(blocks):
            o_ref[j, r] = piece_of(cols, j, width).astype(bf16)


def taps_kernel(taps, gw, w_ref, o_ref):
    zero = jnp.zeros((LANES, LANES), bf16)
    o_ref[0] = zero
    o_ref[taps + 1] = zero
    o_ref[taps + 2] = zero

    def body(k, carry):
        w = w_ref[pl.ds(pl.multiple_of(k * gw, 16), gw), :]
        lane = lane_of(w.shape)
        o_ref[k + 1, 0:gw, :] = jnp.where(lane < gw, w, jnp.zeros_like(w))
        o_ref[k + 1, gw : 2 * gw, :] = jnp.where(lane >= gw, w, jnp.zeros_like(w))
        o_ref[k + 1, 2 * gw :, :] = jnp.zeros((LANES - 2 * gw, LANES), bf16)
        return carry

    lax.fori_loop(0, taps, body, 0)


def phases_from_frames(x_ref, xf, ph, rows, frames, half):
    blocks, block = x_ref.shape[0], x_ref.shape[2]
    span = frames + 2 * half
    for r in range(rows):
        xf[r * span : r * span + half, :] = jnp.zeros((half, LANES), f32)
        xf[r * span + half + frames : (r + 1) * span, :] = jnp.zeros((half, LANES), f32)
        for s in range(blocks):
            at = r * span + half + s * block
            xf[at : at + block, :] = x_ref[s, r].astype(f32)
    for p in range(16):
        n = (span // 2) if p == 0 else (span // 2 - 16)
        for r in range(rows):
            for b in range(2):
                ph[p, r, 0:n, b * LANES : (b + 1) * LANES] = xf[
                    pl.ds(r * span + 2 * p + b, n, stride=2), :
                ].astype(bf16)


def window(ph, m, rows, n):
    p, a = lax.rem(m, 16), m // 16
    part = ph[p, :, pl.ds(pl.multiple_of(a * 16, 16), n), :]
    return part.reshape(rows * n, part.shape[-1])


def conv_kernel(rows, frames, half, c_ref, x_ref, w_ref, b_ref, pre_ref, keep_ref, send_ref, ph_ref, xf, acc):
    n = frames // 2
    phases_from_frames(x_ref, xf, ph_ref, rows, frames, half)
    acc[...] = jnp.zeros_like(acc)

    def body(i, carry):
        total = None
        for t in range(5):
            m = i * 5 + t
            here, before, after = w_ref[2 * m + 1], w_ref[2 * m], w_ref[2 * m + 2]
            rhs = jnp.concatenate(
                [jnp.concatenate([here, before], 1), jnp.concatenate([after, here], 1)], 0
            )
            part = dot_nn(window(ph_ref, m, rows, n), rhs)
            total = part if total is None else total + part
        acc[...] += total
        return carry

    lax.fori_loop(0, (half + 1) // 5, body, 0)
    bias = jnp.concatenate([b_ref[...], b_ref[...]], 1)
    c = c_ref[1]
    for r in range(rows):
        pre = acc[r * n : (r + 1) * n, :] + bias
        pre_ref[r] = pre
        x = ph_ref[0, r, half // 2 : half // 2 + n, :].astype(f32)
        s = (x + gelu_and_slope(pre)[0]).astype(bf16)
        for zf in range(4):
            for xq in range(2):
                for cf in range(2):
                    u = ((zf * 2 + xq) * 2 + cf) * 16
                    blk = s[u : u + 16, :]

                    @pl.when(c == cf)
                    def _(blk=blk, r=r, xq=xq, zf=zf):
                        keep_ref[r, xq, zf * 16 : zf * 16 + 16, :] = blk

                    @pl.when(c != cf)
                    def _(blk=blk, r=r, xq=xq, zf=zf):
                        send_ref[r, xq, zf * 16 : zf * 16 + 16, :] = blk


def normed(values):
    centre = jnp.mean(values, axis=-1, keepdims=True)
    centred = values - centre
    spread = jnp.mean(centred * centred, axis=-1, keepdims=True)
    inverse = lax.rsqrt(spread + epsilon)
    return centred * inverse, inverse


def stem_norm_kernel(width, r_ref, g_ref, b_ref, h_ref, low_ref, n_ref, i_ref):
    halves = []
    for a in range(2):
        pieces = [r_ref[j, :, a * LANES : (a + 1) * LANES].astype(f32) for j in range(r_ref.shape[0])]
        halves.append(jnp.concatenate(tiles_of(pieces, width), axis=1))
    s = jnp.concatenate(halves, axis=0)
    n, inv = normed(s)
    h = n * g_ref[0:1, :] + b_ref[1:2, :]
    h_ref[...] = h
    low_ref[...] = h.astype(bf16)
    n_ref[...] = n
    i_ref[...] = inv


def attend_kernel(base, hl0, hl1, hl2, hl3, w_ref, m_ref, bq_ref, segr, segc,
                  q_ref, k_ref, v_ref, at_ref, lse_ref, keep_ref, send_ref):
    t = hl0.shape[0]
    hl = jnp.concatenate([hl0[...], hl1[...], hl2[...], hl3[...]], axis=0)
    proj = dot_nn(hl, w_ref[...])
    q = ((proj[:, 0:256] + bq_ref[0:1, :]) * 0.125).astype(bf16)
    k = proj[:, 256:512].astype(bf16)
    v = (proj[:, 512:768] + bq_ref[1:2, :]).astype(bf16)
    q_ref[...] = q
    k_ref[...] = k
    v_ref[...] = v
    allowed = segc[...] == segr[...]
    lane = lane_of((1, LANES))
    parts = []
    for head in range(3):
        tile = head // 2
        cols = slice(tile * LANES, (tile + 1) * LANES)
        mine = (lane < 64) if head % 2 == 0 else (lane >= 64)
        qh = jnp.where(mine, q[:, cols], jnp.zeros((), bf16))
        s = dot_nt(qh, k[:, cols])
        s = jnp.where(allowed, s, masked_score)
        top = jnp.max(s, axis=-1, keepdims=True)
        e = jnp.exp(s - top)
        total = jnp.sum(e, axis=-1, keepdims=True)
        lse_ref[head] = top + jnp.log(total)
        p = (e * (1.0 / total)).astype(bf16)
        parts.append(dot_nn(p, v[:, cols]))
    att = jnp.concatenate([jnp.where(lane < 64, parts[0], parts[1]), parts[2]], axis=1).astype(bf16)
    at_ref[...] = att
    branch = dot_nn(att, m_ref[...]).astype(bf16)
    for dx in range(2):
        keep_ref[dx] = branch[2 * dx * t : (2 * dx + 1) * t]
        send_ref[dx] = branch[(2 * dx + 1) * t : (2 * dx + 2) * t]


def half_sum_kernel(a_ref, b_ref, own_ref, send_ref):
    own_ref[...] = a_ref[0].astype(f32) + b_ref[0].astype(f32)
    send_ref[...] = (a_ref[1].astype(f32) + b_ref[1].astype(f32)).astype(bf16)


def norm_kernel(gain_row, bias_row, shift_row, h_ref, a_ref, r_ref, g_ref, b_ref, o_ref, low_ref, n_ref, i_ref):
    v = h_ref[...] + (a_ref[...].astype(f32) + r_ref[...].astype(f32) + b_ref[bias_row : bias_row + 1, :])
    n, inv = normed(v)
    o = n * g_ref[gain_row : gain_row + 1, :] + b_ref[shift_row : shift_row + 1, :]
    o_ref[...] = o
    low_ref[...] = o.astype(bf16)
    n_ref[...] = n
    i_ref[...] = inv


def feed_kernel(f0, f1, u0, u1, d0, d1, b_ref, act_ref, slope_ref, own_ref, send_ref):
    t = f0.shape[0]
    first = jnp.concatenate([f0[...], f1[...]], axis=0)
    total = None
    for i, (u, d) in enumerate(((u0, d0), (u1, d1))):
        up = dot_nn(first, u[...]) + b_ref[i : i + 1, :]
        act, slope = gelu_and_slope(up)
        act = act.astype(bf16)
        act_ref[i] = act
        slope_ref[i] = slope.astype(bf16)
        part = dot_nt(act, d[...])
        total = part if total is None else total + part
    own_ref[...] = total[:t]
    send_ref[...] = total[t:].astype(bf16)


def norm_back(g, n, inv, gain):
    scaled = g * gain
    m1 = jnp.mean(scaled, axis=-1, keepdims=True)
    m2 = jnp.mean(scaled * n, axis=-1, keepdims=True)
    return inv * (scaled - m1 - n * m2)


def norm_sums(g, n, d, o_ref):
    o_ref[0:1, :] = jnp.sum(g * n, axis=0, keepdims=True)
    o_ref[1:2, :] = jnp.sum(g, axis=0, keepdims=True)
    o_ref[2:3, :] = jnp.sum(d, axis=0, keepdims=True)
    o_ref[3:8, :] = jnp.zeros((5, o_ref.shape[1]), f32)


def norm_back_kernel(gain_row, count, *refs):
    given, (g_ref, n_ref, i_ref, d_ref, low_ref, s_ref) = refs[:count], refs[count:]
    g = given[0][...].astype(f32)
    for r in given[1:]:
        g = g + r[...].astype(f32)
    n = n_ref[...]
    d = norm_back(g, n, i_ref[...], g_ref[gain_row : gain_row + 1, :])
    d_ref[...] = d
    low_ref[...] = d.astype(bf16)
    norm_sums(g, n, d, s_ref)


def stem_norm_back_kernel(width, count, *refs):
    given, (g_ref, n_ref, i_ref, o_ref, s_ref) = refs[:count], refs[count:]
    g = given[0][...].astype(f32)
    for r in given[1:]:
        g = g + r[...].astype(f32)
    n = n_ref[...]
    d = norm_back(g, n, i_ref[...], g_ref[0:1, :])
    norm_sums(g, n, d, s_ref)
    t = d.shape[0] // 2
    for a in range(2):
        part = d[a * t : (a + 1) * t]
        cols = [part[:, LANES * v : LANES * (v + 1)] for v in range(part.shape[1] // LANES)]
        for j in range(o_ref.shape[0]):
            o_ref[j, :, a * LANES : (a + 1) * LANES] = piece_of(cols, j, width).astype(bf16)


def feed_back_kernel(e0, e1, u0, u1, d0, d1, slope_ref, dup_ref, own_ref, send_ref, bias_ref):
    t = e0.shape[0]
    d2 = jnp.concatenate([e0[...], e1[...]], axis=0)
    total = None
    for i, (u, d) in enumerate(((u0, d0), (u1, d1))):
        dup = dot_nn(d2, d[...]) * slope_ref[i].astype(f32)
        bias_ref[i : i + 1, :] = jnp.sum(dup, axis=0, keepdims=True)
        dup = dup.astype(bf16)
        dup_ref[i] = dup
        part = dot_nt(dup, u[...])
        total = part if total is None else total + part
    bias_ref[2:8, :] = jnp.zeros((6, bias_ref.shape[1]), f32)
    own_ref[...] = total[:t]
    send_ref[...] = total[t:].astype(bf16)


def feed_grad_kernel(place, f0, f1, e0, e1, act_ref, dup_ref, keep_ref, send_ref):
    z, x = place[2], place[3]
    width = keep_ref.shape[3]
    first = jnp.concatenate([f0[...], f1[...]], axis=0)
    d2 = jnp.concatenate([e0[...], e1[...]], axis=0)
    for i, out in enumerate((keep_ref, send_ref)):
        for kind, (a, b) in enumerate(((first, dup_ref[i]), (d2, act_ref[i]))):
            g = dot_tn(a, b).astype(bf16)
            for j in range(8):
                zi, xi = j // 2, j % 2
                out[zi ^ z, xi ^ x, kind] = g[j * width : (j + 1) * width]


def attend_back_kernel(e0, e1, e2, e3, q_ref, k_ref, v_ref, lse_ref, w_ref, m_ref, segr, segc,
                       dp_ref, dc_ref, keep_ref, send_ref, bias_ref):
    t = e0.shape[0]
    d1 = jnp.concatenate([e0[...], e1[...], e2[...], e3[...]], axis=0)
    da = dot_nt(d1, m_ref[...]).astype(bf16)
    q, k, v = q_ref[...], k_ref[...], v_ref[...]
    allowed = segc[...] == segr[...]
    lane = lane_of((1, LANES))
    dq, dk, dv = [None] * 2, [None] * 2, [None] * 2
    for head in range(3):
        tile = head // 2
        cols = slice(tile * LANES, (tile + 1) * LANES)
        mine = (lane < 64) if head % 2 == 0 else (lane >= 64)
        zero = jnp.zeros((), bf16)
        qh = jnp.where(mine, q[:, cols], zero)
        dah = jnp.where(mine, da[:, cols], zero)
        s = dot_nt(qh, k[:, cols])
        p = jnp.where(allowed, jnp.exp(s - lse_ref[head]), 0.0)
        dp = dot_nt(dah, v[:, cols])
        delta = jnp.sum(p * dp, axis=-1, keepdims=True)
        ds = (p * (dp - delta)).astype(bf16)
        a = dot_nn(ds, jnp.where(mine, k[:, cols], zero))
        b = dot_tn(ds, qh)
        c = dot_tn(p.astype(bf16), dah)
        for held, new in ((dq, a), (dk, b), (dv, c)):
            held[tile] = new if held[tile] is None else held[tile] + new
    dq = [(d.astype(bf16) * jnp.array(0.125, bf16)).astype(f32) for d in dq]
    dk = [d.astype(bf16).astype(f32) for d in dk]
    dv = [d.astype(bf16).astype(f32) for d in dv]
    wide = jnp.concatenate(dq + dk + dv, axis=1).astype(bf16)
    dp_ref[...] = wide
    bias_ref[0:1, :] = jnp.concatenate([jnp.sum(d, axis=0, keepdims=True) for d in dq], axis=1)
    bias_ref[1:2, :] = jnp.concatenate([jnp.sum(d, axis=0, keepdims=True) for d in dv], axis=1)
    bias_ref[2:8, :] = jnp.zeros((6, 256), f32)
    k01 = pltpu.roll(dk[0], 64, 1)
    dense = [dq[0], jnp.where(lane < 64, dq[1], k01), jnp.where(lane < 64, k01, pltpu.roll(dk[1], 64, 1)), dv[0], dv[1]]
    dc_ref[...] = jnp.concatenate(dense, axis=1).astype(bf16)
    out = dot_nt(wide, w_ref[...]).astype(bf16)
    for dx in range(2):
        keep_ref[dx] = out[2 * dx * t : (2 * dx + 1) * t]
        send_ref[dx] = out[(2 * dx + 1) * t : (2 * dx + 2) * t]


def attend_grad_kernel(place, hl0, hl1, hl2, hl3, e0, e1, e2, e3, at_ref, dc_ref, o_ref, m_ref):
    z, x = place[2], place[3]
    hl = jnp.concatenate([hl0[...], hl1[...], hl2[...], hl3[...]], axis=0)
    d1 = jnp.concatenate([e0[...], e1[...], e2[...], e3[...]], axis=0)
    g = dot_tn(hl, dc_ref[...]).astype(bf16)
    width = o_ref.shape[2]
    for j in range(8):
        zi, xi = j // 2, j % 2
        o_ref[zi ^ z, xi ^ x] = g[j * width : (j + 1) * width]
    m_ref[...] = dot_tn(at_ref[...], d1)[0 : m_ref.shape[0]].astype(bf16)


def stem_slope_kernel(rows, place, keep_ref, recv_ref, pre_ref, low_ref, ds_ref, bias_ref):
    c = place[1]
    for r in range(rows):
        for zf in range(4):
            for xq in range(2):
                for rel, src in enumerate((keep_ref, recv_ref)):
                    u = pl.multiple_of(((zf * 2 + xq) * 2 + (c ^ rel)) * 16, 16)
                    ds_ref[r, pl.ds(u, 16), :] = src[r, xq, zf * 16 : zf * 16 + 16, :]
    total = None
    for r in range(rows):
        dpre = ds_ref[r].astype(f32) * gelu_and_slope(pre_ref[r])[1]
        part = jnp.sum(dpre, axis=0, keepdims=True)
        total = part if total is None else total + part
        low_ref[r] = dpre.astype(bf16)
    bias_ref[0:1, :] = total[:, 0:LANES] + total[:, LANES : 2 * LANES]
    bias_ref[1:8, :] = jnp.zeros((7, LANES), f32)


def stem_grad_kernel(rows, taps, gw, place, ph_ref, low_ref, keep_ref, send_ref):
    n = low_ref.shape[1]
    y, c = place[0], place[1]
    left = jnp.concatenate([low_ref[r] for r in range(rows)], axis=0).T
    lane = lane_of((gw, LANES))
    per = taps // 4
    for rc, out in enumerate((keep_ref, send_ref)):
        for ry in range(2):
            block = (y ^ ry) * 2 + (c ^ rc)

            def win(i):
                at = pl.multiple_of((block + i // 16) * 16, 16)
                return ph_ref[i % 16, :, pl.ds(at, n), :].reshape(rows * n, 2 * LANES)

            def save(k, t, out=out, ry=ry):
                out[ry, k * gw : (k + 1) * gw, :] = jnp.where(lane < gw, t[0:gw], t[gw : 2 * gw]).astype(bf16)

            held = None
            for i in range(per // 2 + 1):
                if i < per // 2:
                    g = dot_nn(left, win(i))
                    cross = g[LANES:, 0:LANES]
                else:
                    cross = dot_nn(left[LANES:], win(i)[:, 0:LANES])
                if held is not None:
                    save(2 * i - 1, held + cross)
                if i < per // 2:
                    save(2 * i, g[0:LANES, 0:LANES] + g[LANES:, LANES:])
                    held = g[0:LANES, LANES:]


def stem_input_grad_kernel(rows, half, low_ref, ds_ref, w_ref, o_ref, qf, ph, acc):
    n = low_ref.shape[1]
    span = n + half
    for r in range(rows):
        qf[r, 0 : half // 2, :] = jnp.zeros((half // 2, 2 * LANES), f32)
        qf[r, half // 2 + n :, :] = jnp.zeros((half // 2, 2 * LANES), f32)
        qf[r, half // 2 : half // 2 + n, :] = low_ref[r].astype(f32)
    for p in range(16):
        m = span if p == 0 else span - 16
        for r in range(rows):
            ph[p, r, 0:m, :] = qf[r, p : p + m, :].astype(bf16)
    acc[...] = jnp.zeros_like(acc)

    def body(i, carry):
        total = None
        for t in range(5):
            m = i * 5 + t
            here, before, after = w_ref[2 * half + 1 - 2 * m], w_ref[2 * half - 2 * m], w_ref[2 * half + 2 - 2 * m]
            rhs = jnp.concatenate(
                [jnp.concatenate([here, before], 1), jnp.concatenate([after, here], 1)], 0
            )
            part = dot_nt(window(ph, m, rows, n), rhs)
            total = part if total is None else total + part
        acc[...] += total
        return carry

    lax.fori_loop(0, (half + 1) // 5, body, 0)
    per = n // o_ref.shape[0]
    for r in range(rows):
        g = (acc[r * n : (r + 1) * n, :] + ds_ref[r].astype(f32)).astype(bf16)
        for j in range(o_ref.shape[0]):
            o_ref[j, r] = g[j * per : (j + 1) * per, :]


def join_kernel(width, r_ref, o_ref, mixed):
    blocks, rows, per = r_ref.shape[0], r_ref.shape[1], r_ref.shape[2]
    for r in range(rows):
        for a in range(2):
            pieces = [r_ref[j, r, :, a * LANES : (a + 1) * LANES].astype(f32) for j in range(blocks)]
            for v, col in enumerate(tiles_of(pieces, width)):
                mixed[pl.ds(v * 2 * per + a, per, stride=2), :] = col
        for v in range(o_ref.shape[2] // LANES):
            o_ref[r, :, v * LANES : (v + 1) * LANES] = mixed[v * 2 * per : (v + 1) * 2 * per, :]


def swapped(v, axis):
    return lax.ppermute(v, axis, [(0, 1), (1, 0)])


def across(v, axis, bit):
    count = lax.axis_size(axis)
    return lax.ppermute(v, axis, [(i, i ^ bit) for i in range(count)])


def plus(a, b):
    return (a.astype(f32) + b.astype(f32)).astype(bf16)


def halved_z(v):
    v = plus(v[0::2], across(v[1::2], "z", 1))
    return plus(v[0], across(v[1], "z", 2))


def local_rows(
    features, cotangent, segments, stem_weight, projection_weight, mixing_weight,
    feedforward_weight, norm_gains, biases, *state,
):
    rows, toks, width = features.shape
    yi, ci, zi, xi = (lax.axis_index(a) for a in ("y", "c", "z", "x"))
    place = jnp.stack([yi, ci, zi, xi]).astype(jnp.int32)
    seq_i, row_i = zi * 2 + xi, yi * 2 + ci
    seq = ("z", "x")
    blocks = 8
    share = width // blocks
    gw = width // GROUPS
    frames = toks * blocks
    half = KERNEL // 2
    layers = projection_weight.shape[0]
    ff_rows = feedforward_weight.shape[3] // width
    head_share = width // 4
    group = 2 * xi + ci
    t = rows * toks

    stem_share = jnp.pad(
        lax.dynamic_slice_in_dim(stem_weight, seq_i * share, share, 1), ((0, 0), (0, LANES - share))
    )
    taps = whole_call(
        functools.partial(taps_kernel, KERNEL, gw), sds((KERNEL + 3, LANES, LANES), bf16), [stem_share]
    )

    def attend_weights(l):
        parts = []
        for i in range(3):
            part = lax.dynamic_slice(
                projection_weight, (l, 0, i * width + group * head_share), (1, width, head_share)
            )[0]
            parts.append(jnp.pad(part, ((0, 0), (0, 256 - head_share))))
        mix = lax.dynamic_slice(mixing_weight, (l, group * head_share, 0), (1, head_share, width))[0]
        base = 2 + l * (6 + ff_rows)
        both = lax.dynamic_slice(biases, (base, group * head_share), (2, head_share))
        return (
            jnp.concatenate(parts, axis=1),
            jnp.pad(mix, ((0, 256 - head_share), (0, 0))),
            jnp.pad(both, ((0, 0), (0, 256 - head_share))),
        )

    def feed_weights(l):
        ups, downs, ids = [], [], []
        base = 2 + l * (6 + ff_rows)
        for ry in range(2):
            block = 2 * (yi ^ ry) + ci
            part = lax.dynamic_slice(
                feedforward_weight, (l, 0, 0, block * width), (1, width, 2, width)
            )[0]
            ups.append(part[:, 0, :])
            downs.append(part[:, 1, :])
            ids.append(lax.dynamic_slice_in_dim(biases, base + 6 + block, 1, 0))
        return ups, downs, jnp.concatenate(ids, axis=0)

    other = swapped(segments, "c")
    four = jnp.where(ci == 0, jnp.concatenate([segments, other]), jnp.concatenate([other, segments]))
    row_ids = lax.dynamic_index_in_dim(four, zi, 0, keepdims=False)
    row_ids = row_ids.reshape(4, 2, 2, 16, 2).transpose(1, 2, 4, 0, 3)
    row_ids = jnp.where(xi == 0, row_ids, row_ids[::-1])
    row_ids = jnp.where(ci == 0, row_ids, row_ids[:, ::-1]).reshape(-1)
    seg_row, seg_col = row_ids[None, :], row_ids[:, None]

    sent = whole_call(
        functools.partial(split_kernel, blocks, share), sds((blocks, rows, toks, LANES), bf16), [features]
    )
    mine = lax.all_to_all(sent, seq, 0, 0, tiled=True)
    conv_bias = jnp.pad(
        lax.dynamic_slice(biases, (0, seq_i * share), (1, share)), ((0, 0), (0, LANES - share))
    )
    n = frames // 2
    exchange = sds((rows, 2, 64, 2 * LANES), bf16)
    pre_act, kept, away, phases = whole_call(
        functools.partial(conv_kernel, rows, frames, half),
        [sds((rows, n, 2 * LANES), f32), exchange, exchange, sds((16, rows, (frames + 2 * half) // 2, 2 * LANES), bf16)],
        [place, mine, taps, conv_bias],
        scalars=1,
        scratch=[pltpu.VMEM((rows * (frames + 2 * half), LANES), f32), pltpu.VMEM((rows * n, 2 * LANES), f32)],
        flops=2 * rows * n * 256 * 256 * 65,
    )
    came = swapped(away, "c")
    slots = jnp.where(ci == 0, jnp.concatenate([kept, came]), jnp.concatenate([came, kept]))
    joined = lax.all_to_all(slots.reshape(blocks, 64, 2 * LANES), seq, 0, 0, tiled=True)
    wide = sds((t, width), f32)
    thin = sds((t, width), bf16)
    column = sds((t, 1), f32)
    hidden, hidden_low, normed_stem, inverse_stem = whole_call(
        functools.partial(stem_norm_kernel, share), [wide, thin, wide, column], [joined, norm_gains, biases]
    )

    def gathered(v):
        over_c = swapped(v, "c")
        over_x = swapped(v, "x")
        return [v, over_c, over_x, swapped(over_x, "c")]

    def summed(keep, send):
        own, pass_on = whole_call(half_sum_kernel, [wide, thin], [keep, swapped(send, "c")])
        return own, swapped(pass_on, "x")

    saved = []
    two = sds((2, t, width), bf16)
    full = 4 * t
    for l in range(layers):
        base = 2 + l * (6 + ff_rows)
        in_w, mix_w, both_b = attend_weights(l)
        ups, downs, up_b = feed_weights(l)
        hl = gathered(hidden_low)
        q, k, v, att, lse, keep, send = whole_call(
            functools.partial(attend_kernel, base),
            [sds((full, 256), bf16)] * 4 + [sds((3, full, 1), f32), two, two],
            hl + [in_w, mix_w, both_b, seg_row, seg_col],
            flops=2 * full * (768 * 768 + 256 * 768 + 3 * full * 256),
        )
        own, rest = summed(keep, send)
        first, first_low, n1, i1 = whole_call(
            functools.partial(norm_kernel, 1 + 2 * l, base + 2, base + 3),
            [wide, thin, wide, column],
            [hidden, own, rest, norm_gains, biases],
        )
        first_other = swapped(first_low, "c")
        act, slope, own, send = whole_call(
            feed_kernel,
            [sds((2, 2 * t, width), bf16)] * 2 + [wide, thin],
            [first_low, first_other, *ups, *downs, up_b],
            flops=2 * 2 * t * width * width * 4,
        )
        hidden, hidden_low, n2, i2 = whole_call(
            functools.partial(norm_kernel, 2 + 2 * l, base + 4, base + 5),
            [wide, thin, wide, column],
            [first, own, swapped(send, "c"), norm_gains, biases],
        )
        saved.append((in_w, mix_w, ups, downs, hl, q, k, v, att, lse, n1, i1, first_low, first_other, act, slope, n2, i2))

    by_z = hidden.astype(bf16).reshape(2, 4, 16, width).transpose(1, 2, 0, 3).reshape(4, 32, width)
    by_z = lax.all_to_all(by_z, "z", 0, 0, tiled=True).reshape(2, 2, 32, width)
    stay = lax.dynamic_index_in_dim(by_z, ci, 0, keepdims=False)
    move = swapped(lax.dynamic_index_in_dim(by_z, 1 - ci, 0, keepdims=False), "c")
    encoded = jnp.where(ci == 0, jnp.stack([stay, move], 1), jnp.stack([move, stay], 1))
    encoded = encoded.reshape(rows, toks, width).astype(f32)

    cot = cotangent.reshape(rows, 2, 16, 2, width).transpose(1, 0, 3, 2, 4)
    stay = lax.dynamic_index_in_dim(cot, ci, 0, keepdims=False)
    move = swapped(lax.dynamic_index_in_dim(cot, 1 - ci, 0, keepdims=False), "c")
    cot = jnp.where(ci == 0, jnp.concatenate([stay, move]), jnp.concatenate([move, stay]))
    cot = lax.all_to_all(cot, "z", 0, 0, tiled=True)
    cot = cot.transpose(1, 0, 2, 3).reshape(t, width)

    sums = sds((8, width), f32)
    terms = [cot]
    gain_grads = [None] * norm_gains.shape[0]
    bias_grads = [None] * biases.shape[0]
    feed_grads, in_grads, mix_grads = [None] * layers, [None] * layers, [None] * layers
    part_shape = sds((4, 2, 2, share, width), bf16)
    for l in reversed(range(layers)):
        base = 2 + l * (6 + ff_rows)
        in_w, mix_w, ups, downs, hl, q, k, v, att, lse, n1, i1, first_low, first_other, act, slope, n2, i2 = saved[l]
        d2, d2_low, small = whole_call(
            functools.partial(norm_back_kernel, 2 + 2 * l, len(terms)), [wide, thin, sums], terms + [norm_gains, n2, i2]
        )
        gain_grads[2 + 2 * l], bias_grads[base + 5], bias_grads[base + 4] = small[0], small[1], small[2]
        d2_other = swapped(d2_low, "c")
        dup, own, send, up_sums = whole_call(
            feed_back_kernel,
            [sds((2, 2 * t, width), bf16), wide, thin, sums],
            [d2_low, d2_other, *ups, *downs, slope],
            flops=2 * 2 * t * width * width * 4,
        )
        zero_row = jnp.zeros((ff_rows, width), f32)
        for ry in range(2):
            zero_row = lax.dynamic_update_slice_in_dim(zero_row, up_sums[ry : ry + 1], 2 * (yi ^ ry) + ci, 0)
        for i in range(ff_rows):
            bias_grads[base + 6 + i] = zero_row[i]
        d1, d1_low, small = whole_call(
            functools.partial(norm_back_kernel, 1 + 2 * l, 3),
            [wide, thin, sums],
            [d2, own, swapped(send, "c"), norm_gains, n1, i1],
        )
        gain_grads[1 + 2 * l], bias_grads[base + 3], bias_grads[base + 2] = small[0], small[1], small[2]
        dl = gathered(d1_low)
        keep, send = whole_call(
            feed_grad_kernel,
            [part_shape, part_shape],
            [place, first_low, first_other, d2_low, d2_other, act, dup],
            scalars=1,
            flops=2 * 2 * t * width * width * 4,
        )
        part = plus(keep, swapped(send, "y"))
        part = halved_z(part)
        feed_grads[l] = plus(part[0], swapped(part[1], "x"))
        wide_dp, dense_dp, keep, send, small = whole_call(
            attend_back_kernel,
            [sds((full, 768), bf16), sds((full, 640), bf16), two, two, sds((8, 256), f32)],
            dl + [q, k, v, lse, in_w, mix_w, seg_row, seg_col],
            flops=2 * full * (768 * 768 + 256 * 768 + 3 * full * 640),
        )
        for i in range(2):
            bias_grads[base + i] = lax.dynamic_update_slice_in_dim(
                jnp.zeros((width,), f32), small[i, :head_share], group * head_share, 0
            )
        own, rest = summed(keep, send)
        terms = [d1, own, rest]
        in_part, mix_part = whole_call(
            attend_grad_kernel,
            [sds((4, 2, share, 640), bf16), sds((head_share, width), bf16)],
            [place] + hl + dl + [att, dense_dp],
            scalars=1,
            flops=2 * full * width * (640 + 256),
        )
        part = halved_z(in_part)
        mine_cols, other_cols = part[0, :, : 3 * head_share], swapped(part[1], "x")[:, : 3 * head_share]
        low_g = jnp.where(xi == 0, mine_cols, other_cols).reshape(share, 3, head_share)
        high_g = jnp.where(xi == 0, other_cols, mine_cols).reshape(share, 3, head_share)
        upper = jnp.stack([low_g[:, 0], high_g[:, 0], low_g[:, 1]])
        lower = jnp.stack([high_g[:, 1], low_g[:, 2], high_g[:, 2]])
        stay = jnp.where(yi == 0, upper, lower)
        move = swapped(jnp.where(yi == 0, lower, upper), "y")
        part = plus(stay, move)
        swap_in = swapped(jnp.where(ci == 0, part[2], part[0]), "c")
        first_block = jnp.where(ci == 0, part[0], part[1])
        last_block = jnp.where(ci == 0, part[1], part[2])
        in_grads[l] = jnp.concatenate([first_block, swap_in, last_block], axis=1).astype(f32)
        part = mix_part.reshape(2, share, 2, 2, head_share).transpose(2, 0, 3, 1, 4)
        stay = lax.dynamic_index_in_dim(part, yi, 0, keepdims=False)
        move = swapped(lax.dynamic_index_in_dim(part, 1 - yi, 0, keepdims=False), "y")
        part = plus(stay, move).reshape(4, share, head_share)
        lane0 = jnp.where((zi & 1) == 0, part, part.reshape(2, 2, share, head_share)[:, ::-1].reshape(part.shape))
        part = jnp.where((zi & 2) == 0, lane0, lane0.reshape(2, 2, share, head_share)[::-1].reshape(part.shape))
        part = halved_z(part)
        route = []
        for c in range(2):
            for z in range(4):
                for x in range(2):
                    route.append(((c * 4 + z) * 2 + x, ((z & 1) * 4 + (2 * x + c)) * 2 + (z >> 1)))
        mix_grads[l] = lax.ppermute(part, ("c", "z", "x"), route).astype(f32)

    ds_sent, small = whole_call(
        functools.partial(stem_norm_back_kernel, share, len(terms)),
        [sds((blocks, 64, 2 * LANES), bf16), sums],
        terms + [norm_gains, normed_stem, inverse_stem],
    )
    gain_grads[0], bias_grads[1] = small[0], small[1]
    bias_grads[0] = jnp.zeros((width,), f32)
    slots = lax.all_to_all(ds_sent, seq, 0, 0, tiled=True).reshape(2, 2, 2, 64, 2 * LANES)
    stay = lax.dynamic_index_in_dim(slots, ci, 0, keepdims=False)
    move = swapped(lax.dynamic_index_in_dim(slots, 1 - ci, 0, keepdims=False), "c")
    pair = sds((rows, n, 2 * LANES), bf16)
    dpre_low, ds, stem_sums = whole_call(
        functools.partial(stem_slope_kernel, rows), [pair, pair, sds((8, LANES), f32)],
        [place, stay, move, pre_act], scalars=1,
    )
    quarter = sds((2, KERNEL // 4 * gw, LANES), bf16)
    keep, send = whole_call(
        functools.partial(stem_grad_kernel, rows, KERNEL, gw), [quarter, quarter], [place, phases, dpre_low],
        scalars=1, flops=2 * rows * n * 256 * 256 * 65,
    )
    part = plus(keep, swapped(send, "c"))
    stem_grad = plus(part[0], swapped(part[1], "y"))[:, : 2 * gw].astype(f32)
    stem_grad = stem_grad.reshape(KERNEL // 4, gw, 2, gw).transpose(0, 3, 2, 1).reshape(KERNEL // 4 * gw, 2 * gw)
    back = whole_call(
        functools.partial(stem_input_grad_kernel, rows, half),
        sds((blocks, rows, toks // 2, 2 * LANES), bf16),
        [dpre_low, ds, taps],
        scratch=[
            pltpu.VMEM((rows, n + half, 2 * LANES), f32),
            pltpu.VMEM((16, rows, n + half, 2 * LANES), bf16),
            pltpu.VMEM((rows * n, 2 * LANES), f32),
        ],
        flops=2 * rows * n * 256 * 256 * 65,
    )
    back = lax.all_to_all(back, seq, 0, 0, tiled=True)
    features_gradient = whole_call(
        functools.partial(join_kernel, share), sds((rows, toks, width), f32), [back],
        scratch=[pltpu.VMEM((width // LANES * toks, LANES), f32)],
    )

    smalls = jnp.stack(gain_grads + bias_grads)
    smalls = smalls.reshape(smalls.shape[0], blocks, share).transpose(1, 0, 2)
    smalls = jnp.sum(lax.all_to_all(smalls, seq, 0, 0, tiled=True), axis=0)
    gain_count = norm_gains.shape[0]
    smalls = smalls.at[gain_count].add(stem_sums[0, :share])
    smalls = smalls + swapped(smalls, "c")
    smalls = smalls + swapped(smalls, "y")

    totals = (
        stem_grad,
        jnp.stack(in_grads),
        jnp.stack(mix_grads),
        jnp.stack(feed_grads).transpose(0, 2, 1, 3).astype(f32),
        smalls[:gain_count],
        smalls[gain_count:],
    )
    rate_base = 1.0 / math.sqrt(rows * 4 * frames)
    olds = (stem_weight, projection_weight, mixing_weight, feedforward_weight, norm_gains, biases)
    return (encoded, features_gradient, *updates(totals, olds, state, seq_i, row_i, 8, 4, rate_base))


def updates(totals, olds, state, seq_index, row_index, seq_count, row_total, rate_base):
    momenta, averaged, updated = [], [], []
    for param_index in range(6):
        old_share = olds[param_index]
        share_width = old_share.shape[1] // seq_count
        old_share = lax.dynamic_slice_in_dim(old_share, seq_index * share_width, share_width, 1)
        if param_index < 4:
            split_dim = row_dims[param_index]
            piece_size = old_share.shape[split_dim] // row_total
            old_share = lax.dynamic_slice_in_dim(
                old_share, row_index * piece_size, piece_size, split_dim
            )
        old_share = old_share.astype(jnp.float32)
        moment_new = momentum_decay * state[param_index] + totals[param_index]
        weight_new = old_share - rate_factors[param_index] * rate_base * (
            totals[param_index] + momentum_decay * moment_new
        )
        momenta.append(moment_new)
        updated.append(weight_new)
        averaged.append(
            average_decay * state[6 + param_index] + (1.0 - average_decay) * weight_new
        )
    return (*momenta, *averaged, *updated)


def solution(mesh):
    if mesh.shape["row"] == 4 and mesh.shape["seq"] == 8:
        body, mesh = local_rows, Mesh(mesh.devices.reshape(2, 2, 4, 2), ("y", "c", "z", "x"))
        row, seq = ("y", "c"), ("z", "x")
    else:
        body, row, seq = local, "row", "seq"
    in_specs = (
        P(row, seq, None),
        P(row, seq, None),
        P(row, None),
        P(),
        P(),
        P(),
        P(),
        P(),
        P(),
        P(row, seq),
        P(None, seq, row),
        P(None, seq, row),
        P(None, seq, None, row),
        P(None, seq),
        P(None, seq),
        P(row, seq),
        P(None, seq, row),
        P(None, seq, row),
        P(None, seq, None, row),
        P(None, seq),
        P(None, seq),
    )
    out_specs = (
        P(row, seq, None),
        P(row, seq, None),
        P(row, seq),
        P(None, seq, row),
        P(None, seq, row),
        P(None, seq, None, row),
        P(None, seq),
        P(None, seq),
        P(row, seq),
        P(None, seq, row),
        P(None, seq, row),
        P(None, seq, None, row),
        P(None, seq),
        P(None, seq),
        P(row, seq),
        P(None, seq, row),
        P(None, seq, row),
        P(None, seq, None, row),
        P(None, seq),
        P(None, seq),
    )
    return jax.shard_map(body, mesh=mesh, in_specs=in_specs, out_specs=out_specs, check_vma=False)
```

```python
import functools
import math

import jax
import jax.numpy as jnp
from jax import lax
from jax.experimental import pallas as pl
from jax.experimental.pallas import tpu as pltpu
from jax.sharding import Mesh
from jax.sharding import PartitionSpec as P

HEADS = 12
KERNEL = 128
GROUPS = 16


epsilon = 1e-05
masked_score = -1e30
momentum_decay = 0.9
average_decay = 0.5
rate_factors = (0.012, 0.08, 0.6, 0.03, 0.06, 0.09)
row_dims = (0, 2, 2, 3)


def extended_2(cells, sides, width):
    for axis, dim in sides:
        count = lax.axis_size(axis)
        ends = count - 1
        head = lax.slice_in_dim(cells, 0, width, axis=dim)
        tail = lax.slice_in_dim(cells, cells.shape[dim] - width, cells.shape[dim], axis=dim)
        cells = jnp.concatenate(
            [
                lax.ppermute(tail, axis, [(i, (i + 1) % count) for i in range(ends)]),
                cells,
                lax.ppermute(head, axis, [((i + 1) % count, i) for i in range(ends)]),
            ],
            axis=dim,
        )
    return cells


def layer_norm(values, gain_row, shift_row):
    centre = jnp.mean(values, axis=-1, keepdims=True)
    centred = values - centre
    spread = jnp.mean(centred * centred, axis=-1, keepdims=True)
    inverse = lax.rsqrt(spread + epsilon)
    normed = centred * inverse
    return (normed * gain_row + shift_row, normed, inverse)


def layer_norm_back(upstream, normed, inverse, gain_row):
    scaled = upstream * gain_row
    first_mean = jnp.mean(scaled, axis=-1, keepdims=True)
    second_mean = jnp.mean(scaled * normed, axis=-1, keepdims=True)
    downstream = inverse * (scaled - first_mean - normed * second_mean)
    return (downstream, jnp.sum(upstream * normed, axis=(0, 1)), jnp.sum(upstream, axis=(0, 1)))


def gelu_exact(values):
    return jax.nn.gelu(values, approximate=False)


def gelu_back(inputs, upstream):
    _, pullback = jax.vjp(gelu_exact, inputs)
    return pullback(upstream)[0]


def group_conv(extended, kernel_taps, group_count):
    return lax.conv_general_dilated(
        extended,
        kernel_taps,
        (1,),
        "VALID",
        dimension_numbers=("NWC", "WIO", "NWC"),
        feature_group_count=group_count,
        preferred_element_type=jnp.float32,
    )


def group_conv_kernel_grad(extended, upstream_low, group_count):
    return lax.conv_general_dilated(
        extended,
        upstream_low,
        (1,),
        "VALID",
        dimension_numbers=("CWN", "IWO", "WNC"),
        batch_group_count=group_count,
        preferred_element_type=jnp.float32,
    )


def flipped_taps(kernel_taps, group_count):
    tap_count, group_width, model_width = kernel_taps.shape
    split_taps = kernel_taps.reshape(tap_count, group_width, group_count, group_width)
    swapped = jnp.transpose(split_taps, (0, 3, 2, 1)).reshape(tap_count, group_width, model_width)
    return swapped[::-1]


def masked_scores(query_part, key_part, query_segments, key_segments):
    scores = jnp.einsum("rqhe,rkhe->rhqk", query_part, key_part, preferred_element_type=jnp.float32)
    allowed = query_segments[:, None, :, None] == key_segments[:, None, None, :]
    return jnp.where(allowed, scores, masked_score)


def key_slice(kv_whole, segments, start, key_block, head_count):
    row_count = kv_whole.shape[0]
    model_width = kv_whole.shape[2] // 2
    head_width = model_width // head_count
    part_rows = lax.dynamic_slice_in_dim(kv_whole, start, key_block, 1)
    part_segments = lax.dynamic_slice_in_dim(segments, start, key_block, 1)
    key_part = part_rows[:, :, :model_width].reshape(row_count, key_block, head_count, head_width)
    value_part = part_rows[:, :, model_width:].reshape(row_count, key_block, head_count, head_width)
    return (key_part, value_part, part_segments)


def attend(query_heads, kv_whole, query_segments, segments, head_count):
    row_count = query_heads.shape[0]
    tok_count = query_heads.shape[1]
    key_block = math.gcd(kv_whole.shape[1], 1024)
    block_count = kv_whole.shape[1] // key_block

    def stats_step(step_index, state):
        running_max, running_sum = state
        key_part, value_part, part_segments = key_slice(
            kv_whole, segments, step_index * key_block, key_block, head_count
        )
        scores = masked_scores(query_heads, key_part, query_segments, part_segments)
        new_max = jnp.maximum(running_max, jnp.max(scores, axis=-1))
        running_sum = running_sum * jnp.exp(running_max - new_max) + jnp.sum(
            jnp.exp(scores - new_max[..., None]), axis=-1
        )
        return (new_max, running_sum)

    start_state = (
        jnp.full((row_count, head_count, tok_count), masked_score, jnp.float32),
        jnp.zeros((row_count, head_count, tok_count), jnp.float32),
    )
    running_max, running_sum = lax.fori_loop(0, block_count, stats_step, start_state)
    log_sum = running_max + jnp.log(running_sum)

    def value_step(step_index, state):
        coarse, residue = state
        key_part, value_part, part_segments = key_slice(
            kv_whole, segments, step_index * key_block, key_block, head_count
        )
        probability = jnp.exp(
            masked_scores(query_heads, key_part, query_segments, part_segments) - log_sum[..., None]
        )
        probability_low = probability.astype(jnp.bfloat16)
        remainder_low = (probability - probability_low.astype(jnp.float32)).astype(jnp.bfloat16)
        coarse = coarse + jnp.einsum(
            "rhqk,rkhe->rqhe", probability_low, value_part, preferred_element_type=jnp.float32
        )
        residue = residue + jnp.einsum(
            "rhqk,rkhe->rqhe", remainder_low, value_part, preferred_element_type=jnp.float32
        )
        return (coarse, residue)

    zero_out = jnp.zeros(query_heads.shape, jnp.float32)
    coarse, residue = lax.fori_loop(0, block_count, value_step, (zero_out, zero_out))
    return (coarse, coarse + residue, log_sum)


def attend_back(
    query_heads, grad_heads, kv_whole, query_segments, segments, log_sum, delta, head_count
):
    row_count = query_heads.shape[0]
    frame_count = kv_whole.shape[1]
    model_width = kv_whole.shape[2] // 2
    key_block = math.gcd(frame_count, 1024)
    block_count = frame_count // key_block

    def back_step(step_index, state):
        grad_query, key_terms = state
        start = step_index * key_block
        key_part, value_part, part_segments = key_slice(
            kv_whole, segments, start, key_block, head_count
        )
        probability = jnp.exp(
            masked_scores(query_heads, key_part, query_segments, part_segments) - log_sum[..., None]
        )
        grad_prob = jnp.einsum(
            "rqhe,rkhe->rhqk", grad_heads, value_part, preferred_element_type=jnp.float32
        )
        grad_scores = (probability * (grad_prob - delta[..., None])).astype(jnp.bfloat16)
        grad_query = grad_query + jnp.einsum(
            "rhqk,rkhe->rqhe", grad_scores, key_part, preferred_element_type=jnp.float32
        )
        grad_keys = jnp.einsum(
            "rhqk,rqhe->rkhe", grad_scores, query_heads, preferred_element_type=jnp.float32
        )
        grad_values = jnp.einsum(
            "rhqk,rqhe->rkhe",
            probability.astype(jnp.bfloat16),
            grad_heads,
            preferred_element_type=jnp.float32,
        )
        both_terms = jnp.concatenate(
            [
                grad_keys.reshape(row_count, key_block, model_width),
                grad_values.reshape(row_count, key_block, model_width),
            ],
            axis=-1,
        )
        key_terms = lax.dynamic_update_slice_in_dim(key_terms, both_terms, start, 1)
        return (grad_query, key_terms)

    term_start = jnp.zeros((row_count, frame_count, 2 * model_width), jnp.float32)
    return lax.fori_loop(
        0, block_count, back_step, (jnp.zeros(query_heads.shape, jnp.float32), term_start)
    )


def local(
    features,
    cotangent,
    segments,
    stem_weight,
    projection_weight,
    mixing_weight,
    feedforward_weight,
    norm_gains,
    biases,
    stem_moment,
    projection_moment,
    mixing_moment,
    feedforward_moment,
    gain_moment,
    bias_moment,
    stem_average,
    projection_average,
    mixing_average,
    feedforward_average,
    gain_average,
    bias_average,
):
    row_count, tok_count, model_width = features.shape
    head_count = HEADS
    head_width = model_width // head_count
    group_count = GROUPS
    group_width = model_width // group_count
    tap_count = KERNEL
    half_taps = tap_count // 2
    layer_count = projection_weight.shape[0]
    ff_rows = feedforward_weight.shape[3] // model_width
    score_scale = 1.0 / math.sqrt(head_width)
    seq_index = lax.axis_index("seq")
    query_segments = lax.dynamic_slice_in_dim(segments, seq_index * tok_count, tok_count, 1)
    kernel_taps = stem_weight.reshape(tap_count, group_width, model_width)
    extended = extended_2(features, (("seq", 1),), half_taps)
    conv_input = extended[:, : tok_count + tap_count - 1]
    conv_pre = group_conv(conv_input, kernel_taps, group_count) + biases[0]
    summed = features.astype(jnp.float32) + gelu_exact(conv_pre)
    hidden, normed_stem, inverse_stem = layer_norm(summed, norm_gains[0], biases[1])
    saved_layers = []
    for layer_index in range(layer_count):
        bias_base = 2 + layer_index * (6 + ff_rows)
        hidden_low = hidden.astype(jnp.bfloat16)
        projected = jnp.einsum(
            "rtd,de->rte",
            hidden_low,
            projection_weight[layer_index],
            preferred_element_type=jnp.float32,
        )
        queries = ((projected[..., :model_width] + biases[bias_base]) * score_scale).astype(
            jnp.bfloat16
        )
        keys_low = projected[..., model_width : 2 * model_width].astype(jnp.bfloat16)
        values_low = (projected[..., 2 * model_width :] + biases[bias_base + 1]).astype(
            jnp.bfloat16
        )
        kv_local = jnp.concatenate([keys_low, values_low], axis=-1)
        kv_whole = lax.all_gather(kv_local, "seq", axis=1, tiled=True)
        query_heads = queries.reshape(row_count, tok_count, head_count, head_width)
        coarse, fine, log_sum = attend(query_heads, kv_whole, query_segments, segments, head_count)
        mixed_low = coarse.reshape(row_count, tok_count, model_width).astype(jnp.bfloat16)
        branch = (
            jnp.einsum(
                "rte,ed->rtd",
                mixed_low,
                mixing_weight[layer_index],
                preferred_element_type=jnp.float32,
            )
            + biases[bias_base + 2]
        )
        first_norm, normed_one, inverse_one = layer_norm(
            hidden + branch, norm_gains[1 + 2 * layer_index], biases[bias_base + 3]
        )
        first_low = first_norm.astype(jnp.bfloat16)
        up_bias = biases[bias_base + 6 : bias_base + 6 + ff_rows].reshape(-1)
        up_pre = (
            jnp.einsum(
                "rtd,dj->rtj",
                first_low,
                feedforward_weight[layer_index, :, 0, :],
                preferred_element_type=jnp.float32,
            )
            + up_bias
        )
        up_low = gelu_exact(up_pre).astype(jnp.bfloat16)
        down_out = (
            jnp.einsum(
                "rtj,dj->rtd",
                up_low,
                feedforward_weight[layer_index, :, 1, :],
                preferred_element_type=jnp.float32,
            )
            + biases[bias_base + 4]
        )
        hidden_next, normed_two, inverse_two = layer_norm(
            first_norm + down_out, norm_gains[2 + 2 * layer_index], biases[bias_base + 5]
        )
        saved_layers.append(
            (
                hidden_low,
                query_heads,
                kv_whole,
                log_sum,
                fine,
                mixed_low,
                normed_one,
                inverse_one,
                first_low,
                up_pre,
                up_low,
                normed_two,
                inverse_two,
            )
        )
        hidden = hidden_next
    upstream = cotangent.astype(jnp.float32)
    gain_grads = [None] * norm_gains.shape[0]
    bias_grads = [None] * biases.shape[0]
    projection_grads = [None] * layer_count
    mixing_grads = [None] * layer_count
    feedforward_grads = [None] * layer_count
    for layer_index in reversed(range(layer_count)):
        (
            hidden_low,
            query_heads,
            kv_whole,
            log_sum,
            fine,
            mixed_low,
            normed_one,
            inverse_one,
            first_low,
            up_pre,
            up_low,
            normed_two,
            inverse_two,
        ) = saved_layers[layer_index]
        bias_base = 2 + layer_index * (6 + ff_rows)
        in_matrix = projection_weight[layer_index]
        mix_matrix = mixing_weight[layer_index]
        up_matrix = feedforward_weight[layer_index, :, 0, :]
        down_matrix = feedforward_weight[layer_index, :, 1, :]
        grad_second, gain_grads[2 + 2 * layer_index], bias_grads[bias_base + 5] = layer_norm_back(
            upstream, normed_two, inverse_two, norm_gains[2 + 2 * layer_index]
        )
        bias_grads[bias_base + 4] = jnp.sum(grad_second, axis=(0, 1))
        down_low = grad_second.astype(jnp.bfloat16)
        grad_down = jnp.einsum("rtd,rtj->dj", down_low, up_low, preferred_element_type=jnp.float32)
        grad_act = jnp.einsum(
            "rtd,dj->rtj", down_low, down_matrix, preferred_element_type=jnp.float32
        )
        grad_up_pre = gelu_back(up_pre, grad_act)
        up_bias_grad = jnp.sum(grad_up_pre, axis=(0, 1)).reshape(ff_rows, model_width)
        for offset in range(ff_rows):
            bias_grads[bias_base + 6 + offset] = up_bias_grad[offset]
        up_grad_low = grad_up_pre.astype(jnp.bfloat16)
        grad_up = jnp.einsum(
            "rtd,rtj->dj", first_low, up_grad_low, preferred_element_type=jnp.float32
        )
        grad_first = grad_second + jnp.einsum(
            "rtj,dj->rtd", up_grad_low, up_matrix, preferred_element_type=jnp.float32
        )
        feedforward_grads[layer_index] = jnp.stack([grad_up, grad_down], axis=1)
        grad_resid, gain_grads[1 + 2 * layer_index], bias_grads[bias_base + 3] = layer_norm_back(
            grad_first, normed_one, inverse_one, norm_gains[1 + 2 * layer_index]
        )
        bias_grads[bias_base + 2] = jnp.sum(grad_resid, axis=(0, 1))
        branch_low = grad_resid.astype(jnp.bfloat16)
        mixing_grads[layer_index] = jnp.einsum(
            "rte,rtd->ed", mixed_low, branch_low, preferred_element_type=jnp.float32
        )
        grad_mixed = jnp.einsum(
            "rtd,ed->rte", branch_low, mix_matrix, preferred_element_type=jnp.float32
        )
        mixed_grad_low = grad_mixed.astype(jnp.bfloat16).reshape(
            row_count, tok_count, head_count, head_width
        )
        delta = jnp.transpose(
            jnp.sum(mixed_grad_low.astype(jnp.float32) * fine, axis=-1), (0, 2, 1)
        )
        grad_query, key_terms = attend_back(
            query_heads,
            mixed_grad_low,
            kv_whole,
            query_segments,
            segments,
            log_sum,
            delta,
            head_count,
        )
        grad_kv = lax.psum_scatter(key_terms, "seq", scatter_dimension=1, tiled=True)
        query_grad_low = grad_query.reshape(row_count, tok_count, model_width).astype(jnp.bfloat16)
        key_grad_low = grad_kv[..., :model_width].astype(jnp.bfloat16)
        value_grad_low = grad_kv[..., model_width:].astype(jnp.bfloat16)
        bias_grads[bias_base] = (
            jnp.sum(query_grad_low.astype(jnp.float32), axis=(0, 1)) * score_scale
        )
        bias_grads[bias_base + 1] = jnp.sum(value_grad_low.astype(jnp.float32), axis=(0, 1))
        grad_projected = jnp.concatenate(
            [query_grad_low * score_scale, key_grad_low, value_grad_low], axis=-1
        )
        projection_grads[layer_index] = jnp.einsum(
            "rtd,rte->de", hidden_low, grad_projected, preferred_element_type=jnp.float32
        )
        upstream = grad_resid + jnp.einsum(
            "rte,de->rtd", grad_projected, in_matrix, preferred_element_type=jnp.float32
        )
    grad_summed, gain_grads[0], bias_grads[1] = layer_norm_back(
        upstream, normed_stem, inverse_stem, norm_gains[0]
    )
    grad_conv = gelu_back(conv_pre, grad_summed)
    bias_grads[0] = jnp.sum(grad_conv, axis=(0, 1))
    conv_grad_low = grad_conv.astype(jnp.bfloat16)
    grad_extended = extended_2(conv_grad_low, (("seq", 1),), half_taps)
    features_gradient = grad_summed + group_conv(
        grad_extended[:, 1:], flipped_taps(kernel_taps, group_count), group_count
    )
    seq_count = lax.axis_size("seq")
    share_width = model_width // seq_count
    layer_partials = (
        jnp.stack(projection_grads),
        jnp.stack(mixing_grads),
        jnp.stack(feedforward_grads),
        jnp.stack(gain_grads),
        jnp.stack(bias_grads),
    )
    grad_stem = group_conv_kernel_grad(conv_input, conv_grad_low, group_count).reshape(
        tap_count * group_width, model_width
    )
    shares = (
        lax.psum_scatter(grad_stem, "seq", scatter_dimension=1, tiled=True),
        lax.psum_scatter(layer_partials[0], "seq", scatter_dimension=1, tiled=True),
        lax.psum_scatter(layer_partials[1], "seq", scatter_dimension=1, tiled=True),
        lax.psum_scatter(layer_partials[2], "seq", scatter_dimension=1, tiled=True),
        lax.psum_scatter(layer_partials[3], "seq", scatter_dimension=1, tiled=True),
        lax.psum_scatter(layer_partials[4], "seq", scatter_dimension=1, tiled=True),
    )
    matrix_totals = (
        lax.psum_scatter(
            shares[0].astype(jnp.bfloat16), "row", scatter_dimension=0, tiled=True
        ).astype(jnp.float32),
        lax.psum_scatter(
            shares[1].astype(jnp.bfloat16), "row", scatter_dimension=2, tiled=True
        ).astype(jnp.float32),
        lax.psum_scatter(
            shares[2].astype(jnp.bfloat16), "row", scatter_dimension=2, tiled=True
        ).astype(jnp.float32),
        lax.psum_scatter(
            shares[3].astype(jnp.bfloat16), "row", scatter_dimension=3, tiled=True
        ).astype(jnp.float32),
    )
    small_totals = lax.psum((shares[4], shares[5]), "row")
    totals = (
        matrix_totals[0],
        matrix_totals[1],
        matrix_totals[2],
        matrix_totals[3],
        small_totals[0],
        small_totals[1],
    )
    share_start = seq_index * share_width
    row_index = lax.axis_index("row")
    row_total = lax.axis_size("row")
    rate_base = 1.0 / math.sqrt(row_count * row_total * tok_count * seq_count)
    old_params = (
        stem_weight,
        projection_weight,
        mixing_weight,
        feedforward_weight,
        norm_gains,
        biases,
    )
    old_moments = (
        stem_moment,
        projection_moment,
        mixing_moment,
        feedforward_moment,
        gain_moment,
        bias_moment,
    )
    old_averages = (
        stem_average,
        projection_average,
        mixing_average,
        feedforward_average,
        gain_average,
        bias_average,
    )
    momenta = []
    averaged = []
    updated = []
    for param_index in range(6):
        old_share = lax.dynamic_slice_in_dim(old_params[param_index], share_start, share_width, 1)
        if param_index < 4:
            split_dim = row_dims[param_index]
            piece_size = old_share.shape[split_dim] // row_total
            old_share = lax.dynamic_slice_in_dim(
                old_share, row_index * piece_size, piece_size, split_dim
            )
        old_share = old_share.astype(jnp.float32)
        moment_new = momentum_decay * old_moments[param_index] + totals[param_index]
        weight_new = old_share - rate_factors[param_index] * rate_base * (
            totals[param_index] + momentum_decay * moment_new
        )
        momenta.append(moment_new)
        updated.append(weight_new)
        averaged.append(
            average_decay * old_averages[param_index] + (1.0 - average_decay) * weight_new
        )
    return (
        hidden,
        features_gradient,
        momenta[0],
        momenta[1],
        momenta[2],
        momenta[3],
        momenta[4],
        momenta[5],
        averaged[0],
        averaged[1],
        averaged[2],
        averaged[3],
        averaged[4],
        averaged[5],
        updated[0],
        updated[1],
        updated[2],
        updated[3],
        updated[4],
        updated[5],
    )


LANES = 128
PAIRS = 2
VMEM_BYTES = 16 * 1024 * 1024
WIDE_BYTES = 24 * 1024 * 1024
FAR_BYTES = 56 * 1024 * 1024
bf16 = jnp.bfloat16
f32 = jnp.float32


def whole_call(kernel, outs, operands, scalars=0, scratch=(), after=(), far=(), token=False, vmem=VMEM_BYTES):
    given, waits, made = len(operands), len(after), len(outs)

    def body(*refs):
        kernel(*refs[:given], *refs[given + waits : given + waits + made], *refs[given + waits + made + token :])

    in_specs = [
        pl.BlockSpec(memory_space=pltpu.SMEM if i < scalars else pl.ANY if i in far else pltpu.VMEM)
        for i in range(given)
    ] + [pl.BlockSpec(memory_space=pl.ANY)] * waits
    out_specs = [pl.BlockSpec(memory_space=pltpu.VMEM)] * made + [pl.BlockSpec(memory_space=pl.ANY)] * token
    return pl.pallas_call(
        body,
        out_shape=[*outs, *[jax.ShapeDtypeStruct((8, LANES), jnp.float32)] * token],
        in_specs=in_specs,
        out_specs=out_specs,
        scratch_shapes=list(scratch),
        compiler_params=pltpu.CompilerParams(vmem_limit_bytes=vmem),
        cost_estimate=pl.CostEstimate(flops=1, bytes_accessed=1, transcendentals=0),
    )(*operands, *after)


def sds(shape, dtype):
    return jax.ShapeDtypeStruct(shape, dtype)


def dot_nn(a, b):
    return lax.dot_general(a, b, (((1,), (0,)), ((), ())), preferred_element_type=f32)


def dot_nt(a, b):
    return lax.dot_general(a, b, (((1,), (1,)), ((), ())), preferred_element_type=f32)


def dot_tn(a, b):
    return lax.dot_general(a, b, (((0,), (0,)), ((), ())), preferred_element_type=f32)


def gelu_and_slope(v):
    cdf = 0.5 * (1.0 + lax.erf(v * math.sqrt(0.5)))
    return v * cdf, cdf + v * jnp.exp(-0.5 * v * v) * (1.0 / math.sqrt(2.0 * math.pi))


def lane_of(shape):
    return lax.broadcasted_iota(jnp.int32, shape, len(shape) - 1)


def piece_of(cols, j, width):
    off, v = (width * j) % LANES, (width * j) // LANES
    lane = lane_of(cols[0].shape)
    if off == 0:
        t = cols[v]
    else:
        t = pltpu.roll(cols[v], LANES - off, 1)
        if off + width > LANES:
            t = jnp.where(lane < LANES - off, t, pltpu.roll(cols[v + 1], LANES - off, 1))
    return jnp.where(lane < width, t, 0.0)


def tiles_of(pieces, width):
    count = len(pieces) * width // LANES
    cols = [None] * count

    def put(v, t):
        cols[v] = t if cols[v] is None else cols[v] + t

    for j, piece in enumerate(pieces):
        off, v = (width * j) % LANES, (width * j) // LANES
        if off == 0:
            put(v, piece)
            continue
        rolled = pltpu.roll(piece, off, 1)
        if off + width > LANES:
            lane = lane_of(piece.shape)
            put(v, jnp.where(lane >= off, rolled, 0.0))
            put(v + 1, jnp.where(lane < off, rolled, 0.0))
        else:
            put(v, rolled)
    return cols


def split_kernel(blocks, width, x_ref, o_ref):
    rows = x_ref.shape[0]
    for r in range(rows):
        x = x_ref[r].astype(f32)
        cols = [x[:, LANES * v : LANES * (v + 1)] for v in range(x.shape[1] // LANES)]
        for j in range(blocks):
            o_ref[j, r] = piece_of(cols, j, width).astype(bf16)


def fill_taps(taps, gw, w_ref, o_ref):
    zero = jnp.zeros((LANES, LANES), bf16)
    o_ref[0] = zero
    o_ref[taps + 1] = zero
    o_ref[taps + 2] = zero

    def body(k, carry):
        w = w_ref[pl.ds(pl.multiple_of(k * gw, 16), gw), :]
        lane = lane_of(w.shape)
        o_ref[k + 1, 0:gw, :] = jnp.where(lane < gw, w, jnp.zeros_like(w))
        o_ref[k + 1, gw : 2 * gw, :] = jnp.where(lane >= gw, w, jnp.zeros_like(w))
        o_ref[k + 1, 2 * gw :, :] = jnp.zeros((LANES - 2 * gw, LANES), bf16)
        return carry

    lax.fori_loop(0, taps, body, 0)


def phases_from_frames(x_ref, xf, ph, rows, frames, half):
    blocks, block = x_ref.shape[0], x_ref.shape[2]
    span = frames + 2 * half
    for r in range(rows):
        xf[r * span : r * span + half, :] = jnp.zeros((half, LANES), f32)
        xf[r * span + half + frames : (r + 1) * span, :] = jnp.zeros((half, LANES), f32)
        for s in range(blocks):
            at = r * span + half + s * block
            xf[at : at + block, :] = x_ref[s, r].astype(f32)
    for p in range(16):
        n = (span // 2) if p == 0 else (span // 2 - 16)
        for r in range(rows):
            for b in range(2):
                ph[p, r, 0:n, b * LANES : (b + 1) * LANES] = xf[
                    pl.ds(r * span + 2 * p + b, n, stride=2), :
                ].astype(bf16)


def window(ph, m, rows, n):
    p, a = lax.rem(m, 16), m // 16
    part = ph[p, :, pl.ds(pl.multiple_of(a * 16, 16), n), :]
    return part.reshape(rows * n, part.shape[-1])


def phases_kernel(rows, frames, half, gw, x_ref, share_ref, ph_ref, w_ref, xf):
    phases_from_frames(x_ref, xf, ph_ref, rows, frames, half)
    fill_taps(2 * half, gw, share_ref, w_ref)


def conv_kernel(rows, frames, half, gw, c_ref, x_ref, share_ref, b_ref, pre_ref, keep_ref, send_ref, ph_ref, xf, acc, w_ref):
    n = frames // 2
    fill_taps(2 * half, gw, share_ref, w_ref)
    phases_from_frames(x_ref, xf, ph_ref, rows, frames, half)
    acc[...] = jnp.zeros_like(acc)

    def body(i, carry):
        left, right = [], []
        for t in range(5):
            m = i * 5 + t
            here, before, after = w_ref[2 * m + 1], w_ref[2 * m], w_ref[2 * m + 2]
            right += [jnp.concatenate([here, before], 1), jnp.concatenate([after, here], 1)]
            left.append(window(ph_ref, m, rows, n))
        acc[...] += dot_nn(jnp.concatenate(left, 1), jnp.concatenate(right, 0))
        return carry

    lax.fori_loop(0, (half + 1) // 5, body, 0)
    bias = jnp.concatenate([b_ref[...], b_ref[...]], 1)
    c = c_ref[1]
    for r in range(rows):
        pre = acc[r * n : (r + 1) * n, :] + bias
        pre_ref[r] = pre
        x = ph_ref[0, r, half // 2 : half // 2 + n, :].astype(f32)
        s = (x + gelu_and_slope(pre)[0]).astype(bf16)
        for zf in range(4):
            for xq in range(2):
                for cf in range(2):
                    u = ((zf * 2 + xq) * 2 + cf) * 16
                    blk = s[u : u + 16, :]

                    @pl.when(c == cf)
                    def _(blk=blk, r=r, xq=xq, zf=zf):
                        keep_ref[r, xq, zf * 16 : zf * 16 + 16, :] = blk

                    @pl.when(c != cf)
                    def _(blk=blk, r=r, xq=xq, zf=zf):
                        send_ref[r, xq, zf * 16 : zf * 16 + 16, :] = blk


def normed(values):
    centre = jnp.mean(values, axis=-1, keepdims=True)
    centred = values - centre
    spread = jnp.mean(centred * centred, axis=-1, keepdims=True)
    inverse = lax.rsqrt(spread + epsilon)
    return centred * inverse, inverse


def stem_norm_kernel(width, r_ref, g_ref, b_ref, h_ref, low_ref, n_ref, i_ref):
    halves = []
    for a in range(2):
        pieces = [r_ref[j, :, a * LANES : (a + 1) * LANES].astype(f32) for j in range(r_ref.shape[0])]
        halves.append(jnp.concatenate(tiles_of(pieces, width), axis=1))
    s = jnp.concatenate(halves, axis=0)
    n, inv = normed(s)
    h = n * g_ref[0:1, :] + b_ref[1:2, :]
    h_ref[...] = h
    low_ref[...] = h.astype(bf16)
    n_ref[...] = n
    i_ref[...] = inv


def cotangent_split_kernel(place, x_ref, keep_ref, send_ref, mixed):
    c = place[1]
    rows, toks, width = x_ref.shape
    for r in range(rows):
        for v in range(width // LANES):
            mixed[v * toks : (v + 1) * toks, :] = x_ref[r, :, v * LANES : (v + 1) * LANES].astype(f32)
        for cf in range(2):
            for a in range(2):
                parts = [mixed[pl.ds(v * toks + cf * 32 + a, 16, stride=2), :] for v in range(width // LANES)]
                blk = jnp.concatenate(parts, axis=1).astype(bf16)

                @pl.when(c == cf)
                def _(blk=blk, r=r, a=a):
                    keep_ref[r, a * 16 : a * 16 + 16, :] = blk

                @pl.when(c != cf)
                def _(blk=blk, r=r, a=a):
                    send_ref[r, a * 16 : a * 16 + 16, :] = blk


def cotangent_route_kernel(place, keep_ref, recv_ref, *outs):
    c, z = place[1], place[2]
    for rel, out in enumerate(outs):
        to = z ^ rel
        mine = (to // 2) == c

        @pl.when(mine)
        def _(out=out, to=to):
            out[...] = keep_ref[to % 2]

        @pl.when(jnp.logical_not(mine))
        def _(out=out, to=to):
            out[...] = recv_ref[to % 2]


def cotangent_join_kernel(place, r0, r1, r2, r3, o_ref):
    z = place[2]
    for rel, src in enumerate((r0, r1, r2, r3)):
        for a in range(2):
            at = pl.multiple_of(a * 64 + (z ^ rel) * 16, 16)
            o_ref[pl.ds(at, 16), :] = src[a * 16 : a * 16 + 16, :]


def segments_kernel(place, own_ref, other_ref, row_ref, col_ref):
    c, z, x = place[1], place[2], place[3]
    frames = own_ref.shape[1]
    mine = (z // 2) == c
    odd = (z % 2) == 1
    own = jnp.where(odd, own_ref[1:2, :], own_ref[0:1, :])
    other = jnp.where(odd, other_ref[1:2, :], other_ref[0:1, :])
    ids = jnp.broadcast_to(jnp.where(mine, own, other).astype(f32), (LANES, frames)).astype(bf16)
    f = lax.broadcasted_iota(jnp.int32, (frames, frames), 0)
    p = lax.broadcasted_iota(jnp.int32, (frames, frames), 1)
    source = (
        ((p >> 4) & 3) * 128 + (x ^ (p >> 8)) * 64 + (c ^ ((p >> 7) & 1)) * 32 + (p & 15) * 2 + ((p >> 6) & 1)
    )
    chosen = jnp.where(f == source, 1.0, 0.0).astype(bf16)
    row_ref[...] = dot_nn(ids, chosen)[0:1, :]
    col_ref[...] = dot_tn(chosen, ids.T)[:, 0:1]


def slots_kernel(place, keep_ref, recv_ref, o_ref):
    c = place[1]
    for r in range(2):
        for q in range(2):
            o_ref[((c * 2) + r) * 2 + q] = keep_ref[r, q]
            o_ref[(((1 - c) * 2) + r) * 2 + q] = recv_ref[r, q]


def fetched(copies):
    for copy in copies:
        copy.start()
    return copies


def feed_copies(l, place, w_ref, buf, sems, width):
    steps = w_ref.shape[1] // LANES
    copies = []
    for i in range(2):
        at = pl.multiple_of((2 * (place[0] ^ i) + place[1]) * width, LANES)
        for k in range(steps):
            copies.append(
                pltpu.make_async_copy(
                    w_ref.at[l, pl.ds(k * LANES, LANES), :, pl.ds(at, width)],
                    buf.at[i, pl.ds(k * LANES, LANES)],
                    sems.at[i * steps + k],
                )
            )
    return fetched(copies)


def feed_parted(copies, buf, outs):
    depth, width = buf.shape[1], buf.shape[3]
    steps = depth // LANES
    parting = parting_matrix(2 * LANES)
    for i in range(2):
        flat = buf.at[i].reshape(2 * depth, width)
        for k in range(steps):
            copies[i * steps + k].wait()
            g = dot_nn(parting, flat[2 * LANES * k : 2 * LANES * (k + 1), :]).astype(bf16)
            outs[i][LANES * k : LANES * (k + 1), :] = g[:LANES]
            outs[2 + i][LANES * k : LANES * (k + 1), :] = g[LANES:]


def feed_weights_kernel(l, place, w_ref, *refs):
    outs, (buf, sems) = refs[:4], refs[4:]
    feed_parted(feed_copies(l, place, w_ref, buf, sems, outs[0].shape[1]), buf, outs)


def parting_matrix(size):
    r = lax.broadcasted_iota(jnp.int32, (size, size), 0)
    c = lax.broadcasted_iota(jnp.int32, (size, size), 1)
    return jnp.where(c == jnp.where(r < size // 2, 2 * r, 2 * r - size + 1), 1.0, 0.0).astype(bf16)


def later_weights_kernel(layers, bases, share, place, w_ref, p_ref, m_ref, b_ref, *refs):
    feeds = 4 * (layers - 1)
    feed_outs, outs = refs[:feeds], refs[feeds : feeds + 3 * layers]
    buf, wide, feed_sems, sems = refs[feeds + 3 * layers :]
    c, x = place[1], place[3]
    group = 2 * x + c
    width = m_ref.shape[2]
    start = ((group * share) // LANES) * LANES
    copies = []
    row = pl.multiple_of(group * share, 64)
    for l in range(layers):
        for i in range(3):
            at = pl.multiple_of(i * width + start, LANES)
            copies.append(pltpu.make_async_copy(p_ref.at[l, :, pl.ds(at, 256)], wide.at[l, i], sems.at[4 * l + i]))
        mix_ref = outs[3 * l + 1]
        copies.append(
            pltpu.make_async_copy(m_ref.at[l, pl.ds(row, share), :], mix_ref.at[pl.ds(0, share), :], sems.at[4 * l + 3])
        )
    fetched(copies)
    feed_in = [feed_copies(l, place, w_ref, buf.at[l - 1], feed_sems.at[l - 1], width) for l in range(1, layers)]
    odd = (group % 2) == 1

    def settle(v):
        lane = lane_of(v.shape)
        return jnp.where(lane < share, jnp.where(odd, pltpu.roll(v, 256 - 64, 1), v), 0.0)

    for l in range(layers):
        in_ref, mix_ref, both_ref = outs[3 * l : 3 * l + 3]
        mix_ref[share:, :] = jnp.zeros((256 - share, width), bf16)
        both_ref[...] = settle(b_ref[bases[l] : bases[l] + 2, pl.ds(pl.multiple_of(start, LANES), 256)])
        for i in range(3):
            copies[4 * l + i].wait()
            in_ref[:, i * 256 : (i + 1) * 256] = settle(wide[l, i].astype(f32)).astype(bf16)
        copies[4 * l + 3].wait()
    for l in range(1, layers):
        feed_parted(feed_in[l - 1], buf.at[l - 1], feed_outs[4 * (l - 1) : 4 * l])


def attend_kernel(base, hl0, hl1, hl2, hl3, w_ref, m_ref, bq_ref, segr, segc,
                  q_ref, k_ref, v_ref, at_ref, lse_ref, keep_ref, send_ref):
    t = hl0.shape[0]
    hl = jnp.concatenate([hl0[...], hl1[...], hl2[...], hl3[...]], axis=0)
    proj = dot_nn(hl, w_ref[...])
    q = ((proj[:, 0:256] + bq_ref[0:1, :]) * 0.125).astype(bf16)
    k = proj[:, 256:512].astype(bf16)
    v = (proj[:, 512:768] + bq_ref[1:2, :]).astype(bf16)
    q_ref[...] = q
    k_ref[...] = k
    v_ref[...] = v
    allowed = segc[...] == segr[...]
    lane = lane_of((1, LANES))
    parts = []
    for head in range(3):
        tile = head // 2
        cols = slice(tile * LANES, (tile + 1) * LANES)
        mine = (lane < 64) if head % 2 == 0 else (lane >= 64)
        qh = jnp.where(mine, q[:, cols], jnp.zeros((), bf16))
        s = dot_nt(qh, k[:, cols])
        s = jnp.where(allowed, s, masked_score)
        top = jnp.max(s, axis=-1, keepdims=True)
        e = jnp.exp(s - top)
        total = jnp.sum(e, axis=-1, keepdims=True)
        lse_ref[head] = top + jnp.log(total)
        p = (e * (1.0 / total)).astype(bf16)
        parts.append(dot_nn(p, v[:, cols]))
    att = jnp.concatenate([jnp.where(lane < 64, parts[0], parts[1]), parts[2]], axis=1).astype(bf16)
    at_ref[...] = att
    branch = dot_nn(att, m_ref[...]).astype(bf16)
    for dx in range(2):
        keep_ref[dx] = branch[2 * dx * t : (2 * dx + 1) * t]
        send_ref[dx] = branch[(2 * dx + 1) * t : (2 * dx + 2) * t]


def half_sum_kernel(a_ref, b_ref, own_ref, send_ref):
    own_ref[...] = a_ref[0].astype(f32) + b_ref[0].astype(f32)
    send_ref[...] = (a_ref[1].astype(f32) + b_ref[1].astype(f32)).astype(bf16)


def norm_kernel(gain_row, bias_row, shift_row, h_ref, a_ref, r_ref, g_ref, b_ref, o_ref, low_ref, n_ref, i_ref):
    v = h_ref[...] + (a_ref[...].astype(f32) + r_ref[...].astype(f32) + b_ref[bias_row : bias_row + 1, :])
    n, inv = normed(v)
    o = n * g_ref[gain_row : gain_row + 1, :] + b_ref[shift_row : shift_row + 1, :]
    o_ref[...] = o
    low_ref[...] = o.astype(bf16)
    n_ref[...] = n
    i_ref[...] = inv


def feed_kernel(row, place, f0, f1, u0, u1, d0, d1, b_ref, act_ref, slope_ref, own_ref, send_ref):
    t = f0.shape[0]
    first = jnp.concatenate([f0[...], f1[...]], axis=0)
    total = None
    for i, (u, d) in enumerate(((u0, d0), (u1, d1))):
        up = dot_nn(first, u[...]) + b_ref[pl.ds(row + 2 * (place[0] ^ i) + place[1], 1), :]
        act, slope = gelu_and_slope(up)
        act = act.astype(bf16)
        act_ref[i] = act
        slope_ref[i] = slope.astype(bf16)
        part = dot_nt(act, d[...])
        total = part if total is None else total + part
    own_ref[...] = total[:t]
    send_ref[...] = total[t:].astype(bf16)


def norm_back(g, n, inv, gain):
    scaled = g * gain
    m1 = jnp.mean(scaled, axis=-1, keepdims=True)
    m2 = jnp.mean(scaled * n, axis=-1, keepdims=True)
    return inv * (scaled - m1 - n * m2)


def norm_sums(g, n, d, o_ref):
    o_ref[0:1, :] = jnp.sum(g * n, axis=0, keepdims=True)
    o_ref[1:2, :] = jnp.sum(g, axis=0, keepdims=True)
    o_ref[2:3, :] = jnp.sum(d, axis=0, keepdims=True)
    o_ref[3:8, :] = jnp.zeros((5, o_ref.shape[1]), f32)


def norm_back_kernel(gain_row, count, *refs):
    given, (g_ref, n_ref, i_ref, d_ref, low_ref, s_ref) = refs[:count], refs[count:]
    g = given[0][...].astype(f32)
    for r in given[1:]:
        g = g + r[...].astype(f32)
    n = n_ref[...]
    d = norm_back(g, n, i_ref[...], g_ref[gain_row : gain_row + 1, :])
    d_ref[...] = d
    low_ref[...] = d.astype(bf16)
    norm_sums(g, n, d, s_ref)


def stem_norm_back_kernel(width, count, place, *refs):
    given, (g_ref, n_ref, i_ref, keep_ref, send_ref, s_ref) = refs[:count], refs[count:]
    z, x = place[2], place[3]
    g = given[0][...].astype(f32)
    for r in given[1:]:
        g = g + r[...].astype(f32)
    n = n_ref[...]
    d = norm_back(g, n, i_ref[...], g_ref[0:1, :])
    norm_sums(g, n, d, s_ref)
    t = d.shape[0] // 2
    for a in range(2):
        part = d[a * t : (a + 1) * t]
        cols = [part[:, LANES * v : LANES * (v + 1)] for v in range(part.shape[1] // LANES)]
        for j in range(8):
            blk = piece_of(cols, j, width).astype(bf16)
            to_x(keep_ref, send_ref, x, j % 2, (j // 2) ^ z, (slice(None), slice(a * LANES, (a + 1) * LANES)), blk)


def to_x(keep_ref, send_ref, x, xi, rel, where, blk):
    @pl.when(x == xi)
    def _():
        keep_ref[(rel, *where)] = blk

    @pl.when(x != xi)
    def _():
        send_ref[(rel, *where)] = blk


def along_z_kernel(a_ref, b_ref, *outs):
    for rel, out in enumerate(outs):
        out[0] = a_ref[rel]
        out[1] = b_ref[rel]


def feed_back_kernel(e0, e1, u0, u1, d0, d1, slope_ref, dup_ref, own_ref, send_ref, bias_ref):
    t = e0.shape[0]
    d2 = jnp.concatenate([e0[...], e1[...]], axis=0)
    total = None
    for i, (u, d) in enumerate(((u0, d0), (u1, d1))):
        dup = dot_nn(d2, d[...]) * slope_ref[i].astype(f32)
        bias_ref[i : i + 1, :] = jnp.sum(dup, axis=0, keepdims=True)
        dup = dup.astype(bf16)
        dup_ref[i] = dup
        part = dot_nt(dup, u[...])
        total = part if total is None else total + part
    bias_ref[2:8, :] = jnp.zeros((6, bias_ref.shape[1]), f32)
    own_ref[...] = total[:t]
    send_ref[...] = total[t:].astype(bf16)


def feed_grad_kernel(place, a0, a1, b_ref, keep_ref, send_ref):
    z, x = place[2], place[3]
    left = jnp.concatenate([a0[...], a1[...]], axis=0)
    width = keep_ref.shape[-2]
    for i in range(2):
        g = dot_tn(left, b_ref[i]).astype(bf16)
        for j in range(8):
            zi, xi = j // 2, j % 2
            blk = g[j * width : (j + 1) * width]
            rz, rx = zi ^ z, xi ^ x
            (send_ref if i else keep_ref)[rx, rz % 2, rz // 2] = blk


def halves_kernel(count, *refs):
    given, made = refs[: 2 * count], refs[2 * count :]
    for i in range(count):
        a, b = given[2 * i], given[2 * i + 1]
        for h in range(2):
            out = made[2 * i + h]
            out[...] = (a[h].astype(f32) + b[h].astype(f32)).astype(out.dtype)


def one_kernel(a, b, o):
    o[...] = (a[...].astype(f32) + b[...].astype(f32)).astype(o.dtype)


def attend_back_kernel(e0, e1, e2, e3, q_ref, k_ref, v_ref, lse_ref, w_ref, m_ref, segr, segc,
                       dc_ref, keep_ref, send_ref, bias_ref, da_ref, dq_ref, dk_ref, dv_ref):
    t = e0.shape[0]
    d1 = jnp.concatenate([e0[...], e1[...], e2[...], e3[...]], axis=0)
    da_ref[...] = dot_nt(d1, m_ref[...]).astype(bf16)
    lane = lane_of((1, LANES))
    for ref in (dq_ref, dk_ref, dv_ref):
        ref[...] = jnp.zeros_like(ref)

    def one_head(head, carry):
        cols = pl.ds(pl.multiple_of((head // 2) * LANES, LANES), LANES)
        mine = (lane // 64) == lax.rem(head, 2)
        zero = jnp.zeros((), bf16)
        qh = jnp.where(mine, q_ref[:, cols], zero)
        dah = jnp.where(mine, da_ref[:, cols], zero)
        k = k_ref[:, cols]
        s = dot_nt(qh, k)
        p = jnp.where(segc[...] == segr[...], jnp.exp(s - lse_ref[head]), 0.0)
        dp = dot_nt(dah, v_ref[:, cols])
        delta = jnp.sum(p * dp, axis=-1, keepdims=True)
        ds = (p * (dp - delta)).astype(bf16)
        dq_ref[:, cols] += dot_nn(ds, jnp.where(mine, k, zero))
        dk_ref[:, cols] += dot_tn(ds, qh)
        dv_ref[:, cols] += dot_tn(p.astype(bf16), dah)
        return carry

    lax.fori_loop(0, 3, one_head, 0)
    tiles = [slice(0, LANES), slice(LANES, 2 * LANES)]
    dq = [dq_ref[:, c].astype(bf16).astype(f32) * 0.125 for c in tiles]
    dk = [dk_ref[:, c].astype(bf16).astype(f32) for c in tiles]
    dv = [dv_ref[:, c].astype(bf16).astype(f32) for c in tiles]
    wide = jnp.concatenate(dq + dk + dv, axis=1).astype(bf16)
    bias_ref[0:1, :] = jnp.concatenate([jnp.sum(d, axis=0, keepdims=True) for d in dq], axis=1)
    bias_ref[1:2, :] = jnp.concatenate([jnp.sum(d, axis=0, keepdims=True) for d in dv], axis=1)
    bias_ref[2:8, :] = jnp.zeros((6, 256), f32)
    dense = [dq[0], jnp.where(lane < 64, dq[1], pltpu.roll(dk[1], 64, 1)), dk[0], dv[0], dv[1]]
    dc_ref[...] = jnp.concatenate(dense, axis=1).astype(bf16)
    out = dot_nt(wide, w_ref[...]).astype(bf16)
    for dx in range(2):
        keep_ref[dx] = out[2 * dx * t : (2 * dx + 1) * t]
        send_ref[dx] = out[(2 * dx + 1) * t : (2 * dx + 2) * t]


def attend_grad_kernel(place, hl0, hl1, hl2, hl3, e0, e1, e2, e3, at_ref, dc_ref, keep_ref, send_ref):
    z, x = place[2], place[3]
    hl = jnp.concatenate([hl0[...], hl1[...], hl2[...], hl3[...]], axis=0)
    d1 = jnp.concatenate([e0[...], e1[...], e2[...], e3[...]], axis=0)
    width = keep_ref.shape[2]

    def put(zi, tile, blk):
        rel = zi ^ z

        @pl.when((zi ^ z) % 2 == 0)
        def _():
            keep_ref[rel // 2, tile] = blk

        @pl.when((zi ^ z) % 2 == 1)
        def _():
            send_ref[rel // 2, tile] = blk

    g = dot_tn(hl, dc_ref[...]).astype(bf16)
    for j in range(8):
        zi, xi = j // 2, j % 2
        for t in range(5):
            put(zi, (xi ^ x) * 5 + t, g[j * width : (j + 1) * width, t * LANES : (t + 1) * LANES])
    m = dot_tn(at_ref[...], d1)
    lane = lane_of((1, LANES))
    for xp in range(2):
        t = [m[xp * width : (xp + 1) * width, i * LANES : (i + 1) * LANES] for i in range(6)]
        first = [t[0], t[3], jnp.where(lane < 64, t[1], pltpu.roll(t[4], 64, 1))]
        second = [t[2], t[5], jnp.where(lane < 64, pltpu.roll(t[1], 64, 1), t[4])]
        for cp, tiles in enumerate((first, second)):
            for i, tile in enumerate(tiles):
                put(2 * xp + cp, 10 + i, tile.astype(bf16))


def pick_kernel(layers, place, *refs):
    own, came = refs[:layers], refs[layers]
    stay_ref, move_ref = refs[layers + 1 :]
    y, x = place[0], place[3]
    lane = lane_of((1, LANES))
    for l in range(layers):
        mine = [own[l][t].astype(f32) for t in range(5)]
        other = [came[l, t].astype(f32) for t in range(5)]

        def blocks(t):
            return [(t[0], t[1]), (t[2], pltpu.roll(t[1], 64, 1)), (t[3], t[4])]

        first = x == 0
        lowb, highb = blocks(mine), blocks(other)
        low_g = [tuple(jnp.where(first, a, b) for a, b in zip(m, o)) for m, o in zip(lowb, highb)]
        high_g = [tuple(jnp.where(first, b, a) for a, b in zip(m, o)) for m, o in zip(lowb, highb)]
        upper = [low_g[0], high_g[0], low_g[1]]
        lower = [high_g[1], low_g[2], high_g[2]]
        for i in range(3):
            for j in range(2):
                a, b = upper[i][j], lower[i][j]
                stay_ref[l, i, j] = jnp.where(y == 0, a, b).astype(bf16)
                move_ref[l, i, j] = jnp.where(y == 0, b, a).astype(bf16)
        m = [own[l][10 + t].astype(f32) for t in range(3)]
        stay_ref[l, 3, 0] = jnp.where(y == 0, m[0], m[1]).astype(bf16)
        move_ref[l, 3, 0] = jnp.where(y == 0, m[1], m[0]).astype(bf16)
        stay_ref[l, 3, 1] = m[2].astype(bf16)
        move_ref[l, 3, 1] = m[2].astype(bf16)


def settle_kernel(layers, place, a, b, part_ref, swap_ref, mix_ref):
    c = place[1]
    for l in range(layers):
        v = [[a[l, i, j].astype(f32) + b[l, i, j].astype(f32) for j in range(2)] for i in range(4)]
        for j in range(2):
            part_ref[l, 0, j] = jnp.where(c == 0, v[0][j], v[1][j]).astype(bf16)
            part_ref[l, 1, j] = jnp.where(c == 0, v[1][j], v[2][j]).astype(bf16)
            swap_ref[l, j] = jnp.where(c == 0, v[2][j], v[0][j]).astype(bf16)
            mix_ref[l, j] = v[3][j].astype(bf16)


def step_of(factor, g, m, a, w):
    moment = momentum_decay * m + g
    new = w.astype(f32) - factor * (g + momentum_decay * moment)
    return moment, average_decay * a + (1.0 - average_decay) * new, new


def tile_from(win, t, odd):
    cols = [win[:, i * LANES : (i + 1) * LANES].astype(f32) for i in (t, t + 1) if (i + 1) * LANES <= win.shape[1]]
    turned = [pltpu.roll(v, 64, 1) for v in cols]
    shifted = turned[0] if len(cols) == 1 else jnp.where(lane_of(cols[0].shape) < 64, turned[0], turned[1])
    return jnp.where(odd, shifted, cols[0])


def stepped(factor, l, at, t, m_ref, a_ref, w, outs):
    to = at + t.shape[1]
    for o, v in zip(outs, step_of(factor, t, m_ref[l, :, at:to], a_ref[l, :, at:to], w[:, : t.shape[1]])):
        o[l, :, at:to] = v
    return to


def window_copy(w_ref, win, sems, place, step, span):
    rows = win.shape[1]
    row = (2 * place[2] + place[3]) * rows
    start = (((2 * place[0] + place[1]) * step) // LANES) * LANES
    return fetched(
        [
            pltpu.make_async_copy(
                w_ref.at[l, pl.ds(pl.multiple_of(row, 32), rows), pl.ds(pl.multiple_of(start, LANES), span)],
                win.at[l],
                sems.at[l],
            )
            for l in range(win.shape[0])
        ]
    )


def olds_kernel(layers, gw, place, s_ref, p_ref, m_ref, f_ref, so, po, mo, fo, win_s, win_p, win_m, win_f, sems):
    y, c, z, x = (place[i] for i in range(4))
    seq_i, row_i = 2 * z + x, 2 * y + c
    rows, width = win_f.shape[1], win_f.shape[3]
    column = seq_i * 2 * gw
    start = jnp.minimum(column // LANES, 4) * LANES
    taps = win_s.shape[0]
    stem = pltpu.make_async_copy(
        s_ref.at[pl.ds(pl.multiple_of(row_i * taps, LANES), taps), pl.ds(pl.multiple_of(start, LANES), 256)],
        win_s, sems.at[0],
    )
    feeds = [
        pltpu.make_async_copy(
            f_ref.at[l, pl.ds(seq_i * rows, rows), :, pl.ds(pl.multiple_of(row_i * width, LANES), width)],
            win_f.at[l], sems.at[1 + l],
        )
        for l in range(layers)
    ]
    fetched([stem, *feeds])
    ins = window_copy(p_ref, win_p, sems.at[pl.ds(1 + layers, layers)], place, 576, 640)
    mixes = window_copy(m_ref, win_m, sems.at[pl.ds(1 + 2 * layers, layers)], place, 192, 256)
    r = lax.broadcasted_iota(jnp.int32, (LANES, 256), 0)
    k = lax.broadcasted_iota(jnp.int32, (LANES, 256), 1)
    chosen = jnp.where(k == r + (column - start), 1.0, 0.0).astype(bf16)
    parting = parting_matrix(2 * rows)
    odd = c == 1
    stem.wait()
    so[...] = dot_nt(chosen, win_s[...])[0 : 2 * gw].astype(bf16)
    for l in range(layers):
        feeds[l].wait()
        fo[l] = dot_nn(parting, win_f.at[l].reshape(2 * rows, width)[...]).astype(bf16)
        ins[l].wait()
        for t in range(5):
            po[l, :, t * LANES : (t + 1) * LANES] = tile_from(win_p[l], t, odd).astype(bf16)
        mixes[l].wait()
        for t in range(2):
            mo[l, :, t * LANES : (t + 1) * LANES] = tile_from(win_m[l], t, odd).astype(bf16)


def projection_step_kernel(factor, place, w_ref, part_ref, swap_ref, m_ref, a_ref, *outs):
    lane = lane_of((1, LANES))
    for l in range(m_ref.shape[0]):
        b0 = [part_ref[l, 0, j].astype(f32) for j in range(2)]
        b2 = [part_ref[l, 1, j].astype(f32) for j in range(2)]
        b1 = [pltpu.roll(swap_ref[l, j].astype(f32), 64, 1) for j in range(2)]
        tiles = [b0[0], jnp.where(lane < 64, b0[1], b1[0]), jnp.where(lane < 64, b1[0], b1[1]), b2[0], b2[1][:, :64]]
        at = 0
        for i, t in enumerate(tiles):
            at = stepped(factor, l, at, t, m_ref, a_ref, w_ref[l, :, i * LANES : (i + 1) * LANES], outs)


def mixing_step_kernel(factor, place, w_ref, mix_ref, m_ref, a_ref, *outs):
    y, c = place[0], place[1]
    lane = lane_of((1, LANES))
    for l in range(m_ref.shape[0]):
        full, half = mix_ref[l, 0].astype(f32), mix_ref[l, 1].astype(f32)
        turned = pltpu.roll(full, 64, 1)
        half = jnp.where(y == 0, half, pltpu.roll(half, 64, 1))
        tiles = [
            jnp.where(c == 0, full, jnp.where(lane < 64, half, turned)),
            jnp.where(c == 0, half, turned)[:, :64],
        ]
        at = 0
        for i, t in enumerate(tiles):
            at = stepped(factor, l, at, t, m_ref, a_ref, w_ref[l, :, i * LANES : (i + 1) * LANES], outs)


def feed_step_kernel(factor, place, w_ref, *refs):
    layers = w_ref.shape[0]
    parts, (m_ref, a_ref), outs = refs[: 4 * layers], refs[4 * layers : 4 * layers + 2], refs[4 * layers + 2 :]
    rows = m_ref.shape[1]
    for l in range(layers):
        for kind in range(2):
            a, b = parts[4 * l + 2 * kind], parts[4 * l + 2 * kind + 1]
            g = a[...].astype(f32) + b[...].astype(f32)
            w = w_ref[l, kind * rows : (kind + 1) * rows, :]
            for o, v in zip(outs, step_of(factor, g, m_ref[l, :, kind, :], a_ref[l, :, kind, :], w)):
                o[l, :, kind, :] = v


def stem_step_kernel(factor, gw, place, w_ref, p_ref, r_ref, m_ref, a_ref, *outs):
    count = p_ref.shape[0] // gw
    lane = lane_of((gw, LANES))
    for group in range(2):
        pieces = []
        for k in range(count):
            rows_k = slice(k * gw, (k + 1) * gw)
            v = p_ref[rows_k, :].astype(f32) + r_ref[rows_k, :].astype(f32)
            v = v if group == 0 else pltpu.roll(v, LANES - gw, 1)
            pieces.append(jnp.where(lane < gw, v, 0.0))
        mine = slice(group * gw, (group + 1) * gw)
        for i, t in enumerate(tiles_of(pieces, gw)):
            cols = slice(i * LANES, (i + 1) * LANES)
            for o, v in zip(outs, step_of(factor, t, m_ref[mine, cols], a_ref[mine, cols], w_ref[mine, cols])):
                o[mine, cols] = v


def smalls_kernel(layers, ff_rows, gains, width, head_share, place, *refs):
    norms, ups, atts = refs[: 2 * layers + 1], refs[2 * layers + 1 : 3 * layers + 1], refs[3 * layers + 1 : 4 * layers + 1]
    keep_ref, send_ref, all_ref = refs[4 * layers + 1 :]
    y, c, z, x = (place[i] for i in range(4))
    all_ref[...] = jnp.zeros_like(all_ref)
    all_ref[0:1, :] = norms[0][0:1, :]
    all_ref[gains + 1 : gains + 2, :] = norms[0][1:2, :]
    for l in range(layers):
        base = gains + 2 + l * (6 + ff_rows)
        for k, (gain, shift, plain) in enumerate(((1, 3, 2), (2, 5, 4))):
            s = norms[1 + 2 * l + k]
            all_ref[gain + 2 * l : gain + 2 * l + 1, :] = s[0:1, :]
            all_ref[base + shift : base + shift + 1, :] = s[1:2, :]
            all_ref[base + plain : base + plain + 1, :] = s[2:3, :]
        for ry in range(2):
            all_ref[pl.ds(base + 6 + 2 * (y ^ ry) + c, 1), :] = ups[l][ry : ry + 1, :]
        for group in range(4):

            @pl.when(2 * x + c == group)
            def _(l=l, base=base, group=group):
                for i in range(2):
                    pieces = [jnp.zeros((1, LANES), f32)] * (width // 64)
                    for h in range(3):
                        t = atts[l][i : i + 1, (h // 2) * LANES : (h // 2 + 1) * LANES]
                        t = t if h % 2 == 0 else pltpu.roll(t, 64, 1)
                        pieces[3 * group + h] = jnp.where(lane_of(t.shape) < 64, t, 0.0)
                    all_ref[base + i : base + i + 1, :] = jnp.concatenate(tiles_of(pieces, 64), axis=1)

    whole = all_ref[...]
    cols = [whole[:, LANES * v : LANES * (v + 1)] for v in range(width // LANES)]
    for j in range(8):
        blk = piece_of(cols, j, width // 8)
        rel = (j // 2) ^ z
        at = (rel % 2) * 2 + rel // 2

        @pl.when(x == j % 2)
        def _(blk=blk, at=at):
            keep_ref[at] = blk

        @pl.when(x != j % 2)
        def _(blk=blk, at=at):
            send_ref[at] = blk


def small_total_kernel(row, a_ref, r_ref, b_ref, o_ref):
    total = a_ref[...] + r_ref[...]
    o_ref[...] = total
    o_ref[row : row + 1, :] = total[row : row + 1, :] + b_ref[0:1, :]


def encoded_split_kernel(place, x_ref, *outs):
    z = place[2]
    for rel, out in enumerate(outs):
        for a in range(2):
            at = pl.multiple_of(a * 64 + (z ^ rel) * 16, 16)
            out[a * 16 : a * 16 + 16, :] = x_ref[pl.ds(at, 16), :]


def encoded_route_kernel(place, r0, r1, r2, r3, keep_ref, send_ref):
    c, z = place[1], place[2]
    for rel, src in enumerate((r0, r1, r2, r3)):
        row = z ^ rel
        mine = (row // 2) == c

        @pl.when(mine)
        def _(src=src, row=row):
            keep_ref[row % 2] = src[...]

        @pl.when(jnp.logical_not(mine))
        def _(src=src, row=row):
            send_ref[row % 2] = src[...]


def encoded_join_kernel(place, keep_ref, recv_ref, o_ref, mixed):
    c = place[1]
    rows, toks, width = o_ref.shape
    for r in range(rows):
        for v in range(width // LANES):
            cols = slice(v * LANES, (v + 1) * LANES)
            for rel, src in enumerate((keep_ref, recv_ref)):
                for a in range(2):
                    at = v * toks + (c ^ rel) * 32 + a
                    mixed[pl.ds(at, 16, stride=2), :] = src[r, a * 16 : a * 16 + 16, cols].astype(f32)
            o_ref[r, :, cols] = mixed[v * toks : (v + 1) * toks, :]


def take_kernel(place, r0, r1, r2, r3, keep_ref, send_ref):
    c, z, x = place[1], place[2], place[3]
    for rel, src in enumerate((r0, r1, r2, r3)):
        row = z ^ rel
        mine = (row // 2) == c
        for h in range(2):

            @pl.when(mine)
            def _(src=src, row=row, h=h):
                keep_ref[row % 2, x ^ h] = src[h]

            @pl.when(jnp.logical_not(mine))
            def _(src=src, row=row, h=h):
                send_ref[row % 2, x ^ h] = src[h]


def stem_slope_kernel(rows, place, keep_ref, recv_ref, pre_ref, low_ref, ds_ref, bias_ref):
    c = place[1]
    for r in range(rows):
        for zf in range(4):
            for xq in range(2):
                for rel, src in enumerate((keep_ref, recv_ref)):
                    u = pl.multiple_of(((zf * 2 + xq) * 2 + (c ^ rel)) * 16, 16)
                    ds_ref[r, pl.ds(u, 16), :] = src[r, xq, zf * 16 : zf * 16 + 16, :]
    total = None
    for r in range(rows):
        dpre = ds_ref[r].astype(f32) * gelu_and_slope(pre_ref[r])[1]
        part = jnp.sum(dpre, axis=0, keepdims=True)
        total = part if total is None else total + part
        low_ref[r] = dpre.astype(bf16)
    bias_ref[0:1, :] = total[:, 0:LANES] + total[:, LANES : 2 * LANES]
    bias_ref[1:8, :] = jnp.zeros((7, LANES), f32)


def stem_grad_kernel(rows, taps, gw, place, ph_ref, low_ref, keep_ref, send_ref):
    n = low_ref.shape[1]
    y, c = place[0], place[1]
    left = jnp.concatenate([low_ref[r] for r in range(rows)], axis=0).T
    lane = lane_of((gw, LANES))
    per = taps // 4
    for rc, out in enumerate((keep_ref, send_ref)):
        for ry in range(2):
            block = (y ^ ry) * 2 + (c ^ rc)

            def win(i):
                at = pl.multiple_of((block + i // 16) * 16, 16)
                return ph_ref[i % 16, :, pl.ds(at, n), :].reshape(rows * n, 2 * LANES)

            def save(k, t, out=out, ry=ry):
                out[ry, k * gw : (k + 1) * gw, :] = jnp.where(lane < gw, t[0:gw], t[gw : 2 * gw]).astype(bf16)

            held = None
            for i in range(per // 2 + 1):
                if i < per // 2:
                    g = dot_nn(left, win(i))
                    cross = g[LANES:, 0:LANES]
                else:
                    cross = dot_nn(left[LANES:], win(i)[:, 0:LANES])
                if held is not None:
                    save(2 * i - 1, held + cross)
                if i < per // 2:
                    save(2 * i, g[0:LANES, 0:LANES] + g[LANES:, LANES:])
                    held = g[0:LANES, LANES:]


def stem_input_grad_kernel(rows, half, place, low_ref, ds_ref, w_ref, keep_ref, send_ref, qf, ph, acc):
    n = low_ref.shape[1]
    span = n + half
    for r in range(rows):
        qf[r, 0 : half // 2, :] = jnp.zeros((half // 2, 2 * LANES), f32)
        qf[r, half // 2 + n :, :] = jnp.zeros((half // 2, 2 * LANES), f32)
        qf[r, half // 2 : half // 2 + n, :] = low_ref[r].astype(f32)
    for p in range(16):
        m = span if p == 0 else span - 16
        for r in range(rows):
            ph[p, r, 0:m, :] = qf[r, p : p + m, :].astype(bf16)
    acc[...] = jnp.zeros_like(acc)

    def body(i, carry):
        left, upper, lower = [], [], []
        for t in range(5):
            m = i * 5 + t
            here, before, after = w_ref[2 * half + 1 - 2 * m], w_ref[2 * half - 2 * m], w_ref[2 * half + 2 - 2 * m]
            upper += [here, before]
            lower += [after, here]
            left.append(window(ph, m, rows, n))
        right = jnp.concatenate([jnp.concatenate(upper, 1), jnp.concatenate(lower, 1)], 0)
        acc[...] += dot_nt(jnp.concatenate(left, 1), right)
        return carry

    lax.fori_loop(0, (half + 1) // 5, body, 0)
    per = n // 8
    for r in range(rows):
        g = (acc[r * n : (r + 1) * n, :] + ds_ref[r].astype(f32)).astype(bf16)
        for j in range(8):
            to_x(keep_ref, send_ref, place[3], j % 2, (j // 2) ^ place[2], (r,), g[j * per : (j + 1) * per, :])


def join_kernel(width, place, r0, r1, r2, r3, o_ref, mixed, by_channel):
    z, x = place[2], place[3]
    rows, per = r0.shape[1], r0.shape[2]
    for rel, src in enumerate((r0, r1, r2, r3)):
        for h in range(2):
            by_channel[(z ^ rel) * 2 + (x ^ h)] = src[h]
    for r in range(rows):
        for a in range(2):
            pieces = [by_channel[j, r, :, a * LANES : (a + 1) * LANES].astype(f32) for j in range(8)]
            for v, col in enumerate(tiles_of(pieces, width)):
                mixed[pl.ds(v * 2 * per + a, per, stride=2), :] = col
        for v in range(o_ref.shape[2] // LANES):
            o_ref[r, :, v * LANES : (v + 1) * LANES] = mixed[v * 2 * per : (v + 1) * 2 * per, :]


def swapped(v, axis):
    return lax.ppermute(v, axis, [(0, 1), (1, 0)])


def across(v, axis, bit):
    count = lax.axis_size(axis)
    return lax.ppermute(v, axis, [(i, i ^ bit) for i in range(count)])


def one_sum(a, b):
    return whole_call(one_kernel, [sds(a.shape, a.dtype)], [a, b])[0]


def local_rows(
    features, cotangent, segments, stem_weight, projection_weight, mixing_weight,
    feedforward_weight, norm_gains, biases, *state,
):
    rows, toks, width = features.shape
    yi, ci, zi, xi = (lax.axis_index(a) for a in ("y", "c", "z", "x"))
    place = jnp.stack([yi, ci, zi, xi]).astype(jnp.int32)
    seq_i, row_i = zi * 2 + xi, yi * 2 + ci
    seq = ("z", "x")
    blocks = 8
    share = width // blocks
    gw = width // GROUPS
    frames = toks * blocks
    half = KERNEL // 2
    layers = projection_weight.shape[0]
    ff_rows = feedforward_weight.shape[3] // width
    head_share = width // 4
    group = 2 * xi + ci
    t = rows * toks

    stem_share = jnp.pad(
        lax.dynamic_slice_in_dim(stem_weight, seq_i * share, share, 1), ((0, 0), (0, LANES - share))
    )

    steps = width // LANES
    square = sds((width, width), bf16)
    *feed_first, feed_there = whole_call(
        functools.partial(feed_weights_kernel, 0), [square] * 4, [place, feedforward_weight],
        scalars=1, far=(1,), token=True, vmem=FAR_BYTES,
        scratch=[pltpu.VMEM((2, width, 2, width), bf16), pltpu.SemaphoreType.DMA((2 * steps,))],
    )

    (sent,) = whole_call(
        functools.partial(split_kernel, blocks, share), [sds((blocks, rows, toks, LANES), bf16)], [features]
    )
    mine = lax.all_to_all(sent, seq, 0, 0, tiled=True)
    conv_bias = jnp.pad(
        lax.dynamic_slice(biases, (0, seq_i * share), (1, share)), ((0, 0), (0, LANES - share))
    )
    n = frames // 2
    exchange = sds((rows, 2, 64, 2 * LANES), bf16)
    tap_scratch = pltpu.VMEM((KERNEL + 3, LANES, LANES), bf16)
    phased = (16, rows, (frames + 2 * half) // 2, 2 * LANES)
    row_scratch = pltpu.VMEM((rows * (frames + 2 * half), LANES), f32)
    pre_act, kept, away = whole_call(
        functools.partial(conv_kernel, rows, frames, half, gw),
        [sds((rows, n, 2 * LANES), f32), exchange, exchange],
        [place, mine, stem_share, conv_bias],
        after=[feed_there],
        scalars=1,
        scratch=[pltpu.VMEM(phased, bf16), row_scratch, pltpu.VMEM((rows * n, 2 * LANES), f32), tap_scratch],
        vmem=WIDE_BYTES,
    )
    (slots,) = whole_call(
        slots_kernel, [sds((blocks, 64, 2 * LANES), bf16)], [place, kept, swapped(away, "c")], scalars=1
    )
    *later, later_there = whole_call(
        functools.partial(later_weights_kernel, layers, [2 + l * (6 + ff_rows) for l in range(layers)], head_share),
        [square] * (4 * (layers - 1)) + [square, sds((256, width), bf16), sds((2, 256), f32)] * layers,
        [place, feedforward_weight, projection_weight, mixing_weight, biases],
        scalars=1, far=(1, 2, 3), token=True, vmem=FAR_BYTES, after=[slots],
        scratch=[
            pltpu.VMEM((layers - 1, 2, width, 2, width), bf16),
            pltpu.VMEM((layers, 3, width, 256), bf16),
            pltpu.SemaphoreType.DMA((layers - 1, 2 * steps)),
            pltpu.SemaphoreType.DMA((4 * layers,)),
        ],
    )
    feed_w = [feed_first, *(later[4 * i : 4 * i + 4] for i in range(layers - 1))]
    attend_w = [later[4 * (layers - 1) + 3 * l :][:3] for l in range(layers)]
    joined = lax.all_to_all(slots, seq, 0, 0, tiled=True)
    wide = sds((t, width), f32)
    thin = sds((t, width), bf16)
    column = sds((t, 1), f32)
    hidden, hidden_low, normed_stem, inverse_stem = whole_call(
        functools.partial(stem_norm_kernel, share), [wide, thin, wide, column], [joined, norm_gains, biases],
        after=[later_there],
    )

    def gathered(v):
        over_c = swapped(v, "c")
        over_x = swapped(v, "x")
        return [v, over_c, over_x, swapped(over_x, "c")]

    saved = []
    segments_other = swapped(segments, "c")
    quarter_row = sds((32, width), bf16)
    two = sds((2, t, width), bf16)
    full = 4 * t
    for l in range(layers):
        base = 2 + l * (6 + ff_rows)
        in_w, mix_w, both_b = attend_w[l]
        ups, downs = feed_w[l][:2], feed_w[l][2:]
        hl = gathered(hidden_low)
        before = []
        if l == 0:
            seg_row, seg_col = whole_call(
                segments_kernel, [sds((1, frames), f32), sds((frames, 1), f32)], [place, segments, segments_other],
                scalars=1, after=[hidden_low],
            )
            stay, move, cot_there = whole_call(
                cotangent_split_kernel, [sds((rows, 32, width), bf16)] * 2, [place, cotangent],
                scalars=1, after=[hidden_low], token=True,
                scratch=[pltpu.VMEM((width // LANES * toks, LANES), f32)],
            )
            before = [cot_there]
        elif l == 1:
            cot, cot_there = whole_call(
                cotangent_join_kernel, [sds((t, width), bf16)],
                [place, routed[0], *(across(routed[rel], "z", rel) for rel in range(1, 4))],
                scalars=1, after=[hidden_low], token=True,
            )
            before = [cot_there]
        q, k, v, att, lse, keep, send = whole_call(
            functools.partial(attend_kernel, base),
            [sds((full, 256), bf16)] * 4 + [sds((3, full, 1), f32), two, two],
            hl + [in_w, mix_w, both_b, seg_row, seg_col],
            after=before,
        )
        own, pass_on = whole_call(half_sum_kernel, [wide, thin], [keep, swapped(send, "c")])
        rest = swapped(pass_on, "x")
        before = []
        if l == 0:
            *routed, cot_there = whole_call(
                cotangent_route_kernel, [quarter_row] * 4, [place, stay, swapped(move, "c")],
                scalars=1, after=[pass_on], token=True,
            )
            before = [cot_there]
        first, first_low, n1, i1 = whole_call(
            functools.partial(norm_kernel, 1 + 2 * l, base + 2, base + 3),
            [wide, thin, wide, column],
            [hidden, own, rest, norm_gains, biases],
            after=before,
        )
        first_other = swapped(first_low, "c")
        act, slope, own, send = whole_call(
            functools.partial(feed_kernel, base + 6),
            [sds((2, 2 * t, width), bf16)] * 2 + [wide, thin],
            [place, first_low, first_other, *ups, *downs, biases],
            scalars=1,
        )
        hidden, hidden_low, n2, i2 = whole_call(
            functools.partial(norm_kernel, 2 + 2 * l, base + 4, base + 5),
            [wide, thin, wide, column],
            [first, own, swapped(send, "c"), norm_gains, biases],
        )
        saved.append((in_w, mix_w, ups, downs, hl, q, k, v, att, lse, n1, i1, first_low, first_other, act, slope, n2, i2))

    encoded_low = hidden_low
    sums = sds((8, width), f32)
    terms = [cot]
    norm_sum = [None] * norm_gains.shape[0]
    up_sum, att_sum = [None] * layers, [None] * layers
    feed_a, feed_b, att_parts = [None] * layers, [None] * layers, [None] * layers
    parted = sds((2, 2, 2, share, width), bf16)
    tiles = sds((13, share, LANES), bf16)
    tiles_z = sds((2, 13, share, LANES), bf16)

    def send_on(parts, after):
        outs, operands = [], []
        for keep, recv, _ in parts:
            outs += [sds(keep.shape[1:], keep.dtype)] * 2
            operands += [keep, recv]
        made = whole_call(
            functools.partial(halves_kernel, len(parts)), outs, operands, after=after, token=True
        )
        return [(made[2 * i], how(made[2 * i + 1])) for i, (_, _, how) in enumerate(parts)], made[-1]

    over_x, over_y = (lambda v: swapped(v, "x")), (lambda v: swapped(v, "y"))
    over_z1, over_z2 = (lambda v: across(v, "z", 1)), (lambda v: across(v, "z", 2))
    before = []
    for l in reversed(range(layers)):
        base = 2 + l * (6 + ff_rows)
        in_w, mix_w, ups, downs, hl, q, k, v, att, lse, n1, i1, first_low, first_other, act, slope, n2, i2 = saved[l]
        d2, d2_low, norm_sum[2 + 2 * l] = whole_call(
            functools.partial(norm_back_kernel, 2 + 2 * l, len(terms)), [wide, thin, sums], terms + [norm_gains, n2, i2],
            after=before,
        )
        d2_other = swapped(d2_low, "c")
        dup, own, send, up_sum[l] = whole_call(
            feed_back_kernel,
            [sds((2, 2 * t, width), bf16), wide, thin, sums],
            [d2_low, d2_other, *ups, *downs, slope],
        )
        b_keep, b_send, b_there = whole_call(
            feed_grad_kernel, [parted] * 2, [place, d2_low, d2_other, act], scalars=1, after=[send], token=True,
        )
        feed_b[l] = (b_keep, over_y(b_send))
        d1, d1_low, norm_sum[1 + 2 * l] = whole_call(
            functools.partial(norm_back_kernel, 1 + 2 * l, 3),
            [wide, thin, sums],
            [d2, own, swapped(send, "c"), norm_gains, n1, i1],
            after=[b_there, *([] if l else [feed_b[1][1]])],
        )
        dl = gathered(d1_low)
        a_keep, a_send, a_there = whole_call(
            feed_grad_kernel, [parted] * 2, [place, first_low, first_other, dup], scalars=1, after=[d1_low], token=True,
        )
        feed_a[l] = (a_keep, over_y(a_send))
        before = [a_there]
        if l == 1:
            *encoded_parts, there = whole_call(
                encoded_split_kernel, [quarter_row] * 4, [place, encoded_low], scalars=1, after=[d1_low], token=True,
            )
            before += [there]
        else:
            encoded, there = whole_call(
                encoded_join_kernel, [sds((rows, toks, width), f32)], [place, stay, swapped(move, "c")],
                scalars=1, after=[d1_low], token=True,
                scratch=[pltpu.VMEM((width // LANES * toks, LANES), f32)],
            )
            before += [there]
            (feed_a[1], feed_b[1], att_parts[1]), there = send_on(
                [(*feed_a[1], over_x), (*feed_b[1], over_z1), (*att_parts[1], over_z2)], [d1_low]
            )
            before += [there]
        dense_dp, keep, send, att_sum[l] = whole_call(
            attend_back_kernel,
            [sds((full, 640), bf16), two, two, sds((8, 256), f32)],
            dl + [q, k, v, lse, in_w, mix_w, seg_row, seg_col],
            after=before,
            scratch=[pltpu.VMEM((full, 256), bf16)] + [pltpu.VMEM((full, 256), f32)] * 3,
        )
        own, pass_on = whole_call(
            half_sum_kernel, [wide, thin], [keep, swapped(send, "c")], after=[] if l else [feed_a[1][1]]
        )
        rest = swapped(pass_on, "x")
        terms = [d1, own, rest]

        def attend_grad(after, hl=hl, dl=dl, att=att, dense_dp=dense_dp):
            return whole_call(
                attend_grad_kernel, [tiles_z, tiles_z], [place] + hl + dl + [att, dense_dp],
                scalars=1, after=after, token=True,
            )

        before = []
        if l == 1:
            keep, send, there = attend_grad([pass_on])
            att_parts[l] = (keep, over_z1(send))
            stay, move, route_there = whole_call(
                encoded_route_kernel, [sds((2, 32, width), bf16)] * 2,
                [place, encoded_parts[0], *(across(encoded_parts[rel], "z", rel) for rel in range(1, 4))],
                scalars=1, after=[pass_on], token=True,
            )
            (feed_b[l],), sent_there = send_on([(*feed_b[l], over_x)], [pass_on])
            before = [there, route_there, sent_there]
        else:
            (feed_a[1],), there = send_on([(*feed_a[1], over_z1)], [pass_on])
            before = [there]

    quad = sds((4, 64, 2 * LANES), bf16)
    ds_keep, ds_sent, norm_sum[0] = whole_call(
        functools.partial(stem_norm_back_kernel, share, len(terms)),
        [quad, quad, sums],
        [place, *terms, norm_gains, normed_stem, inverse_stem],
        scalars=1,
        after=before,
    )

    def spread(keep, send):
        four = whole_call(
            along_z_kernel, [sds((2, *keep.shape[1:]), bf16)] * 4, [keep, swapped(send, "x")]
        )
        return four[0], [four[0], *(across(four[rel], "z", rel) for rel in range(1, 4))]

    ds_first, ds_blocks = spread(ds_keep, ds_sent)
    gain_count, bias_count = norm_gains.shape[0], biases.shape[0]
    small_half = sds((4, 32, LANES), f32)
    small_keep, small_send, small_there = whole_call(
        functools.partial(smalls_kernel, layers, ff_rows, gain_count, width, head_share),
        [small_half, small_half],
        [place, *norm_sum, *up_sum, *att_sum],
        scalars=1,
        scratch=[pltpu.VMEM((32, width), f32)],
        token=True,
        after=[ds_sent],
    )
    smalls = (small_keep.reshape(2, 2, 32, LANES), swapped(small_send, "x").reshape(2, 2, 32, LANES))
    phases, taps, phases_there = whole_call(
        functools.partial(phases_kernel, rows, frames, half, gw),
        [sds(phased, bf16), sds((KERNEL + 3, LANES, LANES), bf16)], [mine, stem_share], scratch=[row_scratch],
        after=[ds_sent], token=True,
    )
    keep, send, att_there = attend_grad([ds_first])
    att_parts[0] = (keep, over_z1(send))
    (feed_b[0], feed_b[1]), there = send_on([(*feed_b[0], over_x), (*feed_b[1], over_z2)], [ds_first])
    stay, move = whole_call(
        take_kernel, [sds((2, 2, 64, 2 * LANES), bf16)] * 2, [place, *ds_blocks], scalars=1,
        after=[small_there, phases_there, att_there, there],
    )
    pair = sds((rows, n, 2 * LANES), bf16)
    dpre_low, ds, stem_sums = whole_call(
        functools.partial(stem_slope_kernel, rows), [pair, pair, sds((8, LANES), f32)],
        [place, stay, swapped(move, "c"), pre_act], scalars=1,
    )
    quarter = sds((2, KERNEL // 4 * gw, LANES), bf16)
    keep, send = whole_call(
        functools.partial(stem_grad_kernel, rows, KERNEL, gw), [quarter, quarter], [place, phases, dpre_low], scalars=1,
    )
    stem_part = (keep, swapped(send, "c"))
    (feed_a[0], feed_b[0], feed_a[1], att_parts[0]), there = send_on(
        [(*feed_a[0], over_x), (*feed_b[0], over_z1), (*feed_a[1], over_z2), (*att_parts[0], over_z2)], [send]
    )
    back_shape = sds((4, rows, toks // 2, 2 * LANES), bf16)
    back_keep, back = whole_call(
        functools.partial(stem_input_grad_kernel, rows, half),
        [back_shape] * 2,
        [place, dpre_low, ds, taps],
        scalars=1,
        scratch=[
            pltpu.VMEM((rows, n + half, 2 * LANES), f32),
            pltpu.VMEM((16, rows, n + half, 2 * LANES), bf16),
            pltpu.VMEM((rows * n, 2 * LANES), f32),
        ],
        after=[there],
        vmem=WIDE_BYTES,
    )
    olds = whole_call(
        functools.partial(olds_kernel, layers, gw),
        [
            sds((share, KERNEL // 4 * gw), bf16),
            sds((layers, share, 640), bf16),
            sds((layers, share, 256), bf16),
            sds((layers, 2 * share, width), bf16),
        ],
        [place, stem_weight, projection_weight, mixing_weight, feedforward_weight],
        scalars=1, far=(1, 2, 3, 4), vmem=WIDE_BYTES, after=[back], token=True,
        scratch=[
            pltpu.VMEM((KERNEL // 4 * gw, 256), bf16),
            pltpu.VMEM((layers, share, 640), bf16),
            pltpu.VMEM((layers, share, 256), bf16),
            pltpu.VMEM((layers, share, 2, width), bf16),
            pltpu.SemaphoreType.DMA((1 + 3 * layers,)),
        ],
    )
    back_first, back_blocks = spread(back_keep, back)
    (stem_part,), there = send_on([(*stem_part, over_y)], [back_first])
    (features_gradient,) = whole_call(
        functools.partial(join_kernel, share), [sds((rows, toks, width), f32)], [place, *back_blocks], scalars=1,
        scratch=[
            pltpu.VMEM((width // LANES * toks, LANES), f32),
            pltpu.VMEM((blocks, rows, toks // 2, 2 * LANES), bf16),
        ],
        after=[there, olds[-1]],
    )
    (feed_a[0], feed_b[0], smalls), there = send_on(
        [(*feed_a[0], over_z1), (*feed_b[0], over_z2), (*smalls, over_z1)], [features_gradient]
    )
    att_grads = [whole_call(one_kernel, [tiles], list(part), after=[there])[0] for part in att_parts]
    att_came = swapped(jnp.stack([a[5:10] for a in att_grads]), "x")
    settled = sds((layers, 4, 2, share, LANES), bf16)
    stay, move = whole_call(
        functools.partial(pick_kernel, layers), [settled] * 2, [place, *att_grads, att_came], scalars=1,
    )
    (feed_a[0], smalls), there = send_on([(*feed_a[0], over_z2), (*smalls, over_z2)], [move])
    (small_total,) = whole_call(
        functools.partial(small_total_kernel, gain_count), [sds((32, LANES), f32)], [*smalls, stem_sums], after=[there]
    )
    in_part, swap_part, mix_part = whole_call(
        functools.partial(settle_kernel, layers),
        [sds((layers, 2, 2, share, LANES), bf16)] + [sds((layers, 2, share, LANES), bf16)] * 2,
        [place, stay, swapped(move, "y")],
        scalars=1,
    )
    swap_part = swapped(swap_part, "c")
    route = []
    for c in range(2):
        for z in range(4):
            for x in range(2):
                route.append(((c * 4 + z) * 2 + x, ((z & 1) * 4 + (2 * x + c)) * 2 + (z >> 1)))
    mix_part = lax.ppermute(mix_part, ("c", "z", "x"), route)
    small_total = one_sum(small_total, swapped(small_total, "c"))
    small_total = one_sum(small_total, swapped(small_total, "y"))

    rate_base = 1.0 / math.sqrt(rows * 4 * frames)

    def step(index, kernel, operands, turn=False):
        m, a = state[index], state[6 + index]
        if turn:
            m, a = m.T, a.T
        made = whole_call(
            functools.partial(kernel, rate_factors[index] * rate_base), [sds(m.shape, f32)] * 3,
            [place, olds[index], *operands, m, a], scalars=1,
        )
        return [o.T for o in made] if turn else made

    results = [
        step(0, lambda f, *r: stem_step_kernel(f, gw, *r), list(stem_part), turn=True),
        step(1, projection_step_kernel, [in_part, swap_part]),
        step(2, mixing_step_kernel, [mix_part]),
        step(3, feed_step_kernel, [part for l in range(layers) for kind in (feed_a, feed_b) for part in kind[l]]),
    ]
    for index, w, g in ((4, norm_gains, small_total[:gain_count]), (5, biases, small_total[gain_count : gain_count + bias_count])):
        w = lax.dynamic_slice_in_dim(w, seq_i * share, share, 1)
        results.append(step_of(rate_factors[index] * rate_base, g[:, :share], state[index], state[6 + index], w))
    return (encoded, features_gradient, *(results[i][k] for k in range(3) for i in range(6)))


def solution(mesh):
    if mesh.shape["row"] == 4 and mesh.shape["seq"] == 8:
        body, mesh = local_rows, Mesh(mesh.devices.reshape(2, 2, 4, 2), ("y", "c", "z", "x"))
        row, seq = ("y", "c"), ("z", "x")
    else:
        body, row, seq = local, "row", "seq"
    in_specs = (
        P(row, seq, None),
        P(row, seq, None),
        P(row, None),
        P(),
        P(),
        P(),
        P(),
        P(),
        P(),
        P(row, seq),
        P(None, seq, row),
        P(None, seq, row),
        P(None, seq, None, row),
        P(None, seq),
        P(None, seq),
        P(row, seq),
        P(None, seq, row),
        P(None, seq, row),
        P(None, seq, None, row),
        P(None, seq),
        P(None, seq),
    )
    out_specs = (
        P(row, seq, None),
        P(row, seq, None),
        P(row, seq),
        P(None, seq, row),
        P(None, seq, row),
        P(None, seq, None, row),
        P(None, seq),
        P(None, seq),
        P(row, seq),
        P(None, seq, row),
        P(None, seq, row),
        P(None, seq, None, row),
        P(None, seq),
        P(None, seq),
        P(row, seq),
        P(None, seq, row),
        P(None, seq, row),
        P(None, seq, None, row),
        P(None, seq),
        P(None, seq),
    )
    return jax.shard_map(body, mesh=mesh, in_specs=in_specs, out_specs=out_specs, check_vma=False)
```

```python
import functools
import math

import jax
import jax.numpy as jnp
from jax import lax
from jax.experimental import pallas as pl
from jax.experimental.pallas import tpu as pltpu
from jax.sharding import Mesh
from jax.sharding import PartitionSpec as P

HEADS = 12
KERNEL = 128
GROUPS = 16


epsilon = 1e-05
masked_score = -1e30
momentum_decay = 0.9
average_decay = 0.5
rate_factors = (0.012, 0.08, 0.6, 0.03, 0.06, 0.09)
row_dims = (0, 2, 2, 3)


def extended_2(cells, sides, width):
    for axis, dim in sides:
        count = lax.axis_size(axis)
        ends = count - 1
        head = lax.slice_in_dim(cells, 0, width, axis=dim)
        tail = lax.slice_in_dim(cells, cells.shape[dim] - width, cells.shape[dim], axis=dim)
        cells = jnp.concatenate(
            [
                lax.ppermute(tail, axis, [(i, (i + 1) % count) for i in range(ends)]),
                cells,
                lax.ppermute(head, axis, [((i + 1) % count, i) for i in range(ends)]),
            ],
            axis=dim,
        )
    return cells


def layer_norm(values, gain_row, shift_row):
    centre = jnp.mean(values, axis=-1, keepdims=True)
    centred = values - centre
    spread = jnp.mean(centred * centred, axis=-1, keepdims=True)
    inverse = lax.rsqrt(spread + epsilon)
    normed = centred * inverse
    return (normed * gain_row + shift_row, normed, inverse)


def layer_norm_back(upstream, normed, inverse, gain_row):
    scaled = upstream * gain_row
    first_mean = jnp.mean(scaled, axis=-1, keepdims=True)
    second_mean = jnp.mean(scaled * normed, axis=-1, keepdims=True)
    downstream = inverse * (scaled - first_mean - normed * second_mean)
    return (downstream, jnp.sum(upstream * normed, axis=(0, 1)), jnp.sum(upstream, axis=(0, 1)))


def gelu_exact(values):
    return jax.nn.gelu(values, approximate=False)


def gelu_back(inputs, upstream):
    _, pullback = jax.vjp(gelu_exact, inputs)
    return pullback(upstream)[0]


def group_conv(extended, kernel_taps, group_count):
    return lax.conv_general_dilated(
        extended,
        kernel_taps,
        (1,),
        "VALID",
        dimension_numbers=("NWC", "WIO", "NWC"),
        feature_group_count=group_count,
        preferred_element_type=jnp.float32,
    )


def group_conv_kernel_grad(extended, upstream_low, group_count):
    return lax.conv_general_dilated(
        extended,
        upstream_low,
        (1,),
        "VALID",
        dimension_numbers=("CWN", "IWO", "WNC"),
        batch_group_count=group_count,
        preferred_element_type=jnp.float32,
    )


def flipped_taps(kernel_taps, group_count):
    tap_count, group_width, model_width = kernel_taps.shape
    split_taps = kernel_taps.reshape(tap_count, group_width, group_count, group_width)
    swapped = jnp.transpose(split_taps, (0, 3, 2, 1)).reshape(tap_count, group_width, model_width)
    return swapped[::-1]


def masked_scores(query_part, key_part, query_segments, key_segments):
    scores = jnp.einsum("rqhe,rkhe->rhqk", query_part, key_part, preferred_element_type=jnp.float32)
    allowed = query_segments[:, None, :, None] == key_segments[:, None, None, :]
    return jnp.where(allowed, scores, masked_score)


def key_slice(kv_whole, segments, start, key_block, head_count):
    row_count = kv_whole.shape[0]
    model_width = kv_whole.shape[2] // 2
    head_width = model_width // head_count
    part_rows = lax.dynamic_slice_in_dim(kv_whole, start, key_block, 1)
    part_segments = lax.dynamic_slice_in_dim(segments, start, key_block, 1)
    key_part = part_rows[:, :, :model_width].reshape(row_count, key_block, head_count, head_width)
    value_part = part_rows[:, :, model_width:].reshape(row_count, key_block, head_count, head_width)
    return (key_part, value_part, part_segments)


def attend(query_heads, kv_whole, query_segments, segments, head_count):
    row_count = query_heads.shape[0]
    tok_count = query_heads.shape[1]
    key_block = math.gcd(kv_whole.shape[1], 1024)
    block_count = kv_whole.shape[1] // key_block

    def stats_step(step_index, state):
        running_max, running_sum = state
        key_part, value_part, part_segments = key_slice(
            kv_whole, segments, step_index * key_block, key_block, head_count
        )
        scores = masked_scores(query_heads, key_part, query_segments, part_segments)
        new_max = jnp.maximum(running_max, jnp.max(scores, axis=-1))
        running_sum = running_sum * jnp.exp(running_max - new_max) + jnp.sum(
            jnp.exp(scores - new_max[..., None]), axis=-1
        )
        return (new_max, running_sum)

    start_state = (
        jnp.full((row_count, head_count, tok_count), masked_score, jnp.float32),
        jnp.zeros((row_count, head_count, tok_count), jnp.float32),
    )
    running_max, running_sum = lax.fori_loop(0, block_count, stats_step, start_state)
    log_sum = running_max + jnp.log(running_sum)

    def value_step(step_index, state):
        coarse, residue = state
        key_part, value_part, part_segments = key_slice(
            kv_whole, segments, step_index * key_block, key_block, head_count
        )
        probability = jnp.exp(
            masked_scores(query_heads, key_part, query_segments, part_segments) - log_sum[..., None]
        )
        probability_low = probability.astype(jnp.bfloat16)
        remainder_low = (probability - probability_low.astype(jnp.float32)).astype(jnp.bfloat16)
        coarse = coarse + jnp.einsum(
            "rhqk,rkhe->rqhe", probability_low, value_part, preferred_element_type=jnp.float32
        )
        residue = residue + jnp.einsum(
            "rhqk,rkhe->rqhe", remainder_low, value_part, preferred_element_type=jnp.float32
        )
        return (coarse, residue)

    zero_out = jnp.zeros(query_heads.shape, jnp.float32)
    coarse, residue = lax.fori_loop(0, block_count, value_step, (zero_out, zero_out))
    return (coarse, coarse + residue, log_sum)


def attend_back(
    query_heads, grad_heads, kv_whole, query_segments, segments, log_sum, delta, head_count
):
    row_count = query_heads.shape[0]
    frame_count = kv_whole.shape[1]
    model_width = kv_whole.shape[2] // 2
    key_block = math.gcd(frame_count, 1024)
    block_count = frame_count // key_block

    def back_step(step_index, state):
        grad_query, key_terms = state
        start = step_index * key_block
        key_part, value_part, part_segments = key_slice(
            kv_whole, segments, start, key_block, head_count
        )
        probability = jnp.exp(
            masked_scores(query_heads, key_part, query_segments, part_segments) - log_sum[..., None]
        )
        grad_prob = jnp.einsum(
            "rqhe,rkhe->rhqk", grad_heads, value_part, preferred_element_type=jnp.float32
        )
        grad_scores = (probability * (grad_prob - delta[..., None])).astype(jnp.bfloat16)
        grad_query = grad_query + jnp.einsum(
            "rhqk,rkhe->rqhe", grad_scores, key_part, preferred_element_type=jnp.float32
        )
        grad_keys = jnp.einsum(
            "rhqk,rqhe->rkhe", grad_scores, query_heads, preferred_element_type=jnp.float32
        )
        grad_values = jnp.einsum(
            "rhqk,rqhe->rkhe",
            probability.astype(jnp.bfloat16),
            grad_heads,
            preferred_element_type=jnp.float32,
        )
        both_terms = jnp.concatenate(
            [
                grad_keys.reshape(row_count, key_block, model_width),
                grad_values.reshape(row_count, key_block, model_width),
            ],
            axis=-1,
        )
        key_terms = lax.dynamic_update_slice_in_dim(key_terms, both_terms, start, 1)
        return (grad_query, key_terms)

    term_start = jnp.zeros((row_count, frame_count, 2 * model_width), jnp.float32)
    return lax.fori_loop(
        0, block_count, back_step, (jnp.zeros(query_heads.shape, jnp.float32), term_start)
    )


def local(
    features,
    cotangent,
    segments,
    stem_weight,
    projection_weight,
    mixing_weight,
    feedforward_weight,
    norm_gains,
    biases,
    stem_moment,
    projection_moment,
    mixing_moment,
    feedforward_moment,
    gain_moment,
    bias_moment,
    stem_average,
    projection_average,
    mixing_average,
    feedforward_average,
    gain_average,
    bias_average,
):
    row_count, tok_count, model_width = features.shape
    head_count = HEADS
    head_width = model_width // head_count
    group_count = GROUPS
    group_width = model_width // group_count
    tap_count = KERNEL
    half_taps = tap_count // 2
    layer_count = projection_weight.shape[0]
    ff_rows = feedforward_weight.shape[3] // model_width
    score_scale = 1.0 / math.sqrt(head_width)
    seq_index = lax.axis_index("seq")
    query_segments = lax.dynamic_slice_in_dim(segments, seq_index * tok_count, tok_count, 1)
    kernel_taps = stem_weight.reshape(tap_count, group_width, model_width)
    extended = extended_2(features, (("seq", 1),), half_taps)
    conv_input = extended[:, : tok_count + tap_count - 1]
    conv_pre = group_conv(conv_input, kernel_taps, group_count) + biases[0]
    summed = features.astype(jnp.float32) + gelu_exact(conv_pre)
    hidden, normed_stem, inverse_stem = layer_norm(summed, norm_gains[0], biases[1])
    saved_layers = []
    for layer_index in range(layer_count):
        bias_base = 2 + layer_index * (6 + ff_rows)
        hidden_low = hidden.astype(jnp.bfloat16)
        projected = jnp.einsum(
            "rtd,de->rte",
            hidden_low,
            projection_weight[layer_index],
            preferred_element_type=jnp.float32,
        )
        queries = ((projected[..., :model_width] + biases[bias_base]) * score_scale).astype(
            jnp.bfloat16
        )
        keys_low = projected[..., model_width : 2 * model_width].astype(jnp.bfloat16)
        values_low = (projected[..., 2 * model_width :] + biases[bias_base + 1]).astype(
            jnp.bfloat16
        )
        kv_local = jnp.concatenate([keys_low, values_low], axis=-1)
        kv_whole = lax.all_gather(kv_local, "seq", axis=1, tiled=True)
        query_heads = queries.reshape(row_count, tok_count, head_count, head_width)
        coarse, fine, log_sum = attend(query_heads, kv_whole, query_segments, segments, head_count)
        mixed_low = coarse.reshape(row_count, tok_count, model_width).astype(jnp.bfloat16)
        branch = (
            jnp.einsum(
                "rte,ed->rtd",
                mixed_low,
                mixing_weight[layer_index],
                preferred_element_type=jnp.float32,
            )
            + biases[bias_base + 2]
        )
        first_norm, normed_one, inverse_one = layer_norm(
            hidden + branch, norm_gains[1 + 2 * layer_index], biases[bias_base + 3]
        )
        first_low = first_norm.astype(jnp.bfloat16)
        up_bias = biases[bias_base + 6 : bias_base + 6 + ff_rows].reshape(-1)
        up_pre = (
            jnp.einsum(
                "rtd,dj->rtj",
                first_low,
                feedforward_weight[layer_index, :, 0, :],
                preferred_element_type=jnp.float32,
            )
            + up_bias
        )
        up_low = gelu_exact(up_pre).astype(jnp.bfloat16)
        down_out = (
            jnp.einsum(
                "rtj,dj->rtd",
                up_low,
                feedforward_weight[layer_index, :, 1, :],
                preferred_element_type=jnp.float32,
            )
            + biases[bias_base + 4]
        )
        hidden_next, normed_two, inverse_two = layer_norm(
            first_norm + down_out, norm_gains[2 + 2 * layer_index], biases[bias_base + 5]
        )
        saved_layers.append(
            (
                hidden_low,
                query_heads,
                kv_whole,
                log_sum,
                fine,
                mixed_low,
                normed_one,
                inverse_one,
                first_low,
                up_pre,
                up_low,
                normed_two,
                inverse_two,
            )
        )
        hidden = hidden_next
    upstream = cotangent.astype(jnp.float32)
    gain_grads = [None] * norm_gains.shape[0]
    bias_grads = [None] * biases.shape[0]
    projection_grads = [None] * layer_count
    mixing_grads = [None] * layer_count
    feedforward_grads = [None] * layer_count
    for layer_index in reversed(range(layer_count)):
        (
            hidden_low,
            query_heads,
            kv_whole,
            log_sum,
            fine,
            mixed_low,
            normed_one,
            inverse_one,
            first_low,
            up_pre,
            up_low,
            normed_two,
            inverse_two,
        ) = saved_layers[layer_index]
        bias_base = 2 + layer_index * (6 + ff_rows)
        in_matrix = projection_weight[layer_index]
        mix_matrix = mixing_weight[layer_index]
        up_matrix = feedforward_weight[layer_index, :, 0, :]
        down_matrix = feedforward_weight[layer_index, :, 1, :]
        grad_second, gain_grads[2 + 2 * layer_index], bias_grads[bias_base + 5] = layer_norm_back(
            upstream, normed_two, inverse_two, norm_gains[2 + 2 * layer_index]
        )
        bias_grads[bias_base + 4] = jnp.sum(grad_second, axis=(0, 1))
        down_low = grad_second.astype(jnp.bfloat16)
        grad_down = jnp.einsum("rtd,rtj->dj", down_low, up_low, preferred_element_type=jnp.float32)
        grad_act = jnp.einsum(
            "rtd,dj->rtj", down_low, down_matrix, preferred_element_type=jnp.float32
        )
        grad_up_pre = gelu_back(up_pre, grad_act)
        up_bias_grad = jnp.sum(grad_up_pre, axis=(0, 1)).reshape(ff_rows, model_width)
        for offset in range(ff_rows):
            bias_grads[bias_base + 6 + offset] = up_bias_grad[offset]
        up_grad_low = grad_up_pre.astype(jnp.bfloat16)
        grad_up = jnp.einsum(
            "rtd,rtj->dj", first_low, up_grad_low, preferred_element_type=jnp.float32
        )
        grad_first = grad_second + jnp.einsum(
            "rtj,dj->rtd", up_grad_low, up_matrix, preferred_element_type=jnp.float32
        )
        feedforward_grads[layer_index] = jnp.stack([grad_up, grad_down], axis=1)
        grad_resid, gain_grads[1 + 2 * layer_index], bias_grads[bias_base + 3] = layer_norm_back(
            grad_first, normed_one, inverse_one, norm_gains[1 + 2 * layer_index]
        )
        bias_grads[bias_base + 2] = jnp.sum(grad_resid, axis=(0, 1))
        branch_low = grad_resid.astype(jnp.bfloat16)
        mixing_grads[layer_index] = jnp.einsum(
            "rte,rtd->ed", mixed_low, branch_low, preferred_element_type=jnp.float32
        )
        grad_mixed = jnp.einsum(
            "rtd,ed->rte", branch_low, mix_matrix, preferred_element_type=jnp.float32
        )
        mixed_grad_low = grad_mixed.astype(jnp.bfloat16).reshape(
            row_count, tok_count, head_count, head_width
        )
        delta = jnp.transpose(
            jnp.sum(mixed_grad_low.astype(jnp.float32) * fine, axis=-1), (0, 2, 1)
        )
        grad_query, key_terms = attend_back(
            query_heads,
            mixed_grad_low,
            kv_whole,
            query_segments,
            segments,
            log_sum,
            delta,
            head_count,
        )
        grad_kv = lax.psum_scatter(key_terms, "seq", scatter_dimension=1, tiled=True)
        query_grad_low = grad_query.reshape(row_count, tok_count, model_width).astype(jnp.bfloat16)
        key_grad_low = grad_kv[..., :model_width].astype(jnp.bfloat16)
        value_grad_low = grad_kv[..., model_width:].astype(jnp.bfloat16)
        bias_grads[bias_base] = (
            jnp.sum(query_grad_low.astype(jnp.float32), axis=(0, 1)) * score_scale
        )
        bias_grads[bias_base + 1] = jnp.sum(value_grad_low.astype(jnp.float32), axis=(0, 1))
        grad_projected = jnp.concatenate(
            [query_grad_low * score_scale, key_grad_low, value_grad_low], axis=-1
        )
        projection_grads[layer_index] = jnp.einsum(
            "rtd,rte->de", hidden_low, grad_projected, preferred_element_type=jnp.float32
        )
        upstream = grad_resid + jnp.einsum(
            "rte,de->rtd", grad_projected, in_matrix, preferred_element_type=jnp.float32
        )
    grad_summed, gain_grads[0], bias_grads[1] = layer_norm_back(
        upstream, normed_stem, inverse_stem, norm_gains[0]
    )
    grad_conv = gelu_back(conv_pre, grad_summed)
    bias_grads[0] = jnp.sum(grad_conv, axis=(0, 1))
    conv_grad_low = grad_conv.astype(jnp.bfloat16)
    grad_extended = extended_2(conv_grad_low, (("seq", 1),), half_taps)
    features_gradient = grad_summed + group_conv(
        grad_extended[:, 1:], flipped_taps(kernel_taps, group_count), group_count
    )
    seq_count = lax.axis_size("seq")
    share_width = model_width // seq_count
    layer_partials = (
        jnp.stack(projection_grads),
        jnp.stack(mixing_grads),
        jnp.stack(feedforward_grads),
        jnp.stack(gain_grads),
        jnp.stack(bias_grads),
    )
    grad_stem = group_conv_kernel_grad(conv_input, conv_grad_low, group_count).reshape(
        tap_count * group_width, model_width
    )
    shares = (
        lax.psum_scatter(grad_stem, "seq", scatter_dimension=1, tiled=True),
        lax.psum_scatter(layer_partials[0], "seq", scatter_dimension=1, tiled=True),
        lax.psum_scatter(layer_partials[1], "seq", scatter_dimension=1, tiled=True),
        lax.psum_scatter(layer_partials[2], "seq", scatter_dimension=1, tiled=True),
        lax.psum_scatter(layer_partials[3], "seq", scatter_dimension=1, tiled=True),
        lax.psum_scatter(layer_partials[4], "seq", scatter_dimension=1, tiled=True),
    )
    matrix_totals = (
        lax.psum_scatter(
            shares[0].astype(jnp.bfloat16), "row", scatter_dimension=0, tiled=True
        ).astype(jnp.float32),
        lax.psum_scatter(
            shares[1].astype(jnp.bfloat16), "row", scatter_dimension=2, tiled=True
        ).astype(jnp.float32),
        lax.psum_scatter(
            shares[2].astype(jnp.bfloat16), "row", scatter_dimension=2, tiled=True
        ).astype(jnp.float32),
        lax.psum_scatter(
            shares[3].astype(jnp.bfloat16), "row", scatter_dimension=3, tiled=True
        ).astype(jnp.float32),
    )
    small_totals = lax.psum((shares[4], shares[5]), "row")
    totals = (
        matrix_totals[0],
        matrix_totals[1],
        matrix_totals[2],
        matrix_totals[3],
        small_totals[0],
        small_totals[1],
    )
    share_start = seq_index * share_width
    row_index = lax.axis_index("row")
    row_total = lax.axis_size("row")
    rate_base = 1.0 / math.sqrt(row_count * row_total * tok_count * seq_count)
    old_params = (
        stem_weight,
        projection_weight,
        mixing_weight,
        feedforward_weight,
        norm_gains,
        biases,
    )
    old_moments = (
        stem_moment,
        projection_moment,
        mixing_moment,
        feedforward_moment,
        gain_moment,
        bias_moment,
    )
    old_averages = (
        stem_average,
        projection_average,
        mixing_average,
        feedforward_average,
        gain_average,
        bias_average,
    )
    momenta = []
    averaged = []
    updated = []
    for param_index in range(6):
        old_share = lax.dynamic_slice_in_dim(old_params[param_index], share_start, share_width, 1)
        if param_index < 4:
            split_dim = row_dims[param_index]
            piece_size = old_share.shape[split_dim] // row_total
            old_share = lax.dynamic_slice_in_dim(
                old_share, row_index * piece_size, piece_size, split_dim
            )
        old_share = old_share.astype(jnp.float32)
        moment_new = momentum_decay * old_moments[param_index] + totals[param_index]
        weight_new = old_share - rate_factors[param_index] * rate_base * (
            totals[param_index] + momentum_decay * moment_new
        )
        momenta.append(moment_new)
        updated.append(weight_new)
        averaged.append(
            average_decay * old_averages[param_index] + (1.0 - average_decay) * weight_new
        )
    return (
        hidden,
        features_gradient,
        momenta[0],
        momenta[1],
        momenta[2],
        momenta[3],
        momenta[4],
        momenta[5],
        averaged[0],
        averaged[1],
        averaged[2],
        averaged[3],
        averaged[4],
        averaged[5],
        updated[0],
        updated[1],
        updated[2],
        updated[3],
        updated[4],
        updated[5],
    )


LANES = 128
PAIRS = 2
VMEM_BYTES = 16 * 1024 * 1024
WIDE_BYTES = 24 * 1024 * 1024
FAR_BYTES = 56 * 1024 * 1024
bf16 = jnp.bfloat16
f32 = jnp.float32


def whole_call(kernel, outs, operands, scalars=0, scratch=(), after=(), far=(), token=False, vmem=VMEM_BYTES):
    given, waits, made = len(operands), len(after), len(outs)

    def body(*refs):
        kernel(*refs[:given], *refs[given + waits : given + waits + made], *refs[given + waits + made + token :])

    in_specs = [
        pl.BlockSpec(memory_space=pltpu.SMEM if i < scalars else pl.ANY if i in far else pltpu.VMEM)
        for i in range(given)
    ] + [pl.BlockSpec(memory_space=pl.ANY)] * waits
    out_specs = [pl.BlockSpec(memory_space=pltpu.VMEM)] * made + [pl.BlockSpec(memory_space=pl.ANY)] * token
    return pl.pallas_call(
        body,
        out_shape=[*outs, *[jax.ShapeDtypeStruct((8, LANES), jnp.float32)] * token],
        in_specs=in_specs,
        out_specs=out_specs,
        scratch_shapes=list(scratch),
        compiler_params=pltpu.CompilerParams(vmem_limit_bytes=vmem),
        cost_estimate=pl.CostEstimate(flops=1, bytes_accessed=1, transcendentals=0),
    )(*operands, *after)


def sds(shape, dtype):
    return jax.ShapeDtypeStruct(shape, dtype)


def dot_nn(a, b):
    return lax.dot_general(a, b, (((1,), (0,)), ((), ())), preferred_element_type=f32)


def dot_nt(a, b):
    return lax.dot_general(a, b, (((1,), (1,)), ((), ())), preferred_element_type=f32)


def dot_tn(a, b):
    return lax.dot_general(a, b, (((0,), (0,)), ((), ())), preferred_element_type=f32)


def gelu_and_slope(v):
    cdf = 0.5 * (1.0 + lax.erf(v * math.sqrt(0.5)))
    return v * cdf, cdf + v * jnp.exp(-0.5 * v * v) * (1.0 / math.sqrt(2.0 * math.pi))


def lane_of(shape):
    return lax.broadcasted_iota(jnp.int32, shape, len(shape) - 1)


def piece_of(cols, j, width):
    off, v = (width * j) % LANES, (width * j) // LANES
    lane = lane_of(cols[0].shape)
    if off == 0:
        t = cols[v]
    else:
        t = pltpu.roll(cols[v], LANES - off, 1)
        if off + width > LANES:
            t = jnp.where(lane < LANES - off, t, pltpu.roll(cols[v + 1], LANES - off, 1))
    return jnp.where(lane < width, t, 0.0)


def tiles_of(pieces, width):
    count = len(pieces) * width // LANES
    cols = [None] * count

    def put(v, t):
        cols[v] = t if cols[v] is None else cols[v] + t

    for j, piece in enumerate(pieces):
        off, v = (width * j) % LANES, (width * j) // LANES
        if off == 0:
            put(v, piece)
            continue
        rolled = pltpu.roll(piece, off, 1)
        if off + width > LANES:
            lane = lane_of(piece.shape)
            put(v, jnp.where(lane >= off, rolled, 0.0))
            put(v + 1, jnp.where(lane < off, rolled, 0.0))
        else:
            put(v, rolled)
    return cols


def split_kernel(blocks, width, x_ref, o_ref):
    rows = x_ref.shape[0]
    for r in range(rows):
        x = x_ref[r].astype(f32)
        cols = [x[:, LANES * v : LANES * (v + 1)] for v in range(x.shape[1] // LANES)]
        for j in range(blocks):
            o_ref[j, r] = piece_of(cols, j, width).astype(bf16)


def fill_taps(taps, gw, w_ref, o_ref):
    zero = jnp.zeros((LANES, LANES), bf16)
    o_ref[0] = zero
    o_ref[taps + 1] = zero
    o_ref[taps + 2] = zero

    def body(k, carry):
        w = w_ref[pl.ds(pl.multiple_of(k * gw, 16), gw), :]
        lane = lane_of(w.shape)
        o_ref[k + 1, 0:gw, :] = jnp.where(lane < gw, w, jnp.zeros_like(w))
        o_ref[k + 1, gw : 2 * gw, :] = jnp.where(lane >= gw, w, jnp.zeros_like(w))
        o_ref[k + 1, 2 * gw :, :] = jnp.zeros((LANES - 2 * gw, LANES), bf16)
        return carry

    lax.fori_loop(0, taps, body, 0)


def phases_from_frames(x_ref, xf, ph, rows, frames, half):
    blocks, block = x_ref.shape[0], x_ref.shape[2]
    span = frames + 2 * half
    for r in range(rows):
        xf[r * span : r * span + half, :] = jnp.zeros((half, LANES), f32)
        xf[r * span + half + frames : (r + 1) * span, :] = jnp.zeros((half, LANES), f32)
        for s in range(blocks):
            at = r * span + half + s * block
            xf[at : at + block, :] = x_ref[s, r].astype(f32)
    n = span // 2 - 16

    def body(p, carry):
        for r in range(rows):
            for b in range(2):
                ph[p, r, 0:n, b * LANES : (b + 1) * LANES] = xf[
                    pl.ds(r * span + 2 * p + b, n, stride=2), :
                ].astype(bf16)
        return carry

    lax.fori_loop(0, 16, body, 0)
    for r in range(rows):
        for b in range(2):
            ph[0, r, n:, b * LANES : (b + 1) * LANES] = xf[pl.ds(r * span + 2 * n + b, 16, stride=2), :].astype(bf16)


def window(ph, m, rows, n):
    p, a = lax.rem(m, 16), m // 16
    part = ph[p, :, pl.ds(pl.multiple_of(a * 16, 16), n), :]
    return part.reshape(rows * n, part.shape[-1])


def phases_kernel(rows, frames, half, gw, x_ref, share_ref, ph_ref, w_ref, xf):
    phases_from_frames(x_ref, xf, ph_ref, rows, frames, half)
    fill_taps(2 * half, gw, share_ref, w_ref)


def conv_kernel(rows, frames, half, gw, c_ref, x_ref, share_ref, b_ref, pre_ref, keep_ref, send_ref, ph_ref, xf, acc, w_ref):
    n = frames // 2
    fill_taps(2 * half, gw, share_ref, w_ref)
    phases_from_frames(x_ref, xf, ph_ref, rows, frames, half)
    acc[...] = jnp.zeros_like(acc)

    def body(i, carry):
        left, right = [], []
        for t in range(5):
            m = i * 5 + t
            here, before, after = w_ref[2 * m + 1], w_ref[2 * m], w_ref[2 * m + 2]
            right += [jnp.concatenate([here, before], 1), jnp.concatenate([after, here], 1)]
            left.append(window(ph_ref, m, rows, n))
        acc[...] += dot_nn(jnp.concatenate(left, 1), jnp.concatenate(right, 0))
        return carry

    lax.fori_loop(0, (half + 1) // 5, body, 0)
    bias = jnp.concatenate([b_ref[...], b_ref[...]], 1)
    c = c_ref[1]
    for r in range(rows):
        pre = acc[r * n : (r + 1) * n, :] + bias
        pre_ref[r] = pre
        x = ph_ref[0, r, half // 2 : half // 2 + n, :].astype(f32)
        s = (x + gelu_and_slope(pre)[0]).astype(bf16)
        for zf in range(4):
            for xq in range(2):
                for cf in range(2):
                    u = ((zf * 2 + xq) * 2 + cf) * 16
                    blk = s[u : u + 16, :]

                    @pl.when(c == cf)
                    def _(blk=blk, r=r, xq=xq, zf=zf):
                        keep_ref[r, xq, zf * 16 : zf * 16 + 16, :] = blk

                    @pl.when(c != cf)
                    def _(blk=blk, r=r, xq=xq, zf=zf):
                        send_ref[r, xq, zf * 16 : zf * 16 + 16, :] = blk


def normed(values):
    centre = jnp.mean(values, axis=-1, keepdims=True)
    centred = values - centre
    spread = jnp.mean(centred * centred, axis=-1, keepdims=True)
    inverse = lax.rsqrt(spread + epsilon)
    return centred * inverse, inverse


def stem_norm_kernel(width, r_ref, g_ref, b_ref, h_ref, low_ref, n_ref, i_ref):
    halves = []
    for a in range(2):
        pieces = [r_ref[j, :, a * LANES : (a + 1) * LANES].astype(f32) for j in range(r_ref.shape[0])]
        halves.append(jnp.concatenate(tiles_of(pieces, width), axis=1))
    s = jnp.concatenate(halves, axis=0)
    n, inv = normed(s)
    h = n * g_ref[0:1, :] + b_ref[1:2, :]
    h_ref[...] = h
    low_ref[...] = h.astype(bf16)
    n_ref[...] = n
    i_ref[...] = inv


def cotangent_split_kernel(place, x_ref, keep_ref, send_ref, mixed):
    c = place[1]
    rows, toks, width = x_ref.shape
    for r in range(rows):
        for v in range(width // LANES):
            mixed[v * toks : (v + 1) * toks, :] = x_ref[r, :, v * LANES : (v + 1) * LANES].astype(f32)
        for cf in range(2):
            for a in range(2):
                parts = [mixed[pl.ds(v * toks + cf * 32 + a, 16, stride=2), :] for v in range(width // LANES)]
                blk = jnp.concatenate(parts, axis=1).astype(bf16)

                @pl.when(c == cf)
                def _(blk=blk, r=r, a=a):
                    keep_ref[r, a * 16 : a * 16 + 16, :] = blk

                @pl.when(c != cf)
                def _(blk=blk, r=r, a=a):
                    send_ref[r, a * 16 : a * 16 + 16, :] = blk


def cotangent_route_kernel(place, keep_ref, recv_ref, *outs):
    c, z = place[1], place[2]
    for rel, out in enumerate(outs):
        to = z ^ rel
        mine = (to // 2) == c

        @pl.when(mine)
        def _(out=out, to=to):
            out[...] = keep_ref[to % 2]

        @pl.when(jnp.logical_not(mine))
        def _(out=out, to=to):
            out[...] = recv_ref[to % 2]


def cotangent_join_kernel(place, r0, r1, r2, r3, o_ref):
    z = place[2]
    for rel, src in enumerate((r0, r1, r2, r3)):
        for a in range(2):
            at = pl.multiple_of(a * 64 + (z ^ rel) * 16, 16)
            o_ref[pl.ds(at, 16), :] = src[a * 16 : a * 16 + 16, :]


def segments_kernel(place, own_ref, other_ref, row_ref, col_ref):
    c, z, x = place[1], place[2], place[3]
    frames = own_ref.shape[1]
    mine = (z // 2) == c
    odd = (z % 2) == 1
    own = jnp.where(odd, own_ref[1:2, :], own_ref[0:1, :])
    other = jnp.where(odd, other_ref[1:2, :], other_ref[0:1, :])
    ids = jnp.broadcast_to(jnp.where(mine, own, other).astype(f32), (LANES, frames)).astype(bf16)
    f = lax.broadcasted_iota(jnp.int32, (frames, frames), 0)
    p = lax.broadcasted_iota(jnp.int32, (frames, frames), 1)
    source = (
        ((p >> 4) & 3) * 128 + (x ^ (p >> 8)) * 64 + (c ^ ((p >> 7) & 1)) * 32 + (p & 15) * 2 + ((p >> 6) & 1)
    )
    chosen = jnp.where(f == source, 1.0, 0.0).astype(bf16)
    row_ref[...] = dot_nn(ids, chosen)[0:1, :]
    col_ref[...] = dot_tn(chosen, ids.T)[:, 0:1]


def slots_kernel(place, keep_ref, recv_ref, o_ref):
    c = place[1]
    for r in range(2):
        for q in range(2):
            o_ref[((c * 2) + r) * 2 + q] = keep_ref[r, q]
            o_ref[(((1 - c) * 2) + r) * 2 + q] = recv_ref[r, q]


def fetched(copies):
    for copy in copies:
        copy.start()
    return copies


def feed_copies(l, place, w_ref, buf, sems, width):
    steps = w_ref.shape[1] // LANES
    copies = []
    for i in range(2):
        at = pl.multiple_of((2 * (place[0] ^ i) + place[1]) * width, LANES)
        for k in range(steps):
            copies.append(
                pltpu.make_async_copy(
                    w_ref.at[l, pl.ds(k * LANES, LANES), :, pl.ds(at, width)],
                    buf.at[i, pl.ds(k * LANES, LANES)],
                    sems.at[i * steps + k],
                )
            )
    return fetched(copies)


def feed_parted(copies, buf, outs):
    depth, width = buf.shape[1], buf.shape[3]
    steps = depth // LANES
    parting = parting_matrix(2 * LANES)
    for i in range(2):
        for k in range(steps):
            copies[i * steps + k].wait()
        flat = buf.at[i].reshape(2 * depth, width)

        def body(k, carry, i=i, flat=flat):
            g = dot_nn(parting, flat[pl.ds(pl.multiple_of(2 * LANES * k, 2 * LANES), 2 * LANES), :]).astype(bf16)
            at = pl.ds(pl.multiple_of(LANES * k, LANES), LANES)
            outs[i][at, :] = g[:LANES]
            outs[2 + i][at, :] = g[LANES:]
            return carry

        lax.fori_loop(0, steps, body, 0)


def feed_weights_kernel(l, place, w_ref, *refs):
    outs, (buf, sems) = refs[:4], refs[4:]
    feed_parted(feed_copies(l, place, w_ref, buf, sems, outs[0].shape[1]), buf, outs)


def parting_matrix(size):
    r = lax.broadcasted_iota(jnp.int32, (size, size), 0)
    c = lax.broadcasted_iota(jnp.int32, (size, size), 1)
    return jnp.where(c == jnp.where(r < size // 2, 2 * r, 2 * r - size + 1), 1.0, 0.0).astype(bf16)


def later_weights_kernel(layers, bases, share, place, w_ref, p_ref, m_ref, b_ref, *refs):
    feeds = 4 * (layers - 1)
    feed_outs, outs = refs[:feeds], refs[feeds : feeds + 3 * layers]
    buf, wide, feed_sems, sems = refs[feeds + 3 * layers :]
    c, x = place[1], place[3]
    group = 2 * x + c
    width = m_ref.shape[2]
    start = ((group * share) // LANES) * LANES
    copies = []
    row = pl.multiple_of(group * share, 64)
    for l in range(layers):
        for i in range(3):
            at = pl.multiple_of(i * width + start, LANES)
            copies.append(pltpu.make_async_copy(p_ref.at[l, :, pl.ds(at, 256)], wide.at[l, i], sems.at[4 * l + i]))
        mix_ref = outs[3 * l + 1]
        copies.append(
            pltpu.make_async_copy(m_ref.at[l, pl.ds(row, share), :], mix_ref.at[pl.ds(0, share), :], sems.at[4 * l + 3])
        )
    fetched(copies)
    feed_in = [feed_copies(l, place, w_ref, buf.at[l - 1], feed_sems.at[l - 1], width) for l in range(1, layers)]
    odd = (group % 2) == 1

    def settle(v):
        lane = lane_of(v.shape)
        return jnp.where(lane < share, jnp.where(odd, pltpu.roll(v, 256 - 64, 1), v), 0.0)

    for l in range(layers):
        in_ref, mix_ref, both_ref = outs[3 * l : 3 * l + 3]
        mix_ref[share:, :] = jnp.zeros((256 - share, width), bf16)
        both_ref[...] = settle(b_ref[bases[l] : bases[l] + 2, pl.ds(pl.multiple_of(start, LANES), 256)])
        for i in range(3):
            copies[4 * l + i].wait()
            in_ref[:, i * 256 : (i + 1) * 256] = settle(wide[l, i].astype(f32)).astype(bf16)
        copies[4 * l + 3].wait()
    for l in range(1, layers):
        feed_parted(feed_in[l - 1], buf.at[l - 1], feed_outs[4 * (l - 1) : 4 * l])


def attend_kernel(base, hl0, hl1, hl2, hl3, w_ref, m_ref, bq_ref, segr, segc,
                  q_ref, k_ref, v_ref, at_ref, lse_ref, keep_ref, send_ref):
    t = hl0.shape[0]
    hl = jnp.concatenate([hl0[...], hl1[...], hl2[...], hl3[...]], axis=0)
    proj = dot_nn(hl, w_ref[...])
    q = ((proj[:, 0:256] + bq_ref[0:1, :]) * 0.125).astype(bf16)
    k = proj[:, 256:512].astype(bf16)
    v = (proj[:, 512:768] + bq_ref[1:2, :]).astype(bf16)
    q_ref[...] = q
    k_ref[...] = k
    v_ref[...] = v
    allowed = segc[...] == segr[...]
    lane = lane_of((1, LANES))
    parts = []
    for head in range(3):
        tile = head // 2
        cols = slice(tile * LANES, (tile + 1) * LANES)
        mine = (lane < 64) if head % 2 == 0 else (lane >= 64)
        qh = jnp.where(mine, q[:, cols], jnp.zeros((), bf16))
        s = dot_nt(qh, k[:, cols])
        s = jnp.where(allowed, s, masked_score)
        top = jnp.max(s, axis=-1, keepdims=True)
        e = jnp.exp(s - top)
        total = jnp.sum(e, axis=-1, keepdims=True)
        lse_ref[head] = top + jnp.log(total)
        p = (e * (1.0 / total)).astype(bf16)
        parts.append(dot_nn(p, v[:, cols]))
    att = jnp.concatenate([jnp.where(lane < 64, parts[0], parts[1]), parts[2]], axis=1).astype(bf16)
    at_ref[...] = att
    branch = dot_nn(att, m_ref[...]).astype(bf16)
    for dx in range(2):
        keep_ref[dx] = branch[2 * dx * t : (2 * dx + 1) * t]
        send_ref[dx] = branch[(2 * dx + 1) * t : (2 * dx + 2) * t]


def half_sum_kernel(a_ref, b_ref, own_ref, send_ref):
    own_ref[...] = a_ref[0].astype(f32) + b_ref[0].astype(f32)
    send_ref[...] = (a_ref[1].astype(f32) + b_ref[1].astype(f32)).astype(bf16)


def norm_kernel(gain_row, bias_row, shift_row, h_ref, a_ref, r_ref, g_ref, b_ref, o_ref, low_ref, n_ref, i_ref):
    v = h_ref[...] + (a_ref[...].astype(f32) + r_ref[...].astype(f32) + b_ref[bias_row : bias_row + 1, :])
    n, inv = normed(v)
    o = n * g_ref[gain_row : gain_row + 1, :] + b_ref[shift_row : shift_row + 1, :]
    o_ref[...] = o
    low_ref[...] = o.astype(bf16)
    n_ref[...] = n
    i_ref[...] = inv


def feed_kernel(row, place, f0, f1, u0, u1, d0, d1, b_ref, act_ref, slope_ref, own_ref, send_ref):
    t = f0.shape[0]
    first = jnp.concatenate([f0[...], f1[...]], axis=0)
    total = None
    for i, (u, d) in enumerate(((u0, d0), (u1, d1))):
        up = dot_nn(first, u[...]) + b_ref[pl.ds(row + 2 * (place[0] ^ i) + place[1], 1), :]
        act, slope = gelu_and_slope(up)
        act = act.astype(bf16)
        act_ref[i] = act
        slope_ref[i] = slope.astype(bf16)
        part = dot_nt(act, d[...])
        total = part if total is None else total + part
    own_ref[...] = total[:t]
    send_ref[...] = total[t:].astype(bf16)


def norm_back(g, n, inv, gain):
    scaled = g * gain
    m1 = jnp.mean(scaled, axis=-1, keepdims=True)
    m2 = jnp.mean(scaled * n, axis=-1, keepdims=True)
    return inv * (scaled - m1 - n * m2)


def norm_sums(g, n, d, o_ref):
    o_ref[0:1, :] = jnp.sum(g * n, axis=0, keepdims=True)
    o_ref[1:2, :] = jnp.sum(g, axis=0, keepdims=True)
    o_ref[2:3, :] = jnp.sum(d, axis=0, keepdims=True)
    o_ref[3:8, :] = jnp.zeros((5, o_ref.shape[1]), f32)


def norm_back_kernel(gain_row, count, *refs):
    given, (g_ref, n_ref, i_ref, d_ref, low_ref, s_ref) = refs[:count], refs[count:]
    g = given[0][...].astype(f32)
    for r in given[1:]:
        g = g + r[...].astype(f32)
    n = n_ref[...]
    d = norm_back(g, n, i_ref[...], g_ref[gain_row : gain_row + 1, :])
    d_ref[...] = d
    low_ref[...] = d.astype(bf16)
    norm_sums(g, n, d, s_ref)


def stem_norm_back_kernel(width, count, place, *refs):
    given, (g_ref, n_ref, i_ref, keep_ref, send_ref, s_ref) = refs[:count], refs[count:]
    z, x = place[2], place[3]
    g = given[0][...].astype(f32)
    for r in given[1:]:
        g = g + r[...].astype(f32)
    n = n_ref[...]
    d = norm_back(g, n, i_ref[...], g_ref[0:1, :])
    norm_sums(g, n, d, s_ref)
    t = d.shape[0] // 2
    for a in range(2):
        part = d[a * t : (a + 1) * t]
        cols = [part[:, LANES * v : LANES * (v + 1)] for v in range(part.shape[1] // LANES)]
        for j in range(8):
            blk = piece_of(cols, j, width).astype(bf16)
            to_x(keep_ref, send_ref, x, j % 2, (j // 2) ^ z, (slice(None), slice(a * LANES, (a + 1) * LANES)), blk)


def to_x(keep_ref, send_ref, x, xi, rel, where, blk):
    @pl.when(x == xi)
    def _():
        keep_ref[(rel, *where)] = blk

    @pl.when(x != xi)
    def _():
        send_ref[(rel, *where)] = blk


def along_z_kernel(a_ref, b_ref, keep_ref, send_ref):
    for rel in range(4):
        out = send_ref if rel % 2 else keep_ref
        out[rel // 2, 0] = a_ref[rel]
        out[rel // 2, 1] = b_ref[rel]


def onward_kernel(keep_ref, recv_ref, send_ref):
    send_ref[0] = keep_ref[1]
    send_ref[1] = recv_ref[1]


def by_z(keep_ref, near_ref, far_ref):
    return keep_ref.at[0], near_ref.at[0], far_ref.at[0], far_ref.at[1]


def feed_back_kernel(e0, e1, u0, u1, d0, d1, slope_ref, dup_ref, own_ref, send_ref, bias_ref):
    t = e0.shape[0]
    d2 = jnp.concatenate([e0[...], e1[...]], axis=0)
    total = None
    for i, (u, d) in enumerate(((u0, d0), (u1, d1))):
        dup = dot_nn(d2, d[...]) * slope_ref[i].astype(f32)
        bias_ref[i : i + 1, :] = jnp.sum(dup, axis=0, keepdims=True)
        dup = dup.astype(bf16)
        dup_ref[i] = dup
        part = dot_nt(dup, u[...])
        total = part if total is None else total + part
    bias_ref[2:8, :] = jnp.zeros((6, bias_ref.shape[1]), f32)
    own_ref[...] = total[:t]
    send_ref[...] = total[t:].astype(bf16)


def feed_grad_kernel(place, f0, f1, e0, e1, dup_ref, act_ref, keep_ref, send_ref):
    z, x = place[2], place[3]
    width = keep_ref.shape[-2] // 2
    for kind, (a, b, right) in enumerate(((f0, f1, dup_ref), (e0, e1, act_ref))):
        left = jnp.concatenate([a[...], b[...]], axis=0)
        for i in range(2):
            g = dot_tn(left, right[i]).astype(bf16)
            for j in range(8):
                zi, xi = j // 2, j % 2
                rz, rx = zi ^ z, xi ^ x
                blk = g[j * width : (j + 1) * width]
                (send_ref if i else keep_ref)[rx, rz % 2, rz // 2, kind * width : (kind + 1) * width] = blk


def halves_kernel(count, *refs):
    given, made = refs[: 2 * count], refs[2 * count :]
    for i in range(count):
        a, b = given[2 * i], given[2 * i + 1]
        for h in range(2):
            out = made[2 * i + h]
            lead = out.shape[:-2]
            many = math.prod(lead)
            if many == 1:
                out[...] = (a[h].astype(f32) + b[h].astype(f32)).astype(out.dtype)
                continue

            def body(k, carry, a=a, b=b, h=h, out=out, lead=lead):
                at = []
                for size in reversed(lead):
                    at.insert(0, lax.rem(k, size))
                    k = k // size
                at = tuple(at)
                out[at] = (a[(h, *at)].astype(f32) + b[(h, *at)].astype(f32)).astype(out.dtype)
                return carry

            lax.fori_loop(0, many, body, 0)


def one_kernel(a, b, o):
    o[...] = (a[...].astype(f32) + b[...].astype(f32)).astype(o.dtype)


def attend_back_kernel(e0, e1, e2, e3, q_ref, k_ref, v_ref, lse_ref, w_ref, m_ref, segr, segc,
                       dc_ref, keep_ref, send_ref, bias_ref, da_ref, dq_ref, dk_ref, dv_ref):
    t = e0.shape[0]
    d1 = jnp.concatenate([e0[...], e1[...], e2[...], e3[...]], axis=0)
    da_ref[...] = dot_nt(d1, m_ref[...]).astype(bf16)
    lane = lane_of((1, LANES))
    for ref in (dq_ref, dk_ref, dv_ref):
        ref[...] = jnp.zeros_like(ref)

    def one_head(head, carry):
        cols = pl.ds(pl.multiple_of((head // 2) * LANES, LANES), LANES)
        mine = (lane // 64) == lax.rem(head, 2)
        zero = jnp.zeros((), bf16)
        qh = jnp.where(mine, q_ref[:, cols], zero)
        dah = jnp.where(mine, da_ref[:, cols], zero)
        k = k_ref[:, cols]
        s = dot_nt(qh, k)
        p = jnp.where(segc[...] == segr[...], jnp.exp(s - lse_ref[head]), 0.0)
        dp = dot_nt(dah, v_ref[:, cols])
        delta = jnp.sum(p * dp, axis=-1, keepdims=True)
        ds = (p * (dp - delta)).astype(bf16)
        dq_ref[:, cols] += dot_nn(ds, jnp.where(mine, k, zero))
        dk_ref[:, cols] += dot_tn(ds, qh)
        dv_ref[:, cols] += dot_tn(p.astype(bf16), dah)
        return carry

    lax.fori_loop(0, 3, one_head, 0)
    tiles = [slice(0, LANES), slice(LANES, 2 * LANES)]
    dq = [dq_ref[:, c].astype(bf16).astype(f32) * 0.125 for c in tiles]
    dk = [dk_ref[:, c].astype(bf16).astype(f32) for c in tiles]
    dv = [dv_ref[:, c].astype(bf16).astype(f32) for c in tiles]
    wide = jnp.concatenate(dq + dk + dv, axis=1).astype(bf16)
    bias_ref[0:1, :] = jnp.concatenate([jnp.sum(d, axis=0, keepdims=True) for d in dq], axis=1)
    bias_ref[1:2, :] = jnp.concatenate([jnp.sum(d, axis=0, keepdims=True) for d in dv], axis=1)
    bias_ref[2:8, :] = jnp.zeros((6, 256), f32)
    dense = [dq[0], jnp.where(lane < 64, dq[1], pltpu.roll(dk[1], 64, 1)), dk[0], dv[0], dv[1]]
    dc_ref[...] = jnp.concatenate(dense, axis=1).astype(bf16)
    out = dot_nt(wide, w_ref[...]).astype(bf16)
    for dx in range(2):
        keep_ref[dx] = out[2 * dx * t : (2 * dx + 1) * t]
        send_ref[dx] = out[(2 * dx + 1) * t : (2 * dx + 2) * t]


def attend_grad_kernel(place, hl0, hl1, hl2, hl3, e0, e1, e2, e3, at_ref, dc_ref, keep_ref, send_ref):
    z, x = place[2], place[3]
    hl = jnp.concatenate([hl0[...], hl1[...], hl2[...], hl3[...]], axis=0)
    d1 = jnp.concatenate([e0[...], e1[...], e2[...], e3[...]], axis=0)
    width = keep_ref.shape[2]

    def put(zi, tile, blk):
        rel = zi ^ z

        @pl.when((zi ^ z) % 2 == 0)
        def _():
            keep_ref[rel // 2, tile] = blk

        @pl.when((zi ^ z) % 2 == 1)
        def _():
            send_ref[rel // 2, tile] = blk

    g = dot_tn(hl, dc_ref[...]).astype(bf16)
    for j in range(8):
        zi, xi = j // 2, j % 2
        for t in range(5):
            put(zi, (xi ^ x) * 5 + t, g[j * width : (j + 1) * width, t * LANES : (t + 1) * LANES])
    m = dot_tn(at_ref[...], d1)
    lane = lane_of((1, LANES))
    for xp in range(2):
        t = [m[xp * width : (xp + 1) * width, i * LANES : (i + 1) * LANES] for i in range(6)]
        first = [t[0], t[3], jnp.where(lane < 64, t[1], pltpu.roll(t[4], 64, 1))]
        second = [t[2], t[5], jnp.where(lane < 64, pltpu.roll(t[1], 64, 1), t[4])]
        for cp, tiles in enumerate((first, second)):
            for i, tile in enumerate(tiles):
                put(2 * xp + cp, 10 + i, tile.astype(bf16))


def pick_kernel(layers, place, *refs):
    own, came = refs[:layers], refs[layers]
    stay_ref, move_ref = refs[layers + 1 :]
    y, x = place[0], place[3]
    lane = lane_of((1, LANES))
    for l in range(layers):
        mine = [own[l][t].astype(f32) for t in range(5)]
        other = [came[l, t].astype(f32) for t in range(5)]

        def blocks(t):
            return [(t[0], t[1]), (t[2], pltpu.roll(t[1], 64, 1)), (t[3], t[4])]

        first = x == 0
        lowb, highb = blocks(mine), blocks(other)
        low_g = [tuple(jnp.where(first, a, b) for a, b in zip(m, o)) for m, o in zip(lowb, highb)]
        high_g = [tuple(jnp.where(first, b, a) for a, b in zip(m, o)) for m, o in zip(lowb, highb)]
        upper = [low_g[0], high_g[0], low_g[1]]
        lower = [high_g[1], low_g[2], high_g[2]]
        for i in range(3):
            for j in range(2):
                a, b = upper[i][j], lower[i][j]
                stay_ref[l, i, j] = jnp.where(y == 0, a, b).astype(bf16)
                move_ref[l, i, j] = jnp.where(y == 0, b, a).astype(bf16)
        m = [own[l][10 + t].astype(f32) for t in range(3)]
        stay_ref[l, 3, 0] = jnp.where(y == 0, m[0], m[1]).astype(bf16)
        move_ref[l, 3, 0] = jnp.where(y == 0, m[1], m[0]).astype(bf16)
        stay_ref[l, 3, 1] = m[2].astype(bf16)
        move_ref[l, 3, 1] = m[2].astype(bf16)


def settle_kernel(layers, place, a, b, part_ref, swap_ref, mix_ref):
    c = place[1]
    for l in range(layers):
        v = [[a[l, i, j].astype(f32) + b[l, i, j].astype(f32) for j in range(2)] for i in range(4)]
        for j in range(2):
            part_ref[l, 0, j] = jnp.where(c == 0, v[0][j], v[1][j]).astype(bf16)
            part_ref[l, 1, j] = jnp.where(c == 0, v[1][j], v[2][j]).astype(bf16)
            swap_ref[l, j] = jnp.where(c == 0, v[2][j], v[0][j]).astype(bf16)
            mix_ref[l, j] = v[3][j].astype(bf16)


def step_of(factor, g, m, a, w):
    moment = momentum_decay * m + g
    new = w.astype(f32) - factor * (g + momentum_decay * moment)
    return moment, average_decay * a + (1.0 - average_decay) * new, new


def tile_from(win, t, odd):
    cols = [win[:, i * LANES : (i + 1) * LANES].astype(f32) for i in (t, t + 1) if (i + 1) * LANES <= win.shape[1]]
    turned = [pltpu.roll(v, 64, 1) for v in cols]
    shifted = turned[0] if len(cols) == 1 else jnp.where(lane_of(cols[0].shape) < 64, turned[0], turned[1])
    return jnp.where(odd, shifted, cols[0])


def stepped(factor, l, at, t, m_ref, a_ref, w, outs):
    to = at + t.shape[1]
    for o, v in zip(outs, step_of(factor, t, m_ref[l, :, at:to], a_ref[l, :, at:to], w[:, : t.shape[1]])):
        o[l, :, at:to] = v
    return to


def window_copy(w_ref, win, sems, place, step, span):
    rows = win.shape[1]
    row = (2 * place[2] + place[3]) * rows
    start = (((2 * place[0] + place[1]) * step) // LANES) * LANES
    return fetched(
        [
            pltpu.make_async_copy(
                w_ref.at[l, pl.ds(pl.multiple_of(row, 32), rows), pl.ds(pl.multiple_of(start, LANES), span)],
                win.at[l],
                sems.at[l],
            )
            for l in range(win.shape[0])
        ]
    )


def olds_kernel(layers, gw, place, s_ref, p_ref, m_ref, f_ref, so, po, mo, fo, win_s, win_p, win_m, win_f, sems):
    y, c, z, x = (place[i] for i in range(4))
    seq_i, row_i = 2 * z + x, 2 * y + c
    rows, width = win_f.shape[1], win_f.shape[3]
    column = seq_i * 2 * gw
    start = jnp.minimum(column // LANES, 4) * LANES
    taps = win_s.shape[0]
    stem = pltpu.make_async_copy(
        s_ref.at[pl.ds(pl.multiple_of(row_i * taps, LANES), taps), pl.ds(pl.multiple_of(start, LANES), 256)],
        win_s, sems.at[0],
    )
    feeds = [
        pltpu.make_async_copy(
            f_ref.at[l, pl.ds(seq_i * rows, rows), :, pl.ds(pl.multiple_of(row_i * width, LANES), width)],
            win_f.at[l], sems.at[1 + l],
        )
        for l in range(layers)
    ]
    fetched([stem, *feeds])
    ins = window_copy(p_ref, win_p, sems.at[pl.ds(1 + layers, layers)], place, 576, 640)
    mixes = window_copy(m_ref, win_m, sems.at[pl.ds(1 + 2 * layers, layers)], place, 192, 256)
    r = lax.broadcasted_iota(jnp.int32, (LANES, 256), 0)
    k = lax.broadcasted_iota(jnp.int32, (LANES, 256), 1)
    chosen = jnp.where(k == r + (column - start), 1.0, 0.0).astype(bf16)
    parting = parting_matrix(2 * rows)
    odd = c == 1
    stem.wait()
    so[...] = dot_nt(chosen, win_s[...])[0 : 2 * gw].astype(bf16)
    for l in range(layers):
        feeds[l].wait()
        fo[l] = dot_nn(parting, win_f.at[l].reshape(2 * rows, width)[...]).astype(bf16)
        ins[l].wait()
        for t in range(5):
            po[l, :, t * LANES : (t + 1) * LANES] = tile_from(win_p[l], t, odd).astype(bf16)
        mixes[l].wait()
        for t in range(2):
            mo[l, :, t * LANES : (t + 1) * LANES] = tile_from(win_m[l], t, odd).astype(bf16)


def projection_step_kernel(factor, place, w_ref, part_ref, swap_ref, m_ref, a_ref, *outs):
    lane = lane_of((1, LANES))
    for l in range(m_ref.shape[0]):
        b0 = [part_ref[l, 0, j].astype(f32) for j in range(2)]
        b2 = [part_ref[l, 1, j].astype(f32) for j in range(2)]
        b1 = [pltpu.roll(swap_ref[l, j].astype(f32), 64, 1) for j in range(2)]
        tiles = [b0[0], jnp.where(lane < 64, b0[1], b1[0]), jnp.where(lane < 64, b1[0], b1[1]), b2[0], b2[1][:, :64]]
        at = 0
        for i, t in enumerate(tiles):
            at = stepped(factor, l, at, t, m_ref, a_ref, w_ref[l, :, i * LANES : (i + 1) * LANES], outs)


def mixing_step_kernel(factor, place, w_ref, mix_ref, m_ref, a_ref, *outs):
    y, c = place[0], place[1]
    lane = lane_of((1, LANES))
    for l in range(m_ref.shape[0]):
        full, half = mix_ref[l, 0].astype(f32), mix_ref[l, 1].astype(f32)
        turned = pltpu.roll(full, 64, 1)
        half = jnp.where(y == 0, half, pltpu.roll(half, 64, 1))
        tiles = [
            jnp.where(c == 0, full, jnp.where(lane < 64, half, turned)),
            jnp.where(c == 0, half, turned)[:, :64],
        ]
        at = 0
        for i, t in enumerate(tiles):
            at = stepped(factor, l, at, t, m_ref, a_ref, w_ref[l, :, i * LANES : (i + 1) * LANES], outs)


def feed_step_kernel(factor, place, w_ref, *refs):
    layers = w_ref.shape[0]
    parts, (m_ref, a_ref), outs = refs[: 2 * layers], refs[2 * layers : 2 * layers + 2], refs[2 * layers + 2 :]
    rows = m_ref.shape[1]
    for l in range(layers):
        for kind in range(2):
            a, b = parts[2 * l], parts[2 * l + 1]

            def body(k, carry, l=l, kind=kind, a=a, b=b):
                r = pl.ds(pl.multiple_of(k * 32, 32), 32)
                both = pl.ds(pl.multiple_of(kind * rows + k * 32, 32), 32)
                g = a[both, :].astype(f32) + b[both, :].astype(f32)
                w = w_ref[l, both, :]
                for o, v in zip(outs, step_of(factor, g, m_ref[l, r, kind, :], a_ref[l, r, kind, :], w)):
                    o[l, r, kind, :] = v
                return carry

            lax.fori_loop(0, rows // 32, body, 0)


def stem_step_kernel(factor, gw, place, w_ref, p_ref, r_ref, m_ref, a_ref, *outs):
    count = p_ref.shape[0] // gw
    lane = lane_of((gw, LANES))
    for group in range(2):
        pieces = []
        for k in range(count):
            rows_k = slice(k * gw, (k + 1) * gw)
            v = p_ref[rows_k, :].astype(f32) + r_ref[rows_k, :].astype(f32)
            v = v if group == 0 else pltpu.roll(v, LANES - gw, 1)
            pieces.append(jnp.where(lane < gw, v, 0.0))
        mine = slice(group * gw, (group + 1) * gw)
        for i, t in enumerate(tiles_of(pieces, gw)):
            cols = slice(i * LANES, (i + 1) * LANES)
            for o, v in zip(outs, step_of(factor, t, m_ref[mine, cols], a_ref[mine, cols], w_ref[mine, cols])):
                o[mine, cols] = v


def smalls_kernel(layers, ff_rows, gains, width, head_share, place, *refs):
    norms, ups, atts = refs[: 2 * layers + 1], refs[2 * layers + 1 : 3 * layers + 1], refs[3 * layers + 1 : 4 * layers + 1]
    keep_ref, send_ref, all_ref = refs[4 * layers + 1 :]
    y, c, z, x = (place[i] for i in range(4))
    all_ref[...] = jnp.zeros_like(all_ref)
    all_ref[0:1, :] = norms[0][0:1, :]
    all_ref[gains + 1 : gains + 2, :] = norms[0][1:2, :]
    for l in range(layers):
        base = gains + 2 + l * (6 + ff_rows)
        for k, (gain, shift, plain) in enumerate(((1, 3, 2), (2, 5, 4))):
            s = norms[1 + 2 * l + k]
            all_ref[gain + 2 * l : gain + 2 * l + 1, :] = s[0:1, :]
            all_ref[base + shift : base + shift + 1, :] = s[1:2, :]
            all_ref[base + plain : base + plain + 1, :] = s[2:3, :]
        for ry in range(2):
            all_ref[pl.ds(base + 6 + 2 * (y ^ ry) + c, 1), :] = ups[l][ry : ry + 1, :]
        for group in range(4):

            @pl.when(2 * x + c == group)
            def _(l=l, base=base, group=group):
                for i in range(2):
                    pieces = [jnp.zeros((1, LANES), f32)] * (width // 64)
                    for h in range(3):
                        t = atts[l][i : i + 1, (h // 2) * LANES : (h // 2 + 1) * LANES]
                        t = t if h % 2 == 0 else pltpu.roll(t, 64, 1)
                        pieces[3 * group + h] = jnp.where(lane_of(t.shape) < 64, t, 0.0)
                    all_ref[base + i : base + i + 1, :] = jnp.concatenate(tiles_of(pieces, 64), axis=1)

    whole = all_ref[...]
    cols = [whole[:, LANES * v : LANES * (v + 1)] for v in range(width // LANES)]
    for j in range(8):
        blk = piece_of(cols, j, width // 8)
        rel = (j // 2) ^ z
        at = (rel % 2) * 2 + rel // 2

        @pl.when(x == j % 2)
        def _(blk=blk, at=at):
            keep_ref[at] = blk

        @pl.when(x != j % 2)
        def _(blk=blk, at=at):
            send_ref[at] = blk


def small_total_kernel(row, a_ref, r_ref, b_ref, o_ref):
    total = a_ref[...] + r_ref[...]
    o_ref[...] = total
    o_ref[row : row + 1, :] = total[row : row + 1, :] + b_ref[0:1, :]


def encoded_split_kernel(place, x_ref, keep_ref, send_ref):
    z = place[2]
    for rel in range(4):
        out = send_ref if rel % 2 else keep_ref
        for a in range(2):
            at = pl.multiple_of(a * 64 + (z ^ rel) * 16, 16)
            out[rel // 2, a * 16 : a * 16 + 16, :] = x_ref[pl.ds(at, 16), :]


def encoded_route_kernel(place, own_ref, near_ref, far_ref, keep_ref, send_ref):
    c, z = place[1], place[2]
    for rel, src in enumerate(by_z(own_ref, near_ref, far_ref)):
        row = z ^ rel
        mine = (row // 2) == c

        @pl.when(mine)
        def _(src=src, row=row):
            keep_ref[row % 2] = src[...]

        @pl.when(jnp.logical_not(mine))
        def _(src=src, row=row):
            send_ref[row % 2] = src[...]


def encoded_join_kernel(place, keep_ref, recv_ref, o_ref, mixed):
    c = place[1]
    rows, toks, width = o_ref.shape
    for r in range(rows):
        for v in range(width // LANES):
            cols = slice(v * LANES, (v + 1) * LANES)
            for rel, src in enumerate((keep_ref, recv_ref)):
                for a in range(2):
                    at = v * toks + (c ^ rel) * 32 + a
                    mixed[pl.ds(at, 16, stride=2), :] = src[r, a * 16 : a * 16 + 16, cols].astype(f32)
            o_ref[r, :, cols] = mixed[v * toks : (v + 1) * toks, :]


def take_kernel(place, own_ref, near_ref, far_ref, keep_ref, send_ref):
    c, z, x = place[1], place[2], place[3]
    for rel, src in enumerate(by_z(own_ref, near_ref, far_ref)):
        row = z ^ rel
        mine = (row // 2) == c
        for h in range(2):

            @pl.when(mine)
            def _(src=src, row=row, h=h):
                keep_ref[row % 2, x ^ h] = src[h]

            @pl.when(jnp.logical_not(mine))
            def _(src=src, row=row, h=h):
                send_ref[row % 2, x ^ h] = src[h]


def stem_slope_kernel(rows, place, keep_ref, recv_ref, pre_ref, low_ref, ds_ref, bias_ref):
    c = place[1]
    for r in range(rows):
        for zf in range(4):
            for xq in range(2):
                for rel, src in enumerate((keep_ref, recv_ref)):
                    u = pl.multiple_of(((zf * 2 + xq) * 2 + (c ^ rel)) * 16, 16)
                    ds_ref[r, pl.ds(u, 16), :] = src[r, xq, zf * 16 : zf * 16 + 16, :]
    total = None
    for r in range(rows):
        dpre = ds_ref[r].astype(f32) * gelu_and_slope(pre_ref[r])[1]
        part = jnp.sum(dpre, axis=0, keepdims=True)
        total = part if total is None else total + part
        low_ref[r] = dpre.astype(bf16)
    bias_ref[0:1, :] = total[:, 0:LANES] + total[:, LANES : 2 * LANES]
    bias_ref[1:8, :] = jnp.zeros((7, LANES), f32)


def stem_grad_kernel(rows, taps, gw, place, ph_ref, low_ref, keep_ref, send_ref):
    n = low_ref.shape[1]
    y, c = place[0], place[1]
    left = jnp.concatenate([low_ref[r] for r in range(rows)], axis=0).T
    lane = lane_of((gw, LANES))
    per = taps // 4
    for rc, out in enumerate((keep_ref, send_ref)):
        for ry in range(2):
            block = (y ^ ry) * 2 + (c ^ rc)

            def win(i):
                at = pl.multiple_of((block + i // 16) * 16, 16)
                return ph_ref[i % 16, :, pl.ds(at, n), :].reshape(rows * n, 2 * LANES)

            def save(k, t, out=out, ry=ry):
                out[ry, k * gw : (k + 1) * gw, :] = jnp.where(lane < gw, t[0:gw], t[gw : 2 * gw]).astype(bf16)

            held = None
            for i in range(per // 2 + 1):
                if i < per // 2:
                    g = dot_nn(left, win(i))
                    cross = g[LANES:, 0:LANES]
                else:
                    cross = dot_nn(left[LANES:], win(i)[:, 0:LANES])
                if held is not None:
                    save(2 * i - 1, held + cross)
                if i < per // 2:
                    save(2 * i, g[0:LANES, 0:LANES] + g[LANES:, LANES:])
                    held = g[0:LANES, LANES:]


def stem_input_grad_kernel(rows, half, place, low_ref, ds_ref, w_ref, keep_ref, send_ref, qf, ph, acc):
    n = low_ref.shape[1]
    span = n + half
    for r in range(rows):
        qf[r, 0 : half // 2, :] = jnp.zeros((half // 2, 2 * LANES), f32)
        qf[r, half // 2 + n :, :] = jnp.zeros((half // 2, 2 * LANES), f32)
        qf[r, half // 2 : half // 2 + n, :] = low_ref[r].astype(f32)
    for p in range(16):
        m = span if p == 0 else span - 16
        for r in range(rows):
            ph[p, r, 0:m, :] = qf[r, p : p + m, :].astype(bf16)
    acc[...] = jnp.zeros_like(acc)

    def body(i, carry):
        left, upper, lower = [], [], []
        for t in range(5):
            m = i * 5 + t
            here, before, after = w_ref[2 * half + 1 - 2 * m], w_ref[2 * half - 2 * m], w_ref[2 * half + 2 - 2 * m]
            upper += [here, before]
            lower += [after, here]
            left.append(window(ph, m, rows, n))
        right = jnp.concatenate([jnp.concatenate(upper, 1), jnp.concatenate(lower, 1)], 0)
        acc[...] += dot_nt(jnp.concatenate(left, 1), right)
        return carry

    lax.fori_loop(0, (half + 1) // 5, body, 0)
    per = n // 8
    for r in range(rows):
        g = (acc[r * n : (r + 1) * n, :] + ds_ref[r].astype(f32)).astype(bf16)
        for j in range(8):
            to_x(keep_ref, send_ref, place[3], j % 2, (j // 2) ^ place[2], (r,), g[j * per : (j + 1) * per, :])


def join_kernel(width, place, own_ref, near_ref, far_ref, o_ref, mixed, by_channel):
    z, x = place[2], place[3]
    rows, per = own_ref.shape[2], own_ref.shape[3]
    for rel, src in enumerate(by_z(own_ref, near_ref, far_ref)):
        for h in range(2):
            by_channel[(z ^ rel) * 2 + (x ^ h)] = src[h]
    for r in range(rows):
        for a in range(2):
            pieces = [by_channel[j, r, :, a * LANES : (a + 1) * LANES].astype(f32) for j in range(8)]
            for v, col in enumerate(tiles_of(pieces, width)):
                mixed[pl.ds(v * 2 * per + a, per, stride=2), :] = col
        for v in range(o_ref.shape[2] // LANES):
            o_ref[r, :, v * LANES : (v + 1) * LANES] = mixed[v * 2 * per : (v + 1) * 2 * per, :]


def swapped(v, axis):
    return lax.ppermute(v, axis, [(0, 1), (1, 0)])


def across(v, axis, bit):
    count = lax.axis_size(axis)
    return lax.ppermute(v, axis, [(i, i ^ bit) for i in range(count)])


def one_sum(a, b):
    return whole_call(one_kernel, [sds(a.shape, a.dtype)], [a, b])[0]


def local_rows(
    features, cotangent, segments, stem_weight, projection_weight, mixing_weight,
    feedforward_weight, norm_gains, biases, *state,
):
    rows, toks, width = features.shape
    yi, ci, zi, xi = (lax.axis_index(a) for a in ("y", "c", "z", "x"))
    place = jnp.stack([yi, ci, zi, xi]).astype(jnp.int32)
    seq_i, row_i = zi * 2 + xi, yi * 2 + ci
    seq = ("z", "x")
    blocks = 8
    share = width // blocks
    gw = width // GROUPS
    frames = toks * blocks
    half = KERNEL // 2
    layers = projection_weight.shape[0]
    ff_rows = feedforward_weight.shape[3] // width
    head_share = width // 4
    group = 2 * xi + ci
    t = rows * toks

    stem_share = jnp.pad(
        lax.dynamic_slice_in_dim(stem_weight, seq_i * share, share, 1), ((0, 0), (0, LANES - share))
    )

    steps = width // LANES
    square = sds((width, width), bf16)
    *feed_first, feed_there = whole_call(
        functools.partial(feed_weights_kernel, 0), [square] * 4, [place, feedforward_weight],
        scalars=1, far=(1,), token=True, vmem=FAR_BYTES,
        scratch=[pltpu.VMEM((2, width, 2, width), bf16), pltpu.SemaphoreType.DMA((2 * steps,))],
    )

    (sent,) = whole_call(
        functools.partial(split_kernel, blocks, share), [sds((blocks, rows, toks, LANES), bf16)], [features]
    )
    mine = lax.all_to_all(sent, seq, 0, 0, tiled=True)
    conv_bias = jnp.pad(
        lax.dynamic_slice(biases, (0, seq_i * share), (1, share)), ((0, 0), (0, LANES - share))
    )
    n = frames // 2
    exchange = sds((rows, 2, 64, 2 * LANES), bf16)
    tap_scratch = pltpu.VMEM((KERNEL + 3, LANES, LANES), bf16)
    phased = (16, rows, (frames + 2 * half) // 2, 2 * LANES)
    row_scratch = pltpu.VMEM((rows * (frames + 2 * half) + 8, LANES), f32)
    pre_act, kept, away = whole_call(
        functools.partial(conv_kernel, rows, frames, half, gw),
        [sds((rows, n, 2 * LANES), f32), exchange, exchange],
        [place, mine, stem_share, conv_bias],
        after=[feed_there],
        scalars=1,
        scratch=[pltpu.VMEM(phased, bf16), row_scratch, pltpu.VMEM((rows * n, 2 * LANES), f32), tap_scratch],
        vmem=WIDE_BYTES,
    )
    (slots,) = whole_call(
        slots_kernel, [sds((blocks, 64, 2 * LANES), bf16)], [place, kept, swapped(away, "c")], scalars=1
    )
    *later, later_there = whole_call(
        functools.partial(later_weights_kernel, layers, [2 + l * (6 + ff_rows) for l in range(layers)], head_share),
        [square] * (4 * (layers - 1)) + [square, sds((256, width), bf16), sds((2, 256), f32)] * layers,
        [place, feedforward_weight, projection_weight, mixing_weight, biases],
        scalars=1, far=(1, 2, 3), token=True, vmem=FAR_BYTES, after=[slots],
        scratch=[
            pltpu.VMEM((layers - 1, 2, width, 2, width), bf16),
            pltpu.VMEM((layers, 3, width, 256), bf16),
            pltpu.SemaphoreType.DMA((layers - 1, 2 * steps)),
            pltpu.SemaphoreType.DMA((4 * layers,)),
        ],
    )
    feed_w = [feed_first, *(later[4 * i : 4 * i + 4] for i in range(layers - 1))]
    attend_w = [later[4 * (layers - 1) + 3 * l :][:3] for l in range(layers)]
    joined = lax.all_to_all(slots, seq, 0, 0, tiled=True)
    wide = sds((t, width), f32)
    thin = sds((t, width), bf16)
    column = sds((t, 1), f32)
    hidden, hidden_low, normed_stem, inverse_stem = whole_call(
        functools.partial(stem_norm_kernel, share), [wide, thin, wide, column], [joined, norm_gains, biases],
        after=[later_there],
    )

    def gathered(v):
        over_c = swapped(v, "c")
        over_x = swapped(v, "x")
        return [v, over_c, over_x, swapped(over_x, "c")]

    saved = []
    segments_other = swapped(segments, "c")
    quarter_row = sds((32, width), bf16)
    two = sds((2, t, width), bf16)
    full = 4 * t
    for l in range(layers):
        base = 2 + l * (6 + ff_rows)
        in_w, mix_w, both_b = attend_w[l]
        ups, downs = feed_w[l][:2], feed_w[l][2:]
        hl = gathered(hidden_low)
        before = []
        if l == 0:
            seg_row, seg_col = whole_call(
                segments_kernel, [sds((1, frames), f32), sds((frames, 1), f32)], [place, segments, segments_other],
                scalars=1, after=[hidden_low],
            )
            stay, move, cot_there = whole_call(
                cotangent_split_kernel, [sds((rows, 32, width), bf16)] * 2, [place, cotangent],
                scalars=1, after=[hidden_low], token=True,
                scratch=[pltpu.VMEM((width // LANES * toks + 8, LANES), f32)],
            )
            before = [cot_there]
        elif l == 1:
            cot, cot_there = whole_call(
                cotangent_join_kernel, [sds((t, width), bf16)],
                [place, routed[0], *(across(routed[rel], "z", rel) for rel in range(1, 4))],
                scalars=1, after=[hidden_low], token=True,
            )
            before = [cot_there]
        q, k, v, att, lse, keep, send = whole_call(
            functools.partial(attend_kernel, base),
            [sds((full, 256), bf16)] * 4 + [sds((3, full, 1), f32), two, two],
            hl + [in_w, mix_w, both_b, seg_row, seg_col],
            after=before,
        )
        own, pass_on = whole_call(half_sum_kernel, [wide, thin], [keep, swapped(send, "c")])
        rest = swapped(pass_on, "x")
        before = []
        if l == 0:
            *routed, cot_there = whole_call(
                cotangent_route_kernel, [quarter_row] * 4, [place, stay, swapped(move, "c")],
                scalars=1, after=[pass_on], token=True,
            )
            before = [cot_there]
        first, first_low, n1, i1 = whole_call(
            functools.partial(norm_kernel, 1 + 2 * l, base + 2, base + 3),
            [wide, thin, wide, column],
            [hidden, own, rest, norm_gains, biases],
            after=before,
        )
        first_other = swapped(first_low, "c")
        act, slope, own, send = whole_call(
            functools.partial(feed_kernel, base + 6),
            [sds((2, 2 * t, width), bf16)] * 2 + [wide, thin],
            [place, first_low, first_other, *ups, *downs, biases],
            scalars=1,
        )
        hidden, hidden_low, n2, i2 = whole_call(
            functools.partial(norm_kernel, 2 + 2 * l, base + 4, base + 5),
            [wide, thin, wide, column],
            [first, own, swapped(send, "c"), norm_gains, biases],
        )
        saved.append((in_w, mix_w, ups, downs, hl, q, k, v, att, lse, n1, i1, first_low, first_other, act, slope, n2, i2))

    encoded_low = hidden_low
    sums = sds((8, width), f32)
    terms = [cot]
    norm_sum = [None] * norm_gains.shape[0]
    up_sum, att_sum = [None] * layers, [None] * layers
    feed, att_parts = [None] * layers, [None] * layers
    parted = sds((2, 2, 2, 2 * share, width), bf16)
    tiles = sds((13, share, LANES), bf16)
    tiles_z = sds((2, 13, share, LANES), bf16)

    def send_on(parts, after):
        outs, operands = [], []
        for keep, recv, _ in parts:
            outs += [sds(keep.shape[1:], keep.dtype)] * 2
            operands += [keep, recv]
        made = whole_call(
            functools.partial(halves_kernel, len(parts)), outs, operands, after=after, token=True
        )
        return [(made[2 * i], how(made[2 * i + 1])) for i, (_, _, how) in enumerate(parts)], made[-1]

    over_x, over_y = (lambda v: swapped(v, "x")), (lambda v: swapped(v, "y"))
    over_z1, over_z2 = (lambda v: across(v, "z", 1)), (lambda v: across(v, "z", 2))
    before = []
    for l in reversed(range(layers)):
        base = 2 + l * (6 + ff_rows)
        in_w, mix_w, ups, downs, hl, q, k, v, att, lse, n1, i1, first_low, first_other, act, slope, n2, i2 = saved[l]
        d2, d2_low, norm_sum[2 + 2 * l] = whole_call(
            functools.partial(norm_back_kernel, 2 + 2 * l, len(terms)), [wide, thin, sums], terms + [norm_gains, n2, i2],
            after=before,
        )
        d2_other = swapped(d2_low, "c")
        dup, own, send, up_sum[l] = whole_call(
            feed_back_kernel,
            [sds((2, 2 * t, width), bf16), wide, thin, sums],
            [d2_low, d2_other, *ups, *downs, slope],
        )

        def feed_grad(after, first_low=first_low, first_other=first_other, d2_low=d2_low, d2_other=d2_other, dup=dup, act=act):
            keep, send, there = whole_call(
                feed_grad_kernel, [parted] * 2, [place, first_low, first_other, d2_low, d2_other, dup, act],
                scalars=1, after=after, token=True,
            )
            return (keep, over_y(send)), there

        before = []
        if l == 1:
            feed[l], there = feed_grad([send])
            before = [there]
        d1, d1_low, norm_sum[1 + 2 * l] = whole_call(
            functools.partial(norm_back_kernel, 1 + 2 * l, 3),
            [wide, thin, sums],
            [d2, own, swapped(send, "c"), norm_gains, n1, i1],
            after=before,
        )
        dl = gathered(d1_low)
        before = []
        if l == 1:
            two_rows = sds((2, 32, width), bf16)
            row_keep, row_send, there = whole_call(
                encoded_split_kernel, [two_rows] * 2, [place, encoded_low], scalars=1, after=[d1_low], token=True
            )
            row_near = over_z1(row_send)
            before = [there]
        if l == 0:
            feed[l], there = feed_grad([d1_low])
            stay_row, move_row, there = whole_call(
                encoded_route_kernel, [two_rows] * 2, [place, row_keep, row_near, row_far],
                scalars=1, after=[there], token=True,
            )
            (att_parts[1],), there = send_on([(*att_parts[1], over_z2)], [there])
            before = [there]
        dense_dp, keep, send, att_sum[l] = whole_call(
            attend_back_kernel,
            [sds((full, 640), bf16), two, two, sds((8, 256), f32)],
            dl + [q, k, v, lse, in_w, mix_w, seg_row, seg_col],
            after=before,
            scratch=[pltpu.VMEM((full, 256), bf16)] + [pltpu.VMEM((full, 256), f32)] * 3,
        )
        own, pass_on = whole_call(
            half_sum_kernel, [wide, thin], [keep, swapped(send, "c")],
        )
        rest = swapped(pass_on, "x")
        terms = [d1, own, rest]

        def attend_grad(after, hl=hl, dl=dl, att=att, dense_dp=dense_dp):
            return whole_call(
                attend_grad_kernel, [tiles_z, tiles_z], [place] + hl + dl + [att, dense_dp],
                scalars=1, after=after, token=True,
            )

        keep, send, there = attend_grad([pass_on])
        att_parts[l] = (keep, over_z1(send))
        if l == 1:
            row_send, there = whole_call(onward_kernel, [two_rows], [row_keep, row_near], after=[there], token=True)
            row_far = over_z2(row_send)
        else:
            encoded, there = whole_call(
                encoded_join_kernel, [sds((rows, toks, width), f32)], [place, stay_row, swapped(move_row, "c")], scalars=1,
                scratch=[pltpu.VMEM((width // LANES * toks + 8, LANES), f32)], after=[there], token=True,
            )
        before = [there]

    quad = sds((4, 64, 2 * LANES), bf16)
    ds_keep, ds_sent, norm_sum[0] = whole_call(
        functools.partial(stem_norm_back_kernel, share, len(terms)),
        [quad, quad, sums],
        [place, *terms, norm_gains, normed_stem, inverse_stem],
        scalars=1,
        after=before,
    )

    def spread(keep, send, after):
        pair_shape = sds((2, 2, *keep.shape[1:]), bf16)
        stays, goes, there = whole_call(
            along_z_kernel, [pair_shape] * 2, [keep, swapped(send, "x")], after=after, token=True
        )
        near = over_z1(goes)

        def onward(after):
            (far,) = whole_call(onward_kernel, [pair_shape], [stays, near], after=after)
            return [stays, near, over_z2(far)]

        return there, onward

    gain_count, bias_count = norm_gains.shape[0], biases.shape[0]
    small_half = sds((4, 32, LANES), f32)
    small_keep, small_send, small_there = whole_call(
        functools.partial(smalls_kernel, layers, ff_rows, gain_count, width, head_share),
        [small_half, small_half],
        [place, *norm_sum, *up_sum, *att_sum],
        scalars=1,
        scratch=[pltpu.VMEM((32, width), f32)],
        token=True,
        after=[ds_sent],
    )
    smalls = (small_keep.reshape(2, 2, 32, LANES), swapped(small_send, "x").reshape(2, 2, 32, LANES))
    phases, taps, phases_there = whole_call(
        functools.partial(phases_kernel, rows, frames, half, gw),
        [sds(phased, bf16), sds((KERNEL + 3, LANES, LANES), bf16)], [mine, stem_share], scratch=[row_scratch],
        after=[small_there], token=True,
    )
    att_second, there = whole_call(one_kernel, [tiles], list(att_parts[1]), after=[phases_there], token=True)
    there, ds_onward = spread(ds_keep, ds_sent, [there])
    ds_blocks = ds_onward([there])
    (smalls, feed[1], att_parts[0]), there = send_on(
        [(*smalls, over_z1), (*feed[1], over_x), (*att_parts[0], over_z2)], [ds_blocks[1]]
    )
    stay, move, there = whole_call(
        take_kernel, [sds((2, 2, 64, 2 * LANES), bf16)] * 2, [place, *ds_blocks], scalars=1,
        after=[there], token=True,
    )
    pair = sds((rows, n, 2 * LANES), bf16)
    dpre_low, ds, stem_sums = whole_call(
        functools.partial(stem_slope_kernel, rows), [pair, pair, sds((8, LANES), f32)],
        [place, stay, swapped(move, "c"), pre_act], scalars=1, after=[there],
    )
    quarter = sds((2, KERNEL // 4 * gw, LANES), bf16)
    keep, send = whole_call(
        functools.partial(stem_grad_kernel, rows, KERNEL, gw), [quarter, quarter], [place, phases, dpre_low], scalars=1,
    )
    stem_part = (keep, swapped(send, "c"))
    back_shape = sds((4, rows, toks // 2, 2 * LANES), bf16)
    back_keep, back = whole_call(
        functools.partial(stem_input_grad_kernel, rows, half),
        [back_shape] * 2,
        [place, dpre_low, ds, taps],
        scalars=1,
        scratch=[
            pltpu.VMEM((rows, n + half, 2 * LANES), f32),
            pltpu.VMEM((16, rows, n + half, 2 * LANES), bf16),
            pltpu.VMEM((rows * n, 2 * LANES), f32),
        ],
        after=[send],
        vmem=WIDE_BYTES,
    )
    (stem_part, feed[1]), there = send_on([(*stem_part, over_y), (*feed[1], over_z1)], [back])
    there, back_onward = spread(back_keep, back, [there])
    (feed[0],), there = send_on([(*feed[0], over_x)], [there])
    back_blocks = back_onward([there])
    att_first, there = whole_call(one_kernel, [tiles], list(att_parts[0]), after=[back_blocks[1]], token=True)
    att_grads = [att_first, att_second]
    (features_gradient,) = whole_call(
        functools.partial(join_kernel, share), [sds((rows, toks, width), f32)], [place, *back_blocks], scalars=1,
        scratch=[
            pltpu.VMEM((width // LANES * toks + 8, LANES), f32),
            pltpu.VMEM((blocks, rows, toks // 2, 2 * LANES), bf16),
        ],
        after=[there],
    )
    (feed[1],), there = send_on([(*feed[1], over_z2)], [features_gradient])
    att_came = swapped(jnp.stack([a[5:10] for a in att_grads]), "x")
    olds = whole_call(
        functools.partial(olds_kernel, layers, gw),
        [
            sds((share, KERNEL // 4 * gw), bf16),
            sds((layers, share, 640), bf16),
            sds((layers, share, 256), bf16),
            sds((layers, 2 * share, width), bf16),
        ],
        [place, stem_weight, projection_weight, mixing_weight, feedforward_weight],
        scalars=1, far=(1, 2, 3, 4), vmem=WIDE_BYTES, after=[there], token=True,
        scratch=[
            pltpu.VMEM((KERNEL // 4 * gw, 256), bf16),
            pltpu.VMEM((layers, share, 640), bf16),
            pltpu.VMEM((layers, share, 256), bf16),
            pltpu.VMEM((layers, share, 2, width), bf16),
            pltpu.SemaphoreType.DMA((1 + 3 * layers,)),
        ],
    )
    (feed[0], smalls), there = send_on([(*feed[0], over_z1), (*smalls, over_z2)], [olds[-1]])
    small_total, there = whole_call(
        functools.partial(small_total_kernel, gain_count), [sds((32, LANES), f32)], [*smalls, stem_sums],
        after=[there], token=True,
    )
    small_total = one_sum(small_total, swapped(small_total, "c"))
    settled = sds((layers, 4, 2, share, LANES), bf16)
    stay, move, there = whole_call(
        functools.partial(pick_kernel, layers), [settled] * 2, [place, *att_grads, att_came], scalars=1,
        after=[there], token=True,
    )
    (feed[0],), there = send_on([(*feed[0], over_z2)], [there])
    in_part, swap_part, mix_part, there = whole_call(
        functools.partial(settle_kernel, layers),
        [sds((layers, 2, 2, share, LANES), bf16)] + [sds((layers, 2, share, LANES), bf16)] * 2,
        [place, stay, swapped(move, "y")],
        scalars=1, after=[there], token=True,
    )
    swap_part = swapped(swap_part, "c")
    route = []
    for c in range(2):
        for z in range(4):
            for x in range(2):
                route.append(((c * 4 + z) * 2 + x, ((z & 1) * 4 + (2 * x + c)) * 2 + (z >> 1)))
    mix_part = lax.ppermute(mix_part, ("c", "z", "x"), route)
    small_total = one_sum(small_total, swapped(small_total, "y"))
    rate_base = 1.0 / math.sqrt(rows * 4 * frames)

    def step(index, kernel, operands, turn=False):
        m, a = state[index], state[6 + index]
        if turn:
            m, a = m.T, a.T
        made = whole_call(
            functools.partial(kernel, rate_factors[index] * rate_base), [sds(m.shape, f32)] * 3,
            [place, olds[index], *operands, m, a], scalars=1,
        )
        return [o.T for o in made] if turn else made

    results = [
        step(0, lambda f, *r: stem_step_kernel(f, gw, *r), list(stem_part), turn=True),
        step(1, projection_step_kernel, [in_part, swap_part]),
        step(2, mixing_step_kernel, [mix_part]),
        step(3, feed_step_kernel, [part for l in range(layers) for part in feed[l]]),
    ]
    for index, w, g in ((4, norm_gains, small_total[:gain_count]), (5, biases, small_total[gain_count : gain_count + bias_count])):
        w = lax.dynamic_slice_in_dim(w, seq_i * share, share, 1)
        results.append(step_of(rate_factors[index] * rate_base, g[:, :share], state[index], state[6 + index], w))
    return (encoded, features_gradient, *(results[i][k] for k in range(3) for i in range(6)))


def solution(mesh):
    if mesh.shape["row"] == 4 and mesh.shape["seq"] == 8:
        body, mesh = local_rows, Mesh(mesh.devices.reshape(2, 2, 4, 2), ("y", "c", "z", "x"))
        row, seq = ("y", "c"), ("z", "x")
    else:
        body, row, seq = local, "row", "seq"
    in_specs = (
        P(row, seq, None),
        P(row, seq, None),
        P(row, None),
        P(),
        P(),
        P(),
        P(),
        P(),
        P(),
        P(row, seq),
        P(None, seq, row),
        P(None, seq, row),
        P(None, seq, None, row),
        P(None, seq),
        P(None, seq),
        P(row, seq),
        P(None, seq, row),
        P(None, seq, row),
        P(None, seq, None, row),
        P(None, seq),
        P(None, seq),
    )
    out_specs = (
        P(row, seq, None),
        P(row, seq, None),
        P(row, seq),
        P(None, seq, row),
        P(None, seq, row),
        P(None, seq, None, row),
        P(None, seq),
        P(None, seq),
        P(row, seq),
        P(None, seq, row),
        P(None, seq, row),
        P(None, seq, None, row),
        P(None, seq),
        P(None, seq),
        P(row, seq),
        P(None, seq, row),
        P(None, seq, row),
        P(None, seq, None, row),
        P(None, seq),
        P(None, seq),
    )
    return jax.shard_map(body, mesh=mesh, in_specs=in_specs, out_specs=out_specs, check_vma=False)
```

```python
import functools
import math

import jax
import jax.numpy as jnp
from jax import lax
from jax.experimental import pallas as pl
from jax.experimental.pallas import tpu as pltpu
from jax.sharding import Mesh
from jax.sharding import PartitionSpec as P

HEADS = 12
KERNEL = 128
GROUPS = 16


epsilon = 1e-05
masked_score = -1e30
momentum_decay = 0.9
average_decay = 0.5
rate_factors = (0.012, 0.08, 0.6, 0.03, 0.06, 0.09)
row_dims = (0, 2, 2, 3)


def extended_2(cells, sides, width):
    for axis, dim in sides:
        count = lax.axis_size(axis)
        ends = count - 1
        head = lax.slice_in_dim(cells, 0, width, axis=dim)
        tail = lax.slice_in_dim(cells, cells.shape[dim] - width, cells.shape[dim], axis=dim)
        cells = jnp.concatenate(
            [
                lax.ppermute(tail, axis, [(i, (i + 1) % count) for i in range(ends)]),
                cells,
                lax.ppermute(head, axis, [((i + 1) % count, i) for i in range(ends)]),
            ],
            axis=dim,
        )
    return cells


def layer_norm(values, gain_row, shift_row):
    centre = jnp.mean(values, axis=-1, keepdims=True)
    centred = values - centre
    spread = jnp.mean(centred * centred, axis=-1, keepdims=True)
    inverse = lax.rsqrt(spread + epsilon)
    normed = centred * inverse
    return (normed * gain_row + shift_row, normed, inverse)


def layer_norm_back(upstream, normed, inverse, gain_row):
    scaled = upstream * gain_row
    first_mean = jnp.mean(scaled, axis=-1, keepdims=True)
    second_mean = jnp.mean(scaled * normed, axis=-1, keepdims=True)
    downstream = inverse * (scaled - first_mean - normed * second_mean)
    return (downstream, jnp.sum(upstream * normed, axis=(0, 1)), jnp.sum(upstream, axis=(0, 1)))


def gelu_exact(values):
    return jax.nn.gelu(values, approximate=False)


def gelu_back(inputs, upstream):
    _, pullback = jax.vjp(gelu_exact, inputs)
    return pullback(upstream)[0]


def group_conv(extended, kernel_taps, group_count):
    return lax.conv_general_dilated(
        extended,
        kernel_taps,
        (1,),
        "VALID",
        dimension_numbers=("NWC", "WIO", "NWC"),
        feature_group_count=group_count,
        preferred_element_type=jnp.float32,
    )


def group_conv_kernel_grad(extended, upstream_low, group_count):
    return lax.conv_general_dilated(
        extended,
        upstream_low,
        (1,),
        "VALID",
        dimension_numbers=("CWN", "IWO", "WNC"),
        batch_group_count=group_count,
        preferred_element_type=jnp.float32,
    )


def flipped_taps(kernel_taps, group_count):
    tap_count, group_width, model_width = kernel_taps.shape
    split_taps = kernel_taps.reshape(tap_count, group_width, group_count, group_width)
    swapped = jnp.transpose(split_taps, (0, 3, 2, 1)).reshape(tap_count, group_width, model_width)
    return swapped[::-1]


def masked_scores(query_part, key_part, query_segments, key_segments):
    scores = jnp.einsum("rqhe,rkhe->rhqk", query_part, key_part, preferred_element_type=jnp.float32)
    allowed = query_segments[:, None, :, None] == key_segments[:, None, None, :]
    return jnp.where(allowed, scores, masked_score)


def key_slice(kv_whole, segments, start, key_block, head_count):
    row_count = kv_whole.shape[0]
    model_width = kv_whole.shape[2] // 2
    head_width = model_width // head_count
    part_rows = lax.dynamic_slice_in_dim(kv_whole, start, key_block, 1)
    part_segments = lax.dynamic_slice_in_dim(segments, start, key_block, 1)
    key_part = part_rows[:, :, :model_width].reshape(row_count, key_block, head_count, head_width)
    value_part = part_rows[:, :, model_width:].reshape(row_count, key_block, head_count, head_width)
    return (key_part, value_part, part_segments)


def attend(query_heads, kv_whole, query_segments, segments, head_count):
    row_count = query_heads.shape[0]
    tok_count = query_heads.shape[1]
    key_block = math.gcd(kv_whole.shape[1], 1024)
    block_count = kv_whole.shape[1] // key_block

    def stats_step(step_index, state):
        running_max, running_sum = state
        key_part, value_part, part_segments = key_slice(
            kv_whole, segments, step_index * key_block, key_block, head_count
        )
        scores = masked_scores(query_heads, key_part, query_segments, part_segments)
        new_max = jnp.maximum(running_max, jnp.max(scores, axis=-1))
        running_sum = running_sum * jnp.exp(running_max - new_max) + jnp.sum(
            jnp.exp(scores - new_max[..., None]), axis=-1
        )
        return (new_max, running_sum)

    start_state = (
        jnp.full((row_count, head_count, tok_count), masked_score, jnp.float32),
        jnp.zeros((row_count, head_count, tok_count), jnp.float32),
    )
    running_max, running_sum = lax.fori_loop(0, block_count, stats_step, start_state)
    log_sum = running_max + jnp.log(running_sum)

    def value_step(step_index, state):
        coarse, residue = state
        key_part, value_part, part_segments = key_slice(
            kv_whole, segments, step_index * key_block, key_block, head_count
        )
        probability = jnp.exp(
            masked_scores(query_heads, key_part, query_segments, part_segments) - log_sum[..., None]
        )
        probability_low = probability.astype(jnp.bfloat16)
        remainder_low = (probability - probability_low.astype(jnp.float32)).astype(jnp.bfloat16)
        coarse = coarse + jnp.einsum(
            "rhqk,rkhe->rqhe", probability_low, value_part, preferred_element_type=jnp.float32
        )
        residue = residue + jnp.einsum(
            "rhqk,rkhe->rqhe", remainder_low, value_part, preferred_element_type=jnp.float32
        )
        return (coarse, residue)

    zero_out = jnp.zeros(query_heads.shape, jnp.float32)
    coarse, residue = lax.fori_loop(0, block_count, value_step, (zero_out, zero_out))
    return (coarse, coarse + residue, log_sum)


def attend_back(
    query_heads, grad_heads, kv_whole, query_segments, segments, log_sum, delta, head_count
):
    row_count = query_heads.shape[0]
    frame_count = kv_whole.shape[1]
    model_width = kv_whole.shape[2] // 2
    key_block = math.gcd(frame_count, 1024)
    block_count = frame_count // key_block

    def back_step(step_index, state):
        grad_query, key_terms = state
        start = step_index * key_block
        key_part, value_part, part_segments = key_slice(
            kv_whole, segments, start, key_block, head_count
        )
        probability = jnp.exp(
            masked_scores(query_heads, key_part, query_segments, part_segments) - log_sum[..., None]
        )
        grad_prob = jnp.einsum(
            "rqhe,rkhe->rhqk", grad_heads, value_part, preferred_element_type=jnp.float32
        )
        grad_scores = (probability * (grad_prob - delta[..., None])).astype(jnp.bfloat16)
        grad_query = grad_query + jnp.einsum(
            "rhqk,rkhe->rqhe", grad_scores, key_part, preferred_element_type=jnp.float32
        )
        grad_keys = jnp.einsum(
            "rhqk,rqhe->rkhe", grad_scores, query_heads, preferred_element_type=jnp.float32
        )
        grad_values = jnp.einsum(
            "rhqk,rqhe->rkhe",
            probability.astype(jnp.bfloat16),
            grad_heads,
            preferred_element_type=jnp.float32,
        )
        both_terms = jnp.concatenate(
            [
                grad_keys.reshape(row_count, key_block, model_width),
                grad_values.reshape(row_count, key_block, model_width),
            ],
            axis=-1,
        )
        key_terms = lax.dynamic_update_slice_in_dim(key_terms, both_terms, start, 1)
        return (grad_query, key_terms)

    term_start = jnp.zeros((row_count, frame_count, 2 * model_width), jnp.float32)
    return lax.fori_loop(
        0, block_count, back_step, (jnp.zeros(query_heads.shape, jnp.float32), term_start)
    )


def local(
    features,
    cotangent,
    segments,
    stem_weight,
    projection_weight,
    mixing_weight,
    feedforward_weight,
    norm_gains,
    biases,
    stem_moment,
    projection_moment,
    mixing_moment,
    feedforward_moment,
    gain_moment,
    bias_moment,
    stem_average,
    projection_average,
    mixing_average,
    feedforward_average,
    gain_average,
    bias_average,
):
    row_count, tok_count, model_width = features.shape
    head_count = HEADS
    head_width = model_width // head_count
    group_count = GROUPS
    group_width = model_width // group_count
    tap_count = KERNEL
    half_taps = tap_count // 2
    layer_count = projection_weight.shape[0]
    ff_rows = feedforward_weight.shape[3] // model_width
    score_scale = 1.0 / math.sqrt(head_width)
    seq_index = lax.axis_index("seq")
    query_segments = lax.dynamic_slice_in_dim(segments, seq_index * tok_count, tok_count, 1)
    kernel_taps = stem_weight.reshape(tap_count, group_width, model_width)
    extended = extended_2(features, (("seq", 1),), half_taps)
    conv_input = extended[:, : tok_count + tap_count - 1]
    conv_pre = group_conv(conv_input, kernel_taps, group_count) + biases[0]
    summed = features.astype(jnp.float32) + gelu_exact(conv_pre)
    hidden, normed_stem, inverse_stem = layer_norm(summed, norm_gains[0], biases[1])
    saved_layers = []
    for layer_index in range(layer_count):
        bias_base = 2 + layer_index * (6 + ff_rows)
        hidden_low = hidden.astype(jnp.bfloat16)
        projected = jnp.einsum(
            "rtd,de->rte",
            hidden_low,
            projection_weight[layer_index],
            preferred_element_type=jnp.float32,
        )
        queries = ((projected[..., :model_width] + biases[bias_base]) * score_scale).astype(
            jnp.bfloat16
        )
        keys_low = projected[..., model_width : 2 * model_width].astype(jnp.bfloat16)
        values_low = (projected[..., 2 * model_width :] + biases[bias_base + 1]).astype(
            jnp.bfloat16
        )
        kv_local = jnp.concatenate([keys_low, values_low], axis=-1)
        kv_whole = lax.all_gather(kv_local, "seq", axis=1, tiled=True)
        query_heads = queries.reshape(row_count, tok_count, head_count, head_width)
        coarse, fine, log_sum = attend(query_heads, kv_whole, query_segments, segments, head_count)
        mixed_low = coarse.reshape(row_count, tok_count, model_width).astype(jnp.bfloat16)
        branch = (
            jnp.einsum(
                "rte,ed->rtd",
                mixed_low,
                mixing_weight[layer_index],
                preferred_element_type=jnp.float32,
            )
            + biases[bias_base + 2]
        )
        first_norm, normed_one, inverse_one = layer_norm(
            hidden + branch, norm_gains[1 + 2 * layer_index], biases[bias_base + 3]
        )
        first_low = first_norm.astype(jnp.bfloat16)
        up_bias = biases[bias_base + 6 : bias_base + 6 + ff_rows].reshape(-1)
        up_pre = (
            jnp.einsum(
                "rtd,dj->rtj",
                first_low,
                feedforward_weight[layer_index, :, 0, :],
                preferred_element_type=jnp.float32,
            )
            + up_bias
        )
        up_low = gelu_exact(up_pre).astype(jnp.bfloat16)
        down_out = (
            jnp.einsum(
                "rtj,dj->rtd",
                up_low,
                feedforward_weight[layer_index, :, 1, :],
                preferred_element_type=jnp.float32,
            )
            + biases[bias_base + 4]
        )
        hidden_next, normed_two, inverse_two = layer_norm(
            first_norm + down_out, norm_gains[2 + 2 * layer_index], biases[bias_base + 5]
        )
        saved_layers.append(
            (
                hidden_low,
                query_heads,
                kv_whole,
                log_sum,
                fine,
                mixed_low,
                normed_one,
                inverse_one,
                first_low,
                up_pre,
                up_low,
                normed_two,
                inverse_two,
            )
        )
        hidden = hidden_next
    upstream = cotangent.astype(jnp.float32)
    gain_grads = [None] * norm_gains.shape[0]
    bias_grads = [None] * biases.shape[0]
    projection_grads = [None] * layer_count
    mixing_grads = [None] * layer_count
    feedforward_grads = [None] * layer_count
    for layer_index in reversed(range(layer_count)):
        (
            hidden_low,
            query_heads,
            kv_whole,
            log_sum,
            fine,
            mixed_low,
            normed_one,
            inverse_one,
            first_low,
            up_pre,
            up_low,
            normed_two,
            inverse_two,
        ) = saved_layers[layer_index]
        bias_base = 2 + layer_index * (6 + ff_rows)
        in_matrix = projection_weight[layer_index]
        mix_matrix = mixing_weight[layer_index]
        up_matrix = feedforward_weight[layer_index, :, 0, :]
        down_matrix = feedforward_weight[layer_index, :, 1, :]
        grad_second, gain_grads[2 + 2 * layer_index], bias_grads[bias_base + 5] = layer_norm_back(
            upstream, normed_two, inverse_two, norm_gains[2 + 2 * layer_index]
        )
        bias_grads[bias_base + 4] = jnp.sum(grad_second, axis=(0, 1))
        down_low = grad_second.astype(jnp.bfloat16)
        grad_down = jnp.einsum("rtd,rtj->dj", down_low, up_low, preferred_element_type=jnp.float32)
        grad_act = jnp.einsum(
            "rtd,dj->rtj", down_low, down_matrix, preferred_element_type=jnp.float32
        )
        grad_up_pre = gelu_back(up_pre, grad_act)
        up_bias_grad = jnp.sum(grad_up_pre, axis=(0, 1)).reshape(ff_rows, model_width)
        for offset in range(ff_rows):
            bias_grads[bias_base + 6 + offset] = up_bias_grad[offset]
        up_grad_low = grad_up_pre.astype(jnp.bfloat16)
        grad_up = jnp.einsum(
            "rtd,rtj->dj", first_low, up_grad_low, preferred_element_type=jnp.float32
        )
        grad_first = grad_second + jnp.einsum(
            "rtj,dj->rtd", up_grad_low, up_matrix, preferred_element_type=jnp.float32
        )
        feedforward_grads[layer_index] = jnp.stack([grad_up, grad_down], axis=1)
        grad_resid, gain_grads[1 + 2 * layer_index], bias_grads[bias_base + 3] = layer_norm_back(
            grad_first, normed_one, inverse_one, norm_gains[1 + 2 * layer_index]
        )
        bias_grads[bias_base + 2] = jnp.sum(grad_resid, axis=(0, 1))
        branch_low = grad_resid.astype(jnp.bfloat16)
        mixing_grads[layer_index] = jnp.einsum(
            "rte,rtd->ed", mixed_low, branch_low, preferred_element_type=jnp.float32
        )
        grad_mixed = jnp.einsum(
            "rtd,ed->rte", branch_low, mix_matrix, preferred_element_type=jnp.float32
        )
        mixed_grad_low = grad_mixed.astype(jnp.bfloat16).reshape(
            row_count, tok_count, head_count, head_width
        )
        delta = jnp.transpose(
            jnp.sum(mixed_grad_low.astype(jnp.float32) * fine, axis=-1), (0, 2, 1)
        )
        grad_query, key_terms = attend_back(
            query_heads,
            mixed_grad_low,
            kv_whole,
            query_segments,
            segments,
            log_sum,
            delta,
            head_count,
        )
        grad_kv = lax.psum_scatter(key_terms, "seq", scatter_dimension=1, tiled=True)
        query_grad_low = grad_query.reshape(row_count, tok_count, model_width).astype(jnp.bfloat16)
        key_grad_low = grad_kv[..., :model_width].astype(jnp.bfloat16)
        value_grad_low = grad_kv[..., model_width:].astype(jnp.bfloat16)
        bias_grads[bias_base] = (
            jnp.sum(query_grad_low.astype(jnp.float32), axis=(0, 1)) * score_scale
        )
        bias_grads[bias_base + 1] = jnp.sum(value_grad_low.astype(jnp.float32), axis=(0, 1))
        grad_projected = jnp.concatenate(
            [query_grad_low * score_scale, key_grad_low, value_grad_low], axis=-1
        )
        projection_grads[layer_index] = jnp.einsum(
            "rtd,rte->de", hidden_low, grad_projected, preferred_element_type=jnp.float32
        )
        upstream = grad_resid + jnp.einsum(
            "rte,de->rtd", grad_projected, in_matrix, preferred_element_type=jnp.float32
        )
    grad_summed, gain_grads[0], bias_grads[1] = layer_norm_back(
        upstream, normed_stem, inverse_stem, norm_gains[0]
    )
    grad_conv = gelu_back(conv_pre, grad_summed)
    bias_grads[0] = jnp.sum(grad_conv, axis=(0, 1))
    conv_grad_low = grad_conv.astype(jnp.bfloat16)
    grad_extended = extended_2(conv_grad_low, (("seq", 1),), half_taps)
    features_gradient = grad_summed + group_conv(
        grad_extended[:, 1:], flipped_taps(kernel_taps, group_count), group_count
    )
    seq_count = lax.axis_size("seq")
    share_width = model_width // seq_count
    layer_partials = (
        jnp.stack(projection_grads),
        jnp.stack(mixing_grads),
        jnp.stack(feedforward_grads),
        jnp.stack(gain_grads),
        jnp.stack(bias_grads),
    )
    grad_stem = group_conv_kernel_grad(conv_input, conv_grad_low, group_count).reshape(
        tap_count * group_width, model_width
    )
    shares = (
        lax.psum_scatter(grad_stem, "seq", scatter_dimension=1, tiled=True),
        lax.psum_scatter(layer_partials[0], "seq", scatter_dimension=1, tiled=True),
        lax.psum_scatter(layer_partials[1], "seq", scatter_dimension=1, tiled=True),
        lax.psum_scatter(layer_partials[2], "seq", scatter_dimension=1, tiled=True),
        lax.psum_scatter(layer_partials[3], "seq", scatter_dimension=1, tiled=True),
        lax.psum_scatter(layer_partials[4], "seq", scatter_dimension=1, tiled=True),
    )
    matrix_totals = (
        lax.psum_scatter(
            shares[0].astype(jnp.bfloat16), "row", scatter_dimension=0, tiled=True
        ).astype(jnp.float32),
        lax.psum_scatter(
            shares[1].astype(jnp.bfloat16), "row", scatter_dimension=2, tiled=True
        ).astype(jnp.float32),
        lax.psum_scatter(
            shares[2].astype(jnp.bfloat16), "row", scatter_dimension=2, tiled=True
        ).astype(jnp.float32),
        lax.psum_scatter(
            shares[3].astype(jnp.bfloat16), "row", scatter_dimension=3, tiled=True
        ).astype(jnp.float32),
    )
    small_totals = lax.psum((shares[4], shares[5]), "row")
    totals = (
        matrix_totals[0],
        matrix_totals[1],
        matrix_totals[2],
        matrix_totals[3],
        small_totals[0],
        small_totals[1],
    )
    share_start = seq_index * share_width
    row_index = lax.axis_index("row")
    row_total = lax.axis_size("row")
    rate_base = 1.0 / math.sqrt(row_count * row_total * tok_count * seq_count)
    old_params = (
        stem_weight,
        projection_weight,
        mixing_weight,
        feedforward_weight,
        norm_gains,
        biases,
    )
    old_moments = (
        stem_moment,
        projection_moment,
        mixing_moment,
        feedforward_moment,
        gain_moment,
        bias_moment,
    )
    old_averages = (
        stem_average,
        projection_average,
        mixing_average,
        feedforward_average,
        gain_average,
        bias_average,
    )
    momenta = []
    averaged = []
    updated = []
    for param_index in range(6):
        old_share = lax.dynamic_slice_in_dim(old_params[param_index], share_start, share_width, 1)
        if param_index < 4:
            split_dim = row_dims[param_index]
            piece_size = old_share.shape[split_dim] // row_total
            old_share = lax.dynamic_slice_in_dim(
                old_share, row_index * piece_size, piece_size, split_dim
            )
        old_share = old_share.astype(jnp.float32)
        moment_new = momentum_decay * old_moments[param_index] + totals[param_index]
        weight_new = old_share - rate_factors[param_index] * rate_base * (
            totals[param_index] + momentum_decay * moment_new
        )
        momenta.append(moment_new)
        updated.append(weight_new)
        averaged.append(
            average_decay * old_averages[param_index] + (1.0 - average_decay) * weight_new
        )
    return (
        hidden,
        features_gradient,
        momenta[0],
        momenta[1],
        momenta[2],
        momenta[3],
        momenta[4],
        momenta[5],
        averaged[0],
        averaged[1],
        averaged[2],
        averaged[3],
        averaged[4],
        averaged[5],
        updated[0],
        updated[1],
        updated[2],
        updated[3],
        updated[4],
        updated[5],
    )


LANES = 128
PAIRS = 2
VMEM_BYTES = 16 * 1024 * 1024
WIDE_BYTES = 24 * 1024 * 1024
FAR_BYTES = 56 * 1024 * 1024
bf16 = jnp.bfloat16
f32 = jnp.float32


def whole_call(kernel, outs, operands, scalars=0, scratch=(), after=(), far=(), token=False, vmem=VMEM_BYTES):
    given, waits, made = len(operands), len(after), len(outs)

    def body(*refs):
        kernel(*refs[:given], *refs[given + waits : given + waits + made], *refs[given + waits + made + token :])

    in_specs = [
        pl.BlockSpec(memory_space=pltpu.SMEM if i < scalars else pl.ANY if i in far else pltpu.VMEM)
        for i in range(given)
    ] + [pl.BlockSpec(memory_space=pl.ANY)] * waits
    out_specs = [pl.BlockSpec(memory_space=pltpu.VMEM)] * made + [pl.BlockSpec(memory_space=pl.ANY)] * token
    return pl.pallas_call(
        body,
        out_shape=[*outs, *[jax.ShapeDtypeStruct((8, LANES), jnp.float32)] * token],
        in_specs=in_specs,
        out_specs=out_specs,
        scratch_shapes=list(scratch),
        compiler_params=pltpu.CompilerParams(vmem_limit_bytes=vmem),
        cost_estimate=pl.CostEstimate(flops=1, bytes_accessed=1, transcendentals=0),
    )(*operands, *after)


def sds(shape, dtype):
    return jax.ShapeDtypeStruct(shape, dtype)


def dot_nn(a, b):
    return lax.dot_general(a, b, (((1,), (0,)), ((), ())), preferred_element_type=f32)


def dot_nt(a, b):
    return lax.dot_general(a, b, (((1,), (1,)), ((), ())), preferred_element_type=f32)


def dot_tn(a, b):
    return lax.dot_general(a, b, (((0,), (0,)), ((), ())), preferred_element_type=f32)


def gelu_and_slope(v):
    cdf = 0.5 * (1.0 + lax.erf(v * math.sqrt(0.5)))
    return v * cdf, cdf + v * jnp.exp(-0.5 * v * v) * (1.0 / math.sqrt(2.0 * math.pi))


def lane_of(shape):
    return lax.broadcasted_iota(jnp.int32, shape, len(shape) - 1)


def piece_of(cols, j, width):
    off, v = (width * j) % LANES, (width * j) // LANES
    lane = lane_of(cols[0].shape)
    if off == 0:
        t = cols[v]
    else:
        t = pltpu.roll(cols[v], LANES - off, 1)
        if off + width > LANES:
            t = jnp.where(lane < LANES - off, t, pltpu.roll(cols[v + 1], LANES - off, 1))
    return jnp.where(lane < width, t, 0.0)


def tiles_of(pieces, width):
    count = len(pieces) * width // LANES
    cols = [None] * count

    def put(v, t):
        cols[v] = t if cols[v] is None else cols[v] + t

    for j, piece in enumerate(pieces):
        off, v = (width * j) % LANES, (width * j) // LANES
        if off == 0:
            put(v, piece)
            continue
        rolled = pltpu.roll(piece, off, 1)
        if off + width > LANES:
            lane = lane_of(piece.shape)
            put(v, jnp.where(lane >= off, rolled, 0.0))
            put(v + 1, jnp.where(lane < off, rolled, 0.0))
        else:
            put(v, rolled)
    return cols


def split_kernel(blocks, width, x_ref, o_ref):
    rows = x_ref.shape[0]
    for r in range(rows):
        x = x_ref[r].astype(f32)
        cols = [x[:, LANES * v : LANES * (v + 1)] for v in range(x.shape[1] // LANES)]
        for j in range(blocks):
            o_ref[j, r] = piece_of(cols, j, width).astype(bf16)


def fill_taps(taps, gw, w_ref, o_ref):
    zero = jnp.zeros((LANES, LANES), bf16)
    o_ref[0] = zero
    o_ref[taps + 1] = zero
    o_ref[taps + 2] = zero

    def body(k, carry):
        w = w_ref[pl.ds(pl.multiple_of(k * gw, 16), gw), :]
        lane = lane_of(w.shape)
        o_ref[k + 1, 0:gw, :] = jnp.where(lane < gw, w, jnp.zeros_like(w))
        o_ref[k + 1, gw : 2 * gw, :] = jnp.where(lane >= gw, w, jnp.zeros_like(w))
        o_ref[k + 1, 2 * gw :, :] = jnp.zeros((LANES - 2 * gw, LANES), bf16)
        return carry

    lax.fori_loop(0, taps, body, 0)


def phases_from_frames(x_ref, xf, ph, rows, frames, half):
    blocks, block = x_ref.shape[0], x_ref.shape[2]
    span = frames + 2 * half
    for r in range(rows):
        xf[r * span : r * span + half, :] = jnp.zeros((half, LANES), f32)
        xf[r * span + half + frames : (r + 1) * span, :] = jnp.zeros((half, LANES), f32)
        for s in range(blocks):
            at = r * span + half + s * block
            xf[at : at + block, :] = x_ref[s, r].astype(f32)
    n = span // 2 - 16

    def body(p, carry):
        for r in range(rows):
            for b in range(2):
                ph[p, r, 0:n, b * LANES : (b + 1) * LANES] = xf[
                    pl.ds(r * span + 2 * p + b, n, stride=2), :
                ].astype(bf16)
        return carry

    lax.fori_loop(0, 16, body, 0)
    for r in range(rows):
        for b in range(2):
            ph[0, r, n:, b * LANES : (b + 1) * LANES] = xf[pl.ds(r * span + 2 * n + b, 16, stride=2), :].astype(bf16)


def window(ph, m, rows, n):
    p, a = lax.rem(m, 16), m // 16
    part = ph[p, :, pl.ds(pl.multiple_of(a * 16, 16), n), :]
    return part.reshape(rows * n, part.shape[-1])


def phases_kernel(rows, frames, half, gw, x_ref, share_ref, ph_ref, w_ref, xf):
    phases_from_frames(x_ref, xf, ph_ref, rows, frames, half)
    fill_taps(2 * half, gw, share_ref, w_ref)


def conv_kernel(rows, frames, half, gw, c_ref, x_ref, share_ref, b_ref, pre_ref, keep_ref, send_ref, ph_ref, xf, acc, w_ref):
    n = frames // 2
    fill_taps(2 * half, gw, share_ref, w_ref)
    phases_from_frames(x_ref, xf, ph_ref, rows, frames, half)
    acc[...] = jnp.zeros_like(acc)

    def body(i, carry):
        left, right = [], []
        for t in range(5):
            m = i * 5 + t
            here, before, after = w_ref[2 * m + 1], w_ref[2 * m], w_ref[2 * m + 2]
            right += [jnp.concatenate([here, before], 1), jnp.concatenate([after, here], 1)]
            left.append(window(ph_ref, m, rows, n))
        acc[...] += dot_nn(jnp.concatenate(left, 1), jnp.concatenate(right, 0))
        return carry

    lax.fori_loop(0, (half + 1) // 5, body, 0)
    bias = jnp.concatenate([b_ref[...], b_ref[...]], 1)
    c = c_ref[1]
    for r in range(rows):
        pre = acc[r * n : (r + 1) * n, :] + bias
        pre_ref[r] = pre
        x = ph_ref[0, r, half // 2 : half // 2 + n, :].astype(f32)
        s = (x + gelu_and_slope(pre)[0]).astype(bf16)
        for zf in range(4):
            for xq in range(2):
                for cf in range(2):
                    u = ((zf * 2 + xq) * 2 + cf) * 16
                    blk = s[u : u + 16, :]

                    @pl.when(c == cf)
                    def _(blk=blk, r=r, xq=xq, zf=zf):
                        keep_ref[r, xq, zf * 16 : zf * 16 + 16, :] = blk

                    @pl.when(c != cf)
                    def _(blk=blk, r=r, xq=xq, zf=zf):
                        send_ref[r, xq, zf * 16 : zf * 16 + 16, :] = blk


def normed(values):
    centre = jnp.mean(values, axis=-1, keepdims=True)
    centred = values - centre
    spread = jnp.mean(centred * centred, axis=-1, keepdims=True)
    inverse = lax.rsqrt(spread + epsilon)
    return centred * inverse, inverse


def stem_norm_kernel(width, r_ref, g_ref, b_ref, h_ref, low_ref, n_ref, i_ref):
    halves = []
    for a in range(2):
        pieces = [r_ref[j, :, a * LANES : (a + 1) * LANES].astype(f32) for j in range(r_ref.shape[0])]
        halves.append(jnp.concatenate(tiles_of(pieces, width), axis=1))
    s = jnp.concatenate(halves, axis=0)
    n, inv = normed(s)
    h = n * g_ref[0:1, :] + b_ref[1:2, :]
    h_ref[...] = h
    low_ref[...] = h.astype(bf16)
    n_ref[...] = n
    i_ref[...] = inv


def cotangent_split_kernel(place, x_ref, keep_ref, send_ref, mixed):
    c = place[1]
    rows, toks, width = x_ref.shape
    for r in range(rows):
        for v in range(width // LANES):
            mixed[v * toks : (v + 1) * toks, :] = x_ref[r, :, v * LANES : (v + 1) * LANES].astype(f32)
        for cf in range(2):
            for a in range(2):
                parts = [mixed[pl.ds(v * toks + cf * 32 + a, 16, stride=2), :] for v in range(width // LANES)]
                blk = jnp.concatenate(parts, axis=1).astype(bf16)

                @pl.when(c == cf)
                def _(blk=blk, r=r, a=a):
                    keep_ref[r, a * 16 : a * 16 + 16, :] = blk

                @pl.when(c != cf)
                def _(blk=blk, r=r, a=a):
                    send_ref[r, a * 16 : a * 16 + 16, :] = blk


def cotangent_route_kernel(place, keep_ref, recv_ref, *outs):
    c, z = place[1], place[2]
    for rel, out in enumerate(outs):
        to = z ^ rel
        mine = (to // 2) == c

        @pl.when(mine)
        def _(out=out, to=to):
            out[...] = keep_ref[to % 2]

        @pl.when(jnp.logical_not(mine))
        def _(out=out, to=to):
            out[...] = recv_ref[to % 2]


def cotangent_join_kernel(place, r0, r1, r2, r3, o_ref):
    z = place[2]
    for rel, src in enumerate((r0, r1, r2, r3)):
        for a in range(2):
            at = pl.multiple_of(a * 64 + (z ^ rel) * 16, 16)
            o_ref[pl.ds(at, 16), :] = src[a * 16 : a * 16 + 16, :]


def segments_kernel(place, own_ref, other_ref, row_ref, col_ref):
    c, z, x = place[1], place[2], place[3]
    frames = own_ref.shape[1]
    mine = (z // 2) == c
    odd = (z % 2) == 1
    own = jnp.where(odd, own_ref[1:2, :], own_ref[0:1, :])
    other = jnp.where(odd, other_ref[1:2, :], other_ref[0:1, :])
    ids = jnp.broadcast_to(jnp.where(mine, own, other).astype(f32), (LANES, frames)).astype(bf16)
    f = lax.broadcasted_iota(jnp.int32, (frames, frames), 0)
    p = lax.broadcasted_iota(jnp.int32, (frames, frames), 1)
    source = (
        ((p >> 4) & 3) * 128 + (x ^ (p >> 8)) * 64 + (c ^ ((p >> 7) & 1)) * 32 + (p & 15) * 2 + ((p >> 6) & 1)
    )
    chosen = jnp.where(f == source, 1.0, 0.0).astype(bf16)
    row_ref[...] = dot_nn(ids, chosen)[0:1, :]
    col_ref[...] = dot_tn(chosen, ids.T)[:, 0:1]


def slots_kernel(place, keep_ref, recv_ref, o_ref):
    c = place[1]
    for r in range(2):
        for q in range(2):
            o_ref[((c * 2) + r) * 2 + q] = keep_ref[r, q]
            o_ref[(((1 - c) * 2) + r) * 2 + q] = recv_ref[r, q]


def fetched(copies):
    for copy in copies:
        copy.start()
    return copies


def feed_copies(l, place, w_ref, buf, sems, width):
    steps = w_ref.shape[1] // LANES
    copies = []
    for i in range(2):
        at = pl.multiple_of((2 * (place[0] ^ i) + place[1]) * width, LANES)
        for k in range(steps):
            copies.append(
                pltpu.make_async_copy(
                    w_ref.at[l, pl.ds(k * LANES, LANES), :, pl.ds(at, width)],
                    buf.at[i, pl.ds(k * LANES, LANES)],
                    sems.at[i * steps + k],
                )
            )
    return fetched(copies)


def feed_parted(copies, buf, outs):
    depth, width = buf.shape[1], buf.shape[3]
    steps = depth // LANES
    parting = parting_matrix(2 * LANES)
    for i in range(2):
        for k in range(steps):
            copies[i * steps + k].wait()
        flat = buf.at[i].reshape(2 * depth, width)

        def body(k, carry, i=i, flat=flat):
            g = dot_nn(parting, flat[pl.ds(pl.multiple_of(2 * LANES * k, 2 * LANES), 2 * LANES), :]).astype(bf16)
            at = pl.ds(pl.multiple_of(LANES * k, LANES), LANES)
            outs[i][at, :] = g[:LANES]
            outs[2 + i][at, :] = g[LANES:]
            return carry

        lax.fori_loop(0, steps, body, 0)


def feed_weights_kernel(l, place, w_ref, *refs):
    outs, (buf, sems) = refs[:4], refs[4:]
    feed_parted(feed_copies(l, place, w_ref, buf, sems, outs[0].shape[1]), buf, outs)


def parting_matrix(size):
    r = lax.broadcasted_iota(jnp.int32, (size, size), 0)
    c = lax.broadcasted_iota(jnp.int32, (size, size), 1)
    return jnp.where(c == jnp.where(r < size // 2, 2 * r, 2 * r - size + 1), 1.0, 0.0).astype(bf16)


def later_weights_kernel(layers, bases, share, place, w_ref, p_ref, m_ref, b_ref, *refs):
    feeds = 4 * (layers - 1)
    feed_outs, outs = refs[:feeds], refs[feeds : feeds + 3 * layers]
    buf, wide, feed_sems, sems = refs[feeds + 3 * layers :]
    c, x = place[1], place[3]
    group = 2 * x + c
    width = m_ref.shape[2]
    start = ((group * share) // LANES) * LANES
    copies = []
    row = pl.multiple_of(group * share, 64)
    for l in range(layers):
        for i in range(3):
            at = pl.multiple_of(i * width + start, LANES)
            copies.append(pltpu.make_async_copy(p_ref.at[l, :, pl.ds(at, 256)], wide.at[l, i], sems.at[4 * l + i]))
        mix_ref = outs[3 * l + 1]
        copies.append(
            pltpu.make_async_copy(m_ref.at[l, pl.ds(row, share), :], mix_ref.at[pl.ds(0, share), :], sems.at[4 * l + 3])
        )
    fetched(copies)
    feed_in = [feed_copies(l, place, w_ref, buf.at[l - 1], feed_sems.at[l - 1], width) for l in range(1, layers)]
    odd = (group % 2) == 1

    def settle(v):
        lane = lane_of(v.shape)
        return jnp.where(lane < share, jnp.where(odd, pltpu.roll(v, 256 - 64, 1), v), 0.0)

    for l in range(layers):
        in_ref, mix_ref, both_ref = outs[3 * l : 3 * l + 3]
        mix_ref[share:, :] = jnp.zeros((256 - share, width), bf16)
        both_ref[...] = settle(b_ref[bases[l] : bases[l] + 2, pl.ds(pl.multiple_of(start, LANES), 256)])
        for i in range(3):
            copies[4 * l + i].wait()
            in_ref[:, i * 256 : (i + 1) * 256] = settle(wide[l, i].astype(f32)).astype(bf16)
        copies[4 * l + 3].wait()
    for l in range(1, layers):
        feed_parted(feed_in[l - 1], buf.at[l - 1], feed_outs[4 * (l - 1) : 4 * l])


def attend_kernel(base, hl0, hl1, hl2, hl3, w_ref, m_ref, bq_ref, segr, segc,
                  q_ref, k_ref, v_ref, at_ref, lse_ref, keep_ref, send_ref):
    t = hl0.shape[0]
    hl = jnp.concatenate([hl0[...], hl1[...], hl2[...], hl3[...]], axis=0)
    proj = dot_nn(hl, w_ref[...])
    q = ((proj[:, 0:256] + bq_ref[0:1, :]) * 0.125).astype(bf16)
    k = proj[:, 256:512].astype(bf16)
    v = (proj[:, 512:768] + bq_ref[1:2, :]).astype(bf16)
    q_ref[...] = q
    k_ref[...] = k
    v_ref[...] = v
    allowed = segc[...] == segr[...]
    lane = lane_of((1, LANES))
    parts = []
    for head in range(3):
        tile = head // 2
        cols = slice(tile * LANES, (tile + 1) * LANES)
        mine = (lane < 64) if head % 2 == 0 else (lane >= 64)
        qh = jnp.where(mine, q[:, cols], jnp.zeros((), bf16))
        s = dot_nt(qh, k[:, cols])
        s = jnp.where(allowed, s, masked_score)
        top = jnp.max(s, axis=-1, keepdims=True)
        e = jnp.exp(s - top)
        total = jnp.sum(e, axis=-1, keepdims=True)
        lse_ref[head] = top + jnp.log(total)
        p = (e * (1.0 / total)).astype(bf16)
        parts.append(dot_nn(p, v[:, cols]))
    att = jnp.concatenate([jnp.where(lane < 64, parts[0], parts[1]), parts[2]], axis=1).astype(bf16)
    at_ref[...] = att
    branch = dot_nn(att, m_ref[...]).astype(bf16)
    for dx in range(2):
        keep_ref[dx] = branch[2 * dx * t : (2 * dx + 1) * t]
        send_ref[dx] = branch[(2 * dx + 1) * t : (2 * dx + 2) * t]


def half_sum_kernel(a_ref, b_ref, own_ref, send_ref):
    own_ref[...] = a_ref[0].astype(f32) + b_ref[0].astype(f32)
    send_ref[...] = (a_ref[1].astype(f32) + b_ref[1].astype(f32)).astype(bf16)


def norm_kernel(gain_row, bias_row, shift_row, h_ref, a_ref, r_ref, g_ref, b_ref, o_ref, low_ref, n_ref, i_ref):
    v = h_ref[...] + (a_ref[...].astype(f32) + r_ref[...].astype(f32) + b_ref[bias_row : bias_row + 1, :])
    n, inv = normed(v)
    o = n * g_ref[gain_row : gain_row + 1, :] + b_ref[shift_row : shift_row + 1, :]
    o_ref[...] = o
    low_ref[...] = o.astype(bf16)
    n_ref[...] = n
    i_ref[...] = inv


def feed_kernel(row, place, f0, f1, u0, u1, d0, d1, b_ref, act_ref, slope_ref, own_ref, send_ref):
    t = f0.shape[0]
    first = jnp.concatenate([f0[...], f1[...]], axis=0)
    total = None
    for i, (u, d) in enumerate(((u0, d0), (u1, d1))):
        up = dot_nn(first, u[...]) + b_ref[pl.ds(row + 2 * (place[0] ^ i) + place[1], 1), :]
        act, slope = gelu_and_slope(up)
        act = act.astype(bf16)
        act_ref[i] = act
        slope_ref[i] = slope.astype(bf16)
        part = dot_nt(act, d[...])
        total = part if total is None else total + part
    own_ref[...] = total[:t]
    send_ref[...] = total[t:].astype(bf16)


def norm_back(g, n, inv, gain):
    scaled = g * gain
    m1 = jnp.mean(scaled, axis=-1, keepdims=True)
    m2 = jnp.mean(scaled * n, axis=-1, keepdims=True)
    return inv * (scaled - m1 - n * m2)


def norm_sums(g, n, d, o_ref):
    o_ref[0:1, :] = jnp.sum(g * n, axis=0, keepdims=True)
    o_ref[1:2, :] = jnp.sum(g, axis=0, keepdims=True)
    o_ref[2:3, :] = jnp.sum(d, axis=0, keepdims=True)
    o_ref[3:8, :] = jnp.zeros((5, o_ref.shape[1]), f32)


def norm_back_kernel(gain_row, count, *refs):
    given, (g_ref, n_ref, i_ref, d_ref, low_ref, s_ref) = refs[:count], refs[count:]
    g = given[0][...].astype(f32)
    for r in given[1:]:
        g = g + r[...].astype(f32)
    n = n_ref[...]
    d = norm_back(g, n, i_ref[...], g_ref[gain_row : gain_row + 1, :])
    d_ref[...] = d
    low_ref[...] = d.astype(bf16)
    norm_sums(g, n, d, s_ref)


def stem_norm_back_kernel(width, count, place, *refs):
    given, (g_ref, n_ref, i_ref, keep_ref, send_ref, s_ref) = refs[:count], refs[count:]
    z, x = place[2], place[3]
    g = given[0][...].astype(f32)
    for r in given[1:]:
        g = g + r[...].astype(f32)
    n = n_ref[...]
    d = norm_back(g, n, i_ref[...], g_ref[0:1, :])
    norm_sums(g, n, d, s_ref)
    t = d.shape[0] // 2
    for a in range(2):
        part = d[a * t : (a + 1) * t]
        cols = [part[:, LANES * v : LANES * (v + 1)] for v in range(part.shape[1] // LANES)]
        for j in range(8):
            blk = piece_of(cols, j, width).astype(bf16)
            to_x(keep_ref, send_ref, x, j % 2, (j // 2) ^ z, (slice(None), slice(a * LANES, (a + 1) * LANES)), blk)


def to_x(keep_ref, send_ref, x, xi, rel, where, blk):
    @pl.when(x == xi)
    def _():
        keep_ref[(rel, *where)] = blk

    @pl.when(x != xi)
    def _():
        send_ref[(rel, *where)] = blk


def along_z_kernel(a_ref, b_ref, keep_ref, send_ref):
    for rel in range(4):
        out = send_ref if rel % 2 else keep_ref
        out[rel // 2, 0] = a_ref[rel]
        out[rel // 2, 1] = b_ref[rel]


def onward_kernel(keep_ref, recv_ref, send_ref):
    send_ref[0] = keep_ref[1]
    send_ref[1] = recv_ref[1]


def by_z(keep_ref, near_ref, far_ref):
    return keep_ref.at[0], near_ref.at[0], far_ref.at[0], far_ref.at[1]


def feed_back_kernel(e0, e1, u0, u1, d0, d1, slope_ref, dup_ref, own_ref, send_ref, bias_ref):
    t = e0.shape[0]
    d2 = jnp.concatenate([e0[...], e1[...]], axis=0)
    total = None
    for i, (u, d) in enumerate(((u0, d0), (u1, d1))):
        dup = dot_nn(d2, d[...]) * slope_ref[i].astype(f32)
        bias_ref[i : i + 1, :] = jnp.sum(dup, axis=0, keepdims=True)
        dup = dup.astype(bf16)
        dup_ref[i] = dup
        part = dot_nt(dup, u[...])
        total = part if total is None else total + part
    bias_ref[2:8, :] = jnp.zeros((6, bias_ref.shape[1]), f32)
    own_ref[...] = total[:t]
    send_ref[...] = total[t:].astype(bf16)


def feed_grad_kernel(place, f0, f1, e0, e1, dup_ref, act_ref, keep_ref, send_ref):
    z, x = place[2], place[3]
    width = keep_ref.shape[-2] // 2
    for kind, (a, b, right) in enumerate(((f0, f1, dup_ref), (e0, e1, act_ref))):
        left = jnp.concatenate([a[...], b[...]], axis=0)
        for i in range(2):
            g = dot_tn(left, right[i]).astype(bf16)
            for j in range(8):
                zi, xi = j // 2, j % 2
                rz, rx = zi ^ z, xi ^ x
                blk = g[j * width : (j + 1) * width]
                (send_ref if i else keep_ref)[rx, rz % 2, rz // 2, kind * width : (kind + 1) * width] = blk


def halves_kernel(count, *refs):
    given, made = refs[: 2 * count], refs[2 * count :]
    for i in range(count):
        a, b = given[2 * i], given[2 * i + 1]
        for h in range(2):
            out = made[2 * i + h]
            lead = out.shape[:-2]
            many = math.prod(lead)
            if many == 1:
                out[...] = (a[h].astype(f32) + b[h].astype(f32)).astype(out.dtype)
                continue

            def body(k, carry, a=a, b=b, h=h, out=out, lead=lead):
                at = []
                for size in reversed(lead):
                    at.insert(0, lax.rem(k, size))
                    k = k // size
                at = tuple(at)
                out[at] = (a[(h, *at)].astype(f32) + b[(h, *at)].astype(f32)).astype(out.dtype)
                return carry

            lax.fori_loop(0, many, body, 0)


def one_kernel(a, b, o):
    o[...] = (a[...].astype(f32) + b[...].astype(f32)).astype(o.dtype)


def attend_back_kernel(e0, e1, e2, e3, q_ref, k_ref, v_ref, lse_ref, w_ref, m_ref, segr, segc,
                       dc_ref, keep_ref, send_ref, bias_ref, da_ref, dq_ref, dk_ref, dv_ref):
    t = e0.shape[0]
    d1 = jnp.concatenate([e0[...], e1[...], e2[...], e3[...]], axis=0)
    da_ref[...] = dot_nt(d1, m_ref[...]).astype(bf16)
    lane = lane_of((1, LANES))
    for ref in (dq_ref, dk_ref, dv_ref):
        ref[...] = jnp.zeros_like(ref)

    def one_head(head, carry):
        cols = pl.ds(pl.multiple_of((head // 2) * LANES, LANES), LANES)
        mine = (lane // 64) == lax.rem(head, 2)
        zero = jnp.zeros((), bf16)
        qh = jnp.where(mine, q_ref[:, cols], zero)
        dah = jnp.where(mine, da_ref[:, cols], zero)
        k = k_ref[:, cols]
        s = dot_nt(qh, k)
        p = jnp.where(segc[...] == segr[...], jnp.exp(s - lse_ref[head]), 0.0)
        dp = dot_nt(dah, v_ref[:, cols])
        delta = jnp.sum(p * dp, axis=-1, keepdims=True)
        ds = (p * (dp - delta)).astype(bf16)
        dq_ref[:, cols] += dot_nn(ds, jnp.where(mine, k, zero))
        dk_ref[:, cols] += dot_tn(ds, qh)
        dv_ref[:, cols] += dot_tn(p.astype(bf16), dah)
        return carry

    lax.fori_loop(0, 3, one_head, 0)
    tiles = [slice(0, LANES), slice(LANES, 2 * LANES)]
    dq = [dq_ref[:, c].astype(bf16).astype(f32) * 0.125 for c in tiles]
    dk = [dk_ref[:, c].astype(bf16).astype(f32) for c in tiles]
    dv = [dv_ref[:, c].astype(bf16).astype(f32) for c in tiles]
    wide = jnp.concatenate(dq + dk + dv, axis=1).astype(bf16)
    bias_ref[0:1, :] = jnp.concatenate([jnp.sum(d, axis=0, keepdims=True) for d in dq], axis=1)
    bias_ref[1:2, :] = jnp.concatenate([jnp.sum(d, axis=0, keepdims=True) for d in dv], axis=1)
    bias_ref[2:8, :] = jnp.zeros((6, 256), f32)
    dense = [dq[0], jnp.where(lane < 64, dq[1], pltpu.roll(dk[1], 64, 1)), dk[0], dv[0], dv[1]]
    dc_ref[...] = jnp.concatenate(dense, axis=1).astype(bf16)
    out = dot_nt(wide, w_ref[...]).astype(bf16)
    for dx in range(2):
        keep_ref[dx] = out[2 * dx * t : (2 * dx + 1) * t]
        send_ref[dx] = out[(2 * dx + 1) * t : (2 * dx + 2) * t]


def attend_grad_kernel(place, hl0, hl1, hl2, hl3, e0, e1, e2, e3, at_ref, dc_ref, keep_ref, send_ref):
    z, x = place[2], place[3]
    hl = jnp.concatenate([hl0[...], hl1[...], hl2[...], hl3[...]], axis=0)
    d1 = jnp.concatenate([e0[...], e1[...], e2[...], e3[...]], axis=0)
    width = keep_ref.shape[2]

    def put(zi, tile, blk):
        rel = zi ^ z

        @pl.when((zi ^ z) % 2 == 0)
        def _():
            keep_ref[rel // 2, tile] = blk

        @pl.when((zi ^ z) % 2 == 1)
        def _():
            send_ref[rel // 2, tile] = blk

    g = dot_tn(hl, dc_ref[...]).astype(bf16)
    for j in range(8):
        zi, xi = j // 2, j % 2
        for t in range(5):
            put(zi, (xi ^ x) * 5 + t, g[j * width : (j + 1) * width, t * LANES : (t + 1) * LANES])
    m = dot_tn(at_ref[...], d1)
    lane = lane_of((1, LANES))
    for xp in range(2):
        t = [m[xp * width : (xp + 1) * width, i * LANES : (i + 1) * LANES] for i in range(6)]
        first = [t[0], t[3], jnp.where(lane < 64, t[1], pltpu.roll(t[4], 64, 1))]
        second = [t[2], t[5], jnp.where(lane < 64, pltpu.roll(t[1], 64, 1), t[4])]
        for cp, tiles in enumerate((first, second)):
            for i, tile in enumerate(tiles):
                put(2 * xp + cp, 10 + i, tile.astype(bf16))


def pick_kernel(layers, place, *refs):
    own, came = refs[:layers], refs[layers]
    stay_ref, move_ref = refs[layers + 1 :]
    y, x = place[0], place[3]
    lane = lane_of((1, LANES))
    for l in range(layers):
        mine = [own[l][t].astype(f32) for t in range(5)]
        other = [came[l, t].astype(f32) for t in range(5)]

        def blocks(t):
            return [(t[0], t[1]), (t[2], pltpu.roll(t[1], 64, 1)), (t[3], t[4])]

        first = x == 0
        lowb, highb = blocks(mine), blocks(other)
        low_g = [tuple(jnp.where(first, a, b) for a, b in zip(m, o)) for m, o in zip(lowb, highb)]
        high_g = [tuple(jnp.where(first, b, a) for a, b in zip(m, o)) for m, o in zip(lowb, highb)]
        upper = [low_g[0], high_g[0], low_g[1]]
        lower = [high_g[1], low_g[2], high_g[2]]
        for i in range(3):
            for j in range(2):
                a, b = upper[i][j], lower[i][j]
                stay_ref[l, i, j] = jnp.where(y == 0, a, b).astype(bf16)
                move_ref[l, i, j] = jnp.where(y == 0, b, a).astype(bf16)
        m = [own[l][10 + t].astype(f32) for t in range(3)]
        stay_ref[l, 3, 0] = jnp.where(y == 0, m[0], m[1]).astype(bf16)
        move_ref[l, 3, 0] = jnp.where(y == 0, m[1], m[0]).astype(bf16)
        stay_ref[l, 3, 1] = m[2].astype(bf16)
        move_ref[l, 3, 1] = m[2].astype(bf16)


def settle_kernel(layers, place, a, b, part_ref, swap_ref, mix_ref):
    c = place[1]
    for l in range(layers):
        v = [[a[l, i, j].astype(f32) + b[l, i, j].astype(f32) for j in range(2)] for i in range(4)]
        for j in range(2):
            part_ref[l, 0, j] = jnp.where(c == 0, v[0][j], v[1][j]).astype(bf16)
            part_ref[l, 1, j] = jnp.where(c == 0, v[1][j], v[2][j]).astype(bf16)
            swap_ref[l, j] = jnp.where(c == 0, v[2][j], v[0][j]).astype(bf16)
            mix_ref[l, j] = v[3][j].astype(bf16)


def step_of(factor, g, m, a, w):
    moment = momentum_decay * m + g
    new = w.astype(f32) - factor * (g + momentum_decay * moment)
    return moment, average_decay * a + (1.0 - average_decay) * new, new


def tile_from(win, t, odd):
    cols = [win[:, i * LANES : (i + 1) * LANES].astype(f32) for i in (t, t + 1) if (i + 1) * LANES <= win.shape[1]]
    turned = [pltpu.roll(v, 64, 1) for v in cols]
    shifted = turned[0] if len(cols) == 1 else jnp.where(lane_of(cols[0].shape) < 64, turned[0], turned[1])
    return jnp.where(odd, shifted, cols[0])


def stepped(factor, l, at, t, m_ref, a_ref, w, outs):
    to = at + t.shape[1]
    for o, v in zip(outs, step_of(factor, t, m_ref[l, :, at:to], a_ref[l, :, at:to], w[:, : t.shape[1]])):
        o[l, :, at:to] = v
    return to


def window_copy(w_ref, win, sems, place, step, span):
    rows = win.shape[1]
    row = (2 * place[2] + place[3]) * rows
    start = (((2 * place[0] + place[1]) * step) // LANES) * LANES
    return fetched(
        [
            pltpu.make_async_copy(
                w_ref.at[l, pl.ds(pl.multiple_of(row, 32), rows), pl.ds(pl.multiple_of(start, LANES), span)],
                win.at[l],
                sems.at[l],
            )
            for l in range(win.shape[0])
        ]
    )


def olds_kernel(layers, gw, place, s_ref, p_ref, m_ref, f_ref, so, po, mo, fo, win_s, win_p, win_m, win_f, sems):
    y, c, z, x = (place[i] for i in range(4))
    seq_i, row_i = 2 * z + x, 2 * y + c
    rows, width = win_f.shape[1], win_f.shape[3]
    column = seq_i * 2 * gw
    start = jnp.minimum(column // LANES, 4) * LANES
    taps = win_s.shape[0]
    stem = pltpu.make_async_copy(
        s_ref.at[pl.ds(pl.multiple_of(row_i * taps, LANES), taps), pl.ds(pl.multiple_of(start, LANES), 256)],
        win_s, sems.at[0],
    )
    feeds = [
        pltpu.make_async_copy(
            f_ref.at[l, pl.ds(seq_i * rows, rows), :, pl.ds(pl.multiple_of(row_i * width, LANES), width)],
            win_f.at[l], sems.at[1 + l],
        )
        for l in range(layers)
    ]
    fetched([stem, *feeds])
    ins = window_copy(p_ref, win_p, sems.at[pl.ds(1 + layers, layers)], place, 576, 640)
    mixes = window_copy(m_ref, win_m, sems.at[pl.ds(1 + 2 * layers, layers)], place, 192, 256)
    r = lax.broadcasted_iota(jnp.int32, (LANES, 256), 0)
    k = lax.broadcasted_iota(jnp.int32, (LANES, 256), 1)
    chosen = jnp.where(k == r + (column - start), 1.0, 0.0).astype(bf16)
    parting = parting_matrix(2 * rows)
    odd = c == 1
    stem.wait()
    so[...] = dot_nt(chosen, win_s[...])[0 : 2 * gw].astype(bf16)
    for l in range(layers):
        feeds[l].wait()
        fo[l] = dot_nn(parting, win_f.at[l].reshape(2 * rows, width)[...]).astype(bf16)
        ins[l].wait()
        for t in range(5):
            po[l, :, t * LANES : (t + 1) * LANES] = tile_from(win_p[l], t, odd).astype(bf16)
        mixes[l].wait()
        for t in range(2):
            mo[l, :, t * LANES : (t + 1) * LANES] = tile_from(win_m[l], t, odd).astype(bf16)


def projection_step_kernel(factor, place, w_ref, part_ref, swap_ref, m_ref, a_ref, *outs):
    lane = lane_of((1, LANES))
    for l in range(m_ref.shape[0]):
        b0 = [part_ref[l, 0, j].astype(f32) for j in range(2)]
        b2 = [part_ref[l, 1, j].astype(f32) for j in range(2)]
        b1 = [pltpu.roll(swap_ref[l, j].astype(f32), 64, 1) for j in range(2)]
        tiles = [b0[0], jnp.where(lane < 64, b0[1], b1[0]), jnp.where(lane < 64, b1[0], b1[1]), b2[0], b2[1][:, :64]]
        at = 0
        for i, t in enumerate(tiles):
            at = stepped(factor, l, at, t, m_ref, a_ref, w_ref[l, :, i * LANES : (i + 1) * LANES], outs)


def mixing_step_kernel(factor, place, w_ref, mix_ref, m_ref, a_ref, *outs):
    y, c = place[0], place[1]
    lane = lane_of((1, LANES))
    for l in range(m_ref.shape[0]):
        full, half = mix_ref[l, 0].astype(f32), mix_ref[l, 1].astype(f32)
        turned = pltpu.roll(full, 64, 1)
        half = jnp.where(y == 0, half, pltpu.roll(half, 64, 1))
        tiles = [
            jnp.where(c == 0, full, jnp.where(lane < 64, half, turned)),
            jnp.where(c == 0, half, turned)[:, :64],
        ]
        at = 0
        for i, t in enumerate(tiles):
            at = stepped(factor, l, at, t, m_ref, a_ref, w_ref[l, :, i * LANES : (i + 1) * LANES], outs)


def feed_step_kernel(factor, place, w_ref, *refs):
    layers = w_ref.shape[0]
    parts, (m_ref, a_ref), outs = refs[: 2 * layers], refs[2 * layers : 2 * layers + 2], refs[2 * layers + 2 :]
    rows = m_ref.shape[1]
    for l in range(layers):
        for kind in range(2):
            a, b = parts[2 * l], parts[2 * l + 1]

            def body(k, carry, l=l, kind=kind, a=a, b=b):
                r = pl.ds(pl.multiple_of(k * 32, 32), 32)
                both = pl.ds(pl.multiple_of(kind * rows + k * 32, 32), 32)
                g = a[both, :].astype(f32) + b[both, :].astype(f32)
                w = w_ref[l, both, :]
                for o, v in zip(outs, step_of(factor, g, m_ref[l, r, kind, :], a_ref[l, r, kind, :], w)):
                    o[l, r, kind, :] = v
                return carry

            lax.fori_loop(0, rows // 32, body, 0)


def stem_step_kernel(factor, gw, place, w_ref, p_ref, r_ref, m_ref, a_ref, *outs):
    count = p_ref.shape[0] // gw
    lane = lane_of((gw, LANES))
    for group in range(2):
        pieces = []
        for k in range(count):
            rows_k = slice(k * gw, (k + 1) * gw)
            v = p_ref[rows_k, :].astype(f32) + r_ref[rows_k, :].astype(f32)
            v = v if group == 0 else pltpu.roll(v, LANES - gw, 1)
            pieces.append(jnp.where(lane < gw, v, 0.0))
        mine = slice(group * gw, (group + 1) * gw)
        for i, t in enumerate(tiles_of(pieces, gw)):
            cols = slice(i * LANES, (i + 1) * LANES)
            for o, v in zip(outs, step_of(factor, t, m_ref[mine, cols], a_ref[mine, cols], w_ref[mine, cols])):
                o[mine, cols] = v


def smalls_kernel(layers, ff_rows, gains, width, head_share, place, *refs):
    norms, ups, atts = refs[: 2 * layers + 1], refs[2 * layers + 1 : 3 * layers + 1], refs[3 * layers + 1 : 4 * layers + 1]
    keep_ref, send_ref, all_ref = refs[4 * layers + 1 :]
    y, c, z, x = (place[i] for i in range(4))
    all_ref[...] = jnp.zeros_like(all_ref)
    all_ref[0:1, :] = norms[0][0:1, :]
    all_ref[gains + 1 : gains + 2, :] = norms[0][1:2, :]
    for l in range(layers):
        base = gains + 2 + l * (6 + ff_rows)
        for k, (gain, shift, plain) in enumerate(((1, 3, 2), (2, 5, 4))):
            s = norms[1 + 2 * l + k]
            all_ref[gain + 2 * l : gain + 2 * l + 1, :] = s[0:1, :]
            all_ref[base + shift : base + shift + 1, :] = s[1:2, :]
            all_ref[base + plain : base + plain + 1, :] = s[2:3, :]
        for ry in range(2):
            all_ref[pl.ds(base + 6 + 2 * (y ^ ry) + c, 1), :] = ups[l][ry : ry + 1, :]
        for group in range(4):

            @pl.when(2 * x + c == group)
            def _(l=l, base=base, group=group):
                for i in range(2):
                    pieces = [jnp.zeros((1, LANES), f32)] * (width // 64)
                    for h in range(3):
                        t = atts[l][i : i + 1, (h // 2) * LANES : (h // 2 + 1) * LANES]
                        t = t if h % 2 == 0 else pltpu.roll(t, 64, 1)
                        pieces[3 * group + h] = jnp.where(lane_of(t.shape) < 64, t, 0.0)
                    all_ref[base + i : base + i + 1, :] = jnp.concatenate(tiles_of(pieces, 64), axis=1)

    whole = all_ref[...]
    cols = [whole[:, LANES * v : LANES * (v + 1)] for v in range(width // LANES)]
    for j in range(8):
        blk = piece_of(cols, j, width // 8)
        rel = (j // 2) ^ z
        at = (rel % 2) * 2 + rel // 2

        @pl.when(x == j % 2)
        def _(blk=blk, at=at):
            keep_ref[at] = blk

        @pl.when(x != j % 2)
        def _(blk=blk, at=at):
            send_ref[at] = blk


def small_total_kernel(row, a_ref, r_ref, b_ref, o_ref):
    total = a_ref[...] + r_ref[...]
    o_ref[...] = total
    o_ref[row : row + 1, :] = total[row : row + 1, :] + b_ref[0:1, :]


def encoded_split_kernel(place, x_ref, keep_ref, send_ref):
    z = place[2]
    for rel in range(4):
        out = send_ref if rel % 2 else keep_ref
        for a in range(2):
            at = pl.multiple_of(a * 64 + (z ^ rel) * 16, 16)
            out[rel // 2, a * 16 : a * 16 + 16, :] = x_ref[pl.ds(at, 16), :]


def encoded_route_kernel(place, own_ref, near_ref, far_ref, keep_ref, send_ref):
    c, z = place[1], place[2]
    for rel, src in enumerate(by_z(own_ref, near_ref, far_ref)):
        row = z ^ rel
        mine = (row // 2) == c

        @pl.when(mine)
        def _(src=src, row=row):
            keep_ref[row % 2] = src[...]

        @pl.when(jnp.logical_not(mine))
        def _(src=src, row=row):
            send_ref[row % 2] = src[...]


def encoded_join_kernel(place, keep_ref, recv_ref, o_ref, mixed):
    c = place[1]
    rows, toks, width = o_ref.shape
    for r in range(rows):
        for v in range(width // LANES):
            cols = slice(v * LANES, (v + 1) * LANES)
            for rel, src in enumerate((keep_ref, recv_ref)):
                for a in range(2):
                    at = v * toks + (c ^ rel) * 32 + a
                    mixed[pl.ds(at, 16, stride=2), :] = src[r, a * 16 : a * 16 + 16, cols].astype(f32)
            o_ref[r, :, cols] = mixed[v * toks : (v + 1) * toks, :]


def take_kernel(place, own_ref, near_ref, far_ref, keep_ref, send_ref):
    c, z, x = place[1], place[2], place[3]
    for rel, src in enumerate(by_z(own_ref, near_ref, far_ref)):
        row = z ^ rel
        mine = (row // 2) == c
        for h in range(2):

            @pl.when(mine)
            def _(src=src, row=row, h=h):
                keep_ref[row % 2, x ^ h] = src[h]

            @pl.when(jnp.logical_not(mine))
            def _(src=src, row=row, h=h):
                send_ref[row % 2, x ^ h] = src[h]


def stem_slope_kernel(rows, place, keep_ref, recv_ref, pre_ref, low_ref, ds_ref, bias_ref):
    c = place[1]
    for r in range(rows):
        for zf in range(4):
            for xq in range(2):
                for rel, src in enumerate((keep_ref, recv_ref)):
                    u = pl.multiple_of(((zf * 2 + xq) * 2 + (c ^ rel)) * 16, 16)
                    ds_ref[r, pl.ds(u, 16), :] = src[r, xq, zf * 16 : zf * 16 + 16, :]
    total = None
    for r in range(rows):
        dpre = ds_ref[r].astype(f32) * gelu_and_slope(pre_ref[r])[1]
        part = jnp.sum(dpre, axis=0, keepdims=True)
        total = part if total is None else total + part
        low_ref[r] = dpre.astype(bf16)
    bias_ref[0:1, :] = total[:, 0:LANES] + total[:, LANES : 2 * LANES]
    bias_ref[1:8, :] = jnp.zeros((7, LANES), f32)


def stem_grad_kernel(rows, taps, gw, place, ph_ref, low_ref, keep_ref, send_ref):
    n = low_ref.shape[1]
    y, c = place[0], place[1]
    left = jnp.concatenate([low_ref[r] for r in range(rows)], axis=0).T
    lane = lane_of((gw, LANES))
    per = taps // 4
    for rc, out in enumerate((keep_ref, send_ref)):
        for ry in range(2):
            block = (y ^ ry) * 2 + (c ^ rc)

            def win(i):
                at = pl.multiple_of((block + i // 16) * 16, 16)
                return ph_ref[i % 16, :, pl.ds(at, n), :].reshape(rows * n, 2 * LANES)

            def save(k, t, out=out, ry=ry):
                out[ry, k * gw : (k + 1) * gw, :] = jnp.where(lane < gw, t[0:gw], t[gw : 2 * gw]).astype(bf16)

            held = None
            for i in range(per // 2 + 1):
                if i < per // 2:
                    g = dot_nn(left, win(i))
                    cross = g[LANES:, 0:LANES]
                else:
                    cross = dot_nn(left[LANES:], win(i)[:, 0:LANES])
                if held is not None:
                    save(2 * i - 1, held + cross)
                if i < per // 2:
                    save(2 * i, g[0:LANES, 0:LANES] + g[LANES:, LANES:])
                    held = g[0:LANES, LANES:]


def stem_input_grad_kernel(rows, half, place, low_ref, ds_ref, w_ref, keep_ref, send_ref, qf, ph, acc):
    n = low_ref.shape[1]
    span = n + half
    for r in range(rows):
        qf[r, 0 : half // 2, :] = jnp.zeros((half // 2, 2 * LANES), f32)
        qf[r, half // 2 + n :, :] = jnp.zeros((half // 2, 2 * LANES), f32)
        qf[r, half // 2 : half // 2 + n, :] = low_ref[r].astype(f32)
    for p in range(16):
        m = span if p == 0 else span - 16
        for r in range(rows):
            ph[p, r, 0:m, :] = qf[r, p : p + m, :].astype(bf16)
    acc[...] = jnp.zeros_like(acc)

    def body(i, carry):
        left, upper, lower = [], [], []
        for t in range(5):
            m = i * 5 + t
            here, before, after = w_ref[2 * half + 1 - 2 * m], w_ref[2 * half - 2 * m], w_ref[2 * half + 2 - 2 * m]
            upper += [here, before]
            lower += [after, here]
            left.append(window(ph, m, rows, n))
        right = jnp.concatenate([jnp.concatenate(upper, 1), jnp.concatenate(lower, 1)], 0)
        acc[...] += dot_nt(jnp.concatenate(left, 1), right)
        return carry

    lax.fori_loop(0, (half + 1) // 5, body, 0)
    per = n // 8
    for r in range(rows):
        g = (acc[r * n : (r + 1) * n, :] + ds_ref[r].astype(f32)).astype(bf16)
        for j in range(8):
            to_x(keep_ref, send_ref, place[3], j % 2, (j // 2) ^ place[2], (r,), g[j * per : (j + 1) * per, :])


def join_kernel(width, place, own_ref, near_ref, far_ref, o_ref, mixed, by_channel):
    z, x = place[2], place[3]
    rows, per = own_ref.shape[2], own_ref.shape[3]
    for rel, src in enumerate(by_z(own_ref, near_ref, far_ref)):
        for h in range(2):
            by_channel[(z ^ rel) * 2 + (x ^ h)] = src[h]
    for r in range(rows):
        for a in range(2):
            pieces = [by_channel[j, r, :, a * LANES : (a + 1) * LANES].astype(f32) for j in range(8)]
            for v, col in enumerate(tiles_of(pieces, width)):
                mixed[pl.ds(v * 2 * per + a, per, stride=2), :] = col
        for v in range(o_ref.shape[2] // LANES):
            o_ref[r, :, v * LANES : (v + 1) * LANES] = mixed[v * 2 * per : (v + 1) * 2 * per, :]


def swapped(v, axis):
    return lax.ppermute(v, axis, [(0, 1), (1, 0)])


def across(v, axis, bit):
    count = lax.axis_size(axis)
    return lax.ppermute(v, axis, [(i, i ^ bit) for i in range(count)])


def one_sum(a, b):
    return whole_call(one_kernel, [sds(a.shape, a.dtype)], [a, b])[0]


def local_rows(
    features, cotangent, segments, stem_weight, projection_weight, mixing_weight,
    feedforward_weight, norm_gains, biases, *state,
):
    rows, toks, width = features.shape
    yi, ci, zi, xi = (lax.axis_index(a) for a in ("y", "c", "z", "x"))
    place = jnp.stack([yi, ci, zi, xi]).astype(jnp.int32)
    seq_i, row_i = zi * 2 + xi, yi * 2 + ci
    seq = ("z", "x")
    blocks = 8
    share = width // blocks
    gw = width // GROUPS
    frames = toks * blocks
    half = KERNEL // 2
    layers = projection_weight.shape[0]
    ff_rows = feedforward_weight.shape[3] // width
    head_share = width // 4
    group = 2 * xi + ci
    t = rows * toks

    stem_share = jnp.pad(
        lax.dynamic_slice_in_dim(stem_weight, seq_i * share, share, 1), ((0, 0), (0, LANES - share))
    )

    steps = width // LANES
    square = sds((width, width), bf16)
    *feed_first, feed_there = whole_call(
        functools.partial(feed_weights_kernel, 0), [square] * 4, [place, feedforward_weight],
        scalars=1, far=(1,), token=True, vmem=FAR_BYTES,
        scratch=[pltpu.VMEM((2, width, 2, width), bf16), pltpu.SemaphoreType.DMA((2 * steps,))],
    )

    (sent,) = whole_call(
        functools.partial(split_kernel, blocks, share), [sds((blocks, rows, toks, LANES), bf16)], [features]
    )
    mine = lax.all_to_all(sent, seq, 0, 0, tiled=True)
    conv_bias = jnp.pad(
        lax.dynamic_slice(biases, (0, seq_i * share), (1, share)), ((0, 0), (0, LANES - share))
    )
    n = frames // 2
    exchange = sds((rows, 2, 64, 2 * LANES), bf16)
    tap_scratch = pltpu.VMEM((KERNEL + 3, LANES, LANES), bf16)
    phased = (16, rows, (frames + 2 * half) // 2, 2 * LANES)
    row_scratch = pltpu.VMEM((rows * (frames + 2 * half) + 8, LANES), f32)
    pre_act, kept, away = whole_call(
        functools.partial(conv_kernel, rows, frames, half, gw),
        [sds((rows, n, 2 * LANES), f32), exchange, exchange],
        [place, mine, stem_share, conv_bias],
        after=[feed_there],
        scalars=1,
        scratch=[pltpu.VMEM(phased, bf16), row_scratch, pltpu.VMEM((rows * n, 2 * LANES), f32), tap_scratch],
        vmem=WIDE_BYTES,
    )
    (slots,) = whole_call(
        slots_kernel, [sds((blocks, 64, 2 * LANES), bf16)], [place, kept, swapped(away, "c")], scalars=1
    )
    *later, later_there = whole_call(
        functools.partial(later_weights_kernel, layers, [2 + l * (6 + ff_rows) for l in range(layers)], head_share),
        [square] * (4 * (layers - 1)) + [square, sds((256, width), bf16), sds((2, 256), f32)] * layers,
        [place, feedforward_weight, projection_weight, mixing_weight, biases],
        scalars=1, far=(1, 2, 3), token=True, vmem=FAR_BYTES, after=[slots],
        scratch=[
            pltpu.VMEM((layers - 1, 2, width, 2, width), bf16),
            pltpu.VMEM((layers, 3, width, 256), bf16),
            pltpu.SemaphoreType.DMA((layers - 1, 2 * steps)),
            pltpu.SemaphoreType.DMA((4 * layers,)),
        ],
    )
    feed_w = [feed_first, *(later[4 * i : 4 * i + 4] for i in range(layers - 1))]
    attend_w = [later[4 * (layers - 1) + 3 * l :][:3] for l in range(layers)]
    joined = lax.all_to_all(slots, seq, 0, 0, tiled=True)
    wide = sds((t, width), f32)
    thin = sds((t, width), bf16)
    column = sds((t, 1), f32)
    hidden, hidden_low, normed_stem, inverse_stem = whole_call(
        functools.partial(stem_norm_kernel, share), [wide, thin, wide, column], [joined, norm_gains, biases],
        after=[later_there],
    )

    def gathered(v):
        over_c = swapped(v, "c")
        over_x = swapped(v, "x")
        return [v, over_c, over_x, swapped(over_x, "c")]

    saved = []
    segments_other = swapped(segments, "c")
    quarter_row = sds((32, width), bf16)
    two = sds((2, t, width), bf16)
    full = 4 * t
    for l in range(layers):
        base = 2 + l * (6 + ff_rows)
        in_w, mix_w, both_b = attend_w[l]
        ups, downs = feed_w[l][:2], feed_w[l][2:]
        hl = gathered(hidden_low)
        before = []
        if l == 0:
            seg_row, seg_col = whole_call(
                segments_kernel, [sds((1, frames), f32), sds((frames, 1), f32)], [place, segments, segments_other],
                scalars=1, after=[hidden_low],
            )
            stay, move, cot_there = whole_call(
                cotangent_split_kernel, [sds((rows, 32, width), bf16)] * 2, [place, cotangent],
                scalars=1, after=[hidden_low], token=True,
                scratch=[pltpu.VMEM((width // LANES * toks + 8, LANES), f32)],
            )
            before = [cot_there]
        elif l == 1:
            cot, cot_there = whole_call(
                cotangent_join_kernel, [sds((t, width), bf16)],
                [place, routed[0], *(across(routed[rel], "z", rel) for rel in range(1, 4))],
                scalars=1, after=[hidden_low], token=True,
            )
            before = [cot_there]
        q, k, v, att, lse, keep, send = whole_call(
            functools.partial(attend_kernel, base),
            [sds((full, 256), bf16)] * 4 + [sds((3, full, 1), f32), two, two],
            hl + [in_w, mix_w, both_b, seg_row, seg_col],
            after=before,
        )
        own, pass_on = whole_call(half_sum_kernel, [wide, thin], [keep, swapped(send, "c")])
        rest = swapped(pass_on, "x")
        before = []
        if l == 0:
            *routed, cot_there = whole_call(
                cotangent_route_kernel, [quarter_row] * 4, [place, stay, swapped(move, "c")],
                scalars=1, after=[pass_on], token=True,
            )
            before = [cot_there]
        first, first_low, n1, i1 = whole_call(
            functools.partial(norm_kernel, 1 + 2 * l, base + 2, base + 3),
            [wide, thin, wide, column],
            [hidden, own, rest, norm_gains, biases],
            after=before,
        )
        first_other = swapped(first_low, "c")
        act, slope, own, send = whole_call(
            functools.partial(feed_kernel, base + 6),
            [sds((2, 2 * t, width), bf16)] * 2 + [wide, thin],
            [place, first_low, first_other, *ups, *downs, biases],
            scalars=1,
        )
        hidden, hidden_low, n2, i2 = whole_call(
            functools.partial(norm_kernel, 2 + 2 * l, base + 4, base + 5),
            [wide, thin, wide, column],
            [first, own, swapped(send, "c"), norm_gains, biases],
        )
        saved.append((in_w, mix_w, ups, downs, hl, q, k, v, att, lse, n1, i1, first_low, first_other, act, slope, n2, i2))

    encoded_low = hidden_low
    sums = sds((8, width), f32)
    terms = [cot]
    norm_sum = [None] * norm_gains.shape[0]
    up_sum, att_sum = [None] * layers, [None] * layers
    feed, att_parts = [None] * layers, [None] * layers
    parted = sds((2, 2, 2, 2 * share, width), bf16)
    tiles = sds((13, share, LANES), bf16)
    tiles_z = sds((2, 13, share, LANES), bf16)

    def send_on(parts, after):
        outs, operands = [], []
        for keep, recv, _ in parts:
            outs += [sds(keep.shape[1:], keep.dtype)] * 2
            operands += [keep, recv]
        made = whole_call(
            functools.partial(halves_kernel, len(parts)), outs, operands, after=after, token=True
        )
        return [(made[2 * i], how(made[2 * i + 1])) for i, (_, _, how) in enumerate(parts)], made[-1]

    over_x, over_y = (lambda v: swapped(v, "x")), (lambda v: swapped(v, "y"))
    over_z1, over_z2 = (lambda v: across(v, "z", 1)), (lambda v: across(v, "z", 2))
    before = []
    for l in reversed(range(layers)):
        base = 2 + l * (6 + ff_rows)
        in_w, mix_w, ups, downs, hl, q, k, v, att, lse, n1, i1, first_low, first_other, act, slope, n2, i2 = saved[l]
        d2, d2_low, norm_sum[2 + 2 * l] = whole_call(
            functools.partial(norm_back_kernel, 2 + 2 * l, len(terms)), [wide, thin, sums], terms + [norm_gains, n2, i2],
            after=before,
        )
        d2_other = swapped(d2_low, "c")
        dup, own, send, up_sum[l] = whole_call(
            feed_back_kernel,
            [sds((2, 2 * t, width), bf16), wide, thin, sums],
            [d2_low, d2_other, *ups, *downs, slope],
        )

        def feed_grad(after, first_low=first_low, first_other=first_other, d2_low=d2_low, d2_other=d2_other, dup=dup, act=act):
            keep, send, there = whole_call(
                feed_grad_kernel, [parted] * 2, [place, first_low, first_other, d2_low, d2_other, dup, act],
                scalars=1, after=after, token=True,
            )
            return (keep, over_y(send)), there

        before = []
        if l == 1:
            feed[l], there = feed_grad([send])
            before = [there]
        d1, d1_low, norm_sum[1 + 2 * l] = whole_call(
            functools.partial(norm_back_kernel, 1 + 2 * l, 3),
            [wide, thin, sums],
            [d2, own, swapped(send, "c"), norm_gains, n1, i1],
            after=before,
        )
        dl = gathered(d1_low)
        before = []
        if l == 1:
            two_rows = sds((2, 32, width), bf16)
            row_keep, row_send, there = whole_call(
                encoded_split_kernel, [two_rows] * 2, [place, encoded_low], scalars=1, after=[d1_low], token=True
            )
            row_near = over_z1(row_send)
            before = [there]
        if l == 0:
            feed[l], there = feed_grad([d1_low])
            stay_row, move_row, there = whole_call(
                encoded_route_kernel, [two_rows] * 2, [place, row_keep, row_near, row_far],
                scalars=1, after=[there], token=True,
            )
            (att_parts[1],), there = send_on([(*att_parts[1], over_z2)], [there])
            before = [there]
        dense_dp, keep, send, att_sum[l] = whole_call(
            attend_back_kernel,
            [sds((full, 640), bf16), two, two, sds((8, 256), f32)],
            dl + [q, k, v, lse, in_w, mix_w, seg_row, seg_col],
            after=before,
            scratch=[pltpu.VMEM((full, 256), bf16)] + [pltpu.VMEM((full, 256), f32)] * 3,
        )
        own, pass_on = whole_call(
            half_sum_kernel, [wide, thin], [keep, swapped(send, "c")],
        )
        rest = swapped(pass_on, "x")
        terms = [d1, own, rest]

        def attend_grad(after, hl=hl, dl=dl, att=att, dense_dp=dense_dp):
            return whole_call(
                attend_grad_kernel, [tiles_z, tiles_z], [place] + hl + dl + [att, dense_dp],
                scalars=1, after=after, token=True,
            )

        keep, send, there = attend_grad([pass_on])
        att_parts[l] = (keep, over_z1(send))
        if l == 1:
            row_send, there = whole_call(onward_kernel, [two_rows], [row_keep, row_near], after=[there], token=True)
            row_far = over_z2(row_send)
        else:
            encoded, there = whole_call(
                encoded_join_kernel, [sds((rows, toks, width), f32)], [place, stay_row, swapped(move_row, "c")], scalars=1,
                scratch=[pltpu.VMEM((width // LANES * toks + 8, LANES), f32)], after=[there], token=True,
            )
        before = [there]

    quad = sds((4, 64, 2 * LANES), bf16)
    ds_keep, ds_sent, norm_sum[0] = whole_call(
        functools.partial(stem_norm_back_kernel, share, len(terms)),
        [quad, quad, sums],
        [place, *terms, norm_gains, normed_stem, inverse_stem],
        scalars=1,
        after=before,
    )

    def spread(keep, send, after):
        pair_shape = sds((2, 2, *keep.shape[1:]), bf16)
        stays, goes, there = whole_call(
            along_z_kernel, [pair_shape] * 2, [keep, swapped(send, "x")], after=after, token=True
        )
        near = over_z1(goes)

        def onward(after):
            (far,) = whole_call(onward_kernel, [pair_shape], [stays, near], after=after)
            return [stays, near, over_z2(far)]

        return there, onward

    gain_count, bias_count = norm_gains.shape[0], biases.shape[0]
    small_half = sds((4, 32, LANES), f32)
    small_keep, small_send, small_there = whole_call(
        functools.partial(smalls_kernel, layers, ff_rows, gain_count, width, head_share),
        [small_half, small_half],
        [place, *norm_sum, *up_sum, *att_sum],
        scalars=1,
        scratch=[pltpu.VMEM((32, width), f32)],
        token=True,
        after=[ds_sent],
    )
    smalls = (small_keep.reshape(2, 2, 32, LANES), swapped(small_send, "x").reshape(2, 2, 32, LANES))
    phases, taps, phases_there = whole_call(
        functools.partial(phases_kernel, rows, frames, half, gw),
        [sds(phased, bf16), sds((KERNEL + 3, LANES, LANES), bf16)], [mine, stem_share], scratch=[row_scratch],
        after=[small_there], token=True,
    )
    (feed[1],), there = send_on([(*feed[1], over_x)], [phases_there])
    there, ds_onward = spread(ds_keep, ds_sent, [there])
    ds_blocks = ds_onward([there])
    att_second, there = whole_call(one_kernel, [tiles], list(att_parts[1]), after=[ds_blocks[1]], token=True)
    (att_parts[0],), there = send_on([(*att_parts[0], over_z2)], [there])
    stay, move, there = whole_call(
        take_kernel, [sds((2, 2, 64, 2 * LANES), bf16)] * 2, [place, *ds_blocks], scalars=1,
        after=[there], token=True,
    )
    pair = sds((rows, n, 2 * LANES), bf16)
    dpre_low, ds, stem_sums = whole_call(
        functools.partial(stem_slope_kernel, rows), [pair, pair, sds((8, LANES), f32)],
        [place, stay, swapped(move, "c"), pre_act], scalars=1, after=[there],
    )
    quarter = sds((2, KERNEL // 4 * gw, LANES), bf16)
    keep, send = whole_call(
        functools.partial(stem_grad_kernel, rows, KERNEL, gw), [quarter, quarter], [place, phases, dpre_low], scalars=1,
    )
    stem_part = (keep, swapped(send, "c"))
    (feed[1], stem_part), there = send_on([(*feed[1], over_z1), (*stem_part, over_y)], [send])
    back_shape = sds((4, rows, toks // 2, 2 * LANES), bf16)
    back_keep, back = whole_call(
        functools.partial(stem_input_grad_kernel, rows, half),
        [back_shape] * 2,
        [place, dpre_low, ds, taps],
        scalars=1,
        scratch=[
            pltpu.VMEM((rows, n + half, 2 * LANES), f32),
            pltpu.VMEM((16, rows, n + half, 2 * LANES), bf16),
            pltpu.VMEM((rows * n, 2 * LANES), f32),
        ],
        after=[there],
        vmem=WIDE_BYTES,
    )
    there, back_onward = spread(back_keep, back, [back])
    (feed[0],), there = send_on([(*feed[0], over_x)], [there])
    back_blocks = back_onward([there])
    att_first, there = whole_call(one_kernel, [tiles], list(att_parts[0]), after=[back_blocks[1]], token=True)
    att_grads = [att_first, att_second]
    (features_gradient,) = whole_call(
        functools.partial(join_kernel, share), [sds((rows, toks, width), f32)], [place, *back_blocks], scalars=1,
        scratch=[
            pltpu.VMEM((width // LANES * toks + 8, LANES), f32),
            pltpu.VMEM((blocks, rows, toks // 2, 2 * LANES), bf16),
        ],
        after=[there],
    )
    (feed[1], smalls), there = send_on([(*feed[1], over_z2), (*smalls, over_z1)], [features_gradient])
    att_came = swapped(jnp.stack([a[5:10] for a in att_grads]), "x")
    olds = whole_call(
        functools.partial(olds_kernel, layers, gw),
        [
            sds((share, KERNEL // 4 * gw), bf16),
            sds((layers, share, 640), bf16),
            sds((layers, share, 256), bf16),
            sds((layers, 2 * share, width), bf16),
        ],
        [place, stem_weight, projection_weight, mixing_weight, feedforward_weight],
        scalars=1, far=(1, 2, 3, 4), vmem=WIDE_BYTES, after=[there], token=True,
        scratch=[
            pltpu.VMEM((KERNEL // 4 * gw, 256), bf16),
            pltpu.VMEM((layers, share, 640), bf16),
            pltpu.VMEM((layers, share, 256), bf16),
            pltpu.VMEM((layers, share, 2, width), bf16),
            pltpu.SemaphoreType.DMA((1 + 3 * layers,)),
        ],
    )
    (feed[0], smalls), there = send_on([(*feed[0], over_z1), (*smalls, over_z2)], [olds[-1]])
    small_total, there = whole_call(
        functools.partial(small_total_kernel, gain_count), [sds((32, LANES), f32)], [*smalls, stem_sums],
        after=[there], token=True,
    )
    small_total = one_sum(small_total, swapped(small_total, "c"))
    settled = sds((layers, 4, 2, share, LANES), bf16)
    stay, move, there = whole_call(
        functools.partial(pick_kernel, layers), [settled] * 2, [place, *att_grads, att_came], scalars=1,
        after=[there], token=True,
    )
    (feed[0],), there = send_on([(*feed[0], over_z2)], [there])
    in_part, swap_part, mix_part, there = whole_call(
        functools.partial(settle_kernel, layers),
        [sds((layers, 2, 2, share, LANES), bf16)] + [sds((layers, 2, share, LANES), bf16)] * 2,
        [place, stay, swapped(move, "y")],
        scalars=1, after=[there], token=True,
    )
    swap_part = swapped(swap_part, "c")
    route = []
    for c in range(2):
        for z in range(4):
            for x in range(2):
                route.append(((c * 4 + z) * 2 + x, ((z & 1) * 4 + (2 * x + c)) * 2 + (z >> 1)))
    mix_part = lax.ppermute(mix_part, ("c", "z", "x"), route)
    small_total = one_sum(small_total, swapped(small_total, "y"))
    rate_base = 1.0 / math.sqrt(rows * 4 * frames)

    def step(index, kernel, operands, turn=False):
        m, a = state[index], state[6 + index]
        if turn:
            m, a = m.T, a.T
        made = whole_call(
            functools.partial(kernel, rate_factors[index] * rate_base), [sds(m.shape, f32)] * 3,
            [place, olds[index], *operands, m, a], scalars=1,
        )
        return [o.T for o in made] if turn else made

    results = [
        step(0, lambda f, *r: stem_step_kernel(f, gw, *r), list(stem_part), turn=True),
        step(1, projection_step_kernel, [in_part, swap_part]),
        step(2, mixing_step_kernel, [mix_part]),
        step(3, feed_step_kernel, [part for l in range(layers) for part in feed[l]]),
    ]
    for index, w, g in ((4, norm_gains, small_total[:gain_count]), (5, biases, small_total[gain_count : gain_count + bias_count])):
        w = lax.dynamic_slice_in_dim(w, seq_i * share, share, 1)
        results.append(step_of(rate_factors[index] * rate_base, g[:, :share], state[index], state[6 + index], w))
    return (encoded, features_gradient, *(results[i][k] for k in range(3) for i in range(6)))


def solution(mesh):
    if mesh.shape["row"] == 4 and mesh.shape["seq"] == 8:
        body, mesh = local_rows, Mesh(mesh.devices.reshape(2, 2, 4, 2), ("y", "c", "z", "x"))
        row, seq = ("y", "c"), ("z", "x")
    else:
        body, row, seq = local, "row", "seq"
    in_specs = (
        P(row, seq, None),
        P(row, seq, None),
        P(row, None),
        P(),
        P(),
        P(),
        P(),
        P(),
        P(),
        P(row, seq),
        P(None, seq, row),
        P(None, seq, row),
        P(None, seq, None, row),
        P(None, seq),
        P(None, seq),
        P(row, seq),
        P(None, seq, row),
        P(None, seq, row),
        P(None, seq, None, row),
        P(None, seq),
        P(None, seq),
    )
    out_specs = (
        P(row, seq, None),
        P(row, seq, None),
        P(row, seq),
        P(None, seq, row),
        P(None, seq, row),
        P(None, seq, None, row),
        P(None, seq),
        P(None, seq),
        P(row, seq),
        P(None, seq, row),
        P(None, seq, row),
        P(None, seq, None, row),
        P(None, seq),
        P(None, seq),
        P(row, seq),
        P(None, seq, row),
        P(None, seq, row),
        P(None, seq, None, row),
        P(None, seq),
        P(None, seq),
    )
    return jax.shard_map(body, mesh=mesh, in_specs=in_specs, out_specs=out_specs, check_vma=False)
```

```python
import functools
import math

import jax
import jax.numpy as jnp
from jax import lax
from jax.experimental import pallas as pl
from jax.experimental.pallas import tpu as pltpu
from jax.sharding import Mesh
from jax.sharding import PartitionSpec as P

HEADS = 12
KERNEL = 128
GROUPS = 16


epsilon = 1e-05
masked_score = -1e30
momentum_decay = 0.9
average_decay = 0.5
rate_factors = (0.012, 0.08, 0.6, 0.03, 0.06, 0.09)
row_dims = (0, 2, 2, 3)


def extended_2(cells, sides, width):
    for axis, dim in sides:
        count = lax.axis_size(axis)
        ends = count - 1
        head = lax.slice_in_dim(cells, 0, width, axis=dim)
        tail = lax.slice_in_dim(cells, cells.shape[dim] - width, cells.shape[dim], axis=dim)
        cells = jnp.concatenate(
            [
                lax.ppermute(tail, axis, [(i, (i + 1) % count) for i in range(ends)]),
                cells,
                lax.ppermute(head, axis, [((i + 1) % count, i) for i in range(ends)]),
            ],
            axis=dim,
        )
    return cells


def layer_norm(values, gain_row, shift_row):
    centre = jnp.mean(values, axis=-1, keepdims=True)
    centred = values - centre
    spread = jnp.mean(centred * centred, axis=-1, keepdims=True)
    inverse = lax.rsqrt(spread + epsilon)
    normed = centred * inverse
    return (normed * gain_row + shift_row, normed, inverse)


def layer_norm_back(upstream, normed, inverse, gain_row):
    scaled = upstream * gain_row
    first_mean = jnp.mean(scaled, axis=-1, keepdims=True)
    second_mean = jnp.mean(scaled * normed, axis=-1, keepdims=True)
    downstream = inverse * (scaled - first_mean - normed * second_mean)
    return (downstream, jnp.sum(upstream * normed, axis=(0, 1)), jnp.sum(upstream, axis=(0, 1)))


def gelu_exact(values):
    return jax.nn.gelu(values, approximate=False)


def gelu_back(inputs, upstream):
    _, pullback = jax.vjp(gelu_exact, inputs)
    return pullback(upstream)[0]


def group_conv(extended, kernel_taps, group_count):
    return lax.conv_general_dilated(
        extended,
        kernel_taps,
        (1,),
        "VALID",
        dimension_numbers=("NWC", "WIO", "NWC"),
        feature_group_count=group_count,
        preferred_element_type=jnp.float32,
    )


def group_conv_kernel_grad(extended, upstream_low, group_count):
    return lax.conv_general_dilated(
        extended,
        upstream_low,
        (1,),
        "VALID",
        dimension_numbers=("CWN", "IWO", "WNC"),
        batch_group_count=group_count,
        preferred_element_type=jnp.float32,
    )


def flipped_taps(kernel_taps, group_count):
    tap_count, group_width, model_width = kernel_taps.shape
    split_taps = kernel_taps.reshape(tap_count, group_width, group_count, group_width)
    swapped = jnp.transpose(split_taps, (0, 3, 2, 1)).reshape(tap_count, group_width, model_width)
    return swapped[::-1]


def masked_scores(query_part, key_part, query_segments, key_segments):
    scores = jnp.einsum("rqhe,rkhe->rhqk", query_part, key_part, preferred_element_type=jnp.float32)
    allowed = query_segments[:, None, :, None] == key_segments[:, None, None, :]
    return jnp.where(allowed, scores, masked_score)


def key_slice(kv_whole, segments, start, key_block, head_count):
    row_count = kv_whole.shape[0]
    model_width = kv_whole.shape[2] // 2
    head_width = model_width // head_count
    part_rows = lax.dynamic_slice_in_dim(kv_whole, start, key_block, 1)
    part_segments = lax.dynamic_slice_in_dim(segments, start, key_block, 1)
    key_part = part_rows[:, :, :model_width].reshape(row_count, key_block, head_count, head_width)
    value_part = part_rows[:, :, model_width:].reshape(row_count, key_block, head_count, head_width)
    return (key_part, value_part, part_segments)


def attend(query_heads, kv_whole, query_segments, segments, head_count):
    row_count = query_heads.shape[0]
    tok_count = query_heads.shape[1]
    key_block = math.gcd(kv_whole.shape[1], 1024)
    block_count = kv_whole.shape[1] // key_block

    def stats_step(step_index, state):
        running_max, running_sum = state
        key_part, value_part, part_segments = key_slice(
            kv_whole, segments, step_index * key_block, key_block, head_count
        )
        scores = masked_scores(query_heads, key_part, query_segments, part_segments)
        new_max = jnp.maximum(running_max, jnp.max(scores, axis=-1))
        running_sum = running_sum * jnp.exp(running_max - new_max) + jnp.sum(
            jnp.exp(scores - new_max[..., None]), axis=-1
        )
        return (new_max, running_sum)

    start_state = (
        jnp.full((row_count, head_count, tok_count), masked_score, jnp.float32),
        jnp.zeros((row_count, head_count, tok_count), jnp.float32),
    )
    running_max, running_sum = lax.fori_loop(0, block_count, stats_step, start_state)
    log_sum = running_max + jnp.log(running_sum)

    def value_step(step_index, state):
        coarse, residue = state
        key_part, value_part, part_segments = key_slice(
            kv_whole, segments, step_index * key_block, key_block, head_count
        )
        probability = jnp.exp(
            masked_scores(query_heads, key_part, query_segments, part_segments) - log_sum[..., None]
        )
        probability_low = probability.astype(jnp.bfloat16)
        remainder_low = (probability - probability_low.astype(jnp.float32)).astype(jnp.bfloat16)
        coarse = coarse + jnp.einsum(
            "rhqk,rkhe->rqhe", probability_low, value_part, preferred_element_type=jnp.float32
        )
        residue = residue + jnp.einsum(
            "rhqk,rkhe->rqhe", remainder_low, value_part, preferred_element_type=jnp.float32
        )
        return (coarse, residue)

    zero_out = jnp.zeros(query_heads.shape, jnp.float32)
    coarse, residue = lax.fori_loop(0, block_count, value_step, (zero_out, zero_out))
    return (coarse, coarse + residue, log_sum)


def attend_back(
    query_heads, grad_heads, kv_whole, query_segments, segments, log_sum, delta, head_count
):
    row_count = query_heads.shape[0]
    frame_count = kv_whole.shape[1]
    model_width = kv_whole.shape[2] // 2
    key_block = math.gcd(frame_count, 1024)
    block_count = frame_count // key_block

    def back_step(step_index, state):
        grad_query, key_terms = state
        start = step_index * key_block
        key_part, value_part, part_segments = key_slice(
            kv_whole, segments, start, key_block, head_count
        )
        probability = jnp.exp(
            masked_scores(query_heads, key_part, query_segments, part_segments) - log_sum[..., None]
        )
        grad_prob = jnp.einsum(
            "rqhe,rkhe->rhqk", grad_heads, value_part, preferred_element_type=jnp.float32
        )
        grad_scores = (probability * (grad_prob - delta[..., None])).astype(jnp.bfloat16)
        grad_query = grad_query + jnp.einsum(
            "rhqk,rkhe->rqhe", grad_scores, key_part, preferred_element_type=jnp.float32
        )
        grad_keys = jnp.einsum(
            "rhqk,rqhe->rkhe", grad_scores, query_heads, preferred_element_type=jnp.float32
        )
        grad_values = jnp.einsum(
            "rhqk,rqhe->rkhe",
            probability.astype(jnp.bfloat16),
            grad_heads,
            preferred_element_type=jnp.float32,
        )
        both_terms = jnp.concatenate(
            [
                grad_keys.reshape(row_count, key_block, model_width),
                grad_values.reshape(row_count, key_block, model_width),
            ],
            axis=-1,
        )
        key_terms = lax.dynamic_update_slice_in_dim(key_terms, both_terms, start, 1)
        return (grad_query, key_terms)

    term_start = jnp.zeros((row_count, frame_count, 2 * model_width), jnp.float32)
    return lax.fori_loop(
        0, block_count, back_step, (jnp.zeros(query_heads.shape, jnp.float32), term_start)
    )


def local(
    features,
    cotangent,
    segments,
    stem_weight,
    projection_weight,
    mixing_weight,
    feedforward_weight,
    norm_gains,
    biases,
    stem_moment,
    projection_moment,
    mixing_moment,
    feedforward_moment,
    gain_moment,
    bias_moment,
    stem_average,
    projection_average,
    mixing_average,
    feedforward_average,
    gain_average,
    bias_average,
):
    row_count, tok_count, model_width = features.shape
    head_count = HEADS
    head_width = model_width // head_count
    group_count = GROUPS
    group_width = model_width // group_count
    tap_count = KERNEL
    half_taps = tap_count // 2
    layer_count = projection_weight.shape[0]
    ff_rows = feedforward_weight.shape[3] // model_width
    score_scale = 1.0 / math.sqrt(head_width)
    seq_index = lax.axis_index("seq")
    query_segments = lax.dynamic_slice_in_dim(segments, seq_index * tok_count, tok_count, 1)
    kernel_taps = stem_weight.reshape(tap_count, group_width, model_width)
    extended = extended_2(features, (("seq", 1),), half_taps)
    conv_input = extended[:, : tok_count + tap_count - 1]
    conv_pre = group_conv(conv_input, kernel_taps, group_count) + biases[0]
    summed = features.astype(jnp.float32) + gelu_exact(conv_pre)
    hidden, normed_stem, inverse_stem = layer_norm(summed, norm_gains[0], biases[1])
    saved_layers = []
    for layer_index in range(layer_count):
        bias_base = 2 + layer_index * (6 + ff_rows)
        hidden_low = hidden.astype(jnp.bfloat16)
        projected = jnp.einsum(
            "rtd,de->rte",
            hidden_low,
            projection_weight[layer_index],
            preferred_element_type=jnp.float32,
        )
        queries = ((projected[..., :model_width] + biases[bias_base]) * score_scale).astype(
            jnp.bfloat16
        )
        keys_low = projected[..., model_width : 2 * model_width].astype(jnp.bfloat16)
        values_low = (projected[..., 2 * model_width :] + biases[bias_base + 1]).astype(
            jnp.bfloat16
        )
        kv_local = jnp.concatenate([keys_low, values_low], axis=-1)
        kv_whole = lax.all_gather(kv_local, "seq", axis=1, tiled=True)
        query_heads = queries.reshape(row_count, tok_count, head_count, head_width)
        coarse, fine, log_sum = attend(query_heads, kv_whole, query_segments, segments, head_count)
        mixed_low = coarse.reshape(row_count, tok_count, model_width).astype(jnp.bfloat16)
        branch = (
            jnp.einsum(
                "rte,ed->rtd",
                mixed_low,
                mixing_weight[layer_index],
                preferred_element_type=jnp.float32,
            )
            + biases[bias_base + 2]
        )
        first_norm, normed_one, inverse_one = layer_norm(
            hidden + branch, norm_gains[1 + 2 * layer_index], biases[bias_base + 3]
        )
        first_low = first_norm.astype(jnp.bfloat16)
        up_bias = biases[bias_base + 6 : bias_base + 6 + ff_rows].reshape(-1)
        up_pre = (
            jnp.einsum(
                "rtd,dj->rtj",
                first_low,
                feedforward_weight[layer_index, :, 0, :],
                preferred_element_type=jnp.float32,
            )
            + up_bias
        )
        up_low = gelu_exact(up_pre).astype(jnp.bfloat16)
        down_out = (
            jnp.einsum(
                "rtj,dj->rtd",
                up_low,
                feedforward_weight[layer_index, :, 1, :],
                preferred_element_type=jnp.float32,
            )
            + biases[bias_base + 4]
        )
        hidden_next, normed_two, inverse_two = layer_norm(
            first_norm + down_out, norm_gains[2 + 2 * layer_index], biases[bias_base + 5]
        )
        saved_layers.append(
            (
                hidden_low,
                query_heads,
                kv_whole,
                log_sum,
                fine,
                mixed_low,
                normed_one,
                inverse_one,
                first_low,
                up_pre,
                up_low,
                normed_two,
                inverse_two,
            )
        )
        hidden = hidden_next
    upstream = cotangent.astype(jnp.float32)
    gain_grads = [None] * norm_gains.shape[0]
    bias_grads = [None] * biases.shape[0]
    projection_grads = [None] * layer_count
    mixing_grads = [None] * layer_count
    feedforward_grads = [None] * layer_count
    for layer_index in reversed(range(layer_count)):
        (
            hidden_low,
            query_heads,
            kv_whole,
            log_sum,
            fine,
            mixed_low,
            normed_one,
            inverse_one,
            first_low,
            up_pre,
            up_low,
            normed_two,
            inverse_two,
        ) = saved_layers[layer_index]
        bias_base = 2 + layer_index * (6 + ff_rows)
        in_matrix = projection_weight[layer_index]
        mix_matrix = mixing_weight[layer_index]
        up_matrix = feedforward_weight[layer_index, :, 0, :]
        down_matrix = feedforward_weight[layer_index, :, 1, :]
        grad_second, gain_grads[2 + 2 * layer_index], bias_grads[bias_base + 5] = layer_norm_back(
            upstream, normed_two, inverse_two, norm_gains[2 + 2 * layer_index]
        )
        bias_grads[bias_base + 4] = jnp.sum(grad_second, axis=(0, 1))
        down_low = grad_second.astype(jnp.bfloat16)
        grad_down = jnp.einsum("rtd,rtj->dj", down_low, up_low, preferred_element_type=jnp.float32)
        grad_act = jnp.einsum(
            "rtd,dj->rtj", down_low, down_matrix, preferred_element_type=jnp.float32
        )
        grad_up_pre = gelu_back(up_pre, grad_act)
        up_bias_grad = jnp.sum(grad_up_pre, axis=(0, 1)).reshape(ff_rows, model_width)
        for offset in range(ff_rows):
            bias_grads[bias_base + 6 + offset] = up_bias_grad[offset]
        up_grad_low = grad_up_pre.astype(jnp.bfloat16)
        grad_up = jnp.einsum(
            "rtd,rtj->dj", first_low, up_grad_low, preferred_element_type=jnp.float32
        )
        grad_first = grad_second + jnp.einsum(
            "rtj,dj->rtd", up_grad_low, up_matrix, preferred_element_type=jnp.float32
        )
        feedforward_grads[layer_index] = jnp.stack([grad_up, grad_down], axis=1)
        grad_resid, gain_grads[1 + 2 * layer_index], bias_grads[bias_base + 3] = layer_norm_back(
            grad_first, normed_one, inverse_one, norm_gains[1 + 2 * layer_index]
        )
        bias_grads[bias_base + 2] = jnp.sum(grad_resid, axis=(0, 1))
        branch_low = grad_resid.astype(jnp.bfloat16)
        mixing_grads[layer_index] = jnp.einsum(
            "rte,rtd->ed", mixed_low, branch_low, preferred_element_type=jnp.float32
        )
        grad_mixed = jnp.einsum(
            "rtd,ed->rte", branch_low, mix_matrix, preferred_element_type=jnp.float32
        )
        mixed_grad_low = grad_mixed.astype(jnp.bfloat16).reshape(
            row_count, tok_count, head_count, head_width
        )
        delta = jnp.transpose(
            jnp.sum(mixed_grad_low.astype(jnp.float32) * fine, axis=-1), (0, 2, 1)
        )
        grad_query, key_terms = attend_back(
            query_heads,
            mixed_grad_low,
            kv_whole,
            query_segments,
            segments,
            log_sum,
            delta,
            head_count,
        )
        grad_kv = lax.psum_scatter(key_terms, "seq", scatter_dimension=1, tiled=True)
        query_grad_low = grad_query.reshape(row_count, tok_count, model_width).astype(jnp.bfloat16)
        key_grad_low = grad_kv[..., :model_width].astype(jnp.bfloat16)
        value_grad_low = grad_kv[..., model_width:].astype(jnp.bfloat16)
        bias_grads[bias_base] = (
            jnp.sum(query_grad_low.astype(jnp.float32), axis=(0, 1)) * score_scale
        )
        bias_grads[bias_base + 1] = jnp.sum(value_grad_low.astype(jnp.float32), axis=(0, 1))
        grad_projected = jnp.concatenate(
            [query_grad_low * score_scale, key_grad_low, value_grad_low], axis=-1
        )
        projection_grads[layer_index] = jnp.einsum(
            "rtd,rte->de", hidden_low, grad_projected, preferred_element_type=jnp.float32
        )
        upstream = grad_resid + jnp.einsum(
            "rte,de->rtd", grad_projected, in_matrix, preferred_element_type=jnp.float32
        )
    grad_summed, gain_grads[0], bias_grads[1] = layer_norm_back(
        upstream, normed_stem, inverse_stem, norm_gains[0]
    )
    grad_conv = gelu_back(conv_pre, grad_summed)
    bias_grads[0] = jnp.sum(grad_conv, axis=(0, 1))
    conv_grad_low = grad_conv.astype(jnp.bfloat16)
    grad_extended = extended_2(conv_grad_low, (("seq", 1),), half_taps)
    features_gradient = grad_summed + group_conv(
        grad_extended[:, 1:], flipped_taps(kernel_taps, group_count), group_count
    )
    seq_count = lax.axis_size("seq")
    share_width = model_width // seq_count
    layer_partials = (
        jnp.stack(projection_grads),
        jnp.stack(mixing_grads),
        jnp.stack(feedforward_grads),
        jnp.stack(gain_grads),
        jnp.stack(bias_grads),
    )
    grad_stem = group_conv_kernel_grad(conv_input, conv_grad_low, group_count).reshape(
        tap_count * group_width, model_width
    )
    shares = (
        lax.psum_scatter(grad_stem, "seq", scatter_dimension=1, tiled=True),
        lax.psum_scatter(layer_partials[0], "seq", scatter_dimension=1, tiled=True),
        lax.psum_scatter(layer_partials[1], "seq", scatter_dimension=1, tiled=True),
        lax.psum_scatter(layer_partials[2], "seq", scatter_dimension=1, tiled=True),
        lax.psum_scatter(layer_partials[3], "seq", scatter_dimension=1, tiled=True),
        lax.psum_scatter(layer_partials[4], "seq", scatter_dimension=1, tiled=True),
    )
    matrix_totals = (
        lax.psum_scatter(
            shares[0].astype(jnp.bfloat16), "row", scatter_dimension=0, tiled=True
        ).astype(jnp.float32),
        lax.psum_scatter(
            shares[1].astype(jnp.bfloat16), "row", scatter_dimension=2, tiled=True
        ).astype(jnp.float32),
        lax.psum_scatter(
            shares[2].astype(jnp.bfloat16), "row", scatter_dimension=2, tiled=True
        ).astype(jnp.float32),
        lax.psum_scatter(
            shares[3].astype(jnp.bfloat16), "row", scatter_dimension=3, tiled=True
        ).astype(jnp.float32),
    )
    small_totals = lax.psum((shares[4], shares[5]), "row")
    totals = (
        matrix_totals[0],
        matrix_totals[1],
        matrix_totals[2],
        matrix_totals[3],
        small_totals[0],
        small_totals[1],
    )
    share_start = seq_index * share_width
    row_index = lax.axis_index("row")
    row_total = lax.axis_size("row")
    rate_base = 1.0 / math.sqrt(row_count * row_total * tok_count * seq_count)
    old_params = (
        stem_weight,
        projection_weight,
        mixing_weight,
        feedforward_weight,
        norm_gains,
        biases,
    )
    old_moments = (
        stem_moment,
        projection_moment,
        mixing_moment,
        feedforward_moment,
        gain_moment,
        bias_moment,
    )
    old_averages = (
        stem_average,
        projection_average,
        mixing_average,
        feedforward_average,
        gain_average,
        bias_average,
    )
    momenta = []
    averaged = []
    updated = []
    for param_index in range(6):
        old_share = lax.dynamic_slice_in_dim(old_params[param_index], share_start, share_width, 1)
        if param_index < 4:
            split_dim = row_dims[param_index]
            piece_size = old_share.shape[split_dim] // row_total
            old_share = lax.dynamic_slice_in_dim(
                old_share, row_index * piece_size, piece_size, split_dim
            )
        old_share = old_share.astype(jnp.float32)
        moment_new = momentum_decay * old_moments[param_index] + totals[param_index]
        weight_new = old_share - rate_factors[param_index] * rate_base * (
            totals[param_index] + momentum_decay * moment_new
        )
        momenta.append(moment_new)
        updated.append(weight_new)
        averaged.append(
            average_decay * old_averages[param_index] + (1.0 - average_decay) * weight_new
        )
    return (
        hidden,
        features_gradient,
        momenta[0],
        momenta[1],
        momenta[2],
        momenta[3],
        momenta[4],
        momenta[5],
        averaged[0],
        averaged[1],
        averaged[2],
        averaged[3],
        averaged[4],
        averaged[5],
        updated[0],
        updated[1],
        updated[2],
        updated[3],
        updated[4],
        updated[5],
    )


LANES = 128
PAIRS = 2
VMEM_BYTES = 16 * 1024 * 1024
WIDE_BYTES = 24 * 1024 * 1024
FAR_BYTES = 56 * 1024 * 1024
bf16 = jnp.bfloat16
f32 = jnp.float32


def whole_call(kernel, outs, operands, scalars=0, scratch=(), after=(), far=(), token=False, vmem=VMEM_BYTES):
    given, waits, made = len(operands), len(after), len(outs)

    def body(*refs):
        kernel(*refs[:given], *refs[given + waits : given + waits + made], *refs[given + waits + made + token :])

    in_specs = [
        pl.BlockSpec(memory_space=pltpu.SMEM if i < scalars else pl.ANY if i in far else pltpu.VMEM)
        for i in range(given)
    ] + [pl.BlockSpec(memory_space=pl.ANY)] * waits
    out_specs = [pl.BlockSpec(memory_space=pltpu.VMEM)] * made + [pl.BlockSpec(memory_space=pl.ANY)] * token
    return pl.pallas_call(
        body,
        out_shape=[*outs, *[jax.ShapeDtypeStruct((8, LANES), jnp.float32)] * token],
        in_specs=in_specs,
        out_specs=out_specs,
        scratch_shapes=list(scratch),
        compiler_params=pltpu.CompilerParams(vmem_limit_bytes=vmem),
        cost_estimate=pl.CostEstimate(flops=1, bytes_accessed=1, transcendentals=0),
    )(*operands, *after)


def sds(shape, dtype):
    return jax.ShapeDtypeStruct(shape, dtype)


def dot_nn(a, b):
    return lax.dot_general(a, b, (((1,), (0,)), ((), ())), preferred_element_type=f32)


def dot_nt(a, b):
    return lax.dot_general(a, b, (((1,), (1,)), ((), ())), preferred_element_type=f32)


def dot_tn(a, b):
    return lax.dot_general(a, b, (((0,), (0,)), ((), ())), preferred_element_type=f32)


def gelu_and_slope(v):
    cdf = 0.5 * (1.0 + lax.erf(v * math.sqrt(0.5)))
    return v * cdf, cdf + v * jnp.exp(-0.5 * v * v) * (1.0 / math.sqrt(2.0 * math.pi))


def lane_of(shape):
    return lax.broadcasted_iota(jnp.int32, shape, len(shape) - 1)


def piece_of(cols, j, width):
    off, v = (width * j) % LANES, (width * j) // LANES
    lane = lane_of(cols[0].shape)
    if off == 0:
        t = cols[v]
    else:
        t = pltpu.roll(cols[v], LANES - off, 1)
        if off + width > LANES:
            t = jnp.where(lane < LANES - off, t, pltpu.roll(cols[v + 1], LANES - off, 1))
    return jnp.where(lane < width, t, 0.0)


def tiles_of(pieces, width):
    count = len(pieces) * width // LANES
    cols = [None] * count

    def put(v, t):
        cols[v] = t if cols[v] is None else cols[v] + t

    for j, piece in enumerate(pieces):
        off, v = (width * j) % LANES, (width * j) // LANES
        if off == 0:
            put(v, piece)
            continue
        rolled = pltpu.roll(piece, off, 1)
        if off + width > LANES:
            lane = lane_of(piece.shape)
            put(v, jnp.where(lane >= off, rolled, 0.0))
            put(v + 1, jnp.where(lane < off, rolled, 0.0))
        else:
            put(v, rolled)
    return cols


def split_kernel(blocks, width, x_ref, o_ref):
    rows = x_ref.shape[0]
    for r in range(rows):
        x = x_ref[r].astype(f32)
        cols = [x[:, LANES * v : LANES * (v + 1)] for v in range(x.shape[1] // LANES)]
        for j in range(blocks):
            o_ref[j, r] = piece_of(cols, j, width).astype(bf16)


def fill_taps(taps, gw, w_ref, o_ref):
    zero = jnp.zeros((LANES, LANES), bf16)
    o_ref[0] = zero
    o_ref[taps + 1] = zero
    o_ref[taps + 2] = zero

    def body(k, carry):
        w = w_ref[pl.ds(pl.multiple_of(k * gw, 16), gw), :]
        lane = lane_of(w.shape)
        o_ref[k + 1, 0:gw, :] = jnp.where(lane < gw, w, jnp.zeros_like(w))
        o_ref[k + 1, gw : 2 * gw, :] = jnp.where(lane >= gw, w, jnp.zeros_like(w))
        o_ref[k + 1, 2 * gw :, :] = jnp.zeros((LANES - 2 * gw, LANES), bf16)
        return carry

    lax.fori_loop(0, taps, body, 0)


def phases_from_frames(x_ref, xf, ph, rows, frames, half):
    blocks, block = x_ref.shape[0], x_ref.shape[2]
    span = frames + 2 * half
    for r in range(rows):
        xf[r * span : r * span + half, :] = jnp.zeros((half, LANES), f32)
        xf[r * span + half + frames : (r + 1) * span, :] = jnp.zeros((half, LANES), f32)
        for s in range(blocks):
            at = r * span + half + s * block
            xf[at : at + block, :] = x_ref[s, r].astype(f32)
    n = span // 2 - 16

    def body(p, carry):
        for r in range(rows):
            for b in range(2):
                ph[p, r, 0:n, b * LANES : (b + 1) * LANES] = xf[
                    pl.ds(r * span + 2 * p + b, n, stride=2), :
                ].astype(bf16)
        return carry

    lax.fori_loop(0, 16, body, 0)
    for r in range(rows):
        for b in range(2):
            ph[0, r, n:, b * LANES : (b + 1) * LANES] = xf[pl.ds(r * span + 2 * n + b, 16, stride=2), :].astype(bf16)


def window(ph, m, rows, n):
    p, a = lax.rem(m, 16), m // 16
    part = ph[p, :, pl.ds(pl.multiple_of(a * 16, 16), n), :]
    return part.reshape(rows * n, part.shape[-1])


def phases_kernel(rows, frames, half, gw, x_ref, share_ref, ph_ref, w_ref, xf):
    phases_from_frames(x_ref, xf, ph_ref, rows, frames, half)
    fill_taps(2 * half, gw, share_ref, w_ref)


def conv_kernel(rows, frames, half, gw, c_ref, x_ref, share_ref, b_ref, pre_ref, keep_ref, send_ref, ph_ref, xf, acc, w_ref):
    n = frames // 2
    fill_taps(2 * half, gw, share_ref, w_ref)
    phases_from_frames(x_ref, xf, ph_ref, rows, frames, half)
    acc[...] = jnp.zeros_like(acc)

    def body(i, carry):
        left, right = [], []
        for t in range(5):
            m = i * 5 + t
            here, before, after = w_ref[2 * m + 1], w_ref[2 * m], w_ref[2 * m + 2]
            right += [jnp.concatenate([here, before], 1), jnp.concatenate([after, here], 1)]
            left.append(window(ph_ref, m, rows, n))
        acc[...] += dot_nn(jnp.concatenate(left, 1), jnp.concatenate(right, 0))
        return carry

    lax.fori_loop(0, (half + 1) // 5, body, 0)
    bias = jnp.concatenate([b_ref[...], b_ref[...]], 1)
    c = c_ref[1]
    for r in range(rows):
        pre = acc[r * n : (r + 1) * n, :] + bias
        pre_ref[r] = pre
        x = ph_ref[0, r, half // 2 : half // 2 + n, :].astype(f32)
        s = (x + gelu_and_slope(pre)[0]).astype(bf16)
        for zf in range(4):
            for xq in range(2):
                for cf in range(2):
                    u = ((zf * 2 + xq) * 2 + cf) * 16
                    blk = s[u : u + 16, :]

                    @pl.when(c == cf)
                    def _(blk=blk, r=r, xq=xq, zf=zf):
                        keep_ref[r, xq, zf * 16 : zf * 16 + 16, :] = blk

                    @pl.when(c != cf)
                    def _(blk=blk, r=r, xq=xq, zf=zf):
                        send_ref[r, xq, zf * 16 : zf * 16 + 16, :] = blk


def normed(values):
    centre = jnp.mean(values, axis=-1, keepdims=True)
    centred = values - centre
    spread = jnp.mean(centred * centred, axis=-1, keepdims=True)
    inverse = lax.rsqrt(spread + epsilon)
    return centred * inverse, inverse


def stem_norm_kernel(width, r_ref, g_ref, b_ref, h_ref, low_ref, n_ref, i_ref):
    halves = []
    for a in range(2):
        pieces = [r_ref[j, :, a * LANES : (a + 1) * LANES].astype(f32) for j in range(r_ref.shape[0])]
        halves.append(jnp.concatenate(tiles_of(pieces, width), axis=1))
    s = jnp.concatenate(halves, axis=0)
    n, inv = normed(s)
    h = n * g_ref[0:1, :] + b_ref[1:2, :]
    h_ref[...] = h
    low_ref[...] = h.astype(bf16)
    n_ref[...] = n
    i_ref[...] = inv


def cotangent_split_kernel(place, x_ref, keep_ref, send_ref, mixed):
    c = place[1]
    rows, toks, width = x_ref.shape
    for r in range(rows):
        for v in range(width // LANES):
            mixed[v * toks : (v + 1) * toks, :] = x_ref[r, :, v * LANES : (v + 1) * LANES].astype(f32)
        for cf in range(2):
            for a in range(2):
                parts = [mixed[pl.ds(v * toks + cf * 32 + a, 16, stride=2), :] for v in range(width // LANES)]
                blk = jnp.concatenate(parts, axis=1).astype(bf16)

                @pl.when(c == cf)
                def _(blk=blk, r=r, a=a):
                    keep_ref[r, a * 16 : a * 16 + 16, :] = blk

                @pl.when(c != cf)
                def _(blk=blk, r=r, a=a):
                    send_ref[r, a * 16 : a * 16 + 16, :] = blk


def cotangent_route_kernel(place, keep_ref, recv_ref, *outs):
    c, z = place[1], place[2]
    for rel, out in enumerate(outs):
        to = z ^ rel
        mine = (to // 2) == c

        @pl.when(mine)
        def _(out=out, to=to):
            out[...] = keep_ref[to % 2]

        @pl.when(jnp.logical_not(mine))
        def _(out=out, to=to):
            out[...] = recv_ref[to % 2]


def cotangent_join_kernel(place, r0, r1, r2, r3, o_ref):
    z = place[2]
    for rel, src in enumerate((r0, r1, r2, r3)):
        for a in range(2):
            at = pl.multiple_of(a * 64 + (z ^ rel) * 16, 16)
            o_ref[pl.ds(at, 16), :] = src[a * 16 : a * 16 + 16, :]


def segments_kernel(place, own_ref, other_ref, row_ref, col_ref):
    c, z, x = place[1], place[2], place[3]
    frames = own_ref.shape[1]
    mine = (z // 2) == c
    odd = (z % 2) == 1
    own = jnp.where(odd, own_ref[1:2, :], own_ref[0:1, :])
    other = jnp.where(odd, other_ref[1:2, :], other_ref[0:1, :])
    ids = jnp.broadcast_to(jnp.where(mine, own, other).astype(f32), (LANES, frames)).astype(bf16)
    f = lax.broadcasted_iota(jnp.int32, (frames, frames), 0)
    p = lax.broadcasted_iota(jnp.int32, (frames, frames), 1)
    source = (
        ((p >> 4) & 3) * 128 + (x ^ (p >> 8)) * 64 + (c ^ ((p >> 7) & 1)) * 32 + (p & 15) * 2 + ((p >> 6) & 1)
    )
    chosen = jnp.where(f == source, 1.0, 0.0).astype(bf16)
    row_ref[...] = dot_nn(ids, chosen)[0:1, :]
    col_ref[...] = dot_tn(chosen, ids.T)[:, 0:1]


def slots_kernel(place, keep_ref, recv_ref, o_ref):
    c = place[1]
    for r in range(2):
        for q in range(2):
            o_ref[((c * 2) + r) * 2 + q] = keep_ref[r, q]
            o_ref[(((1 - c) * 2) + r) * 2 + q] = recv_ref[r, q]


def fetched(copies):
    for copy in copies:
        copy.start()
    return copies


def feed_copies(l, place, w_ref, buf, sems, width):
    steps = w_ref.shape[1] // LANES
    copies = []
    for i in range(2):
        at = pl.multiple_of((2 * (place[0] ^ i) + place[1]) * width, LANES)
        for k in range(steps):
            copies.append(
                pltpu.make_async_copy(
                    w_ref.at[l, pl.ds(k * LANES, LANES), :, pl.ds(at, width)],
                    buf.at[i, pl.ds(k * LANES, LANES)],
                    sems.at[i * steps + k],
                )
            )
    return fetched(copies)


def feed_parted(copies, buf, outs):
    depth, width = buf.shape[1], buf.shape[3]
    steps = depth // LANES
    parting = parting_matrix(2 * LANES)
    for i in range(2):
        for k in range(steps):
            copies[i * steps + k].wait()
        flat = buf.at[i].reshape(2 * depth, width)

        def body(k, carry, i=i, flat=flat):
            g = dot_nn(parting, flat[pl.ds(pl.multiple_of(2 * LANES * k, 2 * LANES), 2 * LANES), :]).astype(bf16)
            at = pl.ds(pl.multiple_of(LANES * k, LANES), LANES)
            outs[i][at, :] = g[:LANES]
            outs[2 + i][at, :] = g[LANES:]
            return carry

        lax.fori_loop(0, steps, body, 0)


def feed_weights_kernel(l, place, w_ref, *refs):
    outs, (buf, sems) = refs[:4], refs[4:]
    feed_parted(feed_copies(l, place, w_ref, buf, sems, outs[0].shape[1]), buf, outs)


def parting_matrix(size):
    r = lax.broadcasted_iota(jnp.int32, (size, size), 0)
    c = lax.broadcasted_iota(jnp.int32, (size, size), 1)
    return jnp.where(c == jnp.where(r < size // 2, 2 * r, 2 * r - size + 1), 1.0, 0.0).astype(bf16)


def later_weights_kernel(layers, bases, share, place, w_ref, p_ref, m_ref, b_ref, *refs):
    feeds = 4 * (layers - 1)
    feed_outs, outs = refs[:feeds], refs[feeds : feeds + 3 * layers]
    buf, wide, feed_sems, sems = refs[feeds + 3 * layers :]
    c, x = place[1], place[3]
    group = 2 * x + c
    width = m_ref.shape[2]
    start = ((group * share) // LANES) * LANES
    copies = []
    row = pl.multiple_of(group * share, 64)
    for l in range(layers):
        for i in range(3):
            at = pl.multiple_of(i * width + start, LANES)
            copies.append(pltpu.make_async_copy(p_ref.at[l, :, pl.ds(at, 256)], wide.at[l, i], sems.at[4 * l + i]))
        mix_ref = outs[3 * l + 1]
        copies.append(
            pltpu.make_async_copy(m_ref.at[l, pl.ds(row, share), :], mix_ref.at[pl.ds(0, share), :], sems.at[4 * l + 3])
        )
    fetched(copies)
    feed_in = [feed_copies(l, place, w_ref, buf.at[l - 1], feed_sems.at[l - 1], width) for l in range(1, layers)]
    odd = (group % 2) == 1

    def settle(v):
        lane = lane_of(v.shape)
        return jnp.where(lane < share, jnp.where(odd, pltpu.roll(v, 256 - 64, 1), v), 0.0)

    for l in range(layers):
        in_ref, mix_ref, both_ref = outs[3 * l : 3 * l + 3]
        mix_ref[share:, :] = jnp.zeros((256 - share, width), bf16)
        both_ref[...] = settle(b_ref[bases[l] : bases[l] + 2, pl.ds(pl.multiple_of(start, LANES), 256)])
        for i in range(3):
            copies[4 * l + i].wait()
            in_ref[:, i * 256 : (i + 1) * 256] = settle(wide[l, i].astype(f32)).astype(bf16)
        copies[4 * l + 3].wait()
    for l in range(1, layers):
        feed_parted(feed_in[l - 1], buf.at[l - 1], feed_outs[4 * (l - 1) : 4 * l])


def attend_kernel(base, hl0, hl1, hl2, hl3, w_ref, m_ref, bq_ref, segr, segc,
                  q_ref, k_ref, v_ref, at_ref, lse_ref, keep_ref, send_ref):
    t = hl0.shape[0]
    hl = jnp.concatenate([hl0[...], hl1[...], hl2[...], hl3[...]], axis=0)
    proj = dot_nn(hl, w_ref[...])
    q = ((proj[:, 0:256] + bq_ref[0:1, :]) * 0.125).astype(bf16)
    k = proj[:, 256:512].astype(bf16)
    v = (proj[:, 512:768] + bq_ref[1:2, :]).astype(bf16)
    q_ref[...] = q
    k_ref[...] = k
    v_ref[...] = v
    allowed = segc[...] == segr[...]
    lane = lane_of((1, LANES))
    parts = []
    for head in range(3):
        tile = head // 2
        cols = slice(tile * LANES, (tile + 1) * LANES)
        mine = (lane < 64) if head % 2 == 0 else (lane >= 64)
        qh = jnp.where(mine, q[:, cols], jnp.zeros((), bf16))
        s = dot_nt(qh, k[:, cols])
        s = jnp.where(allowed, s, masked_score)
        top = jnp.max(s, axis=-1, keepdims=True)
        e = jnp.exp(s - top)
        total = jnp.sum(e, axis=-1, keepdims=True)
        lse_ref[head] = top + jnp.log(total)
        p = (e * (1.0 / total)).astype(bf16)
        parts.append(dot_nn(p, v[:, cols]))
    att = jnp.concatenate([jnp.where(lane < 64, parts[0], parts[1]), parts[2]], axis=1).astype(bf16)
    at_ref[...] = att
    branch = dot_nn(att, m_ref[...]).astype(bf16)
    for dx in range(2):
        keep_ref[dx] = branch[2 * dx * t : (2 * dx + 1) * t]
        send_ref[dx] = branch[(2 * dx + 1) * t : (2 * dx + 2) * t]


def half_sum_kernel(a_ref, b_ref, own_ref, send_ref):
    own_ref[...] = a_ref[0].astype(f32) + b_ref[0].astype(f32)
    send_ref[...] = (a_ref[1].astype(f32) + b_ref[1].astype(f32)).astype(bf16)


def norm_kernel(gain_row, bias_row, shift_row, h_ref, a_ref, r_ref, g_ref, b_ref, o_ref, low_ref, n_ref, i_ref):
    v = h_ref[...] + (a_ref[...].astype(f32) + r_ref[...].astype(f32) + b_ref[bias_row : bias_row + 1, :])
    n, inv = normed(v)
    o = n * g_ref[gain_row : gain_row + 1, :] + b_ref[shift_row : shift_row + 1, :]
    o_ref[...] = o
    low_ref[...] = o.astype(bf16)
    n_ref[...] = n
    i_ref[...] = inv


def feed_kernel(row, place, f0, f1, u0, u1, d0, d1, b_ref, act_ref, slope_ref, own_ref, send_ref):
    t = f0.shape[0]
    first = jnp.concatenate([f0[...], f1[...]], axis=0)
    total = None
    for i, (u, d) in enumerate(((u0, d0), (u1, d1))):
        up = dot_nn(first, u[...]) + b_ref[pl.ds(row + 2 * (place[0] ^ i) + place[1], 1), :]
        act, slope = gelu_and_slope(up)
        act = act.astype(bf16)
        act_ref[i] = act
        slope_ref[i] = slope.astype(bf16)
        part = dot_nt(act, d[...])
        total = part if total is None else total + part
    own_ref[...] = total[:t]
    send_ref[...] = total[t:].astype(bf16)


def norm_back(g, n, inv, gain):
    scaled = g * gain
    m1 = jnp.mean(scaled, axis=-1, keepdims=True)
    m2 = jnp.mean(scaled * n, axis=-1, keepdims=True)
    return inv * (scaled - m1 - n * m2)


def norm_sums(g, n, d, o_ref):
    o_ref[0:1, :] = jnp.sum(g * n, axis=0, keepdims=True)
    o_ref[1:2, :] = jnp.sum(g, axis=0, keepdims=True)
    o_ref[2:3, :] = jnp.sum(d, axis=0, keepdims=True)
    o_ref[3:8, :] = jnp.zeros((5, o_ref.shape[1]), f32)


def norm_back_kernel(gain_row, count, *refs):
    given, (g_ref, n_ref, i_ref, d_ref, low_ref, s_ref) = refs[:count], refs[count:]
    g = given[0][...].astype(f32)
    for r in given[1:]:
        g = g + r[...].astype(f32)
    n = n_ref[...]
    d = norm_back(g, n, i_ref[...], g_ref[gain_row : gain_row + 1, :])
    d_ref[...] = d
    low_ref[...] = d.astype(bf16)
    norm_sums(g, n, d, s_ref)


def stem_norm_back_kernel(width, count, place, *refs):
    given, (g_ref, n_ref, i_ref, keep_ref, send_ref, s_ref) = refs[:count], refs[count:]
    z, x = place[2], place[3]
    g = given[0][...].astype(f32)
    for r in given[1:]:
        g = g + r[...].astype(f32)
    n = n_ref[...]
    d = norm_back(g, n, i_ref[...], g_ref[0:1, :])
    norm_sums(g, n, d, s_ref)
    t = d.shape[0] // 2
    for a in range(2):
        part = d[a * t : (a + 1) * t]
        cols = [part[:, LANES * v : LANES * (v + 1)] for v in range(part.shape[1] // LANES)]
        for j in range(8):
            blk = piece_of(cols, j, width).astype(bf16)
            to_x(keep_ref, send_ref, x, j % 2, (j // 2) ^ z, (slice(None), slice(a * LANES, (a + 1) * LANES)), blk)


def to_x(keep_ref, send_ref, x, xi, rel, where, blk):
    @pl.when(x == xi)
    def _():
        keep_ref[(rel, *where)] = blk

    @pl.when(x != xi)
    def _():
        send_ref[(rel, *where)] = blk


def along_z_kernel(a_ref, b_ref, keep_ref, send_ref):
    for rel in range(4):
        out = send_ref if rel % 2 else keep_ref
        out[rel // 2, 0] = a_ref[rel]
        out[rel // 2, 1] = b_ref[rel]


def onward_kernel(keep_ref, recv_ref, send_ref):
    send_ref[0] = keep_ref[1]
    send_ref[1] = recv_ref[1]


def by_z(keep_ref, near_ref, far_ref):
    return keep_ref.at[0], near_ref.at[0], far_ref.at[0], far_ref.at[1]


def feed_back_kernel(e0, e1, u0, u1, d0, d1, slope_ref, dup_ref, own_ref, send_ref, bias_ref):
    t = e0.shape[0]
    d2 = jnp.concatenate([e0[...], e1[...]], axis=0)
    total = None
    for i, (u, d) in enumerate(((u0, d0), (u1, d1))):
        dup = dot_nn(d2, d[...]) * slope_ref[i].astype(f32)
        bias_ref[i : i + 1, :] = jnp.sum(dup, axis=0, keepdims=True)
        dup = dup.astype(bf16)
        dup_ref[i] = dup
        part = dot_nt(dup, u[...])
        total = part if total is None else total + part
    bias_ref[2:8, :] = jnp.zeros((6, bias_ref.shape[1]), f32)
    own_ref[...] = total[:t]
    send_ref[...] = total[t:].astype(bf16)


def feed_grad_kernel(place, f0, f1, e0, e1, dup_ref, act_ref, keep_ref, send_ref):
    z, x = place[2], place[3]
    width = keep_ref.shape[-2] // 2
    for kind, (a, b, right) in enumerate(((f0, f1, dup_ref), (e0, e1, act_ref))):
        left = jnp.concatenate([a[...], b[...]], axis=0)
        for i in range(2):
            g = dot_tn(left, right[i]).astype(bf16)
            for j in range(8):
                zi, xi = j // 2, j % 2
                rz, rx = zi ^ z, xi ^ x
                blk = g[j * width : (j + 1) * width]
                (send_ref if i else keep_ref)[rx, rz % 2, rz // 2, kind * width : (kind + 1) * width] = blk


def halves_kernel(count, *refs):
    given, made = refs[: 2 * count], refs[2 * count :]
    for i in range(count):
        a, b = given[2 * i], given[2 * i + 1]
        for h in range(2):
            out = made[2 * i + h]
            lead = out.shape[:-2]
            many = math.prod(lead)
            if many == 1:
                out[...] = (a[h].astype(f32) + b[h].astype(f32)).astype(out.dtype)
                continue

            def body(k, carry, a=a, b=b, h=h, out=out, lead=lead):
                at = []
                for size in reversed(lead):
                    at.insert(0, lax.rem(k, size))
                    k = k // size
                at = tuple(at)
                out[at] = (a[(h, *at)].astype(f32) + b[(h, *at)].astype(f32)).astype(out.dtype)
                return carry

            lax.fori_loop(0, many, body, 0)


def one_kernel(a, b, o):
    o[...] = (a[...].astype(f32) + b[...].astype(f32)).astype(o.dtype)


def attend_back_kernel(e0, e1, e2, e3, q_ref, k_ref, v_ref, lse_ref, w_ref, m_ref, segr, segc,
                       dc_ref, keep_ref, send_ref, bias_ref, da_ref, dq_ref, dk_ref, dv_ref):
    t = e0.shape[0]
    d1 = jnp.concatenate([e0[...], e1[...], e2[...], e3[...]], axis=0)
    da_ref[...] = dot_nt(d1, m_ref[...]).astype(bf16)
    lane = lane_of((1, LANES))
    for ref in (dq_ref, dk_ref, dv_ref):
        ref[...] = jnp.zeros_like(ref)

    def one_head(head, carry):
        cols = pl.ds(pl.multiple_of((head // 2) * LANES, LANES), LANES)
        mine = (lane // 64) == lax.rem(head, 2)
        zero = jnp.zeros((), bf16)
        qh = jnp.where(mine, q_ref[:, cols], zero)
        dah = jnp.where(mine, da_ref[:, cols], zero)
        k = k_ref[:, cols]
        s = dot_nt(qh, k)
        p = jnp.where(segc[...] == segr[...], jnp.exp(s - lse_ref[head]), 0.0)
        dp = dot_nt(dah, v_ref[:, cols])
        delta = jnp.sum(p * dp, axis=-1, keepdims=True)
        ds = (p * (dp - delta)).astype(bf16)
        dq_ref[:, cols] += dot_nn(ds, jnp.where(mine, k, zero))
        dk_ref[:, cols] += dot_tn(ds, qh)
        dv_ref[:, cols] += dot_tn(p.astype(bf16), dah)
        return carry

    lax.fori_loop(0, 3, one_head, 0)
    tiles = [slice(0, LANES), slice(LANES, 2 * LANES)]
    dq = [dq_ref[:, c].astype(bf16).astype(f32) * 0.125 for c in tiles]
    dk = [dk_ref[:, c].astype(bf16).astype(f32) for c in tiles]
    dv = [dv_ref[:, c].astype(bf16).astype(f32) for c in tiles]
    wide = jnp.concatenate(dq + dk + dv, axis=1).astype(bf16)
    bias_ref[0:1, :] = jnp.concatenate([jnp.sum(d, axis=0, keepdims=True) for d in dq], axis=1)
    bias_ref[1:2, :] = jnp.concatenate([jnp.sum(d, axis=0, keepdims=True) for d in dv], axis=1)
    bias_ref[2:8, :] = jnp.zeros((6, 256), f32)
    dense = [dq[0], jnp.where(lane < 64, dq[1], pltpu.roll(dk[1], 64, 1)), dk[0], dv[0], dv[1]]
    dc_ref[...] = jnp.concatenate(dense, axis=1).astype(bf16)
    out = dot_nt(wide, w_ref[...]).astype(bf16)
    for dx in range(2):
        keep_ref[dx] = out[2 * dx * t : (2 * dx + 1) * t]
        send_ref[dx] = out[(2 * dx + 1) * t : (2 * dx + 2) * t]


def attend_grad_kernel(place, hl0, hl1, hl2, hl3, e0, e1, e2, e3, at_ref, dc_ref, keep_ref, send_ref):
    z, x = place[2], place[3]
    hl = jnp.concatenate([hl0[...], hl1[...], hl2[...], hl3[...]], axis=0)
    d1 = jnp.concatenate([e0[...], e1[...], e2[...], e3[...]], axis=0)
    width = keep_ref.shape[2]

    def put(zi, tile, blk):
        rel = zi ^ z

        @pl.when((zi ^ z) % 2 == 0)
        def _():
            keep_ref[rel // 2, tile] = blk

        @pl.when((zi ^ z) % 2 == 1)
        def _():
            send_ref[rel // 2, tile] = blk

    g = dot_tn(hl, dc_ref[...]).astype(bf16)
    for j in range(8):
        zi, xi = j // 2, j % 2
        for t in range(5):
            put(zi, (xi ^ x) * 5 + t, g[j * width : (j + 1) * width, t * LANES : (t + 1) * LANES])
    m = dot_tn(at_ref[...], d1)
    lane = lane_of((1, LANES))
    for xp in range(2):
        t = [m[xp * width : (xp + 1) * width, i * LANES : (i + 1) * LANES] for i in range(6)]
        first = [t[0], t[3], jnp.where(lane < 64, t[1], pltpu.roll(t[4], 64, 1))]
        second = [t[2], t[5], jnp.where(lane < 64, pltpu.roll(t[1], 64, 1), t[4])]
        for cp, tiles in enumerate((first, second)):
            for i, tile in enumerate(tiles):
                put(2 * xp + cp, 10 + i, tile.astype(bf16))


def pick_kernel(layers, place, *refs):
    own, came = refs[:layers], refs[layers]
    stay_ref, move_ref = refs[layers + 1 :]
    y, x = place[0], place[3]
    lane = lane_of((1, LANES))
    for l in range(layers):
        mine = [own[l][t].astype(f32) for t in range(5)]
        other = [came[l, t].astype(f32) for t in range(5)]

        def blocks(t):
            return [(t[0], t[1]), (t[2], pltpu.roll(t[1], 64, 1)), (t[3], t[4])]

        first = x == 0
        lowb, highb = blocks(mine), blocks(other)
        low_g = [tuple(jnp.where(first, a, b) for a, b in zip(m, o)) for m, o in zip(lowb, highb)]
        high_g = [tuple(jnp.where(first, b, a) for a, b in zip(m, o)) for m, o in zip(lowb, highb)]
        upper = [low_g[0], high_g[0], low_g[1]]
        lower = [high_g[1], low_g[2], high_g[2]]
        for i in range(3):
            for j in range(2):
                a, b = upper[i][j], lower[i][j]
                stay_ref[l, i, j] = jnp.where(y == 0, a, b).astype(bf16)
                move_ref[l, i, j] = jnp.where(y == 0, b, a).astype(bf16)
        m = [own[l][10 + t].astype(f32) for t in range(3)]
        stay_ref[l, 3, 0] = jnp.where(y == 0, m[0], m[1]).astype(bf16)
        move_ref[l, 3, 0] = jnp.where(y == 0, m[1], m[0]).astype(bf16)
        stay_ref[l, 3, 1] = m[2].astype(bf16)
        move_ref[l, 3, 1] = m[2].astype(bf16)


def settle_kernel(layers, place, a, b, part_ref, swap_ref, mix_ref):
    c = place[1]
    for l in range(layers):
        v = [[a[l, i, j].astype(f32) + b[l, i, j].astype(f32) for j in range(2)] for i in range(4)]
        for j in range(2):
            part_ref[l, 0, j] = jnp.where(c == 0, v[0][j], v[1][j]).astype(bf16)
            part_ref[l, 1, j] = jnp.where(c == 0, v[1][j], v[2][j]).astype(bf16)
            swap_ref[l, j] = jnp.where(c == 0, v[2][j], v[0][j]).astype(bf16)
            mix_ref[l, j] = v[3][j].astype(bf16)


def step_of(factor, g, m, a, w):
    moment = momentum_decay * m + g
    new = w.astype(f32) - factor * (g + momentum_decay * moment)
    return moment, average_decay * a + (1.0 - average_decay) * new, new


def tile_from(win, t, odd):
    cols = [win[:, i * LANES : (i + 1) * LANES].astype(f32) for i in (t, t + 1) if (i + 1) * LANES <= win.shape[1]]
    turned = [pltpu.roll(v, 64, 1) for v in cols]
    shifted = turned[0] if len(cols) == 1 else jnp.where(lane_of(cols[0].shape) < 64, turned[0], turned[1])
    return jnp.where(odd, shifted, cols[0])


def stepped(factor, l, at, t, m_ref, a_ref, w, outs):
    to = at + t.shape[1]
    for o, v in zip(outs, step_of(factor, t, m_ref[l, :, at:to], a_ref[l, :, at:to], w[:, : t.shape[1]])):
        o[l, :, at:to] = v
    return to


def window_copy(w_ref, win, sems, place, step, span):
    rows = win.shape[1]
    row = (2 * place[2] + place[3]) * rows
    start = (((2 * place[0] + place[1]) * step) // LANES) * LANES
    return fetched(
        [
            pltpu.make_async_copy(
                w_ref.at[l, pl.ds(pl.multiple_of(row, 32), rows), pl.ds(pl.multiple_of(start, LANES), span)],
                win.at[l],
                sems.at[l],
            )
            for l in range(win.shape[0])
        ]
    )


def olds_kernel(layers, gw, place, s_ref, p_ref, m_ref, f_ref, so, po, mo, fo, win_s, win_p, win_m, win_f, sems):
    y, c, z, x = (place[i] for i in range(4))
    seq_i, row_i = 2 * z + x, 2 * y + c
    rows, width = win_f.shape[1], win_f.shape[3]
    column = seq_i * 2 * gw
    start = jnp.minimum(column // LANES, 4) * LANES
    taps = win_s.shape[0]
    stem = pltpu.make_async_copy(
        s_ref.at[pl.ds(pl.multiple_of(row_i * taps, LANES), taps), pl.ds(pl.multiple_of(start, LANES), 256)],
        win_s, sems.at[0],
    )
    feeds = [
        pltpu.make_async_copy(
            f_ref.at[l, pl.ds(seq_i * rows, rows), :, pl.ds(pl.multiple_of(row_i * width, LANES), width)],
            win_f.at[l], sems.at[1 + l],
        )
        for l in range(layers)
    ]
    fetched([stem, *feeds])
    ins = window_copy(p_ref, win_p, sems.at[pl.ds(1 + layers, layers)], place, 576, 640)
    mixes = window_copy(m_ref, win_m, sems.at[pl.ds(1 + 2 * layers, layers)], place, 192, 256)
    r = lax.broadcasted_iota(jnp.int32, (LANES, 256), 0)
    k = lax.broadcasted_iota(jnp.int32, (LANES, 256), 1)
    chosen = jnp.where(k == r + (column - start), 1.0, 0.0).astype(bf16)
    parting = parting_matrix(2 * rows)
    odd = c == 1
    stem.wait()
    so[...] = dot_nt(chosen, win_s[...])[0 : 2 * gw].astype(bf16)
    for l in range(layers):
        feeds[l].wait()
        fo[l] = dot_nn(parting, win_f.at[l].reshape(2 * rows, width)[...]).astype(bf16)
        ins[l].wait()
        for t in range(5):
            po[l, :, t * LANES : (t + 1) * LANES] = tile_from(win_p[l], t, odd).astype(bf16)
        mixes[l].wait()
        for t in range(2):
            mo[l, :, t * LANES : (t + 1) * LANES] = tile_from(win_m[l], t, odd).astype(bf16)


def projection_step_kernel(factor, place, w_ref, part_ref, swap_ref, m_ref, a_ref, *outs):
    lane = lane_of((1, LANES))
    for l in range(m_ref.shape[0]):
        b0 = [part_ref[l, 0, j].astype(f32) for j in range(2)]
        b2 = [part_ref[l, 1, j].astype(f32) for j in range(2)]
        b1 = [pltpu.roll(swap_ref[l, j].astype(f32), 64, 1) for j in range(2)]
        tiles = [b0[0], jnp.where(lane < 64, b0[1], b1[0]), jnp.where(lane < 64, b1[0], b1[1]), b2[0], b2[1][:, :64]]
        at = 0
        for i, t in enumerate(tiles):
            at = stepped(factor, l, at, t, m_ref, a_ref, w_ref[l, :, i * LANES : (i + 1) * LANES], outs)


def mixing_step_kernel(factor, place, w_ref, mix_ref, m_ref, a_ref, *outs):
    y, c = place[0], place[1]
    lane = lane_of((1, LANES))
    for l in range(m_ref.shape[0]):
        full, half = mix_ref[l, 0].astype(f32), mix_ref[l, 1].astype(f32)
        turned = pltpu.roll(full, 64, 1)
        half = jnp.where(y == 0, half, pltpu.roll(half, 64, 1))
        tiles = [
            jnp.where(c == 0, full, jnp.where(lane < 64, half, turned)),
            jnp.where(c == 0, half, turned)[:, :64],
        ]
        at = 0
        for i, t in enumerate(tiles):
            at = stepped(factor, l, at, t, m_ref, a_ref, w_ref[l, :, i * LANES : (i + 1) * LANES], outs)


def feed_step_kernel(factor, place, w_ref, *refs):
    layers = w_ref.shape[0]
    parts, (m_ref, a_ref), outs = refs[: 2 * layers], refs[2 * layers : 2 * layers + 2], refs[2 * layers + 2 :]
    rows = m_ref.shape[1]
    for l in range(layers):
        for kind in range(2):
            a, b = parts[2 * l], parts[2 * l + 1]

            def body(k, carry, l=l, kind=kind, a=a, b=b):
                r = pl.ds(pl.multiple_of(k * 32, 32), 32)
                both = pl.ds(pl.multiple_of(kind * rows + k * 32, 32), 32)
                g = a[both, :].astype(f32) + b[both, :].astype(f32)
                w = w_ref[l, both, :]
                for o, v in zip(outs, step_of(factor, g, m_ref[l, r, kind, :], a_ref[l, r, kind, :], w)):
                    o[l, r, kind, :] = v
                return carry

            lax.fori_loop(0, rows // 32, body, 0)


def stem_step_kernel(factor, gw, place, w_ref, p_ref, r_ref, m_ref, a_ref, *outs):
    count = p_ref.shape[0] // gw
    lane = lane_of((gw, LANES))
    for group in range(2):
        pieces = []
        for k in range(count):
            rows_k = slice(k * gw, (k + 1) * gw)
            v = p_ref[rows_k, :].astype(f32) + r_ref[rows_k, :].astype(f32)
            v = v if group == 0 else pltpu.roll(v, LANES - gw, 1)
            pieces.append(jnp.where(lane < gw, v, 0.0))
        mine = slice(group * gw, (group + 1) * gw)
        for i, t in enumerate(tiles_of(pieces, gw)):
            cols = slice(i * LANES, (i + 1) * LANES)
            for o, v in zip(outs, step_of(factor, t, m_ref[mine, cols], a_ref[mine, cols], w_ref[mine, cols])):
                o[mine, cols] = v


def smalls_kernel(layers, ff_rows, gains, width, head_share, place, *refs):
    norms, ups, atts = refs[: 2 * layers + 1], refs[2 * layers + 1 : 3 * layers + 1], refs[3 * layers + 1 : 4 * layers + 1]
    keep_ref, send_ref, all_ref = refs[4 * layers + 1 :]
    y, c, z, x = (place[i] for i in range(4))
    all_ref[...] = jnp.zeros_like(all_ref)
    all_ref[0:1, :] = norms[0][0:1, :]
    all_ref[gains + 1 : gains + 2, :] = norms[0][1:2, :]
    for l in range(layers):
        base = gains + 2 + l * (6 + ff_rows)
        for k, (gain, shift, plain) in enumerate(((1, 3, 2), (2, 5, 4))):
            s = norms[1 + 2 * l + k]
            all_ref[gain + 2 * l : gain + 2 * l + 1, :] = s[0:1, :]
            all_ref[base + shift : base + shift + 1, :] = s[1:2, :]
            all_ref[base + plain : base + plain + 1, :] = s[2:3, :]
        for ry in range(2):
            all_ref[pl.ds(base + 6 + 2 * (y ^ ry) + c, 1), :] = ups[l][ry : ry + 1, :]
        for group in range(4):

            @pl.when(2 * x + c == group)
            def _(l=l, base=base, group=group):
                for i in range(2):
                    pieces = [jnp.zeros((1, LANES), f32)] * (width // 64)
                    for h in range(3):
                        t = atts[l][i : i + 1, (h // 2) * LANES : (h // 2 + 1) * LANES]
                        t = t if h % 2 == 0 else pltpu.roll(t, 64, 1)
                        pieces[3 * group + h] = jnp.where(lane_of(t.shape) < 64, t, 0.0)
                    all_ref[base + i : base + i + 1, :] = jnp.concatenate(tiles_of(pieces, 64), axis=1)

    whole = all_ref[...]
    cols = [whole[:, LANES * v : LANES * (v + 1)] for v in range(width // LANES)]
    for j in range(8):
        blk = piece_of(cols, j, width // 8)
        rel = (j // 2) ^ z
        at = (rel % 2) * 2 + rel // 2

        @pl.when(x == j % 2)
        def _(blk=blk, at=at):
            keep_ref[at] = blk

        @pl.when(x != j % 2)
        def _(blk=blk, at=at):
            send_ref[at] = blk


def small_total_kernel(row, a_ref, r_ref, b_ref, o_ref):
    total = a_ref[...] + r_ref[...]
    o_ref[...] = total
    o_ref[row : row + 1, :] = total[row : row + 1, :] + b_ref[0:1, :]


def encoded_split_kernel(place, x_ref, keep_ref, send_ref):
    z = place[2]
    for rel in range(4):
        out = send_ref if rel % 2 else keep_ref
        for a in range(2):
            at = pl.multiple_of(a * 64 + (z ^ rel) * 16, 16)
            out[rel // 2, a * 16 : a * 16 + 16, :] = x_ref[pl.ds(at, 16), :]


def encoded_route_kernel(place, own_ref, near_ref, far_ref, keep_ref, send_ref):
    c, z = place[1], place[2]
    for rel, src in enumerate(by_z(own_ref, near_ref, far_ref)):
        row = z ^ rel
        mine = (row // 2) == c

        @pl.when(mine)
        def _(src=src, row=row):
            keep_ref[row % 2] = src[...]

        @pl.when(jnp.logical_not(mine))
        def _(src=src, row=row):
            send_ref[row % 2] = src[...]


def encoded_join_kernel(place, keep_ref, recv_ref, o_ref, mixed):
    c = place[1]
    rows, toks, width = o_ref.shape
    for r in range(rows):
        for v in range(width // LANES):
            cols = slice(v * LANES, (v + 1) * LANES)
            for rel, src in enumerate((keep_ref, recv_ref)):
                for a in range(2):
                    at = v * toks + (c ^ rel) * 32 + a
                    mixed[pl.ds(at, 16, stride=2), :] = src[r, a * 16 : a * 16 + 16, cols].astype(f32)
            o_ref[r, :, cols] = mixed[v * toks : (v + 1) * toks, :]


def take_kernel(place, own_ref, near_ref, far_ref, keep_ref, send_ref):
    c, z, x = place[1], place[2], place[3]
    for rel, src in enumerate(by_z(own_ref, near_ref, far_ref)):
        row = z ^ rel
        mine = (row // 2) == c
        for h in range(2):

            @pl.when(mine)
            def _(src=src, row=row, h=h):
                keep_ref[row % 2, x ^ h] = src[h]

            @pl.when(jnp.logical_not(mine))
            def _(src=src, row=row, h=h):
                send_ref[row % 2, x ^ h] = src[h]


def stem_slope_kernel(rows, place, keep_ref, recv_ref, pre_ref, low_ref, ds_ref, bias_ref):
    c = place[1]
    for r in range(rows):
        for zf in range(4):
            for xq in range(2):
                for rel, src in enumerate((keep_ref, recv_ref)):
                    u = pl.multiple_of(((zf * 2 + xq) * 2 + (c ^ rel)) * 16, 16)
                    ds_ref[r, pl.ds(u, 16), :] = src[r, xq, zf * 16 : zf * 16 + 16, :]
    total = None
    for r in range(rows):
        dpre = ds_ref[r].astype(f32) * gelu_and_slope(pre_ref[r])[1]
        part = jnp.sum(dpre, axis=0, keepdims=True)
        total = part if total is None else total + part
        low_ref[r] = dpre.astype(bf16)
    bias_ref[0:1, :] = total[:, 0:LANES] + total[:, LANES : 2 * LANES]
    bias_ref[1:8, :] = jnp.zeros((7, LANES), f32)


def stem_grad_kernel(rows, taps, gw, place, ph_ref, low_ref, keep_ref, send_ref):
    n = low_ref.shape[1]
    y, c = place[0], place[1]
    left = jnp.concatenate([low_ref[r] for r in range(rows)], axis=0).T
    lane = lane_of((gw, LANES))
    per = taps // 4
    for rc, out in enumerate((keep_ref, send_ref)):
        for ry in range(2):
            block = (y ^ ry) * 2 + (c ^ rc)

            def win(i):
                at = pl.multiple_of((block + i // 16) * 16, 16)
                return ph_ref[i % 16, :, pl.ds(at, n), :].reshape(rows * n, 2 * LANES)

            def save(k, t, out=out, ry=ry):
                out[ry, k * gw : (k + 1) * gw, :] = jnp.where(lane < gw, t[0:gw], t[gw : 2 * gw]).astype(bf16)

            held = None
            for i in range(per // 2 + 1):
                if i < per // 2:
                    g = dot_nn(left, win(i))
                    cross = g[LANES:, 0:LANES]
                else:
                    cross = dot_nn(left[LANES:], win(i)[:, 0:LANES])
                if held is not None:
                    save(2 * i - 1, held + cross)
                if i < per // 2:
                    save(2 * i, g[0:LANES, 0:LANES] + g[LANES:, LANES:])
                    held = g[0:LANES, LANES:]


def stem_input_grad_kernel(rows, half, place, low_ref, ds_ref, w_ref, keep_ref, send_ref, qf, ph, acc):
    n = low_ref.shape[1]
    span = n + half
    for r in range(rows):
        qf[r, 0 : half // 2, :] = jnp.zeros((half // 2, 2 * LANES), f32)
        qf[r, half // 2 + n :, :] = jnp.zeros((half // 2, 2 * LANES), f32)
        qf[r, half // 2 : half // 2 + n, :] = low_ref[r].astype(f32)
    for p in range(16):
        m = span if p == 0 else span - 16
        for r in range(rows):
            ph[p, r, 0:m, :] = qf[r, p : p + m, :].astype(bf16)
    acc[...] = jnp.zeros_like(acc)

    def body(i, carry):
        left, upper, lower = [], [], []
        for t in range(5):
            m = i * 5 + t
            here, before, after = w_ref[2 * half + 1 - 2 * m], w_ref[2 * half - 2 * m], w_ref[2 * half + 2 - 2 * m]
            upper += [here, before]
            lower += [after, here]
            left.append(window(ph, m, rows, n))
        right = jnp.concatenate([jnp.concatenate(upper, 1), jnp.concatenate(lower, 1)], 0)
        acc[...] += dot_nt(jnp.concatenate(left, 1), right)
        return carry

    lax.fori_loop(0, (half + 1) // 5, body, 0)
    per = n // 8
    for r in range(rows):
        g = (acc[r * n : (r + 1) * n, :] + ds_ref[r].astype(f32)).astype(bf16)
        for j in range(8):
            to_x(keep_ref, send_ref, place[3], j % 2, (j // 2) ^ place[2], (r,), g[j * per : (j + 1) * per, :])


def join_kernel(width, place, own_ref, near_ref, far_ref, o_ref, mixed, by_channel):
    z, x = place[2], place[3]
    rows, per = own_ref.shape[2], own_ref.shape[3]
    for rel, src in enumerate(by_z(own_ref, near_ref, far_ref)):
        for h in range(2):
            by_channel[(z ^ rel) * 2 + (x ^ h)] = src[h]
    for r in range(rows):
        for a in range(2):
            pieces = [by_channel[j, r, :, a * LANES : (a + 1) * LANES].astype(f32) for j in range(8)]
            for v, col in enumerate(tiles_of(pieces, width)):
                mixed[pl.ds(v * 2 * per + a, per, stride=2), :] = col
        for v in range(o_ref.shape[2] // LANES):
            o_ref[r, :, v * LANES : (v + 1) * LANES] = mixed[v * 2 * per : (v + 1) * 2 * per, :]


def swapped(v, axis):
    return lax.ppermute(v, axis, [(0, 1), (1, 0)])


def across(v, axis, bit):
    count = lax.axis_size(axis)
    return lax.ppermute(v, axis, [(i, i ^ bit) for i in range(count)])


def one_sum(a, b):
    return whole_call(one_kernel, [sds(a.shape, a.dtype)], [a, b])[0]


def local_rows(
    features, cotangent, segments, stem_weight, projection_weight, mixing_weight,
    feedforward_weight, norm_gains, biases, *state,
):
    rows, toks, width = features.shape
    yi, ci, zi, xi = (lax.axis_index(a) for a in ("y", "c", "z", "x"))
    place = jnp.stack([yi, ci, zi, xi]).astype(jnp.int32)
    seq_i, row_i = zi * 2 + xi, yi * 2 + ci
    seq = ("z", "x")
    blocks = 8
    share = width // blocks
    gw = width // GROUPS
    frames = toks * blocks
    half = KERNEL // 2
    layers = projection_weight.shape[0]
    ff_rows = feedforward_weight.shape[3] // width
    head_share = width // 4
    group = 2 * xi + ci
    t = rows * toks

    stem_share = jnp.pad(
        lax.dynamic_slice_in_dim(stem_weight, seq_i * share, share, 1), ((0, 0), (0, LANES - share))
    )

    steps = width // LANES
    square = sds((width, width), bf16)
    *feed_first, feed_there = whole_call(
        functools.partial(feed_weights_kernel, 0), [square] * 4, [place, feedforward_weight],
        scalars=1, far=(1,), token=True, vmem=FAR_BYTES,
        scratch=[pltpu.VMEM((2, width, 2, width), bf16), pltpu.SemaphoreType.DMA((2 * steps,))],
    )

    (sent,) = whole_call(
        functools.partial(split_kernel, blocks, share), [sds((blocks, rows, toks, LANES), bf16)], [features]
    )
    mine = lax.all_to_all(sent, seq, 0, 0, tiled=True)
    conv_bias = jnp.pad(
        lax.dynamic_slice(biases, (0, seq_i * share), (1, share)), ((0, 0), (0, LANES - share))
    )
    n = frames // 2
    exchange = sds((rows, 2, 64, 2 * LANES), bf16)
    tap_scratch = pltpu.VMEM((KERNEL + 3, LANES, LANES), bf16)
    phased = (16, rows, (frames + 2 * half) // 2, 2 * LANES)
    row_scratch = pltpu.VMEM((rows * (frames + 2 * half) + 8, LANES), f32)
    pre_act, kept, away = whole_call(
        functools.partial(conv_kernel, rows, frames, half, gw),
        [sds((rows, n, 2 * LANES), f32), exchange, exchange],
        [place, mine, stem_share, conv_bias],
        after=[feed_there],
        scalars=1,
        scratch=[pltpu.VMEM(phased, bf16), row_scratch, pltpu.VMEM((rows * n, 2 * LANES), f32), tap_scratch],
        vmem=WIDE_BYTES,
    )
    (slots,) = whole_call(
        slots_kernel, [sds((blocks, 64, 2 * LANES), bf16)], [place, kept, swapped(away, "c")], scalars=1
    )
    *later, later_there = whole_call(
        functools.partial(later_weights_kernel, layers, [2 + l * (6 + ff_rows) for l in range(layers)], head_share),
        [square] * (4 * (layers - 1)) + [square, sds((256, width), bf16), sds((2, 256), f32)] * layers,
        [place, feedforward_weight, projection_weight, mixing_weight, biases],
        scalars=1, far=(1, 2, 3), token=True, vmem=FAR_BYTES, after=[slots],
        scratch=[
            pltpu.VMEM((layers - 1, 2, width, 2, width), bf16),
            pltpu.VMEM((layers, 3, width, 256), bf16),
            pltpu.SemaphoreType.DMA((layers - 1, 2 * steps)),
            pltpu.SemaphoreType.DMA((4 * layers,)),
        ],
    )
    feed_w = [feed_first, *(later[4 * i : 4 * i + 4] for i in range(layers - 1))]
    attend_w = [later[4 * (layers - 1) + 3 * l :][:3] for l in range(layers)]
    joined = lax.all_to_all(slots, seq, 0, 0, tiled=True)
    wide = sds((t, width), f32)
    thin = sds((t, width), bf16)
    column = sds((t, 1), f32)
    hidden, hidden_low, normed_stem, inverse_stem = whole_call(
        functools.partial(stem_norm_kernel, share), [wide, thin, wide, column], [joined, norm_gains, biases],
        after=[later_there],
    )

    def gathered(v):
        over_c = swapped(v, "c")
        over_x = swapped(v, "x")
        return [v, over_c, over_x, swapped(over_x, "c")]

    saved = []
    segments_other = swapped(segments, "c")
    quarter_row = sds((32, width), bf16)
    two = sds((2, t, width), bf16)
    full = 4 * t
    for l in range(layers):
        base = 2 + l * (6 + ff_rows)
        in_w, mix_w, both_b = attend_w[l]
        ups, downs = feed_w[l][:2], feed_w[l][2:]
        hl = gathered(hidden_low)
        before = []
        if l == 0:
            seg_row, seg_col = whole_call(
                segments_kernel, [sds((1, frames), f32), sds((frames, 1), f32)], [place, segments, segments_other],
                scalars=1, after=[hidden_low],
            )
            stay, move, cot_there = whole_call(
                cotangent_split_kernel, [sds((rows, 32, width), bf16)] * 2, [place, cotangent],
                scalars=1, after=[hidden_low], token=True,
                scratch=[pltpu.VMEM((width // LANES * toks + 8, LANES), f32)],
            )
            before = [cot_there]
        elif l == 1:
            cot, cot_there = whole_call(
                cotangent_join_kernel, [sds((t, width), bf16)],
                [place, routed[0], *(across(routed[rel], "z", rel) for rel in range(1, 4))],
                scalars=1, after=[hidden_low], token=True,
            )
            before = [cot_there]
        q, k, v, att, lse, keep, send = whole_call(
            functools.partial(attend_kernel, base),
            [sds((full, 256), bf16)] * 4 + [sds((3, full, 1), f32), two, two],
            hl + [in_w, mix_w, both_b, seg_row, seg_col],
            after=before,
        )
        own, pass_on = whole_call(half_sum_kernel, [wide, thin], [keep, swapped(send, "c")])
        rest = swapped(pass_on, "x")
        before = []
        if l == 0:
            *routed, cot_there = whole_call(
                cotangent_route_kernel, [quarter_row] * 4, [place, stay, swapped(move, "c")],
                scalars=1, after=[pass_on], token=True,
            )
            before = [cot_there]
        first, first_low, n1, i1 = whole_call(
            functools.partial(norm_kernel, 1 + 2 * l, base + 2, base + 3),
            [wide, thin, wide, column],
            [hidden, own, rest, norm_gains, biases],
            after=before,
        )
        first_other = swapped(first_low, "c")
        act, slope, own, send = whole_call(
            functools.partial(feed_kernel, base + 6),
            [sds((2, 2 * t, width), bf16)] * 2 + [wide, thin],
            [place, first_low, first_other, *ups, *downs, biases],
            scalars=1,
        )
        hidden, hidden_low, n2, i2 = whole_call(
            functools.partial(norm_kernel, 2 + 2 * l, base + 4, base + 5),
            [wide, thin, wide, column],
            [first, own, swapped(send, "c"), norm_gains, biases],
        )
        saved.append((in_w, mix_w, ups, downs, hl, q, k, v, att, lse, n1, i1, first_low, first_other, act, slope, n2, i2))

    encoded_low = hidden_low
    sums = sds((8, width), f32)
    terms = [cot]
    norm_sum = [None] * norm_gains.shape[0]
    up_sum, att_sum = [None] * layers, [None] * layers
    feed, att_parts = [None] * layers, [None] * layers
    parted = sds((2, 2, 2, 2 * share, width), bf16)
    tiles = sds((13, share, LANES), bf16)
    tiles_z = sds((2, 13, share, LANES), bf16)

    def send_on(parts, after):
        outs, operands = [], []
        for keep, recv, _ in parts:
            outs += [sds(keep.shape[1:], keep.dtype)] * 2
            operands += [keep, recv]
        made = whole_call(
            functools.partial(halves_kernel, len(parts)), outs, operands, after=after, token=True
        )
        return [(made[2 * i], how(made[2 * i + 1])) for i, (_, _, how) in enumerate(parts)], made[-1]

    over_x, over_y = (lambda v: swapped(v, "x")), (lambda v: swapped(v, "y"))
    over_z1, over_z2 = (lambda v: across(v, "z", 1)), (lambda v: across(v, "z", 2))
    before = []
    for l in reversed(range(layers)):
        base = 2 + l * (6 + ff_rows)
        in_w, mix_w, ups, downs, hl, q, k, v, att, lse, n1, i1, first_low, first_other, act, slope, n2, i2 = saved[l]
        d2, d2_low, norm_sum[2 + 2 * l] = whole_call(
            functools.partial(norm_back_kernel, 2 + 2 * l, len(terms)), [wide, thin, sums], terms + [norm_gains, n2, i2],
            after=before,
        )
        d2_other = swapped(d2_low, "c")
        dup, own, send, up_sum[l] = whole_call(
            feed_back_kernel,
            [sds((2, 2 * t, width), bf16), wide, thin, sums],
            [d2_low, d2_other, *ups, *downs, slope],
        )

        def feed_grad(after, first_low=first_low, first_other=first_other, d2_low=d2_low, d2_other=d2_other, dup=dup, act=act):
            keep, send, there = whole_call(
                feed_grad_kernel, [parted] * 2, [place, first_low, first_other, d2_low, d2_other, dup, act],
                scalars=1, after=after, token=True,
            )
            return (keep, over_y(send)), there

        before = []
        if l == 1:
            feed[l], there = feed_grad([send])
            before = [there]
        d1, d1_low, norm_sum[1 + 2 * l] = whole_call(
            functools.partial(norm_back_kernel, 1 + 2 * l, 3),
            [wide, thin, sums],
            [d2, own, swapped(send, "c"), norm_gains, n1, i1],
            after=before,
        )
        dl = gathered(d1_low)
        before = []
        if l == 1:
            two_rows = sds((2, 32, width), bf16)
            row_keep, row_send, there = whole_call(
                encoded_split_kernel, [two_rows] * 2, [place, encoded_low], scalars=1, after=[d1_low], token=True
            )
            row_near = over_z1(row_send)
            before = [there]
        if l == 0:
            feed[l], there = feed_grad([d1_low])
            stay_row, move_row, there = whole_call(
                encoded_route_kernel, [two_rows] * 2, [place, row_keep, row_near, row_far],
                scalars=1, after=[there], token=True,
            )
            (att_parts[1],), there = send_on([(*att_parts[1], over_z2)], [there])
            before = [there]
        dense_dp, keep, send, att_sum[l] = whole_call(
            attend_back_kernel,
            [sds((full, 640), bf16), two, two, sds((8, 256), f32)],
            dl + [q, k, v, lse, in_w, mix_w, seg_row, seg_col],
            after=before,
            scratch=[pltpu.VMEM((full, 256), bf16)] + [pltpu.VMEM((full, 256), f32)] * 3,
        )
        own, pass_on = whole_call(
            half_sum_kernel, [wide, thin], [keep, swapped(send, "c")],
        )
        rest = swapped(pass_on, "x")
        terms = [d1, own, rest]

        def attend_grad(after, hl=hl, dl=dl, att=att, dense_dp=dense_dp):
            return whole_call(
                attend_grad_kernel, [tiles_z, tiles_z], [place] + hl + dl + [att, dense_dp],
                scalars=1, after=after, token=True,
            )

        keep, send, there = attend_grad([pass_on])
        att_parts[l] = (keep, over_z1(send))
        if l == 1:
            row_send, there = whole_call(onward_kernel, [two_rows], [row_keep, row_near], after=[there], token=True)
            row_far = over_z2(row_send)
        else:
            encoded, there = whole_call(
                encoded_join_kernel, [sds((rows, toks, width), f32)], [place, stay_row, swapped(move_row, "c")], scalars=1,
                scratch=[pltpu.VMEM((width // LANES * toks + 8, LANES), f32)], after=[there], token=True,
            )
        before = [there]

    quad = sds((4, 64, 2 * LANES), bf16)
    ds_keep, ds_sent, norm_sum[0] = whole_call(
        functools.partial(stem_norm_back_kernel, share, len(terms)),
        [quad, quad, sums],
        [place, *terms, norm_gains, normed_stem, inverse_stem],
        scalars=1,
        after=before,
    )

    def spread(keep, send, after):
        pair_shape = sds((2, 2, *keep.shape[1:]), bf16)
        stays, goes, there = whole_call(
            along_z_kernel, [pair_shape] * 2, [keep, swapped(send, "x")], after=after, token=True
        )
        near = over_z1(goes)

        def onward(after):
            (far,) = whole_call(onward_kernel, [pair_shape], [stays, near], after=after)
            return [stays, near, over_z2(far)]

        return there, onward

    gain_count, bias_count = norm_gains.shape[0], biases.shape[0]
    small_half = sds((4, 32, LANES), f32)
    small_keep, small_send, small_there = whole_call(
        functools.partial(smalls_kernel, layers, ff_rows, gain_count, width, head_share),
        [small_half, small_half],
        [place, *norm_sum, *up_sum, *att_sum],
        scalars=1,
        scratch=[pltpu.VMEM((32, width), f32)],
        token=True,
        after=[ds_sent],
    )
    smalls = (small_keep.reshape(2, 2, 32, LANES), swapped(small_send, "x").reshape(2, 2, 32, LANES))
    phases, taps, phases_there = whole_call(
        functools.partial(phases_kernel, rows, frames, half, gw),
        [sds(phased, bf16), sds((KERNEL + 3, LANES, LANES), bf16)], [mine, stem_share], scratch=[row_scratch],
        after=[small_there], token=True,
    )
    (feed[1],), there = send_on([(*feed[1], over_x)], [phases_there])
    there, ds_onward = spread(ds_keep, ds_sent, [there])
    ds_blocks = ds_onward([there])
    att_second, there = whole_call(one_kernel, [tiles], list(att_parts[1]), after=[ds_blocks[1]], token=True)
    (att_parts[0],), there = send_on([(*att_parts[0], over_z2)], [there])
    stay, move, there = whole_call(
        take_kernel, [sds((2, 2, 64, 2 * LANES), bf16)] * 2, [place, *ds_blocks], scalars=1,
        after=[there], token=True,
    )
    pair = sds((rows, n, 2 * LANES), bf16)
    dpre_low, ds, stem_sums = whole_call(
        functools.partial(stem_slope_kernel, rows), [pair, pair, sds((8, LANES), f32)],
        [place, stay, swapped(move, "c"), pre_act], scalars=1, after=[there],
    )
    quarter = sds((2, KERNEL // 4 * gw, LANES), bf16)
    keep, send = whole_call(
        functools.partial(stem_grad_kernel, rows, KERNEL, gw), [quarter, quarter], [place, phases, dpre_low], scalars=1,
    )
    stem_part = (keep, swapped(send, "c"))
    (feed[1], stem_part), there = send_on([(*feed[1], over_z1), (*stem_part, over_y)], [send])
    back_shape = sds((4, rows, toks // 2, 2 * LANES), bf16)
    back_keep, back = whole_call(
        functools.partial(stem_input_grad_kernel, rows, half),
        [back_shape] * 2,
        [place, dpre_low, ds, taps],
        scalars=1,
        scratch=[
            pltpu.VMEM((rows, n + half, 2 * LANES), f32),
            pltpu.VMEM((16, rows, n + half, 2 * LANES), bf16),
            pltpu.VMEM((rows * n, 2 * LANES), f32),
        ],
        after=[there],
        vmem=WIDE_BYTES,
    )
    there, back_onward = spread(back_keep, back, [back])
    (feed[0],), there = send_on([(*feed[0], over_x)], [there])
    back_blocks = back_onward([there])
    att_first, there = whole_call(one_kernel, [tiles], list(att_parts[0]), after=[back_blocks[1]], token=True)
    att_grads = [att_first, att_second]
    (features_gradient,) = whole_call(
        functools.partial(join_kernel, share), [sds((rows, toks, width), f32)], [place, *back_blocks], scalars=1,
        scratch=[
            pltpu.VMEM((width // LANES * toks + 8, LANES), f32),
            pltpu.VMEM((blocks, rows, toks // 2, 2 * LANES), bf16),
        ],
        after=[there],
    )
    (feed[1], smalls), there = send_on([(*feed[1], over_z2), (*smalls, over_z1)], [features_gradient])
    att_came = swapped(jnp.stack([a[5:10] for a in att_grads]), "x")
    (feed[0], smalls), there = send_on([(*feed[0], over_z1), (*smalls, over_z2)], [there])
    olds = whole_call(
        functools.partial(olds_kernel, layers, gw),
        [
            sds((share, KERNEL // 4 * gw), bf16),
            sds((layers, share, 640), bf16),
            sds((layers, share, 256), bf16),
            sds((layers, 2 * share, width), bf16),
        ],
        [place, stem_weight, projection_weight, mixing_weight, feedforward_weight],
        scalars=1, far=(1, 2, 3, 4), vmem=WIDE_BYTES, after=[there], token=True,
        scratch=[
            pltpu.VMEM((KERNEL // 4 * gw, 256), bf16),
            pltpu.VMEM((layers, share, 640), bf16),
            pltpu.VMEM((layers, share, 256), bf16),
            pltpu.VMEM((layers, share, 2, width), bf16),
            pltpu.SemaphoreType.DMA((1 + 3 * layers,)),
        ],
    )
    there = olds[-1]
    small_total, there = whole_call(
        functools.partial(small_total_kernel, gain_count), [sds((32, LANES), f32)], [*smalls, stem_sums],
        after=[there], token=True,
    )
    small_total = one_sum(small_total, swapped(small_total, "c"))
    settled = sds((layers, 4, 2, share, LANES), bf16)
    stay, move, there = whole_call(
        functools.partial(pick_kernel, layers), [settled] * 2, [place, *att_grads, att_came], scalars=1,
        after=[there], token=True,
    )
    (feed[0],), there = send_on([(*feed[0], over_z2)], [there])
    in_part, swap_part, mix_part, there = whole_call(
        functools.partial(settle_kernel, layers),
        [sds((layers, 2, 2, share, LANES), bf16)] + [sds((layers, 2, share, LANES), bf16)] * 2,
        [place, stay, swapped(move, "y")],
        scalars=1, after=[there], token=True,
    )
    swap_part = swapped(swap_part, "c")
    route = []
    for c in range(2):
        for z in range(4):
            for x in range(2):
                route.append(((c * 4 + z) * 2 + x, ((z & 1) * 4 + (2 * x + c)) * 2 + (z >> 1)))
    mix_part = lax.ppermute(mix_part, ("c", "z", "x"), route)
    small_total = one_sum(small_total, swapped(small_total, "y"))
    rate_base = 1.0 / math.sqrt(rows * 4 * frames)

    def step(index, kernel, operands, turn=False):
        m, a = state[index], state[6 + index]
        if turn:
            m, a = m.T, a.T
        made = whole_call(
            functools.partial(kernel, rate_factors[index] * rate_base), [sds(m.shape, f32)] * 3,
            [place, olds[index], *operands, m, a], scalars=1,
        )
        return [o.T for o in made] if turn else made

    results = [
        step(0, lambda f, *r: stem_step_kernel(f, gw, *r), list(stem_part), turn=True),
        step(1, projection_step_kernel, [in_part, swap_part]),
        step(2, mixing_step_kernel, [mix_part]),
        step(3, feed_step_kernel, [part for l in range(layers) for part in feed[l]]),
    ]
    for index, w, g in ((4, norm_gains, small_total[:gain_count]), (5, biases, small_total[gain_count : gain_count + bias_count])):
        w = lax.dynamic_slice_in_dim(w, seq_i * share, share, 1)
        results.append(step_of(rate_factors[index] * rate_base, g[:, :share], state[index], state[6 + index], w))
    return (encoded, features_gradient, *(results[i][k] for k in range(3) for i in range(6)))


def solution(mesh):
    if mesh.shape["row"] == 4 and mesh.shape["seq"] == 8:
        body, mesh = local_rows, Mesh(mesh.devices.reshape(2, 2, 4, 2), ("y", "c", "z", "x"))
        row, seq = ("y", "c"), ("z", "x")
    else:
        body, row, seq = local, "row", "seq"
    in_specs = (
        P(row, seq, None),
        P(row, seq, None),
        P(row, None),
        P(),
        P(),
        P(),
        P(),
        P(),
        P(),
        P(row, seq),
        P(None, seq, row),
        P(None, seq, row),
        P(None, seq, None, row),
        P(None, seq),
        P(None, seq),
        P(row, seq),
        P(None, seq, row),
        P(None, seq, row),
        P(None, seq, None, row),
        P(None, seq),
        P(None, seq),
    )
    out_specs = (
        P(row, seq, None),
        P(row, seq, None),
        P(row, seq),
        P(None, seq, row),
        P(None, seq, row),
        P(None, seq, None, row),
        P(None, seq),
        P(None, seq),
        P(row, seq),
        P(None, seq, row),
        P(None, seq, row),
        P(None, seq, None, row),
        P(None, seq),
        P(None, seq),
        P(row, seq),
        P(None, seq, row),
        P(None, seq, row),
        P(None, seq, None, row),
        P(None, seq),
        P(None, seq),
    )
    return jax.shard_map(body, mesh=mesh, in_specs=in_specs, out_specs=out_specs, check_vma=False)
```
